32 devices in a mesh: grp: 1, head: 16 (over z, x, core), tile: 2 (over y).
Axes of the slice: x: 2, y: 2, z: 4, core: 2. Of those that a mesh axis runs over, the one named last changes fastest.
Arguments:
- attention: bfloat16 [144, 256, 256], P(('grp', 'head'), None, 'tile'), may hold values from 0 to 16, as said below
- proj_weight: bfloat16 [64, 144], replicated, may hold values from -0.5 to 0.5
- proj_bias: float32 [64], replicated, may hold values from -1.8 to 1.8
- conv_weight: bfloat16 [2, 2, 64, 64, 3, 3], replicated, may hold values from -0.25 to 0.25
- conv_bias: float32 [2, 2, 64], replicated, may hold values from -1.8 to 1.8
- out_weight: float32 [64], replicated, may hold values from -0.75 to 0.75
Outputs:
- logits: float32 [256, 256], P(('grp', 'head'), 'tile')
The draws below stay inside these ranges and needn't reach their ends.
Inputs may be any that keep to these rules, and one draw needn't show every extreme that they name: `attention`: every entry is positive.
All inputs are finite; a program needn't handle non-finite values.
Results may differ from the reference program's by a relative error of at most 0.007.
Values may be sent and summed in bfloat16 or wider, within the bound.
No kernel may reach another device: no remote copies, remote signals or barrier semaphores. Data moves between devices by JAX's collectives and lax.ppermute only.
A program may use at most 128 MiB of HBM per device.

```python
import math
import jax
import jax.numpy as jnp
from jax import lax

MAPS = 144
FEAT = 64
BLOCKS = 2
W = 256


def draw_attention(key, part):
    keys = jax.random.split(jax.random.fold_in(key, 17), 4)
    row_scale = jnp.exp(jax.random.uniform(keys[0], (MAPS, W, 1), jnp.float32, 0.0, math.log(10.0)))
    col_scale = jnp.exp(jax.random.uniform(keys[1], (MAPS, 1, W), jnp.float32, 0.0, math.log(10.0)))
    entries = jax.random.uniform(keys[3], (MAPS, W, W), jnp.float32, 0.05, 1.0)
    return (row_scale * col_scale * entries / 16.0).astype(jnp.bfloat16)


def gaussian(key, extent, scale, most, dtype=jnp.bfloat16):
    return jnp.clip(scale * jax.random.normal(key, extent, jnp.float32), -most, most).astype(dtype)


def setup_inputs(seed: int = 0, part: int = 0) -> dict:
    streams_of = jax.random.split(jax.random.key(seed), 7)
    part_splits = jax.random.split(jax.random.fold_in(streams_of[6], part), 7)
    attention = draw_attention(jax.random.fold_in(jax.random.fold_in(streams_of[6], part), 71), part)
    proj_weight = gaussian(streams_of[1], (FEAT, MAPS), MAPS ** -0.5, 0.5)
    proj_bias = gaussian(streams_of[2], (FEAT,), 0.3, 1.8, jnp.float32)
    conv_weight = gaussian(streams_of[3], (BLOCKS, 2, FEAT, FEAT, 3, 3), (9 * FEAT) ** -0.5, 0.25)
    conv_bias = gaussian(streams_of[4], (BLOCKS, 2, FEAT), 0.3, 1.8, jnp.float32)
    out_weight = gaussian(streams_of[5], (FEAT,), FEAT ** -0.5, 0.75, jnp.float32)
    return dict(attention=attention, proj_weight=proj_weight, proj_bias=proj_bias, conv_weight=conv_weight, conv_bias=conv_bias, out_weight=out_weight)


def convolve(field, kernel, offsets):
    result = lax.conv_general_dilated(field[None], kernel.astype(jnp.float32), (1, 1), ((1, 1), (1, 1)), precision=lax.Precision.HIGHEST)[0]
    return result + offsets[:, None, None]


def reference(attention, proj_weight, proj_bias, conv_weight, conv_bias, out_weight):
    values = attention.astype(jnp.float32)
    symmetric = values + jnp.swapaxes(values, 1, 2)
    rowsum = jnp.sum(symmetric, axis=2)
    grand_total = jnp.sum(rowsum, axis=1)
    corrected = (symmetric - rowsum[:, :, None] * rowsum[:, None, :] / grand_total[:, None, None]).astype(jnp.bfloat16)
    stream = jnp.einsum('kc,crs->krs', proj_weight.astype(jnp.float32), corrected.astype(jnp.float32), precision=lax.Precision.HIGHEST)
    stream = (stream + proj_bias[:, None, None]).astype(jnp.bfloat16)
    for layer_index in range(BLOCKS):
        hidden = jax.nn.elu(convolve(stream.astype(jnp.float32), conv_weight[layer_index, 0], conv_bias[layer_index, 0])).astype(jnp.bfloat16)
        update = convolve(hidden.astype(jnp.float32), conv_weight[layer_index, 1], conv_bias[layer_index, 1])
        stream = (stream.astype(jnp.float32) + update).astype(jnp.bfloat16)
    return jnp.einsum('k,krs->rs', out_weight, stream.astype(jnp.float32), precision=lax.Precision.HIGHEST)
```

```python
import functools
from typing import NamedTuple

import jax
import jax.numpy as jnp
import numpy as np
from jax import lax
from jax.experimental import pallas as pl
from jax.experimental.pallas import tpu as pltpu
from jax.sharding import PartitionSpec as P

BF16, F32 = jnp.bfloat16, jnp.float32
LANES = 128
VMEM_LIMIT = 40 * 1024 * 1024


def up(value, step):
    return -(-value // step) * step


class Plan(NamedTuple):
    maps: int
    width: int
    cols: int
    tiles: int
    heads: int
    feat: int
    convs: int

    @property
    def halo(self):
        return self.convs

    @property
    def sides(self):
        return min(2, self.tiles - 1)

    @property
    def edges(self):
        return self.sides * self.halo

    @property
    def edge_rows(self):
        return up(self.maps * self.edges, 8)

    @property
    def map_rows(self):
        return up(self.maps, 16)

    @property
    def tail_rows(self):
        return up((1 + self.tiles) * self.edge_rows + 3 * self.tiles * self.map_rows, 16)

    @property
    def band(self):
        return self.width // self.heads

    @property
    def rows(self):
        return self.band + 2 * self.halo

    @property
    def slots(self):
        return self.cols // self.rows

    @property
    def groups(self):
        return -(-self.maps // self.slots)

    @property
    def side_rows(self):
        return self.groups * self.edges

    @property
    def block_rows(self):
        return up(self.maps * self.rows + self.side_rows, 16)

    @property
    def stride(self):
        return self.cols + 2 * self.halo

    @property
    def start(self):
        return up(self.stride, LANES) - LANES

    @property
    def chunk(self):
        return 256

    @property
    def lanes(self):
        return up(self.start + self.rows * self.stride, LANES) + 2 * self.chunk + 3 * LANES


def edge_start(plan, tile, side):
    left, right = plan.cols * tile - plan.halo, plan.cols * (tile + 1)
    if plan.sides == 1:
        return jnp.where(tile > 0, left, right)
    return (left, right)[side]


def edge_select(plan, tile, row, position, index):
    hit = None
    for side in range(plan.sides):
        first = index * plan.edges + side * plan.halo
        inside = (row >= first) & (row < first + plan.halo)
        one = inside & (position == row - first + edge_start(plan, tile, side))
        hit = one if hit is None else hit | one
    return hit


def across(a, b):
    return lax.dot_general(a, b, (((1,), (1,)), ((), ())), preferred_element_type=F32)


def dot(a, b):
    return jnp.dot(a, b, preferred_element_type=F32)


def mirror_pack(plan, tile_ref, maps_ref, out_ref, sums_ref, edge_ref):
    me = tile_ref[0]
    count, cols, width, tiles = plan.maps, plan.cols, plan.width, plan.tiles
    head, edge = plan.map_rows, plan.edge_rows

    def pick(rows, span, base, tile, index):
        row = lax.broadcasted_iota(jnp.int32, (rows, span), 0)
        position = lax.broadcasted_iota(jnp.int32, (rows, span), 1) + base
        return edge_select(plan, tile, row, position, index).astype(F32)

    def total(span, index):
        return (lax.broadcasted_iota(jnp.int32, (head, span), 0) == index).astype(F32)

    for shift in range(1, tiles):
        dest = lax.rem(me + shift, tiles)
        by_col = by_row = None
        for index in range(count):
            block = maps_ref[index]
            out_ref[shift - 1, index * cols : (index + 1) * cols, :] = maps_ref[
                index, pl.ds(pl.multiple_of(dest * cols, cols), cols), :
            ]
            left = [pick(edge, cols, me * cols, dest, index)]
            upper = [pick(edge, width, 0, dest, index)]
            if shift == 1:
                left.append(total(cols, index))
                upper.append(total(width, index))
                upper.append(pick(edge, width, 0, me, index))
            by_c = across(jnp.concatenate(left, axis=0).astype(BF16), block)
            by_r = dot(jnp.concatenate(upper, axis=0).astype(BF16), block)
            by_col = by_c if by_col is None else by_col + by_c
            by_row = by_r if by_row is None else by_row + by_r
        if shift == 1:
            sums_ref[...] = by_col[edge : edge + head]
            own = pl.ds(pl.multiple_of(me * cols, cols), cols)
            sums_ref[:, own] = sums_ref[:, own] + by_row[edge : edge + head]
            edge_ref[...] = by_row[edge + head :]
            sums = sums_ref[...]
            high = sums.astype(BF16).astype(F32)
            middle = (sums - high).astype(BF16).astype(F32)
            low = sums - high - middle
        pieces = [by_row[:edge]]
        for wide in (by_col[:edge], high, middle, low):
            pieces += [wide[:, k * cols : (k + 1) * cols] for k in range(tiles)]
        used = (1 + tiles) * edge + 3 * tiles * head
        if plan.tail_rows > used:
            pieces.append(jnp.zeros((plan.tail_rows - used, cols), F32))
        out_ref[shift - 1, count * cols :, :] = jnp.concatenate(pieces, axis=0).astype(BF16)


def correct_pack(
    plan, tile_ref, maps_ref, recv_ref, sums_ref, edge_ref, out_ref, field_ref, turned_ref
):
    me = tile_ref[0]
    count, cols, width, tiles = plan.maps, plan.cols, plan.width, plan.tiles
    head, edge, halo = plan.map_rows, plan.edge_rows, plan.halo
    tails = [recv_ref[k, count * cols :, :].astype(F32) for k in range(tiles - 1)]

    rowsum = []
    for b in range(tiles):
        value = sums_ref[:, b * cols : (b + 1) * cols]
        for tail in tails:
            base = (1 + tiles) * edge
            parts = [
                tail[base + (k * tiles + b) * head : base + (k * tiles + b + 1) * head]
                for k in range(3)
            ]
            value = value + ((parts[0] + parts[1]) + parts[2])
        rowsum.append(value)
    grand = sum(jnp.sum(value, axis=1, keepdims=True) for value in rowsum)
    grand = jnp.where(lax.broadcasted_iota(jnp.int32, (head, 1), 0) < count, grand, 1.0)
    scaled = [value / grand for value in rowsum]
    for b in range(tiles):
        square = jnp.concatenate([rowsum[b], jnp.zeros((LANES - head, cols), F32)], axis=0)
        turned_ref[b * cols : (b + 1) * cols, :] = square.T
    mine = scaled[0]
    for b in range(1, tiles):
        mine = jnp.where(me == b, scaled[b], mine)

    eye = (
        lax.broadcasted_iota(jnp.int32, (cols, cols), 0)
        == lax.broadcasted_iota(jnp.int32, (cols, cols), 1)
    ).astype(F32).astype(BF16)
    margin = 8
    for index in range(count):
        field_ref[index, :margin, :] = jnp.zeros((margin, cols), F32)
        field_ref[index, margin + width :, :] = jnp.zeros((margin, cols), F32)
        for b in range(tiles):
            shift = lax.rem(b - me + tiles, tiles)
            other = recv_ref[
                jnp.maximum(shift - 1, 0), index * cols : (index + 1) * cols, :
            ]
            own = maps_ref[index, b * cols : (b + 1) * cols, :]
            mirror = across(eye, jnp.where(shift == 0, own, other))
            column = turned_ref[b * cols : (b + 1) * cols, index : index + 1]
            field_ref[index, margin + b * cols : margin + (b + 1) * cols, :] = (
                own.astype(F32) + mirror - column * mine[index : index + 1]
            )

    strips = []
    for b in range(tiles):
        strip = edge_ref[...]
        for k, tail in enumerate(tails):
            strip = jnp.where(lax.rem(me + k + 1, tiles) == b, tail[:edge], strip)
        for tail in tails:
            strip = strip + tail[(1 + b) * edge : (2 + b) * edge]
        strips.append(strip)
    strip = jnp.concatenate(strips, axis=1)
    wide = jnp.concatenate(scaled, axis=1)
    before = pl.multiple_of(jnp.maximum(me * cols - 8, 0), 8)
    after = pl.multiple_of(jnp.minimum((me + 1) * cols, width - 8), 8)
    left = turned_ref[pl.ds(before, 8), :][8 - halo :]
    right = turned_ref[pl.ds(after, 8), :][:halo]
    if plan.sides == 1:
        beside = jnp.where(me > 0, left, right)
    else:
        beside = jnp.concatenate([left, right], axis=0)
    lines = [
        strip[k * plan.edges : (k + 1) * plan.edges] - beside[:, k : k + 1] * wide[k : k + 1]
        for k in range(count)
    ]
    rows, slots = plan.rows, plan.slots
    stacks = []
    for slot in range(slots):
        members = []
        for group in range(plan.groups):
            k = group * slots + slot
            members.append(lines[k] if k < count else jnp.zeros((plan.edges, width), F32))
        stacks.append(jnp.concatenate(members, axis=0))
    lane = lax.broadcasted_iota(jnp.int32, (plan.side_rows, cols), 1)
    spare = plan.block_rows - count * rows - plan.side_rows
    for h in range(plan.heads):
        first = h * plan.band - halo
        pieces = [field_ref[k, margin + first : margin + first + rows, :] for k in range(count)]
        side = jnp.zeros((plan.side_rows, cols), F32)
        for slot in range(slots):
            moved = pltpu.roll(stacks[slot], (slot * rows - first) % width, 1)[:, :cols]
            side = jnp.where((lane >= slot * rows) & (lane < (slot + 1) * rows), moved, side)
        pieces.append(side)
        if spare:
            pieces.append(jnp.zeros((spare, cols), F32))
        out_ref[h] = jnp.concatenate(pieces, axis=0).astype(BF16)


def shifted(ref, rows, base, offset, size):
    low = offset // LANES * LANES
    rest = offset - low
    if rest == 0:
        return ref[rows, pl.ds(pl.multiple_of(base + low, LANES), size)]
    value = ref[rows, pl.ds(pl.multiple_of(base + low, LANES), size + LANES)]
    return pltpu.roll(value, size + LANES - rest, 1)[:, :size]


def stack(
    plan, recv_ref, proj_ref, side_ref, kernel_ref, vector_ref, mask_ref, out_ref,
    maps_ref, sides_ref, field_ref, stream_ref, hidden_ref, taps_ref, logit_ref,
):
    count, cols, rows, halo = plan.maps, plan.cols, plan.rows, plan.halo
    heads, feat, chunk, stride = plan.heads, plan.feat, plan.chunk, plan.stride
    body = count * rows
    for s in range(heads):
        block = recv_ref[s].astype(F32)
        maps_ref[s * body : (s + 1) * body, :] = block[:body]
        sides_ref[s * plan.side_rows : (s + 1) * plan.side_rows, :] = block[
            body : body + plan.side_rows
        ]
    bias = vector_ref[:, 0:1]

    slots, members = plan.slots, heads * plan.groups
    lane = lax.broadcasted_iota(jnp.int32, (members, cols), 1)
    placed = []
    for first in range(0, plan.edges, slots):
        parts = [jnp.zeros((members, cols), F32) for _ in range(slots)]
        for at in range(min(slots, plan.edges - first)):
            value = sides_ref[pl.ds(first + at, members, stride=plan.edges), :]
            keep = (lane >= at * rows) & (lane < (at + 1) * rows)
            for slot in range(slots):
                moved = value
                if at != slot:
                    moved = pltpu.roll(value, ((at - slot) * rows) % cols, 1)
                parts[slot] = jnp.where(keep, moved, parts[slot])
        stacked = jnp.concatenate(parts, axis=0).astype(BF16)
        placed.append((first, (dot(side_ref[...], stacked) + bias).astype(BF16)))

    key = lax.broadcasted_iota(jnp.int32, (cols, chunk), 0)
    at = sum((key >= k * rows).astype(jnp.int32) for k in range(1, slots + 1))
    base_target = plan.start + (key - at * rows) * stride
    spots = lax.broadcasted_iota(jnp.int32, (cols, chunk), 1)
    chunks = -(-(rows * stride + plan.start) // chunk)

    def place(i, carry):
        here = spots + i * chunk
        value = None
        for first, columns in placed:
            column = at + first
            fits = (at < slots) & (column < plan.edges)
            if plan.sides == 1:
                target = base_target + column
                hit = (here == target) | (here == target + halo + cols)
            else:
                target = base_target + column + jnp.where(column < halo, 0, cols)
                hit = here == target
            one = dot(columns, (hit & fits).astype(F32).astype(BF16))
            value = one if value is None else value + one
        field_ref[:, pl.ds(pl.multiple_of(i * chunk, chunk), chunk)] = value
        return carry

    lax.fori_loop(0, chunks, place, 0)

    weight = proj_ref[...]
    spot = lax.broadcasted_iota(jnp.int32, (feat, cols), 1)
    per = 2
    for r in range(0, rows, per):
        blocks = [
            maps_ref[pl.ds(r + k, heads * count, stride=rows), :].astype(BF16)
            for k in range(per)
        ]
        pair = dot(weight, jnp.concatenate(blocks, axis=1)) + bias
        for k in range(per):
            begin = plan.start + (r + k) * stride + halo
            low, rest = begin // LANES * LANES, begin % LANES
            value = pair[:, k * cols : (k + 1) * cols]
            if rest == 0:
                field_ref[:, low : low + cols] += value
                continue
            value = pltpu.roll(value, rest, 1)
            field_ref[:, low : low + cols] += jnp.where(spot >= rest, value, 0.0)
            field_ref[:, low + cols : low + 2 * cols] += jnp.where(spot < rest, value, 0.0)

    def settle(i, carry):
        here = pl.ds(pl.multiple_of(i * chunk, chunk), chunk)
        stream_ref[:, here] = jnp.where(mask_ref[:, here] > 0, field_ref[:, here], 0.0).astype(BF16)
        return carry

    lax.fori_loop(0, chunks, settle, 0)

    everything = slice(None)
    for n in range(plan.convs):
        source = hidden_ref if n % 2 else stream_ref
        low = (plan.start + (n + 1) * stride) // LANES * LANES
        steps = -(-(plan.start + (rows - n - 1) * stride - low) // chunk)
        offsets = vector_ref[:, n + 1 : n + 2]

        def multiply(i, carry):
            base = low + i * chunk
            window = jnp.concatenate(
                [shifted(source, everything, base, d * stride, chunk) for d in (-1, 0, 1)], axis=0
            )
            taps_ref[:, pl.ds(pl.multiple_of(base, LANES), chunk)] = dot(kernel_ref[n], window)
            return carry

        lax.fori_loop(0, steps, multiply, 0)

        def finish(i, carry):
            base = low + i * chunk
            here = pl.ds(pl.multiple_of(base, LANES), chunk)
            value = taps_ref[feat : 2 * feat, here]
            value = value + shifted(taps_ref, slice(0, feat), base, -1, chunk)
            value = value + shifted(taps_ref, slice(2 * feat, 3 * feat), base, 1, chunk)
            value = value + offsets
            keep = mask_ref[:, here] > 0
            if n % 2 == 0:
                value = jnp.where(value > 0, value, jnp.exp(jnp.minimum(value, 0.0)) - 1.0)
                hidden_ref[:, here] = jnp.where(keep, value, 0.0).astype(BF16)
                return carry
            value = (stream_ref[:, here].astype(F32) + value).astype(BF16)
            if n < plan.convs - 1:
                stream_ref[:, here] = jnp.where(keep, value.astype(F32), 0.0).astype(BF16)
                return carry
            readout = vector_ref[:, plan.convs + 1 : plan.convs + 2]
            logit_ref[0:1, here] = jnp.sum(value.astype(F32) * readout, axis=0, keepdims=True)
            return carry

        lax.fori_loop(0, steps, finish, 0)

    for r in range(plan.band):
        begin = plan.start + (r + halo) * stride + halo
        low = begin // LANES * LANES
        out_ref[r : r + 1, :] = shifted(logit_ref, slice(0, 1), low, begin - low, cols)


def whole(space=pltpu.VMEM):
    return pl.BlockSpec(memory_space=space)


def on_device(attention, proj_weight, proj_bias, conv_weight, conv_bias, out_weight):
    maps, width, cols = attention.shape
    feat = proj_weight.shape[0]
    blocks, convs = conv_weight.shape[:2]
    tiles, heads = lax.axis_size("tile"), lax.axis_size("head")
    plan = Plan(maps, width, cols, tiles, heads, feat, blocks * convs)
    me = lax.axis_index("tile").astype(jnp.int32)
    tile = me.reshape(1)
    params = pltpu.CompilerParams(vmem_limit_bytes=VMEM_LIMIT)

    payload_rows = maps * cols + plan.tail_rows
    payload, sums, edge = pl.pallas_call(
        functools.partial(mirror_pack, plan),
        out_shape=[
            jax.ShapeDtypeStruct((tiles - 1, payload_rows, cols), BF16),
            jax.ShapeDtypeStruct((plan.map_rows, width), F32),
            jax.ShapeDtypeStruct((plan.edge_rows, cols), F32),
        ],
        in_specs=[whole(pltpu.SMEM), whole()],
        out_specs=[whole()] * 3,
        compiler_params=params,
        name="mirror_pack",
    )(tile, attention)
    received = jnp.stack(
        [
            lax.ppermute(payload[s - 1], "tile", [(i, (i + s) % tiles) for i in range(tiles)])
            for s in range(tiles - 1, 0, -1)
        ]
    )

    stride, start = plan.stride, plan.start
    side_weight = proj_weight.reshape(feat, heads, maps)
    side_weight = jnp.pad(side_weight, ((0, 0), (0, 0), (0, plan.groups * plan.slots - maps)))
    side_weight = side_weight.reshape(feat, heads, plan.groups, plan.slots)
    side_weight = side_weight.transpose(0, 3, 1, 2).reshape(feat, -1)
    kernels = conv_weight.transpose(0, 1, 5, 2, 4, 3).reshape(plan.convs, 3 * feat, 3 * feat)
    vectors = jnp.concatenate(
        [proj_bias[None], conv_bias.reshape(-1, feat), out_weight[None]], axis=0
    ).T
    spot = np.arange(plan.lanes) - start
    row = lax.axis_index("head") * plan.band - plan.halo + (spot // stride).astype(np.int32)
    col = me * cols - plan.halo + (spot % stride).astype(np.int32)
    mask = (row >= 0) & (row < width) & (col >= 0) & (col < width)
    mask = mask.astype(F32)[None]

    packed = pl.pallas_call(
        functools.partial(correct_pack, plan),
        out_shape=jax.ShapeDtypeStruct((heads, plan.block_rows, cols), BF16),
        in_specs=[whole(pltpu.SMEM)] + [whole()] * 4,
        out_specs=whole(),
        scratch_shapes=[
            pltpu.VMEM((maps, width + 16, cols), F32),
            pltpu.VMEM((width, LANES), F32),
        ],
        compiler_params=params,
        name="correct_pack",
    )(tile, attention, received, sums, edge)
    grouped = lax.all_to_all(packed, "head", split_axis=0, concat_axis=0, tiled=True)

    return pl.pallas_call(
        functools.partial(stack, plan),
        out_shape=jax.ShapeDtypeStruct((plan.band, cols), F32),
        in_specs=[whole()] * 6,
        out_specs=whole(),
        scratch_shapes=[
            pltpu.VMEM((heads * maps * plan.rows, cols), F32),
            pltpu.VMEM((heads * plan.side_rows, cols), F32),
            pltpu.VMEM((feat, plan.lanes), F32),
            pltpu.VMEM((feat, plan.lanes), BF16),
            pltpu.VMEM((feat, plan.lanes), BF16),
            pltpu.VMEM((3 * feat, plan.lanes), F32),
            pltpu.VMEM((8, plan.lanes), F32),
        ],
        compiler_params=params,
        name="stack",
    )(grouped, proj_weight, side_weight, kernels, vectors, mask)


def solution(mesh):
    return jax.shard_map(
        on_device,
        mesh=mesh,
        in_specs=(P(("grp", "head"), None, "tile"), P(), P(), P(), P(), P()),
        out_specs=P(("grp", "head"), "tile"),
        check_vma=False,
    )
```

```python
import functools
from typing import NamedTuple

import jax
import jax.numpy as jnp
import numpy as np
from jax import lax
from jax.experimental import pallas as pl
from jax.experimental.pallas import tpu as pltpu
from jax.sharding import PartitionSpec as P

BF16, F32 = jnp.bfloat16, jnp.float32
LANES = 128
VMEM_LIMIT = 48 * 1024 * 1024


def up(value, step):
    return -(-value // step) * step


class Plan(NamedTuple):
    maps: int
    width: int
    cols: int
    tiles: int
    heads: int
    feat: int
    convs: int

    @property
    def halo(self):
        return self.convs

    @property
    def sides(self):
        return min(2, self.tiles - 1)

    @property
    def edges(self):
        return self.sides * self.halo

    @property
    def edge_rows(self):
        return up(self.maps * self.edges, 8)

    @property
    def map_rows(self):
        return up(self.maps, 16)

    @property
    def tail_rows(self):
        return up((1 + self.tiles) * self.edge_rows + 3 * self.tiles * self.map_rows, 16)

    @property
    def band(self):
        return self.width // self.heads

    @property
    def rows(self):
        return self.band + 2 * self.halo

    @property
    def slots(self):
        return self.cols // self.rows

    @property
    def groups(self):
        return -(-self.maps // self.slots)

    @property
    def side_rows(self):
        return self.groups * self.edges

    @property
    def block_rows(self):
        return up(self.maps * self.rows + self.side_rows, 16)

    @property
    def stride(self):
        return self.cols + 2 * self.halo

    @property
    def start(self):
        return up(self.stride, LANES) - LANES

    @property
    def chunk(self):
        return 256

    @property
    def lanes(self):
        return up(self.start + self.rows * self.stride, LANES) + 2 * self.chunk + 3 * LANES


def edge_start(plan, tile, side):
    left, right = plan.cols * tile - plan.halo, plan.cols * (tile + 1)
    if plan.sides == 1:
        return jnp.where(tile > 0, left, right)
    return (left, right)[side]


def edge_select(plan, tile, row, position, index):
    hit = None
    for side in range(plan.sides):
        first = index * plan.edges + side * plan.halo
        inside = (row >= first) & (row < first + plan.halo)
        one = inside & (position == row - first + edge_start(plan, tile, side))
        hit = one if hit is None else hit | one
    return hit


def across(a, b):
    return lax.dot_general(a, b, (((1,), (1,)), ((), ())), preferred_element_type=F32)


def dot(a, b):
    return jnp.dot(a, b, preferred_element_type=F32)


def mirror_pack(plan, tile_ref, maps_ref, out_ref, sums_ref, edge_ref):
    me = tile_ref[0]
    count, cols, width, tiles = plan.maps, plan.cols, plan.width, plan.tiles
    head, edge = plan.map_rows, plan.edge_rows

    def pick(rows, span, base, tile, index):
        row = lax.broadcasted_iota(jnp.int32, (rows, span), 0)
        position = lax.broadcasted_iota(jnp.int32, (rows, span), 1) + base
        return edge_select(plan, tile, row, position, index).astype(F32)

    def total(span, index):
        return (lax.broadcasted_iota(jnp.int32, (head, span), 0) == index).astype(F32)

    for shift in range(1, tiles):
        dest = lax.rem(me + shift, tiles)
        by_col = by_row = None
        for index in range(count):
            block = maps_ref[index]
            out_ref[shift - 1, index * cols : (index + 1) * cols, :] = maps_ref[
                index, pl.ds(pl.multiple_of(dest * cols, cols), cols), :
            ]
            left = [pick(edge, cols, me * cols, dest, index)]
            upper = [pick(edge, width, 0, dest, index)]
            if shift == 1:
                left.append(total(cols, index))
                upper.append(total(width, index))
                upper.append(pick(edge, width, 0, me, index))
            by_c = across(jnp.concatenate(left, axis=0).astype(BF16), block)
            by_r = dot(jnp.concatenate(upper, axis=0).astype(BF16), block)
            by_col = by_c if by_col is None else by_col + by_c
            by_row = by_r if by_row is None else by_row + by_r
        if shift == 1:
            sums_ref[...] = by_col[edge : edge + head]
            own = pl.ds(pl.multiple_of(me * cols, cols), cols)
            sums_ref[:, own] = sums_ref[:, own] + by_row[edge : edge + head]
            edge_ref[...] = by_row[edge + head :]
            sums = sums_ref[...]
            high = sums.astype(BF16).astype(F32)
            middle = (sums - high).astype(BF16).astype(F32)
            low = sums - high - middle
        pieces = [by_row[:edge]]
        for wide in (by_col[:edge], high, middle, low):
            pieces += [wide[:, k * cols : (k + 1) * cols] for k in range(tiles)]
        used = (1 + tiles) * edge + 3 * tiles * head
        if plan.tail_rows > used:
            pieces.append(jnp.zeros((plan.tail_rows - used, cols), F32))
        out_ref[shift - 1, count * cols :, :] = jnp.concatenate(pieces, axis=0).astype(BF16)


def correct_pack(
    plan, tile_ref, maps_ref, recv_ref, sums_ref, edge_ref, out_ref, field_ref, turned_ref
):
    me = tile_ref[0]
    count, cols, width, tiles = plan.maps, plan.cols, plan.width, plan.tiles
    head, edge, halo = plan.map_rows, plan.edge_rows, plan.halo
    tails = [recv_ref[k, count * cols :, :].astype(F32) for k in range(tiles - 1)]

    rowsum = []
    for b in range(tiles):
        value = sums_ref[:, b * cols : (b + 1) * cols]
        for tail in tails:
            base = (1 + tiles) * edge
            parts = [
                tail[base + (k * tiles + b) * head : base + (k * tiles + b + 1) * head]
                for k in range(3)
            ]
            value = value + ((parts[0] + parts[1]) + parts[2])
        rowsum.append(value)
    grand = sum(jnp.sum(value, axis=1, keepdims=True) for value in rowsum)
    grand = jnp.where(lax.broadcasted_iota(jnp.int32, (head, 1), 0) < count, grand, 1.0)
    scaled = [value / grand for value in rowsum]
    for b in range(tiles):
        square = jnp.concatenate([rowsum[b], jnp.zeros((LANES - head, cols), F32)], axis=0)
        turned_ref[b * cols : (b + 1) * cols, :] = square.T
    mine = scaled[0]
    for b in range(1, tiles):
        mine = jnp.where(me == b, scaled[b], mine)

    eye = (
        lax.broadcasted_iota(jnp.int32, (cols, cols), 0)
        == lax.broadcasted_iota(jnp.int32, (cols, cols), 1)
    ).astype(F32).astype(BF16)
    margin = 8
    for index in range(count):
        field_ref[index, :margin, :] = jnp.zeros((margin, cols), F32)
        field_ref[index, margin + width :, :] = jnp.zeros((margin, cols), F32)
        for b in range(tiles):
            shift = lax.rem(b - me + tiles, tiles)
            other = recv_ref[
                jnp.maximum(shift - 1, 0), index * cols : (index + 1) * cols, :
            ]
            own = maps_ref[index, b * cols : (b + 1) * cols, :]
            mirror = across(eye, jnp.where(shift == 0, own, other))
            column = turned_ref[b * cols : (b + 1) * cols, index : index + 1]
            field_ref[index, margin + b * cols : margin + (b + 1) * cols, :] = (
                own.astype(F32) + mirror - column * mine[index : index + 1]
            )

    strips = []
    for b in range(tiles):
        strip = edge_ref[...]
        for k, tail in enumerate(tails):
            strip = jnp.where(lax.rem(me + k + 1, tiles) == b, tail[:edge], strip)
        for tail in tails:
            strip = strip + tail[(1 + b) * edge : (2 + b) * edge]
        strips.append(strip)
    strip = jnp.concatenate(strips, axis=1)
    wide = jnp.concatenate(scaled, axis=1)
    before = pl.multiple_of(jnp.maximum(me * cols - 8, 0), 8)
    after = pl.multiple_of(jnp.minimum((me + 1) * cols, width - 8), 8)
    left = turned_ref[pl.ds(before, 8), :][8 - halo :]
    right = turned_ref[pl.ds(after, 8), :][:halo]
    if plan.sides == 1:
        beside = jnp.where(me > 0, left, right)
    else:
        beside = jnp.concatenate([left, right], axis=0)
    lines = [
        strip[k * plan.edges : (k + 1) * plan.edges] - beside[:, k : k + 1] * wide[k : k + 1]
        for k in range(count)
    ]
    rows, slots = plan.rows, plan.slots
    stacks = []
    for slot in range(slots):
        members = []
        for group in range(plan.groups):
            k = group * slots + slot
            members.append(lines[k] if k < count else jnp.zeros((plan.edges, width), F32))
        stacks.append(jnp.concatenate(members, axis=0))
    lane = lax.broadcasted_iota(jnp.int32, (plan.side_rows, cols), 1)
    spare = plan.block_rows - count * rows - plan.side_rows
    for h in range(plan.heads):
        first = h * plan.band - halo
        pieces = [field_ref[k, margin + first : margin + first + rows, :] for k in range(count)]
        side = jnp.zeros((plan.side_rows, cols), F32)
        for slot in range(slots):
            moved = pltpu.roll(stacks[slot], (slot * rows - first) % width, 1)[:, :cols]
            side = jnp.where((lane >= slot * rows) & (lane < (slot + 1) * rows), moved, side)
        pieces.append(side)
        if spare:
            pieces.append(jnp.zeros((spare, cols), F32))
        out_ref[h] = jnp.concatenate(pieces, axis=0).astype(BF16)


def shifted(ref, rows, base, offset, size):
    begin = base + offset
    low = begin // LANES * LANES
    rest = begin - low
    if rest == 0:
        return ref[rows, low : low + size]
    return pltpu.roll(ref[rows, low : low + size + LANES], size + LANES - rest, 1)[:, :size]


def stack(
    plan, recv_ref, proj_ref, side_ref, kernel_ref, vector_ref, mask_ref, spots_ref, out_ref,
    maps_ref, sides_ref, field_ref, stream_ref, hidden_ref, taps_ref, logit_ref,
):
    count, cols, rows, halo = plan.maps, plan.cols, plan.rows, plan.halo
    heads, feat, chunk, stride = plan.heads, plan.feat, plan.chunk, plan.stride
    body = count * rows
    for s in range(heads):
        block = recv_ref[s].astype(F32)
        maps_ref[s * body : (s + 1) * body, :] = block[:body]
        sides_ref[s * plan.side_rows : (s + 1) * plan.side_rows, :] = block[
            body : body + plan.side_rows
        ]
    bias = vector_ref[:, 0:1]

    slots, members = plan.slots, heads * plan.groups
    lane = lax.broadcasted_iota(jnp.int32, (members, cols), 1)
    placed = []
    for first in range(0, plan.edges, slots):
        parts = [jnp.zeros((members, cols), F32) for _ in range(slots)]
        for at in range(min(slots, plan.edges - first)):
            value = sides_ref[pl.ds(first + at, members, stride=plan.edges), :]
            keep = (lane >= at * rows) & (lane < (at + 1) * rows)
            for slot in range(slots):
                moved = value
                if at != slot:
                    moved = pltpu.roll(value, ((at - slot) * rows) % cols, 1)
                parts[slot] = jnp.where(keep, moved, parts[slot])
        stacked = jnp.concatenate(parts, axis=0).astype(BF16)
        placed.append((dot(side_ref[...], stacked) + bias).astype(BF16))

    chunks = -(-(rows * stride + plan.start) // chunk)
    for i in range(chunks):
        here = slice(i * chunk, (i + 1) * chunk)
        field_ref[:, here] = sum(
            dot(columns, spots_ref[k, :, here]) for k, columns in enumerate(placed)
        )

    weight = proj_ref[...]
    spot = lax.broadcasted_iota(jnp.int32, (feat, cols), 1)
    per = 2
    for r in range(0, rows, per):
        blocks = [
            maps_ref[pl.ds(r + k, heads * count, stride=rows), :].astype(BF16)
            for k in range(per)
        ]
        pair = dot(weight, jnp.concatenate(blocks, axis=1)) + bias
        for k in range(per):
            begin = plan.start + (r + k) * stride + halo
            low, rest = begin // LANES * LANES, begin % LANES
            value = pair[:, k * cols : (k + 1) * cols]
            if rest == 0:
                field_ref[:, low : low + cols] += value
                continue
            value = pltpu.roll(value, rest, 1)
            field_ref[:, low : low + cols] += jnp.where(spot >= rest, value, 0.0)
            field_ref[:, low + cols : low + 2 * cols] += jnp.where(spot < rest, value, 0.0)

    for i in range(chunks):
        here = slice(i * chunk, (i + 1) * chunk)
        stream_ref[:, here] = jnp.where(mask_ref[:, here] > 0, field_ref[:, here], 0.0).astype(BF16)

    everything = slice(None)
    for n in range(plan.convs):
        source = hidden_ref if n % 2 else stream_ref
        low = (plan.start + (n + 1) * stride) // LANES * LANES
        steps = -(-(plan.start + (rows - n - 1) * stride - low) // chunk)
        offsets = vector_ref[:, n + 1 : n + 2]

        def multiply(base):
            window = jnp.concatenate(
                [shifted(source, everything, base, d * stride, chunk) for d in (-1, 0, 1)], axis=0
            )
            taps_ref[:, base : base + chunk] = dot(kernel_ref[n], window)

        def finish(base):
            here = slice(base, base + chunk)
            value = taps_ref[feat : 2 * feat, here]
            value = value + shifted(taps_ref, slice(0, feat), base, -1, chunk)
            value = value + shifted(taps_ref, slice(2 * feat, 3 * feat), base, 1, chunk)
            value = value + offsets
            keep = mask_ref[:, here] > 0
            if n % 2 == 0:
                value = jnp.where(value > 0, value, jnp.exp(jnp.minimum(value, 0.0)) - 1.0)
                hidden_ref[:, here] = jnp.where(keep, value, 0.0).astype(BF16)
                return
            value = (stream_ref[:, here].astype(F32) + value).astype(BF16)
            if n < plan.convs - 1:
                stream_ref[:, here] = jnp.where(keep, value.astype(F32), 0.0).astype(BF16)
                return
            readout = vector_ref[:, plan.convs + 1 : plan.convs + 2]
            logit_ref[0:1, here] = jnp.sum(value.astype(F32) * readout, axis=0, keepdims=True)

        for i in range(steps + 1):
            if i < steps:
                multiply(low + i * chunk)
            if i > 0:
                finish(low + (i - 1) * chunk)

    for r in range(plan.band):
        begin = plan.start + (r + halo) * stride + halo
        low = begin // LANES * LANES
        out_ref[r : r + 1, :] = shifted(logit_ref, slice(0, 1), low, begin - low, cols)


def whole(space=pltpu.VMEM):
    return pl.BlockSpec(memory_space=space)


def on_device(attention, proj_weight, proj_bias, conv_weight, conv_bias, out_weight):
    maps, width, cols = attention.shape
    feat = proj_weight.shape[0]
    blocks, convs = conv_weight.shape[:2]
    tiles, heads = lax.axis_size("tile"), lax.axis_size("head")
    plan = Plan(maps, width, cols, tiles, heads, feat, blocks * convs)
    me = lax.axis_index("tile").astype(jnp.int32)
    tile = me.reshape(1)
    params = pltpu.CompilerParams(vmem_limit_bytes=VMEM_LIMIT)

    payload_rows = maps * cols + plan.tail_rows
    payload, sums, edge = pl.pallas_call(
        functools.partial(mirror_pack, plan),
        out_shape=[
            jax.ShapeDtypeStruct((tiles - 1, payload_rows, cols), BF16),
            jax.ShapeDtypeStruct((plan.map_rows, width), F32),
            jax.ShapeDtypeStruct((plan.edge_rows, cols), F32),
        ],
        in_specs=[whole(pltpu.SMEM), whole()],
        out_specs=[whole()] * 3,
        compiler_params=params,
        name="mirror_pack",
    )(tile, attention)
    received = jnp.stack(
        [
            lax.ppermute(payload[s - 1], "tile", [(i, (i + s) % tiles) for i in range(tiles)])
            for s in range(tiles - 1, 0, -1)
        ]
    )

    stride, start = plan.stride, plan.start
    side_weight = proj_weight.reshape(feat, heads, maps)
    side_weight = jnp.pad(side_weight, ((0, 0), (0, 0), (0, plan.groups * plan.slots - maps)))
    side_weight = side_weight.reshape(feat, heads, plan.groups, plan.slots)
    side_weight = side_weight.transpose(0, 3, 1, 2).reshape(feat, -1)
    kernels = conv_weight.transpose(0, 1, 5, 2, 4, 3).reshape(plan.convs, 3 * feat, 3 * feat)
    vectors = jnp.concatenate(
        [proj_bias[None], conv_bias.reshape(-1, feat), out_weight[None]], axis=0
    ).T
    spot = np.arange(plan.lanes) - start
    row = lax.axis_index("head") * plan.band - plan.halo + (spot // stride).astype(np.int32)
    col = me * cols - plan.halo + (spot % stride).astype(np.int32)
    mask = (row >= 0) & (row < width) & (col >= 0) & (col < width)
    mask = mask.astype(F32)[None]

    key = np.arange(cols)
    member, line = key // plan.rows, key % plan.rows
    spots = []
    for first in range(0, plan.edges, plan.slots):
        column = first + member
        fits = (member < plan.slots) & (column < plan.edges)
        places = (0, plan.halo + cols) if plan.sides == 1 else (np.where(column < plan.halo, 0, cols),)
        target = [np.where(fits, start + line * stride + column + p, -1) for p in places]
        hit = [jnp.arange(plan.lanes)[None] == jnp.asarray(p, jnp.int32)[:, None] for p in target]
        spots.append(functools.reduce(jnp.logical_or, hit).astype(BF16))
    spots = jnp.stack(spots)

    packed = pl.pallas_call(
        functools.partial(correct_pack, plan),
        out_shape=jax.ShapeDtypeStruct((heads, plan.block_rows, cols), BF16),
        in_specs=[whole(pltpu.SMEM)] + [whole()] * 4,
        out_specs=whole(),
        scratch_shapes=[
            pltpu.VMEM((maps, width + 16, cols), F32),
            pltpu.VMEM((width, LANES), F32),
        ],
        compiler_params=params,
        name="correct_pack",
    )(tile, attention, received, sums, edge)
    grouped = lax.all_to_all(packed, "head", split_axis=0, concat_axis=0, tiled=True)

    return pl.pallas_call(
        functools.partial(stack, plan),
        out_shape=jax.ShapeDtypeStruct((plan.band, cols), F32),
        in_specs=[whole()] * 7,
        out_specs=whole(),
        scratch_shapes=[
            pltpu.VMEM((heads * maps * plan.rows, cols), F32),
            pltpu.VMEM((heads * plan.side_rows, cols), F32),
            pltpu.VMEM((feat, plan.lanes), F32),
            pltpu.VMEM((feat, plan.lanes), BF16),
            pltpu.VMEM((feat, plan.lanes), BF16),
            pltpu.VMEM((3 * feat, plan.lanes), F32),
            pltpu.VMEM((8, plan.lanes), F32),
        ],
        compiler_params=params,
        name="stack",
    )(grouped, proj_weight, side_weight, kernels, vectors, mask, spots)


def solution(mesh):
    return jax.shard_map(
        on_device,
        mesh=mesh,
        in_specs=(P(("grp", "head"), None, "tile"), P(), P(), P(), P(), P()),
        out_specs=P(("grp", "head"), "tile"),
        check_vma=False,
    )
```

```python
import functools
from typing import NamedTuple

import jax
import jax.numpy as jnp
import numpy as np
from jax import lax
from jax.experimental import pallas as pl
from jax.experimental.pallas import tpu as pltpu
from jax.sharding import PartitionSpec as P

BF16, F32 = jnp.bfloat16, jnp.float32
LANES = 128
VMEM_LIMIT = 48 * 1024 * 1024


def up(value, step):
    return -(-value // step) * step


class Plan(NamedTuple):
    maps: int
    width: int
    cols: int
    tiles: int
    heads: int
    feat: int
    convs: int

    @property
    def halo(self):
        return self.convs

    @property
    def sides(self):
        return min(2, self.tiles - 1)

    @property
    def edges(self):
        return self.sides * self.halo

    @property
    def edge_rows(self):
        return up(self.maps * self.edges, 8)

    @property
    def map_rows(self):
        return up(self.maps, 16)

    @property
    def tail_rows(self):
        return up((1 + self.tiles) * self.edge_rows + 3 * self.tiles * self.map_rows, 16)

    @property
    def band(self):
        return self.width // self.heads

    @property
    def rows(self):
        return self.band + 2 * self.halo

    @property
    def slots(self):
        return self.cols // self.rows

    @property
    def groups(self):
        return -(-self.maps // self.slots)

    @property
    def side_rows(self):
        return self.groups * self.edges

    @property
    def block_rows(self):
        return up(self.maps * self.rows + self.side_rows, 16)

    @property
    def stride(self):
        return self.cols + 2 * self.halo

    @property
    def start(self):
        return up(self.stride, LANES) - LANES

    @property
    def chunk(self):
        return 256

    @property
    def lanes(self):
        return up(self.start + self.rows * self.stride, LANES) + 2 * self.chunk + 3 * LANES


def partner(mine, step, count, back=False):
    if count & (count - 1) == 0:
        return mine ^ step
    return (mine - step if back else mine + step) % count


def edge_start(plan, tile, side):
    left, right = plan.cols * tile - plan.halo, plan.cols * (tile + 1)
    if plan.sides == 1:
        return jnp.where(tile > 0, left, right)
    return (left, right)[side]


def edge_select(plan, tile, row, position, index):
    hit = None
    for side in range(plan.sides):
        first = index * plan.edges + side * plan.halo
        inside = (row >= first) & (row < first + plan.halo)
        one = inside & (position == row - first + edge_start(plan, tile, side))
        hit = one if hit is None else hit | one
    return hit


def across(a, b):
    return lax.dot_general(a, b, (((1,), (1,)), ((), ())), preferred_element_type=F32)


def dot(a, b):
    return jnp.dot(a, b, preferred_element_type=F32)


def mirror_pack(plan, tile_ref, maps_ref, out_ref, sums_ref, edge_ref):
    me = tile_ref[0]
    count, cols, width, tiles = plan.maps, plan.cols, plan.width, plan.tiles
    head, edge = plan.map_rows, plan.edge_rows

    def pick(rows, span, base, tile, index):
        row = lax.broadcasted_iota(jnp.int32, (rows, span), 0)
        position = lax.broadcasted_iota(jnp.int32, (rows, span), 1) + base
        return edge_select(plan, tile, row, position, index).astype(F32)

    def total(span, index):
        return (lax.broadcasted_iota(jnp.int32, (head, span), 0) == index).astype(F32)

    for shift in range(1, tiles):
        dest = lax.rem(me + shift, tiles)
        by_col = by_row = None
        for index in range(count):
            block = maps_ref[index]
            out_ref[shift - 1, index * cols : (index + 1) * cols, :] = maps_ref[
                index, pl.ds(pl.multiple_of(dest * cols, cols), cols), :
            ]
            left = [pick(edge, cols, me * cols, dest, index)]
            upper = [pick(edge, width, 0, dest, index)]
            if shift == 1:
                left.append(total(cols, index))
                upper.append(total(width, index))
                upper.append(pick(edge, width, 0, me, index))
            by_c = across(jnp.concatenate(left, axis=0).astype(BF16), block)
            by_r = dot(jnp.concatenate(upper, axis=0).astype(BF16), block)
            by_col = by_c if by_col is None else by_col + by_c
            by_row = by_r if by_row is None else by_row + by_r
        if shift == 1:
            sums_ref[...] = by_col[edge : edge + head]
            own = pl.ds(pl.multiple_of(me * cols, cols), cols)
            sums_ref[:, own] = sums_ref[:, own] + by_row[edge : edge + head]
            edge_ref[...] = by_row[edge + head :]
            sums = sums_ref[...]
            high = sums.astype(BF16).astype(F32)
            middle = (sums - high).astype(BF16).astype(F32)
            low = sums - high - middle
        pieces = [by_row[:edge]]
        for wide in (by_col[:edge], high, middle, low):
            pieces += [wide[:, k * cols : (k + 1) * cols] for k in range(tiles)]
        used = (1 + tiles) * edge + 3 * tiles * head
        if plan.tail_rows > used:
            pieces.append(jnp.zeros((plan.tail_rows - used, cols), F32))
        out_ref[shift - 1, count * cols :, :] = jnp.concatenate(pieces, axis=0).astype(BF16)


def correct_pack(plan, tile_ref, maps_ref, recv_ref, sums_ref, edge_ref, *refs):
    *out_refs, field_ref, turned_ref = refs
    me, band_index = tile_ref[0], tile_ref[1]
    count, cols, width, tiles = plan.maps, plan.cols, plan.width, plan.tiles
    head, edge, halo = plan.map_rows, plan.edge_rows, plan.halo
    tails = [recv_ref[k, count * cols :, :].astype(F32) for k in range(tiles - 1)]

    rowsum = []
    for b in range(tiles):
        value = sums_ref[:, b * cols : (b + 1) * cols]
        for tail in tails:
            base = (1 + tiles) * edge
            parts = [
                tail[base + (k * tiles + b) * head : base + (k * tiles + b + 1) * head]
                for k in range(3)
            ]
            value = value + ((parts[0] + parts[1]) + parts[2])
        rowsum.append(value)
    grand = sum(jnp.sum(value, axis=1, keepdims=True) for value in rowsum)
    grand = jnp.where(lax.broadcasted_iota(jnp.int32, (head, 1), 0) < count, grand, 1.0)
    scaled = [value / grand for value in rowsum]
    for b in range(tiles):
        square = jnp.concatenate([rowsum[b], jnp.zeros((LANES - head, cols), F32)], axis=0)
        turned_ref[b * cols : (b + 1) * cols, :] = square.T
    mine = scaled[0]
    for b in range(1, tiles):
        mine = jnp.where(me == b, scaled[b], mine)

    eye = (
        lax.broadcasted_iota(jnp.int32, (cols, cols), 0)
        == lax.broadcasted_iota(jnp.int32, (cols, cols), 1)
    ).astype(F32).astype(BF16)
    margin = 8 + halo
    for index in range(count):
        field_ref[index, :16, :] = jnp.zeros((16, cols), F32)
        field_ref[index, width + 8 :, :] = jnp.zeros((16, cols), F32)
        for b in range(tiles):
            shift = lax.rem(b - me + tiles, tiles)
            other = recv_ref[
                jnp.maximum(shift - 1, 0), index * cols : (index + 1) * cols, :
            ]
            own = maps_ref[index, b * cols : (b + 1) * cols, :]
            mirror = across(eye, jnp.where(shift == 0, own, other))
            column = turned_ref[b * cols : (b + 1) * cols, index : index + 1]
            field_ref[index, margin + b * cols : margin + (b + 1) * cols, :] = (
                own.astype(F32) + mirror - column * mine[index : index + 1]
            )

    strips = []
    for b in range(tiles):
        strip = edge_ref[...]
        for k, tail in enumerate(tails):
            strip = jnp.where(lax.rem(me + k + 1, tiles) == b, tail[:edge], strip)
        for tail in tails:
            strip = strip + tail[(1 + b) * edge : (2 + b) * edge]
        strips.append(strip)
    strip = jnp.concatenate(strips, axis=1)
    wide = jnp.concatenate(scaled, axis=1)
    before = pl.multiple_of(jnp.maximum(me * cols - 8, 0), 8)
    after = pl.multiple_of(jnp.minimum((me + 1) * cols, width - 8), 8)
    left = turned_ref[pl.ds(before, 8), :][8 - halo :]
    right = turned_ref[pl.ds(after, 8), :][:halo]
    if plan.sides == 1:
        beside = jnp.where(me > 0, left, right)
    else:
        beside = jnp.concatenate([left, right], axis=0)
    lines = [
        strip[k * plan.edges : (k + 1) * plan.edges] - beside[:, k : k + 1] * wide[k : k + 1]
        for k in range(count)
    ]
    rows, slots = plan.rows, plan.slots
    stacks = []
    for slot in range(slots):
        members = []
        for group in range(plan.groups):
            k = group * slots + slot
            members.append(lines[k] if k < count else jnp.zeros((plan.edges, width), F32))
        stacks.append(jnp.concatenate(members, axis=0))
    lane = lax.broadcasted_iota(jnp.int32, (plan.side_rows, cols), 1)
    spare = plan.block_rows - count * rows - plan.side_rows
    for step, out_ref in enumerate(out_refs):
        first = partner(band_index, step, plan.heads) * plan.band
        pieces = [field_ref[k, pl.ds(pl.multiple_of(first + 8, 8), rows), :] for k in range(count)]
        side = jnp.zeros((plan.side_rows, cols), F32)
        for slot in range(slots):
            amount = lax.rem(slot * rows + halo + width - first, width)
            moved = pltpu.roll(stacks[slot], amount, 1)[:, :cols]
            side = jnp.where((lane >= slot * rows) & (lane < (slot + 1) * rows), moved, side)
        pieces.append(side)
        if spare:
            pieces.append(jnp.zeros((spare, cols), F32))
        out_ref[...] = jnp.concatenate(pieces, axis=0).astype(BF16)


def shifted(ref, rows, base, offset, size):
    begin = base + offset
    low = begin // LANES * LANES
    rest = begin - low
    if rest == 0:
        return ref[rows, low : low + size]
    return pltpu.roll(ref[rows, low : low + size + LANES], size + LANES - rest, 1)[:, :size]


def stack(plan, tile_ref, *refs):
    recv_refs, refs = refs[: plan.heads], refs[plan.heads :]
    proj_ref, side_ref, kernel_ref, vector_ref, mask_ref, spots_ref, out_ref = refs[:7]
    maps_ref, sides_ref, field_ref, stream_ref, hidden_ref, taps_ref, logit_ref = refs[7:]
    count, cols, rows, halo = plan.maps, plan.cols, plan.rows, plan.halo
    heads, feat, chunk, stride = plan.heads, plan.feat, plan.chunk, plan.stride
    body = count * rows
    for step, recv_ref in enumerate(recv_refs):
        block = recv_ref[...].astype(F32)
        s = partner(tile_ref[1], step, heads, back=True)
        maps_ref[pl.ds(pl.multiple_of(s * body, 8), body), :] = block[:body]
        sides_ref[pl.ds(pl.multiple_of(s * plan.side_rows, 8), plan.side_rows), :] = block[
            body : body + plan.side_rows
        ]
    bias = vector_ref[:, 0:1]

    slots, members = plan.slots, heads * plan.groups
    lane = lax.broadcasted_iota(jnp.int32, (members, cols), 1)
    placed = []
    for first in range(0, plan.edges, slots):
        parts = [jnp.zeros((members, cols), F32) for _ in range(slots)]
        for at in range(min(slots, plan.edges - first)):
            value = sides_ref[pl.ds(first + at, members, stride=plan.edges), :]
            keep = (lane >= at * rows) & (lane < (at + 1) * rows)
            for slot in range(slots):
                moved = value
                if at != slot:
                    moved = pltpu.roll(value, ((at - slot) * rows) % cols, 1)
                parts[slot] = jnp.where(keep, moved, parts[slot])
        stacked = jnp.concatenate(parts, axis=0).astype(BF16)
        placed.append((dot(side_ref[...], stacked) + bias).astype(BF16))

    chunks = -(-(rows * stride + plan.start) // chunk)
    for i in range(chunks):
        here = slice(i * chunk, (i + 1) * chunk)
        field_ref[:, here] = sum(
            dot(columns, spots_ref[k, :, here]) for k, columns in enumerate(placed)
        )

    weight = proj_ref[...]
    spot = lax.broadcasted_iota(jnp.int32, (feat, cols), 1)
    per = 2
    for r in range(0, rows, per):
        blocks = [
            maps_ref[pl.ds(r + k, heads * count, stride=rows), :].astype(BF16)
            for k in range(per)
        ]
        pair = dot(weight, jnp.concatenate(blocks, axis=1)) + bias
        for k in range(per):
            begin = plan.start + (r + k) * stride + halo
            low, rest = begin // LANES * LANES, begin % LANES
            value = pair[:, k * cols : (k + 1) * cols]
            if rest == 0:
                field_ref[:, low : low + cols] += value
                continue
            value = pltpu.roll(value, rest, 1)
            field_ref[:, low : low + cols] += jnp.where(spot >= rest, value, 0.0)
            field_ref[:, low + cols : low + 2 * cols] += jnp.where(spot < rest, value, 0.0)

    for i in range(chunks):
        here = slice(i * chunk, (i + 1) * chunk)
        stream_ref[:, here] = jnp.where(mask_ref[:, here] > 0, field_ref[:, here], 0.0).astype(BF16)

    everything = slice(None)
    for n in range(plan.convs):
        source = hidden_ref if n % 2 else stream_ref
        low = (plan.start + (n + 1) * stride) // LANES * LANES
        steps = -(-(plan.start + (rows - n - 1) * stride - low) // chunk)
        offsets = vector_ref[:, n + 1 : n + 2]

        def multiply(base):
            window = jnp.concatenate(
                [shifted(source, everything, base, d * stride, chunk) for d in (-1, 0, 1)], axis=0
            )
            taps_ref[:, base : base + chunk] = dot(kernel_ref[n], window)

        def finish(base):
            here = slice(base, base + chunk)
            value = taps_ref[feat : 2 * feat, here]
            value = value + shifted(taps_ref, slice(0, feat), base, -1, chunk)
            value = value + shifted(taps_ref, slice(2 * feat, 3 * feat), base, 1, chunk)
            value = value + offsets
            keep = mask_ref[:, here] > 0
            if n % 2 == 0:
                value = jnp.where(value > 0, value, jnp.exp(jnp.minimum(value, 0.0)) - 1.0)
                hidden_ref[:, here] = jnp.where(keep, value, 0.0).astype(BF16)
                return
            value = (stream_ref[:, here].astype(F32) + value).astype(BF16)
            if n < plan.convs - 1:
                stream_ref[:, here] = jnp.where(keep, value.astype(F32), 0.0).astype(BF16)
                return
            readout = vector_ref[:, plan.convs + 1 : plan.convs + 2]
            logit_ref[0:1, here] = jnp.sum(value.astype(F32) * readout, axis=0, keepdims=True)

        for i in range(steps + 1):
            if i < steps:
                multiply(low + i * chunk)
            if i > 0:
                finish(low + (i - 1) * chunk)

    for r in range(plan.band):
        begin = plan.start + (r + halo) * stride + halo
        low = begin // LANES * LANES
        out_ref[r : r + 1, :] = shifted(logit_ref, slice(0, 1), low, begin - low, cols)


def whole(space=pltpu.VMEM):
    return pl.BlockSpec(memory_space=space)


def on_device(attention, proj_weight, proj_bias, conv_weight, conv_bias, out_weight):
    maps, width, cols = attention.shape
    feat = proj_weight.shape[0]
    blocks, convs = conv_weight.shape[:2]
    tiles, heads = lax.axis_size("tile"), lax.axis_size("head")
    plan = Plan(maps, width, cols, tiles, heads, feat, blocks * convs)
    me = lax.axis_index("tile").astype(jnp.int32)
    band_index = lax.axis_index("head").astype(jnp.int32)
    tile = jnp.stack([me, band_index])
    params = pltpu.CompilerParams(vmem_limit_bytes=VMEM_LIMIT)

    payload_rows = maps * cols + plan.tail_rows
    payload, sums, edge = pl.pallas_call(
        functools.partial(mirror_pack, plan),
        out_shape=[
            jax.ShapeDtypeStruct((tiles - 1, payload_rows, cols), BF16),
            jax.ShapeDtypeStruct((plan.map_rows, width), F32),
            jax.ShapeDtypeStruct((plan.edge_rows, cols), F32),
        ],
        in_specs=[whole(pltpu.SMEM), whole()],
        out_specs=[whole()] * 3,
        compiler_params=params,
        name="mirror_pack",
    )(tile, attention)
    received = jnp.stack(
        [
            lax.ppermute(payload[s - 1], "tile", [(i, (i + s) % tiles) for i in range(tiles)])
            for s in range(tiles - 1, 0, -1)
        ]
    )

    stride, start = plan.stride, plan.start
    side_weight = proj_weight.reshape(feat, heads, maps)
    side_weight = jnp.pad(side_weight, ((0, 0), (0, 0), (0, plan.groups * plan.slots - maps)))
    side_weight = side_weight.reshape(feat, heads, plan.groups, plan.slots)
    side_weight = side_weight.transpose(0, 3, 1, 2).reshape(feat, -1)
    kernels = conv_weight.transpose(0, 1, 5, 2, 4, 3).reshape(plan.convs, 3 * feat, 3 * feat)
    vectors = jnp.concatenate(
        [proj_bias[None], conv_bias.reshape(-1, feat), out_weight[None]], axis=0
    ).T
    spot = np.arange(plan.lanes) - start
    row = band_index * plan.band - plan.halo + (spot // stride).astype(np.int32)
    col = me * cols - plan.halo + (spot % stride).astype(np.int32)
    mask = (row >= 0) & (row < width) & (col >= 0) & (col < width)
    mask = mask.astype(F32)[None]

    key = np.arange(cols)
    member, line = key // plan.rows, key % plan.rows
    spots = []
    for first in range(0, plan.edges, plan.slots):
        column = first + member
        fits = (member < plan.slots) & (column < plan.edges)
        places = (0, plan.halo + cols) if plan.sides == 1 else (np.where(column < plan.halo, 0, cols),)
        target = [np.where(fits, start + line * stride + column + p, -1) for p in places]
        hit = [jnp.arange(plan.lanes)[None] == jnp.asarray(p, jnp.int32)[:, None] for p in target]
        spots.append(functools.reduce(jnp.logical_or, hit).astype(BF16))
    spots = jnp.stack(spots)

    blocks = pl.pallas_call(
        functools.partial(correct_pack, plan),
        out_shape=[jax.ShapeDtypeStruct((plan.block_rows, cols), BF16)] * heads,
        in_specs=[whole(pltpu.SMEM)] + [whole()] * 4,
        out_specs=[whole()] * heads,
        scratch_shapes=[
            pltpu.VMEM((maps, width + 24, cols), F32),
            pltpu.VMEM((width, LANES), F32),
        ],
        compiler_params=params,
        name="correct_pack",
    )(tile, attention, received, sums, edge)
    grouped = list(blocks)
    for step in sorted(range(1, heads), key=lambda k: -k):
        pairs = [(i, partner(i, step, heads)) for i in range(heads)]
        grouped[step] = lax.ppermute(blocks[step], "head", pairs)

    return pl.pallas_call(
        functools.partial(stack, plan),
        out_shape=jax.ShapeDtypeStruct((plan.band, cols), F32),
        in_specs=[whole(pltpu.SMEM)] + [whole()] * (heads + 6),
        out_specs=whole(),
        scratch_shapes=[
            pltpu.VMEM((heads * maps * plan.rows, cols), F32),
            pltpu.VMEM((heads * plan.side_rows, cols), F32),
            pltpu.VMEM((feat, plan.lanes), F32),
            pltpu.VMEM((feat, plan.lanes), BF16),
            pltpu.VMEM((feat, plan.lanes), BF16),
            pltpu.VMEM((3 * feat, plan.lanes), F32),
            pltpu.VMEM((8, plan.lanes), F32),
        ],
        compiler_params=params,
        name="stack",
    )(tile, *grouped, proj_weight, side_weight, kernels, vectors, mask, spots)


def solution(mesh):
    return jax.shard_map(
        on_device,
        mesh=mesh,
        in_specs=(P(("grp", "head"), None, "tile"), P(), P(), P(), P(), P()),
        out_specs=P(("grp", "head"), "tile"),
        check_vma=False,
    )
```

```python
import functools
from typing import NamedTuple

import jax
import jax.numpy as jnp
import numpy as np
from jax import lax
from jax.experimental import pallas as pl
from jax.experimental.pallas import tpu as pltpu
from jax.sharding import PartitionSpec as P

BF16, F32 = jnp.bfloat16, jnp.float32
LANES = 128
VMEM_LIMIT = 48 * 1024 * 1024


def up(value, step):
    return -(-value // step) * step


class Plan(NamedTuple):
    first: int
    maps: int
    total: int
    width: int
    cols: int
    tiles: int
    heads: int
    feat: int
    convs: int

    @property
    def halo(self):
        return self.convs

    @property
    def sides(self):
        return min(2, self.tiles - 1)

    @property
    def edges(self):
        return self.sides * self.halo

    @property
    def last(self):
        return self.first + self.maps == self.total

    @property
    def edge_rows(self):
        return up(self.maps * self.edges, 8)

    @property
    def map_rows(self):
        return up(self.maps, 16)

    @property
    def tail_rows(self):
        return up((1 + self.tiles) * self.edge_rows + 3 * self.tiles * self.map_rows, 16)

    @property
    def band(self):
        return self.width // self.heads

    @property
    def rows(self):
        return self.band + 2 * self.halo

    @property
    def slots(self):
        return self.cols // self.rows

    @property
    def groups(self):
        return -(-self.total // self.slots)

    @property
    def side_rows(self):
        return self.groups * self.edges

    @property
    def block_rows(self):
        return up(self.maps * self.rows + (self.side_rows if self.last else 0), 16)

    @property
    def stride(self):
        return self.cols + 2 * self.halo

    @property
    def start(self):
        return up(self.stride, LANES) - LANES

    @property
    def chunk(self):
        return 256

    @property
    def lanes(self):
        return up(self.start + self.rows * self.stride, LANES) + 2 * self.chunk + 3 * LANES


def edge_start(plan, tile, side):
    left, right = plan.cols * tile - plan.halo, plan.cols * (tile + 1)
    if plan.sides == 1:
        return jnp.where(tile > 0, left, right)
    return (left, right)[side]


def edge_select(plan, tile, row, position, index):
    hit = None
    for side in range(plan.sides):
        first = index * plan.edges + side * plan.halo
        inside = (row >= first) & (row < first + plan.halo)
        one = inside & (position == row - first + edge_start(plan, tile, side))
        hit = one if hit is None else hit | one
    return hit


def across(a, b):
    return lax.dot_general(a, b, (((1,), (1,)), ((), ())), preferred_element_type=F32)


def dot(a, b):
    return jnp.dot(a, b, preferred_element_type=F32)


def mirror_pack(plan, tile_ref, maps_ref, out_ref, sums_ref, edge_ref):
    me = tile_ref[0]
    count, cols, width, tiles = plan.maps, plan.cols, plan.width, plan.tiles
    head, edge = plan.map_rows, plan.edge_rows

    def pick(rows, span, base, tile, index):
        row = lax.broadcasted_iota(jnp.int32, (rows, span), 0)
        position = lax.broadcasted_iota(jnp.int32, (rows, span), 1) + base
        return edge_select(plan, tile, row, position, index).astype(F32)

    def total(span, index):
        return (lax.broadcasted_iota(jnp.int32, (head, span), 0) == index).astype(F32)

    for shift in range(1, tiles):
        dest = lax.rem(me + shift, tiles)
        by_col = by_row = None
        for index in range(count):
            block = maps_ref[plan.first + index]
            out_ref[shift - 1, index * cols : (index + 1) * cols, :] = maps_ref[
                plan.first + index, pl.ds(pl.multiple_of(dest * cols, cols), cols), :
            ]
            left = [pick(edge, cols, me * cols, dest, index)]
            upper = [pick(edge, width, 0, dest, index)]
            if shift == 1:
                left.append(total(cols, index))
                upper.append(total(width, index))
                upper.append(pick(edge, width, 0, me, index))
            by_c = across(jnp.concatenate(left, axis=0).astype(BF16), block)
            by_r = dot(jnp.concatenate(upper, axis=0).astype(BF16), block)
            by_col = by_c if by_col is None else by_col + by_c
            by_row = by_r if by_row is None else by_row + by_r
        if shift == 1:
            sums_ref[...] = by_col[edge : edge + head]
            own = pl.ds(pl.multiple_of(me * cols, cols), cols)
            sums_ref[:, own] = sums_ref[:, own] + by_row[edge : edge + head]
            edge_ref[...] = by_row[edge + head :]
            sums = sums_ref[...]
            high = sums.astype(BF16).astype(F32)
            middle = (sums - high).astype(BF16).astype(F32)
            low = sums - high - middle
        pieces = [by_row[:edge]]
        for wide in (by_col[:edge], high, middle, low):
            pieces += [wide[:, k * cols : (k + 1) * cols] for k in range(tiles)]
        used = (1 + tiles) * edge + 3 * tiles * head
        if plan.tail_rows > used:
            pieces.append(jnp.zeros((plan.tail_rows - used, cols), F32))
        out_ref[shift - 1, count * cols :, :] = jnp.concatenate(pieces, axis=0).astype(BF16)


def correct_pack(plan, tile_ref, maps_ref, recv_ref, sums_ref, edge_ref, *refs):
    *line_refs, out_ref, field_ref, turned_ref = refs
    me = tile_ref[0]
    count, cols, width, tiles = plan.maps, plan.cols, plan.width, plan.tiles
    head, edge, halo = plan.map_rows, plan.edge_rows, plan.halo
    tails = [recv_ref[k, count * cols :, :].astype(F32) for k in range(tiles - 1)]

    rowsum = []
    for b in range(tiles):
        value = sums_ref[:, b * cols : (b + 1) * cols]
        for tail in tails:
            base = (1 + tiles) * edge
            parts = [
                tail[base + (k * tiles + b) * head : base + (k * tiles + b + 1) * head]
                for k in range(3)
            ]
            value = value + ((parts[0] + parts[1]) + parts[2])
        rowsum.append(value)
    grand = sum(jnp.sum(value, axis=1, keepdims=True) for value in rowsum)
    grand = jnp.where(lax.broadcasted_iota(jnp.int32, (head, 1), 0) < count, grand, 1.0)
    scaled = [value / grand for value in rowsum]
    for b in range(tiles):
        square = jnp.concatenate([rowsum[b], jnp.zeros((LANES - head, cols), F32)], axis=0)
        turned_ref[b * cols : (b + 1) * cols, :] = square.T
    mine = scaled[0]
    for b in range(1, tiles):
        mine = jnp.where(me == b, scaled[b], mine)

    eye = (
        lax.broadcasted_iota(jnp.int32, (cols, cols), 0)
        == lax.broadcasted_iota(jnp.int32, (cols, cols), 1)
    ).astype(F32).astype(BF16)
    margin = 8
    for index in range(count):
        field_ref[index, :margin, :] = jnp.zeros((margin, cols), F32)
        field_ref[index, margin + width :, :] = jnp.zeros((margin, cols), F32)
        for b in range(tiles):
            shift = lax.rem(b - me + tiles, tiles)
            other = recv_ref[
                jnp.maximum(shift - 1, 0), index * cols : (index + 1) * cols, :
            ]
            own = maps_ref[plan.first + index, b * cols : (b + 1) * cols, :]
            mirror = across(eye, jnp.where(shift == 0, own, other))
            column = turned_ref[b * cols : (b + 1) * cols, index : index + 1]
            field_ref[index, margin + b * cols : margin + (b + 1) * cols, :] = (
                own.astype(F32) + mirror - column * mine[index : index + 1]
            )

    strips = []
    for b in range(tiles):
        strip = edge_ref[...]
        for k, tail in enumerate(tails):
            strip = jnp.where(lax.rem(me + k + 1, tiles) == b, tail[:edge], strip)
        for tail in tails:
            strip = strip + tail[(1 + b) * edge : (2 + b) * edge]
        strips.append(strip)
    strip = jnp.concatenate(strips, axis=1)
    wide = jnp.concatenate(scaled, axis=1)
    before = pl.multiple_of(jnp.maximum(me * cols - 8, 0), 8)
    after = pl.multiple_of(jnp.minimum((me + 1) * cols, width - 8), 8)
    left = turned_ref[pl.ds(before, 8), :][8 - halo :]
    right = turned_ref[pl.ds(after, 8), :][:halo]
    if plan.sides == 1:
        beside = jnp.where(me > 0, left, right)
    else:
        beside = jnp.concatenate([left, right], axis=0)
    lines = [
        strip[k * plan.edges : (k + 1) * plan.edges] - beside[:, k : k + 1] * wide[k : k + 1]
        for k in range(count)
    ]
    rows, slots = plan.rows, plan.slots
    if not plan.last:
        line_ref, out_ref = line_refs[-1], out_ref
        filler = plan.edge_rows - count * plan.edges
        if filler:
            lines = lines + [jnp.zeros((filler, width), F32)]
        line_ref[...] = jnp.concatenate(lines, axis=0)
        for h in range(plan.heads):
            first = h * plan.band - halo
            pieces = [field_ref[k, margin + first : margin + first + rows, :] for k in range(count)]
            spare = plan.block_rows - count * rows
            if spare:
                pieces.append(jnp.zeros((spare, cols), F32))
            out_ref[h] = jnp.concatenate(pieces, axis=0).astype(BF16)
        return
    earlier = []
    for line_ref in line_refs:
        value = line_ref[...]
        earlier += [value[k : k + plan.edges] for k in range(0, value.shape[0], plan.edges)]
    lines = earlier[: plan.first] + lines
    stacks = []
    for slot in range(slots):
        members = []
        for group in range(plan.groups):
            k = group * slots + slot
            members.append(lines[k] if k < plan.total else jnp.zeros((plan.edges, width), F32))
        stacks.append(jnp.concatenate(members, axis=0))
    lane = lax.broadcasted_iota(jnp.int32, (plan.side_rows, cols), 1)
    spare = plan.block_rows - count * rows - plan.side_rows
    for h in range(plan.heads):
        first = h * plan.band - halo
        pieces = [field_ref[k, margin + first : margin + first + rows, :] for k in range(count)]
        side = jnp.zeros((plan.side_rows, cols), F32)
        for slot in range(slots):
            moved = pltpu.roll(stacks[slot], (slot * rows - first) % width, 1)[:, :cols]
            side = jnp.where((lane >= slot * rows) & (lane < (slot + 1) * rows), moved, side)
        pieces.append(side)
        if spare:
            pieces.append(jnp.zeros((spare, cols), F32))
        out_ref[h] = jnp.concatenate(pieces, axis=0).astype(BF16)


def shifted(ref, rows, base, offset, size):
    begin = base + offset
    low = begin // LANES * LANES
    rest = begin - low
    if rest == 0:
        return ref[rows, low : low + size]
    return pltpu.roll(ref[rows, low : low + size + LANES], size + LANES - rest, 1)[:, :size]


def project(plan, recv_ref, proj_ref, out_ref, maps_ref):
    body, cols, rows = plan.maps * plan.rows, plan.cols, plan.rows
    for s in range(plan.heads):
        maps_ref[s * body : (s + 1) * body, :] = recv_ref[s].astype(F32)[:body]
    weight = proj_ref[...]
    for r in range(0, rows, 2):
        pair = [
            maps_ref[pl.ds(r + k, plan.heads * plan.maps, stride=rows), :].astype(BF16)
            for k in range(2)
        ]
        out_ref[:, r * cols : (r + 2) * cols] = dot(weight, jnp.concatenate(pair, axis=1))


def stack(
    plan, recv_ref, part_ref, proj_ref, side_ref, kernel_ref, vector_ref, mask_ref, spots_ref,
    out_ref, maps_ref, sides_ref, field_ref, stream_ref, hidden_ref, taps_ref, logit_ref,
):
    count, cols, rows, halo = plan.maps, plan.cols, plan.rows, plan.halo
    heads, feat, chunk, stride = plan.heads, plan.feat, plan.chunk, plan.stride
    body = count * rows
    for s in range(heads):
        block = recv_ref[s].astype(F32)
        maps_ref[s * body : (s + 1) * body, :] = block[:body]
        sides_ref[s * plan.side_rows : (s + 1) * plan.side_rows, :] = block[
            body : body + plan.side_rows
        ]
    bias = vector_ref[:, 0:1]

    slots, members = plan.slots, heads * plan.groups
    lane = lax.broadcasted_iota(jnp.int32, (members, cols), 1)
    placed = []
    for first in range(0, plan.edges, slots):
        parts = [jnp.zeros((members, cols), F32) for _ in range(slots)]
        for at in range(min(slots, plan.edges - first)):
            value = sides_ref[pl.ds(first + at, members, stride=plan.edges), :]
            keep = (lane >= at * rows) & (lane < (at + 1) * rows)
            for slot in range(slots):
                moved = value
                if at != slot:
                    moved = pltpu.roll(value, ((at - slot) * rows) % cols, 1)
                parts[slot] = jnp.where(keep, moved, parts[slot])
        stacked = jnp.concatenate(parts, axis=0).astype(BF16)
        placed.append((dot(side_ref[...], stacked) + bias).astype(BF16))

    chunks = -(-(rows * stride + plan.start) // chunk)
    for i in range(chunks):
        here = slice(i * chunk, (i + 1) * chunk)
        field_ref[:, here] = sum(
            dot(columns, spots_ref[k, :, here]) for k, columns in enumerate(placed)
        )

    weight = proj_ref[...]
    spot = lax.broadcasted_iota(jnp.int32, (feat, cols), 1)
    per = 2
    for r in range(0, rows, per):
        blocks = [
            maps_ref[pl.ds(r + k, heads * count, stride=rows), :].astype(BF16)
            for k in range(per)
        ]
        pair = dot(weight, jnp.concatenate(blocks, axis=1)) + bias
        pair = pair + part_ref[:, r * cols : (r + per) * cols]
        for k in range(per):
            begin = plan.start + (r + k) * stride + halo
            low, rest = begin // LANES * LANES, begin % LANES
            value = pair[:, k * cols : (k + 1) * cols]
            if rest == 0:
                field_ref[:, low : low + cols] += value
                continue
            value = pltpu.roll(value, rest, 1)
            field_ref[:, low : low + cols] += jnp.where(spot >= rest, value, 0.0)
            field_ref[:, low + cols : low + 2 * cols] += jnp.where(spot < rest, value, 0.0)

    for i in range(chunks):
        here = slice(i * chunk, (i + 1) * chunk)
        stream_ref[:, here] = jnp.where(mask_ref[:, here] > 0, field_ref[:, here], 0.0).astype(BF16)

    everything = slice(None)
    for n in range(plan.convs):
        source = hidden_ref if n % 2 else stream_ref
        low = (plan.start + (n + 1) * stride) // LANES * LANES
        steps = -(-(plan.start + (rows - n - 1) * stride - low) // chunk)
        offsets = vector_ref[:, n + 1 : n + 2]

        def multiply(base):
            window = jnp.concatenate(
                [shifted(source, everything, base, d * stride, chunk) for d in (-1, 0, 1)], axis=0
            )
            taps_ref[:, base : base + chunk] = dot(kernel_ref[n], window)

        def finish(base):
            here = slice(base, base + chunk)
            value = taps_ref[feat : 2 * feat, here]
            value = value + shifted(taps_ref, slice(0, feat), base, -1, chunk)
            value = value + shifted(taps_ref, slice(2 * feat, 3 * feat), base, 1, chunk)
            value = value + offsets
            keep = mask_ref[:, here] > 0
            if n % 2 == 0:
                value = jnp.where(value > 0, value, jnp.exp(jnp.minimum(value, 0.0)) - 1.0)
                hidden_ref[:, here] = jnp.where(keep, value, 0.0).astype(BF16)
                return
            value = (stream_ref[:, here].astype(F32) + value).astype(BF16)
            if n < plan.convs - 1:
                stream_ref[:, here] = jnp.where(keep, value.astype(F32), 0.0).astype(BF16)
                return
            readout = vector_ref[:, plan.convs + 1 : plan.convs + 2]
            logit_ref[0:1, here] = jnp.sum(value.astype(F32) * readout, axis=0, keepdims=True)

        for i in range(steps + 1):
            if i < steps:
                multiply(low + i * chunk)
            if i > 0:
                finish(low + (i - 1) * chunk)

    for r in range(plan.band):
        begin = plan.start + (r + halo) * stride + halo
        low = begin // LANES * LANES
        out_ref[r : r + 1, :] = shifted(logit_ref, slice(0, 1), low, begin - low, cols)


def whole(space=pltpu.VMEM):
    return pl.BlockSpec(memory_space=space)


def on_device(attention, proj_weight, proj_bias, conv_weight, conv_bias, out_weight):
    maps, width, cols = attention.shape
    feat = proj_weight.shape[0]
    blocks, convs = conv_weight.shape[:2]
    tiles, heads = lax.axis_size("tile"), lax.axis_size("head")
    plans = [
        Plan(first, count, maps, width, cols, tiles, heads, feat, blocks * convs)
        for first, count in ((0, maps // 2), (maps // 2, maps - maps // 2))
    ]
    plan = plans[-1]
    me = lax.axis_index("tile").astype(jnp.int32)
    tile = me.reshape(1)
    params = pltpu.CompilerParams(vmem_limit_bytes=VMEM_LIMIT)

    mirrored = []
    for part in plans:
        payload, sums, edge = pl.pallas_call(
            functools.partial(mirror_pack, part),
            out_shape=[
                jax.ShapeDtypeStruct((tiles - 1, part.maps * cols + part.tail_rows, cols), BF16),
                jax.ShapeDtypeStruct((part.map_rows, width), F32),
                jax.ShapeDtypeStruct((part.edge_rows, cols), F32),
            ],
            in_specs=[whole(pltpu.SMEM), whole()],
            out_specs=[whole()] * 3,
            compiler_params=params,
            name="mirror_pack",
        )(tile, attention)
        received = jnp.stack(
            [
                lax.ppermute(payload[s - 1], "tile", [(i, (i + s) % tiles) for i in range(tiles)])
                for s in range(tiles - 1, 0, -1)
            ]
        )
        mirrored.append((received, sums, edge))

    grouped, lines = [], []
    for part, arrays in zip(plans, mirrored):
        shapes = [jax.ShapeDtypeStruct((heads, part.block_rows, cols), BF16)]
        if not part.last:
            shapes.insert(0, jax.ShapeDtypeStruct((part.edge_rows, width), F32))
        *line, packed = pl.pallas_call(
            functools.partial(correct_pack, part),
            out_shape=shapes,
            in_specs=[whole(pltpu.SMEM)] + [whole()] * (4 + len(lines)),
            out_specs=[whole()] * len(shapes),
            scratch_shapes=[
                pltpu.VMEM((part.maps, width + 16, cols), F32),
                pltpu.VMEM((width, LANES), F32),
            ],
            compiler_params=params,
            name="correct_pack",
        )(tile, attention, *arrays, *lines)
        lines += line
        grouped.append(lax.all_to_all(packed, "head", split_axis=0, concat_axis=0, tiled=True))

    stride, start = plan.stride, plan.start
    side_weight = proj_weight.reshape(feat, heads, maps)
    side_weight = jnp.pad(side_weight, ((0, 0), (0, 0), (0, plan.groups * plan.slots - maps)))
    side_weight = side_weight.reshape(feat, heads, plan.groups, plan.slots)
    side_weight = side_weight.transpose(0, 3, 1, 2).reshape(feat, -1)
    kernels = conv_weight.transpose(0, 1, 5, 2, 4, 3).reshape(plan.convs, 3 * feat, 3 * feat)
    vectors = jnp.concatenate(
        [proj_bias[None], conv_bias.reshape(-1, feat), out_weight[None]], axis=0
    ).T
    spot = np.arange(plan.lanes) - start
    row = lax.axis_index("head") * plan.band - plan.halo + (spot // stride).astype(np.int32)
    col = me * cols - plan.halo + (spot % stride).astype(np.int32)
    mask = (row >= 0) & (row < width) & (col >= 0) & (col < width)
    mask = mask.astype(F32)[None]

    key = np.arange(cols)
    member, line = key // plan.rows, key % plan.rows
    spots = []
    for first in range(0, plan.edges, plan.slots):
        column = first + member
        fits = (member < plan.slots) & (column < plan.edges)
        places = (0, plan.halo + cols) if plan.sides == 1 else (np.where(column < plan.halo, 0, cols),)
        target = [np.where(fits, start + line * stride + column + p, -1) for p in places]
        hit = [jnp.arange(plan.lanes)[None] == jnp.asarray(p, jnp.int32)[:, None] for p in target]
        spots.append(functools.reduce(jnp.logical_or, hit).astype(BF16))
    spots = jnp.stack(spots)

    by_map = proj_weight.reshape(feat, heads, maps)
    weights = [
        by_map[:, :, part.first : part.first + part.maps].reshape(feat, -1) for part in plans
    ]
    partial = pl.pallas_call(
        functools.partial(project, plans[0]),
        out_shape=jax.ShapeDtypeStruct((feat, plan.rows * cols), F32),
        in_specs=[whole()] * 2,
        out_specs=whole(),
        scratch_shapes=[pltpu.VMEM((heads * plans[0].maps * plan.rows, cols), F32)],
        compiler_params=params,
        name="project",
    )(grouped[0], weights[0])

    return pl.pallas_call(
        functools.partial(stack, plan),
        out_shape=jax.ShapeDtypeStruct((plan.band, cols), F32),
        in_specs=[whole()] * 8,
        out_specs=whole(),
        scratch_shapes=[
            pltpu.VMEM((heads * plan.maps * plan.rows, cols), F32),
            pltpu.VMEM((heads * plan.side_rows, cols), F32),
            pltpu.VMEM((feat, plan.lanes), F32),
            pltpu.VMEM((feat, plan.lanes), BF16),
            pltpu.VMEM((feat, plan.lanes), BF16),
            pltpu.VMEM((3 * feat, plan.lanes), F32),
            pltpu.VMEM((8, plan.lanes), F32),
        ],
        compiler_params=params,
        name="stack",
    )(grouped[1], partial, weights[1], side_weight, kernels, vectors, mask, spots)


def solution(mesh):
    return jax.shard_map(
        on_device,
        mesh=mesh,
        in_specs=(P(("grp", "head"), None, "tile"), P(), P(), P(), P(), P()),
        out_specs=P(("grp", "head"), "tile"),
        check_vma=False,
    )
```

```python
import functools
from typing import NamedTuple

import jax
import jax.numpy as jnp
import numpy as np
from jax import lax
from jax.experimental import pallas as pl
from jax.experimental.pallas import tpu as pltpu
from jax.sharding import PartitionSpec as P

BF16, F32 = jnp.bfloat16, jnp.float32
LANES = 128
VMEM_LIMIT = 48 * 1024 * 1024


def up(value, step):
    return -(-value // step) * step


class Plan(NamedTuple):
    maps: int
    width: int
    cols: int
    tiles: int
    heads: int
    feat: int
    convs: int

    @property
    def halo(self):
        return self.convs

    @property
    def sides(self):
        return min(2, self.tiles - 1)

    @property
    def edges(self):
        return self.sides * self.halo

    @property
    def edge_rows(self):
        return up(self.maps * self.edges, 8)

    @property
    def map_rows(self):
        return up(self.maps, 16)

    @property
    def tail_rows(self):
        return up((1 + self.tiles) * self.edge_rows + 3 * self.tiles * self.map_rows, 16)

    @property
    def band(self):
        return self.width // self.heads

    @property
    def rows(self):
        return self.band + 2 * self.halo

    @property
    def slots(self):
        return self.cols // self.rows

    @property
    def groups(self):
        return -(-self.maps // self.slots)

    @property
    def side_rows(self):
        return self.groups * self.edges

    @property
    def chips(self):
        return self.heads // 2

    @property
    def lone(self):
        return self.band // 8

    @property
    def shared(self):
        return 2 * self.halo // 8

    @property
    def group_rows(self):
        return 8 * self.maps

    @property
    def lead(self):
        return self.lone * self.group_rows + self.side_rows

    @property
    def half_rows(self):
        return self.lead + self.shared * self.group_rows

    @property
    def block_rows(self):
        return up(self.lead + self.half_rows, 16)

    @property
    def stride(self):
        return self.cols + 2 * self.halo

    @property
    def start(self):
        return up(self.stride, LANES) - LANES

    @property
    def chunk(self):
        return 256

    @property
    def lanes(self):
        return up(self.start + self.rows * self.stride, LANES) + 2 * self.chunk + 3 * LANES


def partner(mine, step, count, back=False):
    if count & (count - 1) == 0:
        return mine ^ step
    return (mine - step if back else mine + step) % count


def half(plan, block, core):
    return jnp.where(
        core == 0, block[: plan.half_rows], block[plan.lead : plan.lead + plan.half_rows]
    )


def edge_start(plan, tile, side):
    left, right = plan.cols * tile - plan.halo, plan.cols * (tile + 1)
    if plan.sides == 1:
        return jnp.where(tile > 0, left, right)
    return (left, right)[side]


def edge_select(plan, tile, row, position, index):
    hit = None
    for side in range(plan.sides):
        first = index * plan.edges + side * plan.halo
        inside = (row >= first) & (row < first + plan.halo)
        one = inside & (position == row - first + edge_start(plan, tile, side))
        hit = one if hit is None else hit | one
    return hit


def across(a, b):
    return lax.dot_general(a, b, (((1,), (1,)), ((), ())), preferred_element_type=F32)


def dot(a, b):
    return jnp.dot(a, b, preferred_element_type=F32)


def mirror_pack(plan, tile_ref, maps_ref, out_ref, sums_ref, edge_ref):
    me = tile_ref[0]
    count, cols, width, tiles = plan.maps, plan.cols, plan.width, plan.tiles
    head, edge = plan.map_rows, plan.edge_rows

    def pick(rows, span, base, tile, index):
        row = lax.broadcasted_iota(jnp.int32, (rows, span), 0)
        position = lax.broadcasted_iota(jnp.int32, (rows, span), 1) + base
        return edge_select(plan, tile, row, position, index).astype(F32)

    def total(span, index):
        return (lax.broadcasted_iota(jnp.int32, (head, span), 0) == index).astype(F32)

    for shift in range(1, tiles):
        dest = lax.rem(me + shift, tiles)
        by_col = by_row = None
        for index in range(count):
            block = maps_ref[index]
            out_ref[shift - 1, index * cols : (index + 1) * cols, :] = maps_ref[
                index, pl.ds(pl.multiple_of(dest * cols, cols), cols), :
            ]
            left = [pick(edge, cols, me * cols, dest, index)]
            upper = [pick(edge, width, 0, dest, index)]
            if shift == 1:
                left.append(total(cols, index))
                upper.append(total(width, index))
                upper.append(pick(edge, width, 0, me, index))
            by_c = across(jnp.concatenate(left, axis=0).astype(BF16), block)
            by_r = dot(jnp.concatenate(upper, axis=0).astype(BF16), block)
            by_col = by_c if by_col is None else by_col + by_c
            by_row = by_r if by_row is None else by_row + by_r
        if shift == 1:
            sums_ref[...] = by_col[edge : edge + head]
            own = pl.ds(pl.multiple_of(me * cols, cols), cols)
            sums_ref[:, own] = sums_ref[:, own] + by_row[edge : edge + head]
            edge_ref[...] = by_row[edge + head :]
            sums = sums_ref[...]
            high = sums.astype(BF16).astype(F32)
            middle = (sums - high).astype(BF16).astype(F32)
            low = sums - high - middle
        pieces = [by_row[:edge]]
        for wide in (by_col[:edge], high, middle, low):
            pieces += [wide[:, k * cols : (k + 1) * cols] for k in range(tiles)]
        used = (1 + tiles) * edge + 3 * tiles * head
        if plan.tail_rows > used:
            pieces.append(jnp.zeros((plan.tail_rows - used, cols), F32))
        out_ref[shift - 1, count * cols :, :] = jnp.concatenate(pieces, axis=0).astype(BF16)


def correct_pack(plan, tile_ref, maps_ref, recv_ref, sums_ref, edge_ref, *refs):
    *out_refs, field_ref, turned_ref = refs
    me, chip = tile_ref[0], tile_ref[1] // 2
    count, cols, width, tiles = plan.maps, plan.cols, plan.width, plan.tiles
    head, edge, halo = plan.map_rows, plan.edge_rows, plan.halo
    tails = [recv_ref[k, count * cols :, :].astype(F32) for k in range(tiles - 1)]

    rowsum = []
    for b in range(tiles):
        value = sums_ref[:, b * cols : (b + 1) * cols]
        for tail in tails:
            base = (1 + tiles) * edge
            parts = [
                tail[base + (k * tiles + b) * head : base + (k * tiles + b + 1) * head]
                for k in range(3)
            ]
            value = value + ((parts[0] + parts[1]) + parts[2])
        rowsum.append(value)
    grand = sum(jnp.sum(value, axis=1, keepdims=True) for value in rowsum)
    grand = jnp.where(lax.broadcasted_iota(jnp.int32, (head, 1), 0) < count, grand, 1.0)
    scaled = [value / grand for value in rowsum]
    for b in range(tiles):
        square = jnp.concatenate([rowsum[b], jnp.zeros((LANES - head, cols), F32)], axis=0)
        turned_ref[b * cols : (b + 1) * cols, :] = square.T
    mine = scaled[0]
    for b in range(1, tiles):
        mine = jnp.where(me == b, scaled[b], mine)

    eye = (
        lax.broadcasted_iota(jnp.int32, (cols, cols), 0)
        == lax.broadcasted_iota(jnp.int32, (cols, cols), 1)
    ).astype(F32).astype(BF16)
    margin = 8 + halo
    for index in range(count):
        field_ref[index, :16, :] = jnp.zeros((16, cols), F32)
        field_ref[index, width + 8 :, :] = jnp.zeros((16, cols), F32)
        for b in range(tiles):
            shift = lax.rem(b - me + tiles, tiles)
            other = recv_ref[
                jnp.maximum(shift - 1, 0), index * cols : (index + 1) * cols, :
            ]
            own = maps_ref[index, b * cols : (b + 1) * cols, :]
            mirror = across(eye, jnp.where(shift == 0, own, other))
            column = turned_ref[b * cols : (b + 1) * cols, index : index + 1]
            field_ref[index, margin + b * cols : margin + (b + 1) * cols, :] = (
                own.astype(F32) + mirror - column * mine[index : index + 1]
            )

    strips = []
    for b in range(tiles):
        strip = edge_ref[...]
        for k, tail in enumerate(tails):
            strip = jnp.where(lax.rem(me + k + 1, tiles) == b, tail[:edge], strip)
        for tail in tails:
            strip = strip + tail[(1 + b) * edge : (2 + b) * edge]
        strips.append(strip)
    strip = jnp.concatenate(strips, axis=1)
    wide = jnp.concatenate(scaled, axis=1)
    before = pl.multiple_of(jnp.maximum(me * cols - 8, 0), 8)
    after = pl.multiple_of(jnp.minimum((me + 1) * cols, width - 8), 8)
    left = turned_ref[pl.ds(before, 8), :][8 - halo :]
    right = turned_ref[pl.ds(after, 8), :][:halo]
    if plan.sides == 1:
        beside = jnp.where(me > 0, left, right)
    else:
        beside = jnp.concatenate([left, right], axis=0)
    lines = [
        strip[k * plan.edges : (k + 1) * plan.edges] - beside[:, k : k + 1] * wide[k : k + 1]
        for k in range(count)
    ]
    rows, slots = plan.rows, plan.slots
    stacks = []
    for slot in range(slots):
        members = []
        for group in range(plan.groups):
            k = group * slots + slot
            members.append(lines[k] if k < count else jnp.zeros((plan.edges, width), F32))
        stacks.append(jnp.concatenate(members, axis=0))
    lane = lax.broadcasted_iota(jnp.int32, (plan.side_rows, cols), 1)
    spare = plan.block_rows - plan.lead - plan.half_rows
    for step, out_ref in zip(reversed(range(plan.chips)), out_refs):
        first = partner(chip, step, plan.chips) * 2 * plan.band
        groups = [
            field_ref[k, pl.ds(pl.multiple_of(first + 8 + 8 * group, 8), 8), :]
            for group in range(2 * plan.lone + plan.shared)
            for k in range(count)
        ]
        sides = []
        for core in range(2):
            side = jnp.zeros((plan.side_rows, cols), F32)
            for slot in range(slots):
                amount = lax.rem(slot * rows + halo + width - core * plan.band - first, width)
                moved = pltpu.roll(stacks[slot], amount, 1)[:, :cols]
                side = jnp.where((lane >= slot * rows) & (lane < (slot + 1) * rows), moved, side)
            sides.append(side)
        lone = plan.lone * count
        pieces = groups[:lone] + sides[:1] + groups[lone:] + sides[1:]
        if spare:
            pieces.append(jnp.zeros((spare, cols), F32))
        out_ref[...] = jnp.concatenate(pieces, axis=0).astype(BF16)


def core_pack(plan, tile_ref, *refs):
    *block_refs, out_ref = refs
    other = 1 - tile_ref[1] % 2
    for k, block_ref in enumerate(block_refs):
        out_ref[k] = half(plan, block_ref[...].astype(F32), other).astype(BF16)


def shifted(ref, rows, base, offset, size):
    begin = base + offset
    low = begin // LANES * LANES
    rest = begin - low
    if rest == 0:
        return ref[rows, low : low + size]
    return pltpu.roll(ref[rows, low : low + size + LANES], size + LANES - rest, 1)[:, :size]


def stack(plan, order, tile_ref, *refs):
    chips = plan.chips
    own_refs, swap_refs, refs = refs[:chips], refs[chips : chips + len(order)], refs[chips + len(order) :]
    proj_ref, side_ref, kernel_ref, vector_ref, mask_ref, spots_ref, out_ref = refs[:7]
    maps_ref, sides_ref, field_ref, stream_ref, hidden_ref, taps_ref, logit_ref = refs[7:]
    count, cols, rows, halo = plan.maps, plan.cols, plan.rows, plan.halo
    heads, feat, chunk, stride = plan.heads, plan.feat, plan.chunk, plan.stride
    chip, core = tile_ref[1] // 2, tile_ref[1] % 2
    group = plan.group_rows

    def spread(block, source):
        for k in range(plan.lone + plan.shared):
            value = block[k * group : (k + 1) * group]
            if k >= plan.lone:
                late = block[plan.side_rows + k * group : plan.side_rows + (k + 1) * group]
                value = jnp.where(core == 0, late, value)
            place = pl.multiple_of((k * heads + source) * group, 8)
            maps_ref[pl.ds(place, group), :] = value
        side = jnp.where(
            core == 0,
            block[plan.lone * group : plan.lead],
            block[plan.half_rows - plan.side_rows : plan.half_rows],
        )
        place = pl.multiple_of(source * plan.side_rows, 8)
        sides_ref[pl.ds(place, plan.side_rows), :] = side

    for steps, swap_ref in zip(order, swap_refs):
        for k, step in enumerate(steps):
            source = 2 * partner(chip, step, chips, back=True)
            spread(half(plan, own_refs[chips - 1 - step][...].astype(F32), core), source + core)
            spread(swap_ref[k].astype(F32), source + 1 - core)
    bias = vector_ref[:, 0:1]

    slots, members = plan.slots, heads * plan.groups
    lane = lax.broadcasted_iota(jnp.int32, (members, cols), 1)
    placed = []
    for first in range(0, plan.edges, slots):
        parts = [jnp.zeros((members, cols), F32) for _ in range(slots)]
        for at in range(min(slots, plan.edges - first)):
            value = sides_ref[pl.ds(first + at, members, stride=plan.edges), :]
            keep = (lane >= at * rows) & (lane < (at + 1) * rows)
            for slot in range(slots):
                moved = value
                if at != slot:
                    moved = pltpu.roll(value, ((at - slot) * rows) % cols, 1)
                parts[slot] = jnp.where(keep, moved, parts[slot])
        stacked = jnp.concatenate(parts, axis=0).astype(BF16)
        placed.append((dot(side_ref[...], stacked) + bias).astype(BF16))

    chunks = -(-(rows * stride + plan.start) // chunk)
    for i in range(chunks):
        here = slice(i * chunk, (i + 1) * chunk)
        field_ref[:, here] = sum(
            dot(columns, spots_ref[k, :, here]) for k, columns in enumerate(placed)
        )

    weight = proj_ref[...]
    spot = lax.broadcasted_iota(jnp.int32, (feat, cols), 1)
    per = 2
    for r in range(0, rows, per):
        blocks = [
            maps_ref[
                pl.ds((r + k) // 8 * heads * group + (r + k) % 8, heads * count, stride=8), :
            ].astype(BF16)
            for k in range(per)
        ]
        pair = dot(weight, jnp.concatenate(blocks, axis=1)) + bias
        for k in range(per):
            begin = plan.start + (r + k) * stride + halo
            low, rest = begin // LANES * LANES, begin % LANES
            value = pair[:, k * cols : (k + 1) * cols]
            if rest == 0:
                field_ref[:, low : low + cols] += value
                continue
            value = pltpu.roll(value, rest, 1)
            field_ref[:, low : low + cols] += jnp.where(spot >= rest, value, 0.0)
            field_ref[:, low + cols : low + 2 * cols] += jnp.where(spot < rest, value, 0.0)

    for i in range(chunks):
        here = slice(i * chunk, (i + 1) * chunk)
        stream_ref[:, here] = jnp.where(mask_ref[:, here] > 0, field_ref[:, here], 0.0).astype(BF16)

    everything = slice(None)
    for n in range(plan.convs):
        source = hidden_ref if n % 2 else stream_ref
        low = (plan.start + (n + 1) * stride) // LANES * LANES
        steps = -(-(plan.start + (rows - n - 1) * stride - low) // chunk)
        offsets = vector_ref[:, n + 1 : n + 2]

        def multiply(base):
            window = jnp.concatenate(
                [shifted(source, everything, base, d * stride, chunk) for d in (-1, 0, 1)], axis=0
            )
            taps_ref[:, base : base + chunk] = dot(kernel_ref[n], window)

        def finish(base):
            here = slice(base, base + chunk)
            value = taps_ref[feat : 2 * feat, here]
            value = value + shifted(taps_ref, slice(0, feat), base, -1, chunk)
            value = value + shifted(taps_ref, slice(2 * feat, 3 * feat), base, 1, chunk)
            value = value + offsets
            keep = mask_ref[:, here] > 0
            if n % 2 == 0:
                value = jnp.where(value > 0, value, jnp.exp(jnp.minimum(value, 0.0)) - 1.0)
                hidden_ref[:, here] = jnp.where(keep, value, 0.0).astype(BF16)
                return
            value = (stream_ref[:, here].astype(F32) + value).astype(BF16)
            if n < plan.convs - 1:
                stream_ref[:, here] = jnp.where(keep, value.astype(F32), 0.0).astype(BF16)
                return
            readout = vector_ref[:, plan.convs + 1 : plan.convs + 2]
            logit_ref[0:1, here] = jnp.sum(value.astype(F32) * readout, axis=0, keepdims=True)

        for i in range(steps + 1):
            if i < steps:
                multiply(low + i * chunk)
            if i > 0:
                finish(low + (i - 1) * chunk)

    for r in range(plan.band):
        begin = plan.start + (r + halo) * stride + halo
        low = begin // LANES * LANES
        out_ref[r : r + 1, :] = shifted(logit_ref, slice(0, 1), low, begin - low, cols)


def whole(space=pltpu.VMEM):
    return pl.BlockSpec(memory_space=space)


def on_device(attention, proj_weight, proj_bias, conv_weight, conv_bias, out_weight):
    maps, width, cols = attention.shape
    feat = proj_weight.shape[0]
    blocks, convs = conv_weight.shape[:2]
    tiles, heads = lax.axis_size("tile"), lax.axis_size("head")
    plan = Plan(maps, width, cols, tiles, heads, feat, blocks * convs)
    me = lax.axis_index("tile").astype(jnp.int32)
    band_index = lax.axis_index("head").astype(jnp.int32)
    tile = jnp.stack([me, band_index])
    params = pltpu.CompilerParams(vmem_limit_bytes=VMEM_LIMIT)

    payload_rows = maps * cols + plan.tail_rows
    payload, sums, edge = pl.pallas_call(
        functools.partial(mirror_pack, plan),
        out_shape=[
            jax.ShapeDtypeStruct((tiles - 1, payload_rows, cols), BF16),
            jax.ShapeDtypeStruct((plan.map_rows, width), F32),
            jax.ShapeDtypeStruct((plan.edge_rows, cols), F32),
        ],
        in_specs=[whole(pltpu.SMEM), whole()],
        out_specs=[whole()] * 3,
        compiler_params=params,
        name="mirror_pack",
    )(tile, attention)
    received = jnp.stack(
        [
            lax.ppermute(payload[s - 1], "tile", [(i, (i + s) % tiles) for i in range(tiles)])
            for s in range(tiles - 1, 0, -1)
        ]
    )

    stride, start = plan.stride, plan.start
    side_weight = proj_weight.reshape(feat, heads, maps)
    side_weight = jnp.pad(side_weight, ((0, 0), (0, 0), (0, plan.groups * plan.slots - maps)))
    side_weight = side_weight.reshape(feat, heads, plan.groups, plan.slots)
    side_weight = side_weight.transpose(0, 3, 1, 2).reshape(feat, -1)
    kernels = conv_weight.transpose(0, 1, 5, 2, 4, 3).reshape(plan.convs, 3 * feat, 3 * feat)
    vectors = jnp.concatenate(
        [proj_bias[None], conv_bias.reshape(-1, feat), out_weight[None]], axis=0
    ).T
    spot = np.arange(plan.lanes) - start
    row = band_index * plan.band - plan.halo + (spot // stride).astype(np.int32)
    col = me * cols - plan.halo + (spot % stride).astype(np.int32)
    mask = (row >= 0) & (row < width) & (col >= 0) & (col < width)
    mask = mask.astype(F32)[None]

    key = np.arange(cols)
    member, line = key // plan.rows, key % plan.rows
    spots = []
    for first in range(0, plan.edges, plan.slots):
        column = first + member
        fits = (member < plan.slots) & (column < plan.edges)
        places = (0, plan.halo + cols) if plan.sides == 1 else (np.where(column < plan.halo, 0, cols),)
        target = [np.where(fits, start + line * stride + column + p, -1) for p in places]
        hit = [jnp.arange(plan.lanes)[None] == jnp.asarray(p, jnp.int32)[:, None] for p in target]
        spots.append(functools.reduce(jnp.logical_or, hit).astype(BF16))
    spots = jnp.stack(spots)

    chips = plan.chips
    blocks = pl.pallas_call(
        functools.partial(correct_pack, plan),
        out_shape=[jax.ShapeDtypeStruct((plan.block_rows, cols), BF16)] * chips,
        in_specs=[whole(pltpu.SMEM)] + [whole()] * 4,
        out_specs=[whole()] * chips,
        scratch_shapes=[
            pltpu.VMEM((maps, width + 24, cols), F32),
            pltpu.VMEM((width, LANES), F32),
        ],
        compiler_params=params,
        name="correct_pack",
    )(tile, attention, received, sums, edge)
    grouped = list(blocks)[::-1]
    for step in reversed(range(1, chips)):
        pairs = [(i, 2 * partner(i // 2, step, chips) + i % 2) for i in range(heads)]
        grouped[step] = lax.ppermute(grouped[step], "head", pairs)
    order = [list(range(chips - 1, chips // 2 - 1, -1)), list(range(chips // 2 - 1, -1, -1))]
    swapped = []
    for steps in order:
        packed = pl.pallas_call(
            functools.partial(core_pack, plan),
            out_shape=jax.ShapeDtypeStruct((len(steps), plan.half_rows, cols), BF16),
            in_specs=[whole(pltpu.SMEM)] + [whole()] * len(steps),
            out_specs=whole(),
            compiler_params=params,
            name="core_pack",
        )(tile, *[grouped[k] for k in steps])
        swapped.append(lax.ppermute(packed, "head", [(i, i ^ 1) for i in range(heads)]))

    return pl.pallas_call(
        functools.partial(stack, plan, order),
        out_shape=jax.ShapeDtypeStruct((plan.band, cols), F32),
        in_specs=[whole(pltpu.SMEM)] + [whole()] * (chips + len(order) + 6),
        out_specs=whole(),
        scratch_shapes=[
            pltpu.VMEM((heads * maps * plan.rows, cols), F32),
            pltpu.VMEM((heads * plan.side_rows, cols), F32),
            pltpu.VMEM((feat, plan.lanes), F32),
            pltpu.VMEM((feat, plan.lanes), BF16),
            pltpu.VMEM((feat, plan.lanes), BF16),
            pltpu.VMEM((3 * feat, plan.lanes), F32),
            pltpu.VMEM((8, plan.lanes), F32),
        ],
        compiler_params=params,
        name="stack",
    )(tile, *grouped[::-1], *swapped, proj_weight, side_weight, kernels, vectors, mask, spots)


def solution(mesh):
    return jax.shard_map(
        on_device,
        mesh=mesh,
        in_specs=(P(("grp", "head"), None, "tile"), P(), P(), P(), P(), P()),
        out_specs=P(("grp", "head"), "tile"),
        check_vma=False,
    )
```

```python
import functools
import math
from typing import NamedTuple

import jax
import jax.numpy as jnp
import numpy as np
from jax import lax
from jax.experimental import pallas as pl
from jax.experimental.pallas import tpu as pltpu
from jax.sharding import PartitionSpec as P

BF16, F32 = jnp.bfloat16, jnp.float32
LANES = 128


def up(value, step):
    return -(-value // step) * step


class Plan(NamedTuple):
    maps: int
    width: int
    cols: int
    tiles: int
    heads: int
    feat: int
    convs: int

    @property
    def halo(self):
        return self.convs

    @property
    def sides(self):
        return min(2, self.tiles - 1)

    @property
    def edges(self):
        return self.sides * self.halo

    @property
    def edge_rows(self):
        return up(self.maps * self.edges, 8)

    @property
    def map_rows(self):
        return up(self.maps, 16)

    @property
    def tail_rows(self):
        return up((1 + self.tiles) * self.edge_rows + 3 * self.tiles * self.map_rows, 16)

    @property
    def band(self):
        return self.width // self.heads

    @property
    def rows(self):
        return self.band + 2 * self.halo

    @property
    def slots(self):
        return self.cols // self.rows

    @property
    def groups(self):
        return -(-self.maps // self.slots)

    @property
    def side_rows(self):
        return self.groups * self.edges

    @property
    def chips(self):
        return self.heads // 2

    @property
    def lone(self):
        return self.band // 8

    @property
    def shared(self):
        return 2 * self.halo // 8

    @property
    def group_rows(self):
        return 8 * self.maps

    @property
    def lead(self):
        return self.lone * self.group_rows + self.side_rows

    @property
    def half_rows(self):
        return self.lead + self.shared * self.group_rows

    @property
    def block_rows(self):
        return up(self.lead + self.half_rows, 16)

    @property
    def stride(self):
        return self.cols + 2 * self.halo

    @property
    def start(self):
        return up(self.stride, LANES) - LANES

    @property
    def chunk(self):
        return 256

    @property
    def lanes(self):
        return up(self.start + self.rows * self.stride, LANES) + 2 * self.chunk + 3 * LANES


def partner(mine, step, count, back=False):
    if count & (count - 1) == 0:
        return mine ^ step
    return (mine - step if back else mine + step) % count


def half(plan, block, core):
    return jnp.where(
        core == 0, block[: plan.half_rows], block[plan.lead : plan.lead + plan.half_rows]
    )


def edge_start(plan, tile, side):
    left, right = plan.cols * tile - plan.halo, plan.cols * (tile + 1)
    if plan.sides == 1:
        return jnp.where(tile > 0, left, right)
    return (left, right)[side]


def edge_select(plan, tile, row, position, index):
    hit = None
    for side in range(plan.sides):
        first = index * plan.edges + side * plan.halo
        inside = (row >= first) & (row < first + plan.halo)
        one = inside & (position == row - first + edge_start(plan, tile, side))
        hit = one if hit is None else hit | one
    return hit


def across(a, b):
    return lax.dot_general(a, b, (((1,), (1,)), ((), ())), preferred_element_type=F32)


def dot(a, b):
    return jnp.dot(a, b, preferred_element_type=F32)


def mirror_pack(plan, tile_ref, maps_ref, out_ref, sums_ref, edge_ref):
    me = tile_ref[0]
    count, cols, width, tiles = plan.maps, plan.cols, plan.width, plan.tiles
    head, edge = plan.map_rows, plan.edge_rows

    def pick(rows, span, base, tile, index):
        row = lax.broadcasted_iota(jnp.int32, (rows, span), 0)
        position = lax.broadcasted_iota(jnp.int32, (rows, span), 1) + base
        return edge_select(plan, tile, row, position, index).astype(F32)

    def total(span, index):
        return (lax.broadcasted_iota(jnp.int32, (head, span), 0) == index).astype(F32)

    for shift in range(1, tiles):
        dest = lax.rem(me + shift, tiles)
        by_col = by_row = None
        for index in range(count):
            block = maps_ref[index]
            out_ref[shift - 1, index * cols : (index + 1) * cols, :] = maps_ref[
                index, pl.ds(pl.multiple_of(dest * cols, cols), cols), :
            ]
            left = [pick(edge, cols, me * cols, dest, index)]
            upper = [pick(edge, width, 0, dest, index)]
            if shift == 1:
                left.append(total(cols, index))
                upper.append(total(width, index))
                upper.append(pick(edge, width, 0, me, index))
            by_c = across(jnp.concatenate(left, axis=0).astype(BF16), block)
            by_r = dot(jnp.concatenate(upper, axis=0).astype(BF16), block)
            by_col = by_c if by_col is None else by_col + by_c
            by_row = by_r if by_row is None else by_row + by_r
        if shift == 1:
            sums_ref[...] = by_col[edge : edge + head]
            own = pl.ds(pl.multiple_of(me * cols, cols), cols)
            sums_ref[:, own] = sums_ref[:, own] + by_row[edge : edge + head]
            edge_ref[...] = by_row[edge + head :]
            sums = sums_ref[...]
            high = sums.astype(BF16).astype(F32)
            middle = (sums - high).astype(BF16).astype(F32)
            low = sums - high - middle
        pieces = [by_row[:edge]]
        for wide in (by_col[:edge], high, middle, low):
            pieces += [wide[:, k * cols : (k + 1) * cols] for k in range(tiles)]
        used = (1 + tiles) * edge + 3 * tiles * head
        if plan.tail_rows > used:
            pieces.append(jnp.zeros((plan.tail_rows - used, cols), F32))
        out_ref[shift - 1, count * cols :, :] = jnp.concatenate(pieces, axis=0).astype(BF16)


def correct_pack(plan, tile_ref, maps_ref, recv_ref, sums_ref, edge_ref, *refs):
    *out_refs, field_ref, turned_ref = refs
    me, chip = tile_ref[0], tile_ref[1] // 2
    count, cols, width, tiles = plan.maps, plan.cols, plan.width, plan.tiles
    head, edge, halo = plan.map_rows, plan.edge_rows, plan.halo
    tails = [recv_ref[k, count * cols :, :].astype(F32) for k in range(tiles - 1)]

    rowsum = []
    for b in range(tiles):
        value = sums_ref[:, b * cols : (b + 1) * cols]
        for tail in tails:
            base = (1 + tiles) * edge
            parts = [
                tail[base + (k * tiles + b) * head : base + (k * tiles + b + 1) * head]
                for k in range(3)
            ]
            value = value + ((parts[0] + parts[1]) + parts[2])
        rowsum.append(value)
    grand = sum(jnp.sum(value, axis=1, keepdims=True) for value in rowsum)
    grand = jnp.where(lax.broadcasted_iota(jnp.int32, (head, 1), 0) < count, grand, 1.0)
    scaled = [value / grand for value in rowsum]
    for b in range(tiles):
        square = jnp.concatenate([rowsum[b], jnp.zeros((LANES - head, cols), F32)], axis=0)
        turned_ref[b * cols : (b + 1) * cols, :] = square.T
    mine = scaled[0]
    for b in range(1, tiles):
        mine = jnp.where(me == b, scaled[b], mine)

    eye = (
        lax.broadcasted_iota(jnp.int32, (cols, cols), 0)
        == lax.broadcasted_iota(jnp.int32, (cols, cols), 1)
    ).astype(F32).astype(BF16)
    margin = 8 + halo
    for index in range(count):
        field_ref[index, :16, :] = jnp.zeros((16, cols), F32)
        field_ref[index, width + 8 :, :] = jnp.zeros((16, cols), F32)
        for b in range(tiles):
            shift = lax.rem(b - me + tiles, tiles)
            other = recv_ref[
                jnp.maximum(shift - 1, 0), index * cols : (index + 1) * cols, :
            ]
            own = maps_ref[index, b * cols : (b + 1) * cols, :]
            mirror = across(eye, jnp.where(shift == 0, own, other))
            column = turned_ref[b * cols : (b + 1) * cols, index : index + 1]
            field_ref[index, margin + b * cols : margin + (b + 1) * cols, :] = (
                own.astype(F32) + mirror - column * mine[index : index + 1]
            )

    strips = []
    for b in range(tiles):
        strip = edge_ref[...]
        for k, tail in enumerate(tails):
            strip = jnp.where(lax.rem(me + k + 1, tiles) == b, tail[:edge], strip)
        for tail in tails:
            strip = strip + tail[(1 + b) * edge : (2 + b) * edge]
        strips.append(strip)
    strip = jnp.concatenate(strips, axis=1)
    wide = jnp.concatenate(scaled, axis=1)
    before = pl.multiple_of(jnp.maximum(me * cols - 8, 0), 8)
    after = pl.multiple_of(jnp.minimum((me + 1) * cols, width - 8), 8)
    left = turned_ref[pl.ds(before, 8), :][8 - halo :]
    right = turned_ref[pl.ds(after, 8), :][:halo]
    if plan.sides == 1:
        beside = jnp.where(me > 0, left, right)
    else:
        beside = jnp.concatenate([left, right], axis=0)
    lines = [
        strip[k * plan.edges : (k + 1) * plan.edges] - beside[:, k : k + 1] * wide[k : k + 1]
        for k in range(count)
    ]
    rows, slots = plan.rows, plan.slots
    stacks = []
    for slot in range(slots):
        members = []
        for group in range(plan.groups):
            k = group * slots + slot
            members.append(lines[k] if k < count else jnp.zeros((plan.edges, width), F32))
        stacks.append(jnp.concatenate(members, axis=0))
    lane = lax.broadcasted_iota(jnp.int32, (plan.side_rows, cols), 1)
    spare = plan.block_rows - plan.lead - plan.half_rows
    for step, out_ref in zip(reversed(range(plan.chips)), out_refs):
        first = partner(chip, step, plan.chips) * 2 * plan.band
        groups = [
            field_ref[k, pl.ds(pl.multiple_of(first + 8 + 8 * group, 8), 8), :]
            for group in range(2 * plan.lone + plan.shared)
            for k in range(count)
        ]
        sides = []
        for core in range(2):
            side = jnp.zeros((plan.side_rows, cols), F32)
            for slot in range(slots):
                amount = lax.rem(slot * rows + halo + width - core * plan.band - first, width)
                moved = pltpu.roll(stacks[slot], amount, 1)[:, :cols]
                side = jnp.where((lane >= slot * rows) & (lane < (slot + 1) * rows), moved, side)
            sides.append(side)
        lone = plan.lone * count
        pieces = groups[:lone] + sides[:1] + groups[lone:] + sides[1:]
        if spare:
            pieces.append(jnp.zeros((spare, cols), F32))
        out_ref[...] = jnp.concatenate(pieces, axis=0).astype(BF16)


def core_pack(plan, tile_ref, *refs):
    *block_refs, out_ref = refs
    other = 1 - tile_ref[1] % 2
    for k, block_ref in enumerate(block_refs):
        out_ref[k] = half(plan, block_ref[...].astype(F32), other).astype(BF16)


def shifted(ref, rows, base, offset, size):
    begin = base + offset
    low = begin // LANES * LANES
    rest = begin - low
    if rest == 0:
        return ref[rows, low : low + size]
    return pltpu.roll(ref[rows, low : low + size + LANES], size + LANES - rest, 1)[:, :size]


def stack(plan, order, tile_ref, *refs):
    chips = plan.chips
    own_refs, swap_refs, refs = refs[:chips], refs[chips : chips + len(order)], refs[chips + len(order) :]
    proj_ref, side_ref, kernel_ref, vector_ref, mask_ref, spots_ref, out_ref = refs[:7]
    maps_ref, sides_ref, field_ref, stream_ref, hidden_ref, taps_ref, logit_ref = refs[7:]
    count, cols, rows, halo = plan.maps, plan.cols, plan.rows, plan.halo
    heads, feat, chunk, stride = plan.heads, plan.feat, plan.chunk, plan.stride
    chip, core = tile_ref[1] // 2, tile_ref[1] % 2
    group = plan.group_rows

    def spread(block, source):
        for k in range(plan.lone + plan.shared):
            value = block[k * group : (k + 1) * group]
            if k >= plan.lone:
                late = block[plan.side_rows + k * group : plan.side_rows + (k + 1) * group]
                value = jnp.where(core == 0, late, value)
            place = pl.multiple_of((k * heads + source) * group, 8)
            maps_ref[pl.ds(place, group), :] = value
        side = jnp.where(
            core == 0,
            block[plan.lone * group : plan.lead],
            block[plan.half_rows - plan.side_rows : plan.half_rows],
        )
        place = pl.multiple_of(source * plan.side_rows, 8)
        sides_ref[pl.ds(place, plan.side_rows), :] = side

    for steps, swap_ref in zip(order, swap_refs):
        for k, step in enumerate(steps):
            source = 2 * partner(chip, step, chips, back=True)
            spread(half(plan, own_refs[chips - 1 - step][...].astype(F32), core), source + core)
            spread(swap_ref[k].astype(F32), source + 1 - core)
    bias = vector_ref[:, 0:1]

    slots, members = plan.slots, heads * plan.groups
    lane = lax.broadcasted_iota(jnp.int32, (members, cols), 1)
    placed = []
    for first in range(0, plan.edges, slots):
        parts = [jnp.zeros((members, cols), F32) for _ in range(slots)]
        for at in range(min(slots, plan.edges - first)):
            value = sides_ref[pl.ds(first + at, members, stride=plan.edges), :]
            keep = (lane >= at * rows) & (lane < (at + 1) * rows)
            for slot in range(slots):
                moved = value
                if at != slot:
                    moved = pltpu.roll(value, ((at - slot) * rows) % cols, 1)
                parts[slot] = jnp.where(keep, moved, parts[slot])
        stacked = jnp.concatenate(parts, axis=0).astype(BF16)
        placed.append((dot(side_ref[...], stacked) + bias).astype(BF16))

    chunks = -(-(rows * stride + plan.start) // chunk)
    for i in range(chunks):
        here = slice(i * chunk, (i + 1) * chunk)
        field_ref[:, here] = sum(
            dot(columns, spots_ref[k, :, here]) for k, columns in enumerate(placed)
        )

    weight = proj_ref[...]
    spot = lax.broadcasted_iota(jnp.int32, (feat, cols), 1)
    per = 2
    for r in range(0, rows, per):
        blocks = [
            maps_ref[
                pl.ds((r + k) // 8 * heads * group + (r + k) % 8, heads * count, stride=8), :
            ].astype(BF16)
            for k in range(per)
        ]
        pair = dot(weight, jnp.concatenate(blocks, axis=1)) + bias
        for k in range(per):
            begin = plan.start + (r + k) * stride + halo
            low, rest = begin // LANES * LANES, begin % LANES
            value = pair[:, k * cols : (k + 1) * cols]
            if rest == 0:
                field_ref[:, low : low + cols] += value
                continue
            value = pltpu.roll(value, rest, 1)
            field_ref[:, low : low + cols] += jnp.where(spot >= rest, value, 0.0)
            field_ref[:, low + cols : low + 2 * cols] += jnp.where(spot < rest, value, 0.0)

    for i in range(chunks):
        here = slice(i * chunk, (i + 1) * chunk)
        stream_ref[:, here] = jnp.where(mask_ref[:, here] > 0, field_ref[:, here], 0.0).astype(BF16)

    everything = slice(None)
    for n in range(plan.convs):
        source = hidden_ref if n % 2 else stream_ref
        low = (plan.start + (n + 1) * stride) // LANES * LANES
        steps = -(-(plan.start + (rows - n - 1) * stride - low) // chunk)
        offsets = vector_ref[:, n + 1 : n + 2]

        def multiply(base):
            window = jnp.concatenate(
                [shifted(source, everything, base, d * stride, chunk) for d in (-1, 0, 1)], axis=0
            )
            taps_ref[:, base : base + chunk] = dot(kernel_ref[n], window)

        def finish(base):
            here = slice(base, base + chunk)
            value = taps_ref[feat : 2 * feat, here]
            value = value + shifted(taps_ref, slice(0, feat), base, -1, chunk)
            value = value + shifted(taps_ref, slice(2 * feat, 3 * feat), base, 1, chunk)
            value = value + offsets
            keep = mask_ref[:, here] > 0
            if n % 2 == 0:
                value = jnp.where(value > 0, value, jnp.exp(jnp.minimum(value, 0.0)) - 1.0)
                hidden_ref[:, here] = jnp.where(keep, value, 0.0).astype(BF16)
                return
            value = (stream_ref[:, here].astype(F32) + value).astype(BF16)
            if n < plan.convs - 1:
                stream_ref[:, here] = jnp.where(keep, value.astype(F32), 0.0).astype(BF16)
                return
            readout = vector_ref[:, plan.convs + 1 : plan.convs + 2]
            logit_ref[0:1, here] = jnp.sum(value.astype(F32) * readout, axis=0, keepdims=True)

        for i in range(steps + 1):
            if i < steps:
                multiply(low + i * chunk)
            if i > 0:
                finish(low + (i - 1) * chunk)

    for r in range(plan.band):
        begin = plan.start + (r + halo) * stride + halo
        low = begin // LANES * LANES
        out_ref[r : r + 1, :] = shifted(logit_ref, slice(0, 1), low, begin - low, cols)


def call(kernel, name, args, outs, scratch=()):
    held = sum(math.prod(x.shape) * jnp.dtype(x.dtype).itemsize for x in [*args, *outs, *scratch])
    vmem = pl.BlockSpec(memory_space=pltpu.VMEM)
    return pl.pallas_call(
        kernel,
        out_shape=list(outs),
        in_specs=[pl.BlockSpec(memory_space=pltpu.SMEM)] + [vmem] * (len(args) - 1),
        out_specs=[vmem] * len(outs),
        scratch_shapes=list(scratch),
        compiler_params=pltpu.CompilerParams(vmem_limit_bytes=held * 5 // 4 + 4 * 1024 * 1024),
        name=name,
    )(*args)


def array(dtype, *shape):
    return jax.ShapeDtypeStruct(shape, dtype)


def on_device(attention, proj_weight, proj_bias, conv_weight, conv_bias, out_weight):
    maps, width, cols = attention.shape
    feat = proj_weight.shape[0]
    blocks, convs = conv_weight.shape[:2]
    tiles, heads = lax.axis_size("tile"), lax.axis_size("head")
    plan = Plan(maps, width, cols, tiles, heads, feat, blocks * convs)
    me = lax.axis_index("tile").astype(jnp.int32)
    band_index = lax.axis_index("head").astype(jnp.int32)
    tile = jnp.stack([me, band_index])

    payload, sums, edge = call(
        functools.partial(mirror_pack, plan),
        "mirror_pack",
        [tile, attention],
        [
            array(BF16, tiles - 1, maps * cols + plan.tail_rows, cols),
            array(F32, plan.map_rows, width),
            array(F32, plan.edge_rows, cols),
        ],
    )
    received = jnp.stack(
        [
            lax.ppermute(payload[s - 1], "tile", [(i, (i + s) % tiles) for i in range(tiles)])
            for s in range(tiles - 1, 0, -1)
        ]
    )

    stride, start = plan.stride, plan.start
    side_weight = proj_weight.reshape(feat, heads, maps)
    side_weight = jnp.pad(side_weight, ((0, 0), (0, 0), (0, plan.groups * plan.slots - maps)))
    side_weight = side_weight.reshape(feat, heads, plan.groups, plan.slots)
    side_weight = side_weight.transpose(0, 3, 1, 2).reshape(feat, -1)
    kernels = conv_weight.transpose(0, 1, 5, 2, 4, 3).reshape(plan.convs, 3 * feat, 3 * feat)
    vectors = jnp.concatenate(
        [proj_bias[None], conv_bias.reshape(-1, feat), out_weight[None]], axis=0
    ).T
    spot = np.arange(plan.lanes) - start
    row = band_index * plan.band - plan.halo + (spot // stride).astype(np.int32)
    col = me * cols - plan.halo + (spot % stride).astype(np.int32)
    mask = (row >= 0) & (row < width) & (col >= 0) & (col < width)
    mask = mask.astype(F32)[None]

    key = np.arange(cols)
    member, line = key // plan.rows, key % plan.rows
    spots = []
    for first in range(0, plan.edges, plan.slots):
        column = first + member
        fits = (member < plan.slots) & (column < plan.edges)
        places = (0, plan.halo + cols) if plan.sides == 1 else (np.where(column < plan.halo, 0, cols),)
        target = [np.where(fits, start + line * stride + column + p, -1) for p in places]
        hit = [jnp.arange(plan.lanes)[None] == jnp.asarray(p, jnp.int32)[:, None] for p in target]
        spots.append(functools.reduce(jnp.logical_or, hit).astype(BF16))
    spots = jnp.stack(spots)

    weights = (side_weight, kernels, vectors, mask, spots)
    received, weights = lax.optimization_barrier((received, weights))

    chips = plan.chips
    blocks = call(
        functools.partial(correct_pack, plan),
        "correct_pack",
        [tile, attention, received, sums, edge],
        [array(BF16, plan.block_rows, cols)] * chips,
        [pltpu.VMEM((maps, width + 24, cols), F32), pltpu.VMEM((width, LANES), F32)],
    )
    grouped = list(blocks)[::-1]
    for step in reversed(range(1, chips)):
        pairs = [(i, 2 * partner(i // 2, step, chips) + i % 2) for i in range(heads)]
        grouped[step] = lax.ppermute(grouped[step], "head", pairs)
    order = [list(range(chips - 1, chips // 2 - 1, -1)), list(range(chips // 2 - 1, -1, -1))]
    swapped = []
    for steps in order:
        (packed,) = call(
            functools.partial(core_pack, plan),
            "core_pack",
            [tile] + [grouped[k] for k in steps],
            [array(BF16, len(steps), plan.half_rows, cols)],
        )
        swapped.append(lax.ppermute(packed, "head", [(i, i ^ 1) for i in range(heads)]))

    (logits,) = call(
        functools.partial(stack, plan, order),
        "stack",
        [tile, *grouped[::-1], *swapped, proj_weight, *weights],
        [array(F32, plan.band, cols)],
        [
            pltpu.VMEM((heads * maps * plan.rows, cols), F32),
            pltpu.VMEM((heads * plan.side_rows, cols), F32),
            pltpu.VMEM((feat, plan.lanes), F32),
            pltpu.VMEM((feat, plan.lanes), BF16),
            pltpu.VMEM((feat, plan.lanes), BF16),
            pltpu.VMEM((3 * feat, plan.lanes), F32),
            pltpu.VMEM((8, plan.lanes), F32),
        ],
    )
    return logits


def solution(mesh):
    return jax.shard_map(
        on_device,
        mesh=mesh,
        in_specs=(P(("grp", "head"), None, "tile"), P(), P(), P(), P(), P()),
        out_specs=P(("grp", "head"), "tile"),
        check_vma=False,
    )
```

```python
import functools
import math
from typing import NamedTuple

import jax
import jax.numpy as jnp
import numpy as np
from jax import lax
from jax.experimental import pallas as pl
from jax.experimental.pallas import tpu as pltpu
from jax.sharding import PartitionSpec as P

BF16, F32 = jnp.bfloat16, jnp.float32
LANES = 128


def up(value, step):
    return -(-value // step) * step


class Plan(NamedTuple):
    first: int
    maps: int
    total: int
    width: int
    cols: int
    tiles: int
    heads: int
    feat: int
    convs: int

    @property
    def halo(self):
        return self.convs

    @property
    def sides(self):
        return min(2, self.tiles - 1)

    @property
    def edges(self):
        return self.sides * self.halo

    @property
    def last(self):
        return self.first + self.maps == self.total

    @property
    def edge_rows(self):
        return up(self.maps * self.edges, 8)

    @property
    def map_rows(self):
        return up(self.maps, 16)

    @property
    def tail_rows(self):
        return up((1 + self.tiles) * self.edge_rows + 3 * self.tiles * self.map_rows, 16)

    @property
    def band(self):
        return self.width // self.heads

    @property
    def rows(self):
        return self.band + 2 * self.halo

    @property
    def slots(self):
        return self.cols // self.rows

    @property
    def groups(self):
        return -(-self.total // self.slots)

    @property
    def side_rows(self):
        return self.groups * self.edges

    @property
    def chips(self):
        return self.heads // 2

    @property
    def lone(self):
        return self.band // 8

    @property
    def shared(self):
        return 2 * self.halo // 8

    @property
    def group_rows(self):
        return 8 * self.maps

    @property
    def lead(self):
        return self.lone * self.group_rows + (self.side_rows if self.last else 0)

    @property
    def half_rows(self):
        return self.lead + self.shared * self.group_rows

    @property
    def block_rows(self):
        return up(self.lead + self.half_rows, 16)

    @property
    def stride(self):
        return self.cols + 2 * self.halo

    @property
    def start(self):
        return up(self.stride, LANES) - LANES

    @property
    def chunk(self):
        return 256

    @property
    def lanes(self):
        return up(self.start + self.rows * self.stride, LANES) + 2 * self.chunk + 3 * LANES


def partner(mine, step, count, back=False):
    if count & (count - 1) == 0:
        return mine ^ step
    return (mine - step if back else mine + step) % count


def half(parts, block, core):
    pieces, base = [], 0
    for plan in parts:
        early = block[base : base + plan.half_rows]
        late = block[base + plan.lead : base + plan.lead + plan.half_rows]
        pieces.append(jnp.where(core == 0, early, late))
        base += plan.block_rows
    return jnp.concatenate(pieces, axis=0)


def far_near(plan):
    steps = list(reversed(range(plan.chips)))
    return steps[: plan.chips // 2], steps[plan.chips // 2 :]


def edge_start(plan, tile, side):
    left, right = plan.cols * tile - plan.halo, plan.cols * (tile + 1)
    if plan.sides == 1:
        return jnp.where(tile > 0, left, right)
    return (left, right)[side]


def edge_select(plan, tile, row, position, index):
    hit = None
    for side in range(plan.sides):
        first = index * plan.edges + side * plan.halo
        inside = (row >= first) & (row < first + plan.halo)
        one = inside & (position == row - first + edge_start(plan, tile, side))
        hit = one if hit is None else hit | one
    return hit


def across(a, b):
    return lax.dot_general(a, b, (((1,), (1,)), ((), ())), preferred_element_type=F32)


def dot(a, b):
    return jnp.dot(a, b, preferred_element_type=F32)


def mirror_pack(parts, maps_ref, *refs):
    for k, plan in enumerate(parts):
        mirror_pack_part(plan, maps_ref, *refs[3 * k : 3 * k + 3])


def mirror_pack_part(plan, maps_ref, out_ref, sums_ref, edge_ref):
    me = lax.axis_index("tile")
    count, cols, width, tiles = plan.maps, plan.cols, plan.width, plan.tiles
    head, edge = plan.map_rows, plan.edge_rows

    def pick(rows, span, base, tile, index):
        row = lax.broadcasted_iota(jnp.int32, (rows, span), 0)
        position = lax.broadcasted_iota(jnp.int32, (rows, span), 1) + base
        return edge_select(plan, tile, row, position, index).astype(F32)

    def total(span, index):
        return (lax.broadcasted_iota(jnp.int32, (head, span), 0) == index).astype(F32)

    for shift in range(1, tiles):
        dest = lax.rem(me + shift, tiles)
        by_col = by_row = None
        for index in range(count):
            block = maps_ref[plan.first + index]
            out_ref[shift - 1, index * cols : (index + 1) * cols, :] = maps_ref[
                plan.first + index, pl.ds(pl.multiple_of(dest * cols, cols), cols), :
            ]
            left = [pick(edge, cols, me * cols, dest, index)]
            upper = [pick(edge, width, 0, dest, index)]
            if shift == 1:
                left.append(total(cols, index))
                upper.append(total(width, index))
                upper.append(pick(edge, width, 0, me, index))
            by_c = across(jnp.concatenate(left, axis=0).astype(BF16), block)
            by_r = dot(jnp.concatenate(upper, axis=0).astype(BF16), block)
            by_col = by_c if by_col is None else by_col + by_c
            by_row = by_r if by_row is None else by_row + by_r
        if shift == 1:
            sums_ref[...] = by_col[edge : edge + head]
            own = pl.ds(pl.multiple_of(me * cols, cols), cols)
            sums_ref[:, own] = sums_ref[:, own] + by_row[edge : edge + head]
            edge_ref[...] = by_row[edge + head :]
            sums = sums_ref[...]
            high = sums.astype(BF16).astype(F32)
            middle = (sums - high).astype(BF16).astype(F32)
            low = sums - high - middle
        pieces = [by_row[:edge]]
        for wide in (by_col[:edge], high, middle, low):
            pieces += [wide[:, k * cols : (k + 1) * cols] for k in range(tiles)]
        used = (1 + tiles) * edge + 3 * tiles * head
        if plan.tail_rows > used:
            pieces.append(jnp.zeros((plan.tail_rows - used, cols), F32))
        out_ref[shift - 1, count * cols :, :] = jnp.concatenate(pieces, axis=0).astype(BF16)


def correct_pack(plan, maps_ref, recv_ref, sums_ref, edge_ref, *refs):
    *refs, field_ref, turned_ref = refs
    far, near = far_near(plan)
    refs, out_refs = refs[: -plan.chips], refs[-plan.chips :]
    (line_ref,) = refs
    me, chip = lax.axis_index("tile"), lax.axis_index("head") // 2
    count, cols, width, tiles = plan.maps, plan.cols, plan.width, plan.tiles
    head, edge, halo = plan.map_rows, plan.edge_rows, plan.halo
    tails = [recv_ref[k, count * cols :, :].astype(F32) for k in range(tiles - 1)]

    rowsum = []
    for b in range(tiles):
        value = sums_ref[:, b * cols : (b + 1) * cols]
        for tail in tails:
            base = (1 + tiles) * edge
            parts = [
                tail[base + (k * tiles + b) * head : base + (k * tiles + b + 1) * head]
                for k in range(3)
            ]
            value = value + ((parts[0] + parts[1]) + parts[2])
        rowsum.append(value)
    grand = sum(jnp.sum(value, axis=1, keepdims=True) for value in rowsum)
    grand = jnp.where(lax.broadcasted_iota(jnp.int32, (head, 1), 0) < count, grand, 1.0)
    scaled = [value / grand for value in rowsum]
    for b in range(tiles):
        square = jnp.concatenate([rowsum[b], jnp.zeros((LANES - head, cols), F32)], axis=0)
        turned_ref[b * cols : (b + 1) * cols, :] = square.T
    mine = scaled[0]
    for b in range(1, tiles):
        mine = jnp.where(me == b, scaled[b], mine)

    eye = (
        lax.broadcasted_iota(jnp.int32, (cols, cols), 0)
        == lax.broadcasted_iota(jnp.int32, (cols, cols), 1)
    ).astype(F32).astype(BF16)
    margin = 8 + halo
    for index in range(count):
        field_ref[index, :16, :] = jnp.zeros((16, cols), F32)
        field_ref[index, width + 8 :, :] = jnp.zeros((16, cols), F32)
        for b in range(tiles):
            shift = lax.rem(b - me + tiles, tiles)
            other = recv_ref[
                jnp.maximum(shift - 1, 0), index * cols : (index + 1) * cols, :
            ]
            own = maps_ref[plan.first + index, b * cols : (b + 1) * cols, :]
            mirror = across(eye, jnp.where(shift == 0, own, other))
            column = turned_ref[b * cols : (b + 1) * cols, index : index + 1]
            field_ref[index, margin + b * cols : margin + (b + 1) * cols, :] = (
                own.astype(F32) + mirror - column * mine[index : index + 1]
            )

    strips = []
    for b in range(tiles):
        strip = edge_ref[...]
        for k, tail in enumerate(tails):
            strip = jnp.where(lax.rem(me + k + 1, tiles) == b, tail[:edge], strip)
        for tail in tails:
            strip = strip + tail[(1 + b) * edge : (2 + b) * edge]
        strips.append(strip)
    strip = jnp.concatenate(strips, axis=1)
    wide = jnp.concatenate(scaled, axis=1)
    before = pl.multiple_of(jnp.maximum(me * cols - 8, 0), 8)
    after = pl.multiple_of(jnp.minimum((me + 1) * cols, width - 8), 8)
    left = turned_ref[pl.ds(before, 8), :][8 - halo :]
    right = turned_ref[pl.ds(after, 8), :][:halo]
    if plan.sides == 1:
        beside = jnp.where(me > 0, left, right)
    else:
        beside = jnp.concatenate([left, right], axis=0)
    lines = [
        strip[k * plan.edges : (k + 1) * plan.edges] - beside[:, k : k + 1] * wide[k : k + 1]
        for k in range(count)
    ]
    rows, slots = plan.rows, plan.slots
    if plan.last:
        earlier = line_ref[...]
        lines = [
            earlier[k * plan.edges : (k + 1) * plan.edges] for k in range(plan.first)
        ] + lines
    else:
        filler = plan.edge_rows - count * plan.edges
        if filler:
            lines = lines + [jnp.zeros((filler, width), F32)]
        line_ref[...] = jnp.concatenate(lines, axis=0)
    stacks = []
    for slot in range(slots if plan.last else 0):
        members = []
        for group in range(plan.groups):
            k = group * slots + slot
            members.append(lines[k] if k < plan.total else jnp.zeros((plan.edges, width), F32))
        stacks.append(jnp.concatenate(members, axis=0))
    lane = lax.broadcasted_iota(jnp.int32, (plan.side_rows, cols), 1)
    spare = plan.block_rows - plan.lead - plan.half_rows
    for step, out_ref in zip(far + near, out_refs):
        first = partner(chip, step, plan.chips) * 2 * plan.band
        groups = [
            field_ref[k, pl.ds(pl.multiple_of(first + 8 + 8 * group, 8), 8), :]
            for group in range(2 * plan.lone + plan.shared)
            for k in range(count)
        ]
        sides = []
        for core in range(2 if plan.last else 0):
            side = jnp.zeros((plan.side_rows, cols), F32)
            for slot in range(slots):
                amount = lax.rem(slot * rows + halo + width - core * plan.band - first, width)
                moved = pltpu.roll(stacks[slot], amount, 1)[:, :cols]
                side = jnp.where((lane >= slot * rows) & (lane < (slot + 1) * rows), moved, side)
            sides.append(side)
        lone = plan.lone * count
        pieces = groups[:lone] + sides[:1] + groups[lone:] + sides[1:]
        if spare:
            pieces.append(jnp.zeros((spare, cols), F32))
        out_ref[...] = jnp.concatenate(pieces, axis=0).astype(BF16)


def core_pack(parts, *refs):
    *block_refs, out_ref = refs
    other = 1 - lax.axis_index("head") % 2
    for k, block_ref in enumerate(block_refs):
        out_ref[k] = half(parts, block_ref[...].astype(F32), other).astype(BF16)


def kernel_pack(blocks_ref, out_ref):
    layers, convs, height, breadth = blocks_ref.shape[:4]
    for b in range(layers):
        for m in range(convs):
            out_ref[b * convs + m] = jnp.concatenate(
                [
                    jnp.concatenate(
                        [blocks_ref[b, m, dy, dx].astype(F32) for dy in range(height)], axis=1
                    )
                    for dx in range(breadth)
                ],
                axis=0,
            ).astype(BF16)


def shifted(ref, rows, base, offset, size):
    begin = base + offset
    low = begin // LANES * LANES
    rest = begin - low
    if rest == 0:
        return ref[rows, low : low + size]
    return pltpu.roll(ref[rows, low : low + size + LANES], size + LANES - rest, 1)[:, :size]


def stack(plan, parcels, *refs):
    own_refs, swap_refs = [], []
    for steps, _ in parcels:
        own_refs.append(refs[: len(steps)])
        swap_refs.append(refs[len(steps)])
        refs = refs[len(steps) + 1 :]
    chips = plan.chips
    proj_ref, side_ref, kernel_ref, vector_ref, mask_ref, spots_ref, out_ref = refs[:7]
    maps_ref, sides_ref, field_ref, stream_ref, hidden_ref, taps_ref, logit_ref = refs[7:]
    count, cols, rows, halo = plan.total, plan.cols, plan.rows, plan.halo
    heads, feat, chunk, stride = plan.heads, plan.feat, plan.chunk, plan.stride
    head = lax.axis_index("head")
    chip, core = head // 2, head % 2

    def spread(parts, halves, source):
        base = 0
        for part in parts:
            block = halves[base : base + part.half_rows]
            base += part.half_rows
            group, skip = part.group_rows, part.side_rows if part.last else 0
            for k in range(part.lone + part.shared):
                value = block[k * group : (k + 1) * group]
                if k >= part.lone and skip:
                    late = block[skip + k * group : skip + (k + 1) * group]
                    value = jnp.where(core == 0, late, value)
                place = ((k * heads + source) * count + part.first) * 8
                maps_ref[pl.ds(pl.multiple_of(place, 8), group), :] = value
            if skip:
                early = block[part.lone * group : part.lead]
                late = block[part.half_rows - skip : part.half_rows]
                place = pl.multiple_of(source * skip, 8)
                sides_ref[pl.ds(place, skip), :] = jnp.where(core == 0, early, late)

    for (steps, parts), blocks, swap_ref in zip(parcels, own_refs, swap_refs):
        for k, step in enumerate(steps):
            source = 2 * partner(chip, step, chips, back=True)
            spread(parts, half(parts, blocks[k][...].astype(F32), core), source + core)
            spread(parts, swap_ref[k].astype(F32), source + 1 - core)
    bias = vector_ref[:, 0:1]

    slots, members = plan.slots, heads * plan.groups
    lane = lax.broadcasted_iota(jnp.int32, (members, cols), 1)
    placed = []
    for first in range(0, plan.edges, slots):
        parts = [jnp.zeros((members, cols), F32) for _ in range(slots)]
        for at in range(min(slots, plan.edges - first)):
            value = sides_ref[pl.ds(first + at, members, stride=plan.edges), :]
            keep = (lane >= at * rows) & (lane < (at + 1) * rows)
            for slot in range(slots):
                moved = value
                if at != slot:
                    moved = pltpu.roll(value, ((at - slot) * rows) % cols, 1)
                parts[slot] = jnp.where(keep, moved, parts[slot])
        stacked = jnp.concatenate(parts, axis=0).astype(BF16)
        placed.append((dot(side_ref[...], stacked) + bias).astype(BF16))

    chunks = -(-(rows * stride + plan.start) // chunk)
    for i in range(chunks):
        here = slice(i * chunk, (i + 1) * chunk)
        field_ref[:, here] = sum(
            dot(columns, spots_ref[k, :, here]) for k, columns in enumerate(placed)
        )

    weight = proj_ref[...]
    spot = lax.broadcasted_iota(jnp.int32, (feat, cols), 1)
    per = 2
    for r in range(0, rows, per):
        blocks = [
            maps_ref[
                pl.ds((r + k) // 8 * heads * count * 8 + (r + k) % 8, heads * count, stride=8), :
            ].astype(BF16)
            for k in range(per)
        ]
        pair = dot(weight, jnp.concatenate(blocks, axis=1)) + bias
        for k in range(per):
            begin = plan.start + (r + k) * stride + halo
            low, rest = begin // LANES * LANES, begin % LANES
            value = pair[:, k * cols : (k + 1) * cols]
            if rest == 0:
                field_ref[:, low : low + cols] += value
                continue
            value = pltpu.roll(value, rest, 1)
            field_ref[:, low : low + cols] += jnp.where(spot >= rest, value, 0.0)
            field_ref[:, low + cols : low + 2 * cols] += jnp.where(spot < rest, value, 0.0)

    for i in range(chunks):
        here = slice(i * chunk, (i + 1) * chunk)
        stream_ref[:, here] = jnp.where(mask_ref[:, here] > 0, field_ref[:, here], 0.0).astype(BF16)

    everything = slice(None)
    for n in range(plan.convs):
        source = hidden_ref if n % 2 else stream_ref
        low = (plan.start + (n + 1) * stride) // LANES * LANES
        steps = -(-(plan.start + (rows - n - 1) * stride - low) // chunk)
        offsets = vector_ref[:, n + 1 : n + 2]

        def multiply(base):
            window = jnp.concatenate(
                [shifted(source, everything, base, d * stride, chunk) for d in (-1, 0, 1)], axis=0
            )
            taps_ref[:, base : base + chunk] = dot(kernel_ref[n], window)

        def finish(base):
            here = slice(base, base + chunk)
            value = taps_ref[feat : 2 * feat, here]
            value = value + shifted(taps_ref, slice(0, feat), base, -1, chunk)
            value = value + shifted(taps_ref, slice(2 * feat, 3 * feat), base, 1, chunk)
            value = value + offsets
            keep = mask_ref[:, here] > 0
            if n % 2 == 0:
                value = jnp.where(value > 0, value, jnp.exp(jnp.minimum(value, 0.0)) - 1.0)
                hidden_ref[:, here] = jnp.where(keep, value, 0.0).astype(BF16)
                return
            value = (stream_ref[:, here].astype(F32) + value).astype(BF16)
            if n < plan.convs - 1:
                stream_ref[:, here] = jnp.where(keep, value.astype(F32), 0.0).astype(BF16)
                return
            readout = vector_ref[:, plan.convs + 1 : plan.convs + 2]
            logit_ref[0:1, here] = jnp.sum(value.astype(F32) * readout, axis=0, keepdims=True)

        for i in range(steps + 1):
            if i < steps:
                multiply(low + i * chunk)
            if i > 0:
                finish(low + (i - 1) * chunk)

    for r in range(plan.band):
        begin = plan.start + (r + halo) * stride + halo
        low = begin // LANES * LANES
        out_ref[r : r + 1, :] = shifted(logit_ref, slice(0, 1), low, begin - low, cols)


def call(kernel, name, args, outs, scratch=()):
    held = sum(math.prod(x.shape) * jnp.dtype(x.dtype).itemsize for x in [*args, *outs, *scratch])
    vmem = pl.BlockSpec(memory_space=pltpu.VMEM)
    return pl.pallas_call(
        kernel,
        out_shape=list(outs),
        in_specs=[vmem] * len(args),
        out_specs=[vmem] * len(outs),
        scratch_shapes=list(scratch),
        compiler_params=pltpu.CompilerParams(vmem_limit_bytes=held * 5 // 4 + 4 * 1024 * 1024),
        name=name,
    )(*args)


def array(dtype, *shape):
    return jax.ShapeDtypeStruct(shape, dtype)


def on_device(attention, proj_weight, proj_bias, conv_weight, conv_bias, out_weight):
    maps, width, cols = attention.shape
    feat = proj_weight.shape[0]
    blocks, convs = conv_weight.shape[:2]
    tiles, heads = lax.axis_size("tile"), lax.axis_size("head")
    parts = [
        Plan(first, count, maps, width, cols, tiles, heads, feat, blocks * convs)
        for first, count in ((0, maps // 2), (maps // 2, maps - maps // 2))
    ]
    plan = parts[-1]
    me, band_index = lax.axis_index("tile"), lax.axis_index("head")

    def mirror(payload):
        return jnp.stack(
            [
                lax.ppermute(payload[s - 1], "tile", [(i, (i + s) % tiles) for i in range(tiles)])
                for s in range(tiles - 1, 0, -1)
            ]
        )

    outs = []
    for part in parts:
        outs += [
            array(BF16, tiles - 1, part.maps * cols + part.tail_rows, cols),
            array(F32, part.map_rows, width),
            array(F32, part.edge_rows, cols),
        ]
    packed = call(functools.partial(mirror_pack, parts), "mirror_pack", [attention], outs)
    received = mirror(packed[0])
    payload, received = lax.optimization_barrier((packed[3], received))
    mirrored = [received, mirror(payload)]

    stride, start = plan.stride, plan.start
    side_weight = proj_weight.reshape(feat, heads, maps)
    side_weight = jnp.pad(side_weight, ((0, 0), (0, 0), (0, plan.groups * plan.slots - maps)))
    side_weight = side_weight.reshape(feat, heads, plan.groups, plan.slots)
    side_weight = side_weight.transpose(0, 3, 1, 2).reshape(feat, -1)
    (kernels,) = call(
        kernel_pack,
        "kernel_pack",
        [conv_weight.transpose(0, 1, 4, 5, 2, 3)],
        [array(BF16, plan.convs, 3 * feat, 3 * feat)],
    )
    vectors = jnp.concatenate(
        [proj_bias[None], conv_bias.reshape(-1, feat), out_weight[None]], axis=0
    ).T
    spot = np.arange(plan.lanes) - start
    row = band_index * plan.band - plan.halo + (spot // stride).astype(np.int32)
    col = me * cols - plan.halo + (spot % stride).astype(np.int32)
    mask = (row >= 0) & (row < width) & (col >= 0) & (col < width)
    mask = mask.astype(F32)[None]

    key = np.arange(cols)
    member, line = key // plan.rows, key % plan.rows
    spots = []
    for first in range(0, plan.edges, plan.slots):
        column = first + member
        fits = (member < plan.slots) & (column < plan.edges)
        places = (0, plan.halo + cols) if plan.sides == 1 else (np.where(column < plan.halo, 0, cols),)
        target = [np.where(fits, start + line * stride + column + p, -1) for p in places]
        hit = [jnp.arange(plan.lanes)[None] == jnp.asarray(p, jnp.int32)[:, None] for p in target]
        spots.append(functools.reduce(jnp.logical_or, hit).astype(BF16))
    spots = jnp.stack(spots)

    weights = (side_weight, kernels, vectors, mask, spots)
    mirrored[-1], weights = lax.optimization_barrier((mirrored[-1], weights))

    chips = plan.chips
    far, near = far_near(plan)
    parcels, arrived = [], []

    def travel(steps, blocks):
        own = []
        for step, block in zip(steps, blocks):
            pairs = [(i, 2 * partner(i // 2, step, chips) + i % 2) for i in range(heads)]
            own.append(lax.ppermute(block, "head", pairs) if step else block)
        return own

    def halve(steps, members, own):
        (halves,) = call(
            functools.partial(core_pack, members),
            "core_pack",
            own,
            [array(BF16, len(steps), sum(part.half_rows for part in members), cols)],
        )
        return steps, members, own, halves

    def swap(steps, members, own, halves):
        parcels.append((steps, members))
        arrived.extend([*own, lax.ppermute(halves, "head", [(i, i ^ 1) for i in range(heads)])])

    line = []
    for k, part in enumerate(parts):
        outs = [array(BF16, part.block_rows, cols)] * chips
        if not part.last:
            outs.insert(0, array(F32, part.edge_rows, width))
        result = call(
            functools.partial(correct_pack, part),
            "correct_pack",
            [attention, mirrored[k], *packed[3 * k + 1 : 3 * k + 3], *line],
            outs,
            [pltpu.VMEM((part.maps, width + 24, cols), F32), pltpu.VMEM((width, LANES), F32)],
        )
        line, result = result[:-chips], result[-chips:]
        own = travel(far + near, result)
        if part.last:
            swap(*halve(far, [part], own[: len(far)]))
            swap(*halve(near, [part], own[len(far) :]))
        else:
            ahead, mirrored[k + 1] = lax.optimization_barrier((own[: len(far)], mirrored[k + 1]))
            swap(*halve(far + near, [part], ahead + own[len(far) :]))

    (logits,) = call(
        functools.partial(stack, plan, parcels),
        "stack",
        [*arrived, proj_weight, *weights],
        [array(F32, plan.band, cols)],
        [
            pltpu.VMEM((heads * maps * plan.rows, cols), F32),
            pltpu.VMEM((heads * plan.side_rows, cols), F32),
            pltpu.VMEM((feat, plan.lanes), F32),
            pltpu.VMEM((feat, plan.lanes), BF16),
            pltpu.VMEM((feat, plan.lanes), BF16),
            pltpu.VMEM((3 * feat, plan.lanes), F32),
            pltpu.VMEM((8, plan.lanes), F32),
        ],
    )
    return logits


def solution(mesh):
    return jax.shard_map(
        on_device,
        mesh=mesh,
        in_specs=(P(("grp", "head"), None, "tile"), P(), P(), P(), P(), P()),
        out_specs=P(("grp", "head"), "tile"),
        check_vma=False,
    )
```

```python
import functools
import math
from typing import NamedTuple

import jax
import jax.numpy as jnp
import numpy as np
from jax import lax
from jax.experimental import pallas as pl
from jax.experimental.pallas import tpu as pltpu
from jax.sharding import PartitionSpec as P

BF16, F32 = jnp.bfloat16, jnp.float32
LANES = 128


def up(value, step):
    return -(-value // step) * step


class Plan(NamedTuple):
    maps: int
    width: int
    cols: int
    tiles: int
    heads: int
    feat: int
    convs: int

    @property
    def halo(self):
        return self.convs

    @property
    def sides(self):
        return min(2, self.tiles - 1)

    @property
    def edges(self):
        return self.sides * self.halo

    @property
    def edge_rows(self):
        return up(self.maps * self.edges, 8)

    @property
    def map_rows(self):
        return up(self.maps, 16)

    @property
    def tail_rows(self):
        return up((1 + self.tiles) * self.edge_rows + 3 * self.tiles * self.map_rows, 16)

    @property
    def band(self):
        return self.width // self.heads

    @property
    def rows(self):
        return self.band + 2 * self.halo

    @property
    def slots(self):
        return self.cols // self.rows

    @property
    def groups(self):
        return -(-self.maps // self.slots)

    @property
    def side_rows(self):
        return self.groups * self.edges

    @property
    def chips(self):
        return self.heads // 2

    @property
    def lone(self):
        return self.band // 8

    @property
    def shared(self):
        return 2 * self.halo // 8

    @property
    def group_rows(self):
        return 8 * self.maps

    @property
    def lead(self):
        return self.lone * self.group_rows + self.side_rows

    @property
    def half_rows(self):
        return self.lead + self.shared * self.group_rows

    @property
    def block_rows(self):
        return up(self.lead + self.half_rows, 16)

    @property
    def stride(self):
        return self.cols + 2 * self.halo

    @property
    def start(self):
        return up(self.stride, LANES) - LANES

    @property
    def chunk(self):
        return 256

    @property
    def lanes(self):
        return up(self.start + self.rows * self.stride, LANES) + 2 * self.chunk + 3 * LANES


def partner(mine, step, count, back=False):
    if count & (count - 1) == 0:
        return mine ^ step
    return (mine - step if back else mine + step) % count


def far_near(plan):
    steps = list(range(plan.chips - 1, 0, -1))
    return steps[: plan.chips // 2], steps[plan.chips // 2 :]


def step_order(plan):
    far, near = far_near(plan)
    return far + near + [0]


def half(plan, block, core):
    return jnp.where(
        core == 0, block[: plan.half_rows], block[plan.lead : plan.lead + plan.half_rows]
    )


def edge_start(plan, tile, side):
    left, right = plan.cols * tile - plan.halo, plan.cols * (tile + 1)
    if plan.sides == 1:
        return jnp.where(tile > 0, left, right)
    return (left, right)[side]


def edge_select(plan, tile, row, position, index):
    hit = None
    for side in range(plan.sides):
        first = index * plan.edges + side * plan.halo
        inside = (row >= first) & (row < first + plan.halo)
        one = inside & (position == row - first + edge_start(plan, tile, side))
        hit = one if hit is None else hit | one
    return hit


def across(a, b):
    return lax.dot_general(a, b, (((1,), (1,)), ((), ())), preferred_element_type=F32)


def dot(a, b):
    return jnp.dot(a, b, preferred_element_type=F32)


def mirror_pack(plan, maps_ref, out_ref, sums_ref, edge_ref):
    me = lax.axis_index("tile")
    count, cols, width, tiles = plan.maps, plan.cols, plan.width, plan.tiles
    head, edge = plan.map_rows, plan.edge_rows

    def pick(rows, span, base, tile, index):
        row = lax.broadcasted_iota(jnp.int32, (rows, span), 0)
        position = lax.broadcasted_iota(jnp.int32, (rows, span), 1) + base
        return edge_select(plan, tile, row, position, index).astype(F32)

    def total(span, index):
        return (lax.broadcasted_iota(jnp.int32, (head, span), 0) == index).astype(F32)

    for shift in range(1, tiles):
        dest = lax.rem(me + shift, tiles)
        by_col = by_row = None
        for index in range(count):
            block = maps_ref[index]
            out_ref[shift - 1, index * cols : (index + 1) * cols, :] = maps_ref[
                index, pl.ds(pl.multiple_of(dest * cols, cols), cols), :
            ]
            left = [pick(edge, cols, me * cols, dest, index)]
            upper = [pick(edge, width, 0, dest, index)]
            if shift == 1:
                left.append(total(cols, index))
                upper.append(total(width, index))
                upper.append(pick(edge, width, 0, me, index))
            by_c = across(jnp.concatenate(left, axis=0).astype(BF16), block)
            by_r = dot(jnp.concatenate(upper, axis=0).astype(BF16), block)
            by_col = by_c if by_col is None else by_col + by_c
            by_row = by_r if by_row is None else by_row + by_r
        if shift == 1:
            sums_ref[...] = by_col[edge : edge + head]
            own = pl.ds(pl.multiple_of(me * cols, cols), cols)
            sums_ref[:, own] = sums_ref[:, own] + by_row[edge : edge + head]
            edge_ref[...] = by_row[edge + head :]
            sums = sums_ref[...]
            high = sums.astype(BF16).astype(F32)
            middle = (sums - high).astype(BF16).astype(F32)
            low = sums - high - middle
        pieces = [by_row[:edge]]
        for wide in (by_col[:edge], high, middle, low):
            pieces += [wide[:, k * cols : (k + 1) * cols] for k in range(tiles)]
        used = (1 + tiles) * edge + 3 * tiles * head
        if plan.tail_rows > used:
            pieces.append(jnp.zeros((plan.tail_rows - used, cols), F32))
        out_ref[shift - 1, count * cols :, :] = jnp.concatenate(pieces, axis=0).astype(BF16)


def correct_pack(plan, maps_ref, recv_ref, sums_ref, edge_ref, *refs):
    *out_refs, field_ref, turned_ref = refs
    me, chip = lax.axis_index("tile"), lax.axis_index("head") // 2
    count, cols, width, tiles = plan.maps, plan.cols, plan.width, plan.tiles
    head, edge, halo = plan.map_rows, plan.edge_rows, plan.halo
    tails = [recv_ref[k, count * cols :, :].astype(F32) for k in range(tiles - 1)]

    rowsum = []
    for b in range(tiles):
        value = sums_ref[:, b * cols : (b + 1) * cols]
        for tail in tails:
            base = (1 + tiles) * edge
            parts = [
                tail[base + (k * tiles + b) * head : base + (k * tiles + b + 1) * head]
                for k in range(3)
            ]
            value = value + ((parts[0] + parts[1]) + parts[2])
        rowsum.append(value)
    grand = sum(jnp.sum(value, axis=1, keepdims=True) for value in rowsum)
    grand = jnp.where(lax.broadcasted_iota(jnp.int32, (head, 1), 0) < count, grand, 1.0)
    scaled = [value / grand for value in rowsum]
    for b in range(tiles):
        square = jnp.concatenate([rowsum[b], jnp.zeros((LANES - head, cols), F32)], axis=0)
        turned_ref[b * cols : (b + 1) * cols, :] = square.T
    mine = scaled[0]
    for b in range(1, tiles):
        mine = jnp.where(me == b, scaled[b], mine)

    eye = (
        lax.broadcasted_iota(jnp.int32, (cols, cols), 0)
        == lax.broadcasted_iota(jnp.int32, (cols, cols), 1)
    ).astype(F32).astype(BF16)
    margin = 8 + halo
    for index in range(count):
        field_ref[index, :16, :] = jnp.zeros((16, cols), F32)
        field_ref[index, width + 8 :, :] = jnp.zeros((16, cols), F32)
        for b in range(tiles):
            shift = lax.rem(b - me + tiles, tiles)
            other = recv_ref[
                jnp.maximum(shift - 1, 0), index * cols : (index + 1) * cols, :
            ]
            own = maps_ref[index, b * cols : (b + 1) * cols, :]
            mirror = across(eye, jnp.where(shift == 0, own, other))
            column = turned_ref[b * cols : (b + 1) * cols, index : index + 1]
            field_ref[index, margin + b * cols : margin + (b + 1) * cols, :] = (
                own.astype(F32) + mirror - column * mine[index : index + 1]
            )

    strips = []
    for b in range(tiles):
        strip = edge_ref[...]
        for k, tail in enumerate(tails):
            strip = jnp.where(lax.rem(me + k + 1, tiles) == b, tail[:edge], strip)
        for tail in tails:
            strip = strip + tail[(1 + b) * edge : (2 + b) * edge]
        strips.append(strip)
    strip = jnp.concatenate(strips, axis=1)
    wide = jnp.concatenate(scaled, axis=1)
    before = pl.multiple_of(jnp.maximum(me * cols - 8, 0), 8)
    after = pl.multiple_of(jnp.minimum((me + 1) * cols, width - 8), 8)
    left = turned_ref[pl.ds(before, 8), :][8 - halo :]
    right = turned_ref[pl.ds(after, 8), :][:halo]
    if plan.sides == 1:
        beside = jnp.where(me > 0, left, right)
    else:
        beside = jnp.concatenate([left, right], axis=0)
    lines = [
        strip[k * plan.edges : (k + 1) * plan.edges] - beside[:, k : k + 1] * wide[k : k + 1]
        for k in range(count)
    ]
    rows, slots = plan.rows, plan.slots
    stacks = []
    for slot in range(slots):
        members = []
        for group in range(plan.groups):
            k = group * slots + slot
            members.append(lines[k] if k < count else jnp.zeros((plan.edges, width), F32))
        stacks.append(jnp.concatenate(members, axis=0))
    lane = lax.broadcasted_iota(jnp.int32, (plan.side_rows, cols), 1)
    spare = plan.block_rows - plan.lead - plan.half_rows
    for step, out_ref in zip(step_order(plan), out_refs):
        first = partner(chip, step, plan.chips) * 2 * plan.band
        groups = [
            field_ref[k, pl.ds(pl.multiple_of(first + 8 + 8 * group, 8), 8), :]
            for group in range(2 * plan.lone + plan.shared)
            for k in range(count)
        ]
        sides = []
        for core in range(2):
            side = jnp.zeros((plan.side_rows, cols), F32)
            for slot in range(slots):
                amount = lax.rem(slot * rows + halo + width - core * plan.band - first, width)
                moved = pltpu.roll(stacks[slot], amount, 1)[:, :cols]
                side = jnp.where((lane >= slot * rows) & (lane < (slot + 1) * rows), moved, side)
            sides.append(side)
        lone = plan.lone * count
        pieces = groups[:lone] + sides[:1] + groups[lone:] + sides[1:]
        if spare:
            pieces.append(jnp.zeros((spare, cols), F32))
        out_ref[...] = jnp.concatenate(pieces, axis=0).astype(BF16)


def core_pack(plan, *refs):
    *block_refs, out_ref = refs
    other = 1 - lax.axis_index("head") % 2
    for k, block_ref in enumerate(block_refs):
        out_ref[k] = half(plan, block_ref[...].astype(F32), other).astype(BF16)


def kernel_pack(blocks_ref, out_ref):
    layers, convs, height, breadth = blocks_ref.shape[:4]
    for b in range(layers):
        for m in range(convs):
            out_ref[b * convs + m] = jnp.concatenate(
                [
                    jnp.concatenate(
                        [blocks_ref[b, m, dy, dx].astype(F32) for dy in range(height)], axis=1
                    )
                    for dx in range(breadth)
                ],
                axis=0,
            ).astype(BF16)


def shifted(ref, rows, base, offset, size):
    begin = base + offset
    low = begin // LANES * LANES
    rest = begin - low
    if rest == 0:
        return ref[rows, low : low + size]
    return pltpu.roll(ref[rows, low : low + size + LANES], size + LANES - rest, 1)[:, :size]


def stack(plan, order, *refs):
    chips = plan.chips
    own_refs, swap_refs = refs[:chips], refs[chips : chips + len(order)]
    refs = refs[chips + len(order) :]
    proj_ref, side_ref, kernel_ref, vector_ref, mask_ref, spots_ref, out_ref = refs[:7]
    maps_ref, sides_ref, field_ref, stream_ref, hidden_ref, taps_ref, logit_ref = refs[7:]
    count, cols, rows, halo = plan.maps, plan.cols, plan.rows, plan.halo
    heads, feat, chunk, stride = plan.heads, plan.feat, plan.chunk, plan.stride
    head = lax.axis_index("head")
    chip, core = head // 2, head % 2
    group = plan.group_rows

    def spread(block, source):
        for k in range(plan.lone + plan.shared):
            value = block[k * group : (k + 1) * group]
            if k >= plan.lone:
                late = block[plan.side_rows + k * group : plan.side_rows + (k + 1) * group]
                value = jnp.where(core == 0, late, value)
            place = pl.multiple_of((k * heads + source) * group, 8)
            maps_ref[pl.ds(place, group), :] = value
        side = jnp.where(
            core == 0,
            block[plan.lone * group : plan.lead],
            block[plan.half_rows - plan.side_rows : plan.half_rows],
        )
        place = pl.multiple_of(source * plan.side_rows, 8)
        sides_ref[pl.ds(place, plan.side_rows), :] = side

    for steps, swap_ref in zip(order, swap_refs):
        for k, step in enumerate(steps):
            source = 2 * partner(chip, step, chips, back=True)
            spread(half(plan, own_refs[step_order(plan).index(step)][...].astype(F32), core), source + core)
            spread(swap_ref[k].astype(F32), source + 1 - core)
    bias = vector_ref[:, 0:1]

    slots, members = plan.slots, heads * plan.groups
    lane = lax.broadcasted_iota(jnp.int32, (members, cols), 1)
    placed = []
    for first in range(0, plan.edges, slots):
        parts = [jnp.zeros((members, cols), F32) for _ in range(slots)]
        for at in range(min(slots, plan.edges - first)):
            value = sides_ref[pl.ds(first + at, members, stride=plan.edges), :]
            keep = (lane >= at * rows) & (lane < (at + 1) * rows)
            for slot in range(slots):
                moved = value
                if at != slot:
                    moved = pltpu.roll(value, ((at - slot) * rows) % cols, 1)
                parts[slot] = jnp.where(keep, moved, parts[slot])
        stacked = jnp.concatenate(parts, axis=0).astype(BF16)
        placed.append((dot(side_ref[...], stacked) + bias).astype(BF16))

    chunks = -(-(rows * stride + plan.start) // chunk)
    for i in range(chunks):
        here = slice(i * chunk, (i + 1) * chunk)
        field_ref[:, here] = sum(
            dot(columns, spots_ref[k, :, here]) for k, columns in enumerate(placed)
        )

    weight = proj_ref[...]
    spot = lax.broadcasted_iota(jnp.int32, (feat, cols), 1)
    per = 2
    for r in range(0, rows, per):
        blocks = [
            maps_ref[
                pl.ds((r + k) // 8 * heads * group + (r + k) % 8, heads * count, stride=8), :
            ].astype(BF16)
            for k in range(per)
        ]
        pair = dot(weight, jnp.concatenate(blocks, axis=1)) + bias
        for k in range(per):
            begin = plan.start + (r + k) * stride + halo
            low, rest = begin // LANES * LANES, begin % LANES
            value = pair[:, k * cols : (k + 1) * cols]
            if rest == 0:
                field_ref[:, low : low + cols] += value
                continue
            value = pltpu.roll(value, rest, 1)
            field_ref[:, low : low + cols] += jnp.where(spot >= rest, value, 0.0)
            field_ref[:, low + cols : low + 2 * cols] += jnp.where(spot < rest, value, 0.0)

    for i in range(chunks):
        here = slice(i * chunk, (i + 1) * chunk)
        stream_ref[:, here] = jnp.where(mask_ref[:, here] > 0, field_ref[:, here], 0.0).astype(BF16)

    everything = slice(None)
    for n in range(plan.convs):
        source = hidden_ref if n % 2 else stream_ref
        low = (plan.start + (n + 1) * stride) // LANES * LANES
        steps = -(-(plan.start + (rows - n - 1) * stride - low) // chunk)
        offsets = vector_ref[:, n + 1 : n + 2]

        def multiply(base):
            window = jnp.concatenate(
                [shifted(source, everything, base, d * stride, chunk) for d in (-1, 0, 1)], axis=0
            )
            taps_ref[:, base : base + chunk] = dot(kernel_ref[n], window)

        def finish(base):
            here = slice(base, base + chunk)
            value = taps_ref[feat : 2 * feat, here]
            value = value + shifted(taps_ref, slice(0, feat), base, -1, chunk)
            value = value + shifted(taps_ref, slice(2 * feat, 3 * feat), base, 1, chunk)
            value = value + offsets
            keep = mask_ref[:, here] > 0
            if n % 2 == 0:
                value = jnp.where(value > 0, value, jnp.exp(jnp.minimum(value, 0.0)) - 1.0)
                hidden_ref[:, here] = jnp.where(keep, value, 0.0).astype(BF16)
                return
            value = (stream_ref[:, here].astype(F32) + value).astype(BF16)
            if n < plan.convs - 1:
                stream_ref[:, here] = jnp.where(keep, value.astype(F32), 0.0).astype(BF16)
                return
            readout = vector_ref[:, plan.convs + 1 : plan.convs + 2]
            logit_ref[0:1, here] = jnp.sum(value.astype(F32) * readout, axis=0, keepdims=True)

        for i in range(steps + 1):
            if i < steps:
                multiply(low + i * chunk)
            if i > 0:
                finish(low + (i - 1) * chunk)

    for r in range(plan.band):
        begin = plan.start + (r + halo) * stride + halo
        low = begin // LANES * LANES
        out_ref[r : r + 1, :] = shifted(logit_ref, slice(0, 1), low, begin - low, cols)


def call(kernel, name, args, outs, scratch=()):
    held = sum(math.prod(x.shape) * jnp.dtype(x.dtype).itemsize for x in [*args, *outs, *scratch])
    vmem = pl.BlockSpec(memory_space=pltpu.VMEM)
    return pl.pallas_call(
        kernel,
        out_shape=list(outs),
        in_specs=[vmem] * len(args),
        out_specs=[vmem] * len(outs),
        scratch_shapes=list(scratch),
        compiler_params=pltpu.CompilerParams(vmem_limit_bytes=held * 5 // 4 + 4 * 1024 * 1024),
        name=name,
    )(*args)


def array(dtype, *shape):
    return jax.ShapeDtypeStruct(shape, dtype)


def on_device(attention, proj_weight, proj_bias, conv_weight, conv_bias, out_weight):
    maps, width, cols = attention.shape
    feat = proj_weight.shape[0]
    blocks, convs = conv_weight.shape[:2]
    tiles, heads = lax.axis_size("tile"), lax.axis_size("head")
    plan = Plan(maps, width, cols, tiles, heads, feat, blocks * convs)
    me, band_index = lax.axis_index("tile"), lax.axis_index("head")

    payload, sums, edge = call(
        functools.partial(mirror_pack, plan),
        "mirror_pack",
        [attention],
        [
            array(BF16, tiles - 1, maps * cols + plan.tail_rows, cols),
            array(F32, plan.map_rows, width),
            array(F32, plan.edge_rows, cols),
        ],
    )
    received = jnp.stack(
        [
            lax.ppermute(payload[s - 1], "tile", [(i, (i + s) % tiles) for i in range(tiles)])
            for s in range(tiles - 1, 0, -1)
        ]
    )

    stride, start = plan.stride, plan.start
    side_weight = proj_weight.reshape(feat, heads, maps)
    side_weight = jnp.pad(side_weight, ((0, 0), (0, 0), (0, plan.groups * plan.slots - maps)))
    side_weight = side_weight.reshape(feat, heads, plan.groups, plan.slots)
    side_weight = side_weight.transpose(0, 3, 1, 2).reshape(feat, -1)
    (kernels,) = call(
        kernel_pack,
        "kernel_pack",
        [conv_weight.transpose(0, 1, 4, 5, 2, 3)],
        [array(BF16, plan.convs, 3 * feat, 3 * feat)],
    )
    vectors = jnp.concatenate(
        [proj_bias[None], conv_bias.reshape(-1, feat), out_weight[None]], axis=0
    ).T
    spot = np.arange(plan.lanes) - start
    row = band_index * plan.band - plan.halo + (spot // stride).astype(np.int32)
    col = me * cols - plan.halo + (spot % stride).astype(np.int32)
    mask = (row >= 0) & (row < width) & (col >= 0) & (col < width)
    mask = mask.astype(F32)[None]

    key = np.arange(cols)
    member, line = key // plan.rows, key % plan.rows
    spots = []
    for first in range(0, plan.edges, plan.slots):
        column = first + member
        fits = (member < plan.slots) & (column < plan.edges)
        places = (0, plan.halo + cols) if plan.sides == 1 else (np.where(column < plan.halo, 0, cols),)
        target = [np.where(fits, start + line * stride + column + p, -1) for p in places]
        hit = [jnp.arange(plan.lanes)[None] == jnp.asarray(p, jnp.int32)[:, None] for p in target]
        spots.append(functools.reduce(jnp.logical_or, hit).astype(BF16))
    spots = jnp.stack(spots)

    weights = (side_weight, kernels, vectors, mask, spots)
    received, weights = lax.optimization_barrier((received, weights))

    chips = plan.chips
    blocks = call(
        functools.partial(correct_pack, plan),
        "correct_pack",
        [attention, received, sums, edge],
        [array(BF16, plan.block_rows, cols)] * chips,
        [pltpu.VMEM((maps, width + 24, cols), F32), pltpu.VMEM((width, LANES), F32)],
    )
    arrived = {}
    for step, block in zip(step_order(plan), blocks):
        pairs = [(i, 2 * partner(i // 2, step, chips) + i % 2) for i in range(heads)]
        arrived[step] = lax.ppermute(block, "head", pairs) if step else block
    far, near = far_near(plan)
    order = [far, near + [0]]
    swapped = []
    for steps in order:
        (packed,) = call(
            functools.partial(core_pack, plan),
            "core_pack",
            [arrived[k] for k in steps],
            [array(BF16, len(steps), plan.half_rows, cols)],
        )
        swapped.append(lax.ppermute(packed, "head", [(i, i ^ 1) for i in range(heads)]))

    (logits,) = call(
        functools.partial(stack, plan, order),
        "stack",
        [*arrived.values(), *swapped, proj_weight, *weights],
        [array(F32, plan.band, cols)],
        [
            pltpu.VMEM((heads * maps * plan.rows, cols), F32),
            pltpu.VMEM((heads * plan.side_rows, cols), F32),
            pltpu.VMEM((feat, plan.lanes), F32),
            pltpu.VMEM((feat, plan.lanes), BF16),
            pltpu.VMEM((feat, plan.lanes), BF16),
            pltpu.VMEM((3 * feat, plan.lanes), F32),
            pltpu.VMEM((8, plan.lanes), F32),
        ],
    )
    return logits


def solution(mesh):
    return jax.shard_map(
        on_device,
        mesh=mesh,
        in_specs=(P(("grp", "head"), None, "tile"), P(), P(), P(), P(), P()),
        out_specs=P(("grp", "head"), "tile"),
        check_vma=False,
    )
```

```python
import functools
import math
from typing import NamedTuple

import jax
import jax.numpy as jnp
import numpy as np
from jax import lax
from jax.experimental import pallas as pl
from jax.experimental.pallas import tpu as pltpu
from jax.sharding import PartitionSpec as P

BF16, F32 = jnp.bfloat16, jnp.float32
LANES = 128


def up(value, step):
    return -(-value // step) * step


class Plan(NamedTuple):
    maps: int
    width: int
    cols: int
    tiles: int
    heads: int
    feat: int
    convs: int

    @property
    def halo(self):
        return self.convs

    @property
    def sides(self):
        return min(2, self.tiles - 1)

    @property
    def edges(self):
        return self.sides * self.halo

    @property
    def edge_rows(self):
        return up(self.maps * self.edges, 8)

    @property
    def map_rows(self):
        return up(self.maps, 16)

    @property
    def tail_rows(self):
        return up((1 + self.tiles) * self.edge_rows + 3 * self.tiles * self.map_rows, 16)

    @property
    def band(self):
        return self.width // self.heads

    @property
    def rows(self):
        return self.band + 2 * self.halo

    @property
    def slots(self):
        return self.cols // self.rows

    @property
    def groups(self):
        return -(-self.maps // self.slots)

    @property
    def side_rows(self):
        return self.groups * self.edges

    @property
    def chips(self):
        return self.heads // 2

    @property
    def lone(self):
        return self.band // 8

    @property
    def shared(self):
        return 2 * self.halo // 8

    @property
    def group_rows(self):
        return 8 * self.maps

    @property
    def lead(self):
        return self.lone * self.group_rows + self.side_rows

    @property
    def half_rows(self):
        return self.lead + self.shared * self.group_rows

    @property
    def block_rows(self):
        return up(self.lead + self.half_rows, 16)

    @property
    def stride(self):
        return self.cols + 2 * self.halo

    @property
    def start(self):
        return up(self.stride, LANES) - LANES

    @property
    def chunk(self):
        return 256

    @property
    def lanes(self):
        return up(self.start + self.rows * self.stride, LANES) + 2 * self.chunk + 3 * LANES


def partner(mine, step, count, back=False):
    if count & (count - 1) == 0:
        return mine ^ step
    return (mine - step if back else mine + step) % count


def far_near(plan):
    steps = list(range(plan.chips - 1, 0, -1))
    return steps[: plan.chips // 2], steps[plan.chips // 2 :]


def step_order(plan):
    far, near = far_near(plan)
    return far + near + [0]


def half(plan, block, core):
    return jnp.where(
        core == 0, block[: plan.half_rows], block[plan.lead : plan.lead + plan.half_rows]
    )


def edge_start(plan, tile, side):
    left, right = plan.cols * tile - plan.halo, plan.cols * (tile + 1)
    if plan.sides == 1:
        return jnp.where(tile > 0, left, right)
    return (left, right)[side]


def edge_select(plan, tile, row, position, index):
    hit = None
    for side in range(plan.sides):
        first = index * plan.edges + side * plan.halo
        inside = (row >= first) & (row < first + plan.halo)
        one = inside & (position == row - first + edge_start(plan, tile, side))
        hit = one if hit is None else hit | one
    return hit


def across(a, b):
    return lax.dot_general(a, b, (((1,), (1,)), ((), ())), preferred_element_type=F32)


def dot(a, b):
    return jnp.dot(a, b, preferred_element_type=F32)


def mirror_pack(plan, source_ref, out_ref, sums_ref, edge_ref, maps_ref, arrived):
    me = lax.axis_index("tile")
    count, cols, width, tiles = plan.maps, plan.cols, plan.width, plan.tiles
    head, edge = plan.map_rows, plan.edge_rows

    def pick(rows, span, base, tile, index):
        row = lax.broadcasted_iota(jnp.int32, (rows, span), 0)
        position = lax.broadcasted_iota(jnp.int32, (rows, span), 1) + base
        return edge_select(plan, tile, row, position, index).astype(F32)

    def total(span, index):
        return (lax.broadcasted_iota(jnp.int32, (head, span), 0) == index).astype(F32)

    copies = [
        pltpu.make_async_copy(source_ref.at[index], maps_ref.at[index], arrived.at[index])
        for index in range(count)
    ]
    for copy in copies:
        copy.start()
    for shift in range(1, tiles):
        dest = lax.rem(me + shift, tiles)
        by_col = by_row = None
        for index in range(count):
            if shift == 1:
                copies[index].wait()
            block = maps_ref[index]
            out_ref[shift - 1, index * cols : (index + 1) * cols, :] = maps_ref[
                index, pl.ds(pl.multiple_of(dest * cols, cols), cols), :
            ]
            left = [pick(edge, cols, me * cols, dest, index)]
            upper = [pick(edge, width, 0, dest, index)]
            if shift == 1:
                left.append(total(cols, index))
                upper.append(total(width, index))
                upper.append(pick(edge, width, 0, me, index))
            by_c = across(jnp.concatenate(left, axis=0).astype(BF16), block)
            by_r = dot(jnp.concatenate(upper, axis=0).astype(BF16), block)
            by_col = by_c if by_col is None else by_col + by_c
            by_row = by_r if by_row is None else by_row + by_r
        if shift == 1:
            sums_ref[...] = by_col[edge : edge + head]
            own = pl.ds(pl.multiple_of(me * cols, cols), cols)
            sums_ref[:, own] = sums_ref[:, own] + by_row[edge : edge + head]
            edge_ref[...] = by_row[edge + head :]
            sums = sums_ref[...]
            high = sums.astype(BF16).astype(F32)
            middle = (sums - high).astype(BF16).astype(F32)
            low = sums - high - middle
        pieces = [by_row[:edge]]
        for wide in (by_col[:edge], high, middle, low):
            pieces += [wide[:, k * cols : (k + 1) * cols] for k in range(tiles)]
        used = (1 + tiles) * edge + 3 * tiles * head
        if plan.tail_rows > used:
            pieces.append(jnp.zeros((plan.tail_rows - used, cols), F32))
        out_ref[shift - 1, count * cols :, :] = jnp.concatenate(pieces, axis=0).astype(BF16)


def correct_pack(plan, maps_ref, recv_ref, sums_ref, edge_ref, *refs):
    *out_refs, field_ref, turned_ref = refs
    me, chip = lax.axis_index("tile"), lax.axis_index("head") // 2
    count, cols, width, tiles = plan.maps, plan.cols, plan.width, plan.tiles
    head, edge, halo = plan.map_rows, plan.edge_rows, plan.halo
    tails = [recv_ref[k, count * cols :, :].astype(F32) for k in range(tiles - 1)]

    rowsum = []
    for b in range(tiles):
        value = sums_ref[:, b * cols : (b + 1) * cols]
        for tail in tails:
            base = (1 + tiles) * edge
            parts = [
                tail[base + (k * tiles + b) * head : base + (k * tiles + b + 1) * head]
                for k in range(3)
            ]
            value = value + ((parts[0] + parts[1]) + parts[2])
        rowsum.append(value)
    grand = sum(jnp.sum(value, axis=1, keepdims=True) for value in rowsum)
    grand = jnp.where(lax.broadcasted_iota(jnp.int32, (head, 1), 0) < count, grand, 1.0)
    scaled = [value / grand for value in rowsum]
    for b in range(tiles):
        square = jnp.concatenate([rowsum[b], jnp.zeros((LANES - head, cols), F32)], axis=0)
        turned_ref[b * cols : (b + 1) * cols, :] = square.T
    mine = scaled[0]
    for b in range(1, tiles):
        mine = jnp.where(me == b, scaled[b], mine)

    eye = (
        lax.broadcasted_iota(jnp.int32, (cols, cols), 0)
        == lax.broadcasted_iota(jnp.int32, (cols, cols), 1)
    ).astype(F32).astype(BF16)
    margin = 8 + halo
    for index in range(count):
        field_ref[index, :16, :] = jnp.zeros((16, cols), F32)
        field_ref[index, width + 8 :, :] = jnp.zeros((16, cols), F32)
        for b in range(tiles):
            shift = lax.rem(b - me + tiles, tiles)
            other = recv_ref[
                jnp.maximum(shift - 1, 0), index * cols : (index + 1) * cols, :
            ]
            own = maps_ref[index, b * cols : (b + 1) * cols, :]
            mirror = across(eye, jnp.where(shift == 0, own, other))
            column = turned_ref[b * cols : (b + 1) * cols, index : index + 1]
            field_ref[index, margin + b * cols : margin + (b + 1) * cols, :] = (
                own.astype(F32) + mirror - column * mine[index : index + 1]
            )

    strips = []
    for b in range(tiles):
        strip = edge_ref[...]
        for k, tail in enumerate(tails):
            strip = jnp.where(lax.rem(me + k + 1, tiles) == b, tail[:edge], strip)
        for tail in tails:
            strip = strip + tail[(1 + b) * edge : (2 + b) * edge]
        strips.append(strip)
    strip = jnp.concatenate(strips, axis=1)
    wide = jnp.concatenate(scaled, axis=1)
    before = pl.multiple_of(jnp.maximum(me * cols - 8, 0), 8)
    after = pl.multiple_of(jnp.minimum((me + 1) * cols, width - 8), 8)
    left = turned_ref[pl.ds(before, 8), :][8 - halo :]
    right = turned_ref[pl.ds(after, 8), :][:halo]
    if plan.sides == 1:
        beside = jnp.where(me > 0, left, right)
    else:
        beside = jnp.concatenate([left, right], axis=0)
    lines = [
        strip[k * plan.edges : (k + 1) * plan.edges] - beside[:, k : k + 1] * wide[k : k + 1]
        for k in range(count)
    ]
    rows, slots = plan.rows, plan.slots
    stacks = []
    for slot in range(slots):
        members = []
        for group in range(plan.groups):
            k = group * slots + slot
            members.append(lines[k] if k < count else jnp.zeros((plan.edges, width), F32))
        stacks.append(jnp.concatenate(members, axis=0))
    lane = lax.broadcasted_iota(jnp.int32, (plan.side_rows, cols), 1)
    spare = plan.block_rows - plan.lead - plan.half_rows
    for step, out_ref in zip(step_order(plan), out_refs):
        first = partner(chip, step, plan.chips) * 2 * plan.band
        groups = [
            field_ref[k, pl.ds(pl.multiple_of(first + 8 + 8 * group, 8), 8), :]
            for group in range(2 * plan.lone + plan.shared)
            for k in range(count)
        ]
        sides = []
        for core in range(2):
            side = jnp.zeros((plan.side_rows, cols), F32)
            for slot in range(slots):
                amount = lax.rem(slot * rows + halo + width - core * plan.band - first, width)
                moved = pltpu.roll(stacks[slot], amount, 1)[:, :cols]
                side = jnp.where((lane >= slot * rows) & (lane < (slot + 1) * rows), moved, side)
            sides.append(side)
        lone = plan.lone * count
        pieces = groups[:lone] + sides[:1] + groups[lone:] + sides[1:]
        if spare:
            pieces.append(jnp.zeros((spare, cols), F32))
        out_ref[...] = jnp.concatenate(pieces, axis=0).astype(BF16)


def core_pack(plan, *refs):
    *block_refs, out_ref = refs
    other = 1 - lax.axis_index("head") % 2
    for k, block_ref in enumerate(block_refs):
        out_ref[k] = half(plan, block_ref[...].astype(F32), other).astype(BF16)


def kernel_pack(blocks_ref, out_ref):
    layers, convs, height, breadth = blocks_ref.shape[:4]
    for b in range(layers):
        for m in range(convs):
            out_ref[b * convs + m] = jnp.concatenate(
                [
                    jnp.concatenate(
                        [blocks_ref[b, m, dy, dx].astype(F32) for dy in range(height)], axis=1
                    )
                    for dx in range(breadth)
                ],
                axis=0,
            ).astype(BF16)


def shifted(ref, rows, base, offset, size):
    begin = base + offset
    low = begin // LANES * LANES
    rest = begin - low
    if rest == 0:
        return ref[rows, low : low + size]
    return pltpu.roll(ref[rows, low : low + size + LANES], size + LANES - rest, 1)[:, :size]


def stack(plan, order, *refs):
    chips = plan.chips
    own_refs, swap_refs = refs[:chips], refs[chips : chips + len(order)]
    refs = refs[chips + len(order) :]
    proj_ref, side_ref, kernel_ref, vector_ref, mask_ref, spots_ref, out_ref = refs[:7]
    maps_ref, sides_ref, field_ref, stream_ref, hidden_ref, taps_ref, logit_ref = refs[7:]
    count, cols, rows, halo = plan.maps, plan.cols, plan.rows, plan.halo
    heads, feat, chunk, stride = plan.heads, plan.feat, plan.chunk, plan.stride
    head = lax.axis_index("head")
    chip, core = head // 2, head % 2
    group = plan.group_rows

    def spread(block, source):
        for k in range(plan.lone + plan.shared):
            value = block[k * group : (k + 1) * group]
            if k >= plan.lone:
                late = block[plan.side_rows + k * group : plan.side_rows + (k + 1) * group]
                value = jnp.where(core == 0, late, value)
            place = pl.multiple_of((k * heads + source) * group, 8)
            maps_ref[pl.ds(place, group), :] = value
        side = jnp.where(
            core == 0,
            block[plan.lone * group : plan.lead],
            block[plan.half_rows - plan.side_rows : plan.half_rows],
        )
        place = pl.multiple_of(source * plan.side_rows, 8)
        sides_ref[pl.ds(place, plan.side_rows), :] = side

    for steps, swap_ref in zip(order, swap_refs):
        for k, step in enumerate(steps):
            source = 2 * partner(chip, step, chips, back=True)
            spread(half(plan, own_refs[step_order(plan).index(step)][...].astype(F32), core), source + core)
            spread(swap_ref[k].astype(F32), source + 1 - core)
    bias = vector_ref[:, 0:1]

    slots, members = plan.slots, heads * plan.groups
    lane = lax.broadcasted_iota(jnp.int32, (members, cols), 1)
    placed = []
    for first in range(0, plan.edges, slots):
        parts = [jnp.zeros((members, cols), F32) for _ in range(slots)]
        for at in range(min(slots, plan.edges - first)):
            value = sides_ref[pl.ds(first + at, members, stride=plan.edges), :]
            keep = (lane >= at * rows) & (lane < (at + 1) * rows)
            for slot in range(slots):
                moved = value
                if at != slot:
                    moved = pltpu.roll(value, ((at - slot) * rows) % cols, 1)
                parts[slot] = jnp.where(keep, moved, parts[slot])
        stacked = jnp.concatenate(parts, axis=0).astype(BF16)
        placed.append((dot(side_ref[...], stacked) + bias).astype(BF16))

    chunks = -(-(rows * stride + plan.start) // chunk)
    for i in range(chunks):
        here = slice(i * chunk, (i + 1) * chunk)
        field_ref[:, here] = sum(
            dot(columns, spots_ref[k, :, here]) for k, columns in enumerate(placed)
        )

    weight = proj_ref[...]
    spot = lax.broadcasted_iota(jnp.int32, (feat, cols), 1)
    per = 2
    for r in range(0, rows, per):
        blocks = [
            maps_ref[
                pl.ds((r + k) // 8 * heads * group + (r + k) % 8, heads * count, stride=8), :
            ].astype(BF16)
            for k in range(per)
        ]
        pair = dot(weight, jnp.concatenate(blocks, axis=1)) + bias
        for k in range(per):
            begin = plan.start + (r + k) * stride + halo
            low, rest = begin // LANES * LANES, begin % LANES
            value = pair[:, k * cols : (k + 1) * cols]
            if rest == 0:
                field_ref[:, low : low + cols] += value
                continue
            value = pltpu.roll(value, rest, 1)
            field_ref[:, low : low + cols] += jnp.where(spot >= rest, value, 0.0)
            field_ref[:, low + cols : low + 2 * cols] += jnp.where(spot < rest, value, 0.0)

    for i in range(chunks):
        here = slice(i * chunk, (i + 1) * chunk)
        stream_ref[:, here] = jnp.where(mask_ref[:, here] > 0, field_ref[:, here], 0.0).astype(BF16)

    everything = slice(None)
    for n in range(plan.convs):
        source = hidden_ref if n % 2 else stream_ref
        low = (plan.start + (n + 1) * stride) // LANES * LANES
        steps = -(-(plan.start + (rows - n - 1) * stride - low) // chunk)
        offsets = vector_ref[:, n + 1 : n + 2]

        def multiply(base):
            window = jnp.concatenate(
                [shifted(source, everything, base, d * stride, chunk) for d in (-1, 0, 1)], axis=0
            )
            taps_ref[:, base : base + chunk] = dot(kernel_ref[n], window)

        def finish(base):
            here = slice(base, base + chunk)
            value = taps_ref[feat : 2 * feat, here]
            value = value + shifted(taps_ref, slice(0, feat), base, -1, chunk)
            value = value + shifted(taps_ref, slice(2 * feat, 3 * feat), base, 1, chunk)
            value = value + offsets
            keep = mask_ref[:, here] > 0
            if n % 2 == 0:
                value = jnp.where(value > 0, value, jnp.exp(jnp.minimum(value, 0.0)) - 1.0)
                hidden_ref[:, here] = jnp.where(keep, value, 0.0).astype(BF16)
                return
            value = (stream_ref[:, here].astype(F32) + value).astype(BF16)
            if n < plan.convs - 1:
                stream_ref[:, here] = jnp.where(keep, value.astype(F32), 0.0).astype(BF16)
                return
            readout = vector_ref[:, plan.convs + 1 : plan.convs + 2]
            logit_ref[0:1, here] = jnp.sum(value.astype(F32) * readout, axis=0, keepdims=True)

        for i in range(steps + 2):
            if i > 1:
                finish(low + (i - 2) * chunk)
            if i < steps:
                multiply(low + i * chunk)

    for r in range(plan.band):
        begin = plan.start + (r + halo) * stride + halo
        low = begin // LANES * LANES
        out_ref[r : r + 1, :] = shifted(logit_ref, slice(0, 1), low, begin - low, cols)


def call(kernel, name, args, outs, scratch=(), space=pltpu.VMEM, semaphores=()):
    held = sum(math.prod(x.shape) * jnp.dtype(x.dtype).itemsize for x in [*args, *outs, *scratch])
    vmem = pl.BlockSpec(memory_space=pltpu.VMEM)
    return pl.pallas_call(
        kernel,
        out_shape=list(outs),
        in_specs=[pl.BlockSpec(memory_space=space)] + [vmem] * (len(args) - 1),
        out_specs=[vmem] * len(outs),
        scratch_shapes=[*scratch, *semaphores],
        compiler_params=pltpu.CompilerParams(vmem_limit_bytes=held * 5 // 4 + 4 * 1024 * 1024),
        name=name,
    )(*args)


def array(dtype, *shape):
    return jax.ShapeDtypeStruct(shape, dtype)


def on_device(attention, proj_weight, proj_bias, conv_weight, conv_bias, out_weight):
    maps, width, cols = attention.shape
    feat = proj_weight.shape[0]
    blocks, convs = conv_weight.shape[:2]
    tiles, heads = lax.axis_size("tile"), lax.axis_size("head")
    plan = Plan(maps, width, cols, tiles, heads, feat, blocks * convs)
    me, band_index = lax.axis_index("tile"), lax.axis_index("head")

    payload, sums, edge = call(
        functools.partial(mirror_pack, plan),
        "mirror_pack",
        [attention],
        [
            array(BF16, tiles - 1, maps * cols + plan.tail_rows, cols),
            array(F32, plan.map_rows, width),
            array(F32, plan.edge_rows, cols),
        ],
        [pltpu.VMEM(attention.shape, BF16)],
        space=pltpu.HBM,
        semaphores=[pltpu.SemaphoreType.DMA((maps,))],
    )
    received = jnp.stack(
        [
            lax.ppermute(payload[s - 1], "tile", [(i, (i + s) % tiles) for i in range(tiles)])
            for s in range(tiles - 1, 0, -1)
        ]
    )

    stride, start = plan.stride, plan.start
    side_weight = proj_weight.reshape(feat, heads, maps)
    side_weight = jnp.pad(side_weight, ((0, 0), (0, 0), (0, plan.groups * plan.slots - maps)))
    side_weight = side_weight.reshape(feat, heads, plan.groups, plan.slots)
    side_weight = side_weight.transpose(0, 3, 1, 2).reshape(feat, -1)
    (kernels,) = call(
        kernel_pack,
        "kernel_pack",
        [conv_weight.transpose(0, 1, 4, 5, 2, 3)],
        [array(BF16, plan.convs, 3 * feat, 3 * feat)],
    )
    vectors = jnp.concatenate(
        [proj_bias[None], conv_bias.reshape(-1, feat), out_weight[None]], axis=0
    ).T
    spot = np.arange(plan.lanes) - start
    row = band_index * plan.band - plan.halo + (spot // stride).astype(np.int32)
    col = me * cols - plan.halo + (spot % stride).astype(np.int32)
    mask = (row >= 0) & (row < width) & (col >= 0) & (col < width)
    mask = mask.astype(F32)[None]

    key = np.arange(cols)
    member, line = key // plan.rows, key % plan.rows
    spots = []
    for first in range(0, plan.edges, plan.slots):
        column = first + member
        fits = (member < plan.slots) & (column < plan.edges)
        places = (0, plan.halo + cols) if plan.sides == 1 else (np.where(column < plan.halo, 0, cols),)
        target = [np.where(fits, start + line * stride + column + p, -1) for p in places]
        hit = [jnp.arange(plan.lanes)[None] == jnp.asarray(p, jnp.int32)[:, None] for p in target]
        spots.append(functools.reduce(jnp.logical_or, hit).astype(BF16))
    spots = jnp.stack(spots)

    weights = (side_weight, kernels, vectors, mask, spots)
    received, weights = lax.optimization_barrier((received, weights))

    chips = plan.chips
    blocks = call(
        functools.partial(correct_pack, plan),
        "correct_pack",
        [attention, received, sums, edge],
        [array(BF16, plan.block_rows, cols)] * chips,
        [pltpu.VMEM((maps, width + 24, cols), F32), pltpu.VMEM((width, LANES), F32)],
    )
    arrived = {}
    for step, block in zip(step_order(plan), blocks):
        pairs = [(i, 2 * partner(i // 2, step, chips) + i % 2) for i in range(heads)]
        arrived[step] = lax.ppermute(block, "head", pairs) if step else block
    far, near = far_near(plan)
    order = [far, near + [0]]
    swapped = []
    for steps in order:
        (packed,) = call(
            functools.partial(core_pack, plan),
            "core_pack",
            [arrived[k] for k in steps],
            [array(BF16, len(steps), plan.half_rows, cols)],
        )
        swapped.append(lax.ppermute(packed, "head", [(i, i ^ 1) for i in range(heads)]))

    (logits,) = call(
        functools.partial(stack, plan, order),
        "stack",
        [*arrived.values(), *swapped, proj_weight, *weights],
        [array(F32, plan.band, cols)],
        [
            pltpu.VMEM((heads * maps * plan.rows, cols), F32),
            pltpu.VMEM((heads * plan.side_rows, cols), F32),
            pltpu.VMEM((feat, plan.lanes), F32),
            pltpu.VMEM((feat, plan.lanes), BF16),
            pltpu.VMEM((feat, plan.lanes), BF16),
            pltpu.VMEM((3 * feat, plan.lanes), F32),
            pltpu.VMEM((8, plan.lanes), F32),
        ],
    )
    return logits


def solution(mesh):
    return jax.shard_map(
        on_device,
        mesh=mesh,
        in_specs=(P(("grp", "head"), None, "tile"), P(), P(), P(), P(), P()),
        out_specs=P(("grp", "head"), "tile"),
        check_vma=False,
    )
```

```python
import functools
import math
from typing import NamedTuple

import jax
import jax.numpy as jnp
import numpy as np
from jax import lax
from jax.experimental import pallas as pl
from jax.experimental.pallas import tpu as pltpu
from jax.sharding import PartitionSpec as P

BF16, F32 = jnp.bfloat16, jnp.float32
LANES = 128


def up(value, step):
    return -(-value // step) * step


class Plan(NamedTuple):
    maps: int
    width: int
    cols: int
    tiles: int
    heads: int
    feat: int
    convs: int

    @property
    def halo(self):
        return self.convs

    @property
    def sides(self):
        return min(2, self.tiles - 1)

    @property
    def edges(self):
        return self.sides * self.halo

    @property
    def edge_rows(self):
        return up(self.maps * self.edges, 8)

    @property
    def map_rows(self):
        return up(self.maps, 16)

    @property
    def tail_rows(self):
        return up((1 + self.tiles) * self.edge_rows + 3 * self.tiles * self.map_rows, 16)

    @property
    def band(self):
        return self.width // self.heads

    @property
    def rows(self):
        return self.band + 2 * self.halo

    @property
    def slots(self):
        return self.cols // self.rows

    @property
    def groups(self):
        return -(-self.maps // self.slots)

    @property
    def side_rows(self):
        return self.groups * self.edges

    @property
    def chips(self):
        return self.heads // 2

    @property
    def lone(self):
        return self.band // 8

    @property
    def shared(self):
        return 2 * self.halo // 8

    @property
    def group_rows(self):
        return 8 * self.maps

    @property
    def lead(self):
        return self.lone * self.group_rows + self.side_rows

    @property
    def half_rows(self):
        return self.lead + self.shared * self.group_rows

    @property
    def block_rows(self):
        return up(self.lead + self.half_rows, 16)

    @property
    def stride(self):
        return self.cols + 2 * self.halo

    @property
    def start(self):
        return up(self.stride, LANES) - LANES

    @property
    def chunk(self):
        return 256

    @property
    def lanes(self):
        return up(self.start + self.rows * self.stride, LANES) + 6 * self.chunk + 3 * LANES


def partner(mine, step, count, back=False):
    if count & (count - 1) == 0:
        return mine ^ step
    return (mine - step if back else mine + step) % count


def far_near(plan):
    steps = list(range(plan.chips - 1, 0, -1))
    return steps[: plan.chips // 2], steps[plan.chips // 2 :]


def step_order(plan):
    far, near = far_near(plan)
    return far + near + [0]


def half(plan, block, core):
    return jnp.where(
        core == 0, block[: plan.half_rows], block[plan.lead : plan.lead + plan.half_rows]
    )


def edge_start(plan, tile, side):
    left, right = plan.cols * tile - plan.halo, plan.cols * (tile + 1)
    if plan.sides == 1:
        return jnp.where(tile > 0, left, right)
    return (left, right)[side]


def edge_select(plan, tile, row, position, index):
    hit = None
    for side in range(plan.sides):
        first = index * plan.edges + side * plan.halo
        inside = (row >= first) & (row < first + plan.halo)
        one = inside & (position == row - first + edge_start(plan, tile, side))
        hit = one if hit is None else hit | one
    return hit


def across(a, b):
    return lax.dot_general(a, b, (((1,), (1,)), ((), ())), preferred_element_type=F32)


def dot(a, b):
    return jnp.dot(a, b, preferred_element_type=F32)


def mirror_pack(plan, maps_ref, out_ref, sums_ref, edge_ref):
    me = lax.axis_index("tile")
    count, cols, width, tiles = plan.maps, plan.cols, plan.width, plan.tiles
    head, edge = plan.map_rows, plan.edge_rows

    def pick(rows, span, base, tile, index):
        row = lax.broadcasted_iota(jnp.int32, (rows, span), 0)
        position = lax.broadcasted_iota(jnp.int32, (rows, span), 1) + base
        return edge_select(plan, tile, row, position, index).astype(F32)

    def total(span, index):
        return (lax.broadcasted_iota(jnp.int32, (head, span), 0) == index).astype(F32)

    for shift in range(1, tiles):
        dest = lax.rem(me + shift, tiles)
        by_col = by_row = None
        for index in range(count):
            block = maps_ref[index]
            out_ref[shift - 1, index * cols : (index + 1) * cols, :] = maps_ref[
                index, pl.ds(pl.multiple_of(dest * cols, cols), cols), :
            ]
            left = [pick(edge, cols, me * cols, dest, index)]
            upper = [pick(edge, width, 0, dest, index)]
            if shift == 1:
                left.append(total(cols, index))
                upper.append(total(width, index))
                upper.append(pick(edge, width, 0, me, index))
            by_c = across(jnp.concatenate(left, axis=0).astype(BF16), block)
            by_r = dot(jnp.concatenate(upper, axis=0).astype(BF16), block)
            by_col = by_c if by_col is None else by_col + by_c
            by_row = by_r if by_row is None else by_row + by_r
        if shift == 1:
            sums_ref[...] = by_col[edge : edge + head]
            own = pl.ds(pl.multiple_of(me * cols, cols), cols)
            sums_ref[:, own] = sums_ref[:, own] + by_row[edge : edge + head]
            edge_ref[...] = by_row[edge + head :]
            sums = sums_ref[...]
            high = sums.astype(BF16).astype(F32)
            middle = (sums - high).astype(BF16).astype(F32)
            low = sums - high - middle
        pieces = [by_row[:edge]]
        for wide in (by_col[:edge], high, middle, low):
            pieces += [wide[:, k * cols : (k + 1) * cols] for k in range(tiles)]
        used = (1 + tiles) * edge + 3 * tiles * head
        if plan.tail_rows > used:
            pieces.append(jnp.zeros((plan.tail_rows - used, cols), F32))
        out_ref[shift - 1, count * cols :, :] = jnp.concatenate(pieces, axis=0).astype(BF16)


def correct_pack(plan, maps_ref, recv_ref, sums_ref, edge_ref, *refs):
    *out_refs, field_ref, turned_ref = refs
    me, chip = lax.axis_index("tile"), lax.axis_index("head") // 2
    count, cols, width, tiles = plan.maps, plan.cols, plan.width, plan.tiles
    head, edge, halo = plan.map_rows, plan.edge_rows, plan.halo
    tails = [recv_ref[k, count * cols :, :].astype(F32) for k in range(tiles - 1)]

    rowsum = []
    for b in range(tiles):
        value = sums_ref[:, b * cols : (b + 1) * cols]
        for tail in tails:
            base = (1 + tiles) * edge
            parts = [
                tail[base + (k * tiles + b) * head : base + (k * tiles + b + 1) * head]
                for k in range(3)
            ]
            value = value + ((parts[0] + parts[1]) + parts[2])
        rowsum.append(value)
    grand = sum(jnp.sum(value, axis=1, keepdims=True) for value in rowsum)
    grand = jnp.where(lax.broadcasted_iota(jnp.int32, (head, 1), 0) < count, grand, 1.0)
    scaled = [value / grand for value in rowsum]
    for b in range(tiles):
        square = jnp.concatenate([rowsum[b], jnp.zeros((LANES - head, cols), F32)], axis=0)
        turned_ref[b * cols : (b + 1) * cols, :] = square.T
    mine = scaled[0]
    for b in range(1, tiles):
        mine = jnp.where(me == b, scaled[b], mine)

    eye = (
        lax.broadcasted_iota(jnp.int32, (cols, cols), 0)
        == lax.broadcasted_iota(jnp.int32, (cols, cols), 1)
    ).astype(F32).astype(BF16)
    margin = 8 + halo
    for index in range(count):
        field_ref[index, :16, :] = jnp.zeros((16, cols), F32)
        field_ref[index, width + 8 :, :] = jnp.zeros((16, cols), F32)
        for b in range(tiles):
            shift = lax.rem(b - me + tiles, tiles)
            other = recv_ref[
                jnp.maximum(shift - 1, 0), index * cols : (index + 1) * cols, :
            ]
            own = maps_ref[index, b * cols : (b + 1) * cols, :]
            mirror = across(eye, jnp.where(shift == 0, own, other))
            column = turned_ref[b * cols : (b + 1) * cols, index : index + 1]
            field_ref[index, margin + b * cols : margin + (b + 1) * cols, :] = (
                own.astype(F32) + mirror - column * mine[index : index + 1]
            )

    strips = []
    for b in range(tiles):
        strip = edge_ref[...]
        for k, tail in enumerate(tails):
            strip = jnp.where(lax.rem(me + k + 1, tiles) == b, tail[:edge], strip)
        for tail in tails:
            strip = strip + tail[(1 + b) * edge : (2 + b) * edge]
        strips.append(strip)
    strip = jnp.concatenate(strips, axis=1)
    wide = jnp.concatenate(scaled, axis=1)
    before = pl.multiple_of(jnp.maximum(me * cols - 8, 0), 8)
    after = pl.multiple_of(jnp.minimum((me + 1) * cols, width - 8), 8)
    left = turned_ref[pl.ds(before, 8), :][8 - halo :]
    right = turned_ref[pl.ds(after, 8), :][:halo]
    if plan.sides == 1:
        beside = jnp.where(me > 0, left, right)
    else:
        beside = jnp.concatenate([left, right], axis=0)
    lines = [
        strip[k * plan.edges : (k + 1) * plan.edges] - beside[:, k : k + 1] * wide[k : k + 1]
        for k in range(count)
    ]
    rows, slots = plan.rows, plan.slots
    stacks = []
    for slot in range(slots):
        members = []
        for group in range(plan.groups):
            k = group * slots + slot
            members.append(lines[k] if k < count else jnp.zeros((plan.edges, width), F32))
        stacks.append(jnp.concatenate(members, axis=0))
    lane = lax.broadcasted_iota(jnp.int32, (plan.side_rows, cols), 1)
    spare = plan.block_rows - plan.lead - plan.half_rows
    for step, out_ref in zip(step_order(plan), out_refs):
        first = partner(chip, step, plan.chips) * 2 * plan.band
        groups = [
            field_ref[k, pl.ds(pl.multiple_of(first + 8 + 8 * group, 8), 8), :]
            for group in range(2 * plan.lone + plan.shared)
            for k in range(count)
        ]
        sides = []
        for core in range(2):
            side = jnp.zeros((plan.side_rows, cols), F32)
            for slot in range(slots):
                amount = lax.rem(slot * rows + halo + width - core * plan.band - first, width)
                moved = pltpu.roll(stacks[slot], amount, 1)[:, :cols]
                side = jnp.where((lane >= slot * rows) & (lane < (slot + 1) * rows), moved, side)
            sides.append(side)
        lone = plan.lone * count
        pieces = groups[:lone] + sides[:1] + groups[lone:] + sides[1:]
        if spare:
            pieces.append(jnp.zeros((spare, cols), F32))
        out_ref[...] = jnp.concatenate(pieces, axis=0).astype(BF16)


def core_pack(plan, *refs):
    *block_refs, out_ref = refs
    other = 1 - lax.axis_index("head") % 2
    for k, block_ref in enumerate(block_refs):
        out_ref[k] = half(plan, block_ref[...].astype(F32), other).astype(BF16)


def kernel_pack(blocks_ref, out_ref):
    layers, convs, height, breadth = blocks_ref.shape[:4]
    for b in range(layers):
        for m in range(convs):
            out_ref[b * convs + m] = jnp.concatenate(
                [
                    jnp.concatenate(
                        [blocks_ref[b, m, dy, dx].astype(F32) for dy in range(height)], axis=1
                    )
                    for dx in range(breadth)
                ],
                axis=0,
            ).astype(BF16)


def lanes(base, size):
    return pl.ds(base if isinstance(base, int) else pl.multiple_of(base, LANES), size)


def shifted(ref, rows, base, offset, size):
    low = offset // LANES * LANES
    rest = offset - low
    if rest == 0:
        return ref[rows, lanes(base + low, size)]
    return pltpu.roll(ref[rows, lanes(base + low, size + LANES)], size + LANES - rest, 1)[:, :size]


def stack(plan, order, *refs):
    chips = plan.chips
    own_refs, swap_refs = refs[:chips], refs[chips : chips + len(order)]
    refs = refs[chips + len(order) :]
    proj_ref, side_ref, kernel_ref, vector_ref, mask_ref, spots_ref, out_ref = refs[:7]
    maps_ref, sides_ref, field_ref, stream_ref, hidden_ref, taps_ref, logit_ref = refs[7:]
    count, cols, rows, halo = plan.maps, plan.cols, plan.rows, plan.halo
    heads, feat, chunk, stride = plan.heads, plan.feat, plan.chunk, plan.stride
    head = lax.axis_index("head")
    chip, core = head // 2, head % 2
    group = plan.group_rows

    def spread(block, source):
        for k in range(plan.lone + plan.shared):
            value = block[k * group : (k + 1) * group]
            if k >= plan.lone:
                late = block[plan.side_rows + k * group : plan.side_rows + (k + 1) * group]
                value = jnp.where(core == 0, late, value)
            place = pl.multiple_of((k * heads + source) * group, 8)
            maps_ref[pl.ds(place, group), :] = value
        side = jnp.where(
            core == 0,
            block[plan.lone * group : plan.lead],
            block[plan.half_rows - plan.side_rows : plan.half_rows],
        )
        place = pl.multiple_of(source * plan.side_rows, 8)
        sides_ref[pl.ds(place, plan.side_rows), :] = side

    for steps, swap_ref in zip(order, swap_refs):
        for k, step in enumerate(steps):
            source = 2 * partner(chip, step, chips, back=True)
            spread(half(plan, own_refs[step_order(plan).index(step)][...].astype(F32), core), source + core)
            spread(swap_ref[k].astype(F32), source + 1 - core)
    bias = vector_ref[:, 0:1]

    slots, members = plan.slots, heads * plan.groups
    lane = lax.broadcasted_iota(jnp.int32, (members, cols), 1)
    placed = []
    for first in range(0, plan.edges, slots):
        parts = [jnp.zeros((members, cols), F32) for _ in range(slots)]
        for at in range(min(slots, plan.edges - first)):
            value = sides_ref[pl.ds(first + at, members, stride=plan.edges), :]
            keep = (lane >= at * rows) & (lane < (at + 1) * rows)
            for slot in range(slots):
                moved = value
                if at != slot:
                    moved = pltpu.roll(value, ((at - slot) * rows) % cols, 1)
                parts[slot] = jnp.where(keep, moved, parts[slot])
        stacked = jnp.concatenate(parts, axis=0).astype(BF16)
        placed.append((dot(side_ref[...], stacked) + bias).astype(BF16))

    chunks = -(-(rows * stride + plan.start) // chunk)
    for i in range(chunks):
        here = slice(i * chunk, (i + 1) * chunk)
        field_ref[:, here] = sum(
            dot(columns, spots_ref[k, :, here]) for k, columns in enumerate(placed)
        )

    weight = proj_ref[...]
    spot = lax.broadcasted_iota(jnp.int32, (feat, cols), 1)
    per = 2
    for r in range(0, rows, per):
        blocks = [
            maps_ref[
                pl.ds((r + k) // 8 * heads * group + (r + k) % 8, heads * count, stride=8), :
            ].astype(BF16)
            for k in range(per)
        ]
        pair = dot(weight, jnp.concatenate(blocks, axis=1)) + bias
        for k in range(per):
            begin = plan.start + (r + k) * stride + halo
            low, rest = begin // LANES * LANES, begin % LANES
            value = pair[:, k * cols : (k + 1) * cols]
            if rest == 0:
                field_ref[:, low : low + cols] += value
                continue
            value = pltpu.roll(value, rest, 1)
            field_ref[:, low : low + cols] += jnp.where(spot >= rest, value, 0.0)
            field_ref[:, low + cols : low + 2 * cols] += jnp.where(spot < rest, value, 0.0)

    for i in range(chunks):
        here = slice(i * chunk, (i + 1) * chunk)
        stream_ref[:, here] = jnp.where(mask_ref[:, here] > 0, field_ref[:, here], 0.0).astype(BF16)

    chunk = 2 * chunk
    everything = slice(None)
    for n in range(plan.convs):
        source = hidden_ref if n % 2 else stream_ref
        low = (plan.start + (n + 1) * stride) // LANES * LANES
        steps = -(-(plan.start + (rows - n - 1) * stride - low + LANES) // chunk)
        offsets = vector_ref[:, n + 1 : n + 2]

        def multiply(base):
            window = jnp.concatenate(
                [shifted(source, everything, base, d * stride, chunk) for d in (-1, 0, 1)], axis=0
            )
            taps_ref[:, lanes(base, chunk)] = dot(kernel_ref[n], window)

        def finish(base):
            here = lanes(base, chunk)
            value = taps_ref[feat : 2 * feat, here]
            value = value + shifted(taps_ref, slice(0, feat), base, -1, chunk)
            value = value + shifted(taps_ref, slice(2 * feat, 3 * feat), base, 1, chunk)
            value = value + offsets
            keep = mask_ref[:, here] > 0
            if n % 2 == 0:
                value = jnp.where(value > 0, value, jnp.exp(jnp.minimum(value, 0.0)) - 1.0)
                hidden_ref[:, here] = jnp.where(keep, value, 0.0).astype(BF16)
                return
            value = (stream_ref[:, here].astype(F32) + value).astype(BF16)
            if n < plan.convs - 1:
                stream_ref[:, here] = jnp.where(keep, value.astype(F32), 0.0).astype(BF16)
                return
            readout = vector_ref[:, plan.convs + 1 : plan.convs + 2]
            logit_ref[0:1, here] = jnp.sum(value.astype(F32) * readout, axis=0, keepdims=True)

        multiply(low)

        def advance(i, carry):
            base = low + i * chunk
            finish(base - LANES)
            multiply(base + chunk)
            return carry

        lax.fori_loop(0, steps, advance, 0)

    for r in range(plan.band):
        begin = plan.start + (r + halo) * stride + halo
        low = begin // LANES * LANES
        out_ref[r : r + 1, :] = shifted(logit_ref, slice(0, 1), low, begin - low, cols)


def call(kernel, name, args, outs, scratch=()):
    held = sum(math.prod(x.shape) * jnp.dtype(x.dtype).itemsize for x in [*args, *outs, *scratch])
    vmem = pl.BlockSpec(memory_space=pltpu.VMEM)
    return pl.pallas_call(
        kernel,
        out_shape=list(outs),
        in_specs=[vmem] * len(args),
        out_specs=[vmem] * len(outs),
        scratch_shapes=list(scratch),
        compiler_params=pltpu.CompilerParams(vmem_limit_bytes=held * 5 // 4 + 4 * 1024 * 1024),
        name=name,
    )(*args)


def array(dtype, *shape):
    return jax.ShapeDtypeStruct(shape, dtype)


def on_device(attention, proj_weight, proj_bias, conv_weight, conv_bias, out_weight):
    maps, width, cols = attention.shape
    feat = proj_weight.shape[0]
    blocks, convs = conv_weight.shape[:2]
    tiles, heads = lax.axis_size("tile"), lax.axis_size("head")
    plan = Plan(maps, width, cols, tiles, heads, feat, blocks * convs)
    me, band_index = lax.axis_index("tile"), lax.axis_index("head")

    payload, sums, edge = call(
        functools.partial(mirror_pack, plan),
        "mirror_pack",
        [attention],
        [
            array(BF16, tiles - 1, maps * cols + plan.tail_rows, cols),
            array(F32, plan.map_rows, width),
            array(F32, plan.edge_rows, cols),
        ],
    )
    received = jnp.stack(
        [
            lax.ppermute(payload[s - 1], "tile", [(i, (i + s) % tiles) for i in range(tiles)])
            for s in range(tiles - 1, 0, -1)
        ]
    )

    stride, start = plan.stride, plan.start
    side_weight = proj_weight.reshape(feat, heads, maps)
    side_weight = jnp.pad(side_weight, ((0, 0), (0, 0), (0, plan.groups * plan.slots - maps)))
    side_weight = side_weight.reshape(feat, heads, plan.groups, plan.slots)
    side_weight = side_weight.transpose(0, 3, 1, 2).reshape(feat, -1)
    (kernels,) = call(
        kernel_pack,
        "kernel_pack",
        [conv_weight.transpose(0, 1, 4, 5, 2, 3)],
        [array(BF16, plan.convs, 3 * feat, 3 * feat)],
    )
    vectors = jnp.concatenate(
        [proj_bias[None], conv_bias.reshape(-1, feat), out_weight[None]], axis=0
    ).T
    spot = np.arange(plan.lanes) - start
    row = band_index * plan.band - plan.halo + (spot // stride).astype(np.int32)
    col = me * cols - plan.halo + (spot % stride).astype(np.int32)
    mask = (row >= 0) & (row < width) & (col >= 0) & (col < width)
    mask = mask.astype(F32)[None]

    key = np.arange(cols)
    member, line = key // plan.rows, key % plan.rows
    spots = []
    for first in range(0, plan.edges, plan.slots):
        column = first + member
        fits = (member < plan.slots) & (column < plan.edges)
        places = (0, plan.halo + cols) if plan.sides == 1 else (np.where(column < plan.halo, 0, cols),)
        target = [np.where(fits, start + line * stride + column + p, -1) for p in places]
        hit = [jnp.arange(plan.lanes)[None] == jnp.asarray(p, jnp.int32)[:, None] for p in target]
        spots.append(functools.reduce(jnp.logical_or, hit).astype(BF16))
    spots = jnp.stack(spots)

    chips = plan.chips
    blocks = call(
        functools.partial(correct_pack, plan),
        "correct_pack",
        [attention, received, sums, edge],
        [array(BF16, plan.block_rows, cols)] * chips,
        [pltpu.VMEM((maps, width + 24, cols), F32), pltpu.VMEM((width, LANES), F32)],
    )
    arrived = {}
    for step, block in zip(step_order(plan), blocks):
        pairs = [(i, 2 * partner(i // 2, step, chips) + i % 2) for i in range(heads)]
        arrived[step] = lax.ppermute(block, "head", pairs) if step else block
    far, near = far_near(plan)
    order = [far, near + [0]]
    weights = (proj_weight, side_weight, kernels, vectors, mask, spots)
    arrived[0], weights = lax.optimization_barrier((arrived[0], weights))
    swapped = []
    for steps in order:
        (packed,) = call(
            functools.partial(core_pack, plan),
            "core_pack",
            [arrived[k] for k in steps],
            [array(BF16, len(steps), plan.half_rows, cols)],
        )
        swapped.append(lax.ppermute(packed, "head", [(i, i ^ 1) for i in range(heads)]))

    (logits,) = call(
        functools.partial(stack, plan, order),
        "stack",
        [*arrived.values(), *swapped, *weights],
        [array(F32, plan.band, cols)],
        [
            pltpu.VMEM((heads * maps * plan.rows, cols), F32),
            pltpu.VMEM((heads * plan.side_rows, cols), F32),
            pltpu.VMEM((feat, plan.lanes), F32),
            pltpu.VMEM((feat, plan.lanes), BF16),
            pltpu.VMEM((feat, plan.lanes), BF16),
            pltpu.VMEM((3 * feat, plan.lanes), F32),
            pltpu.VMEM((8, plan.lanes), F32),
        ],
    )
    return logits


def solution(mesh):
    return jax.shard_map(
        on_device,
        mesh=mesh,
        in_specs=(P(("grp", "head"), None, "tile"), P(), P(), P(), P(), P()),
        out_specs=P(("grp", "head"), "tile"),
        check_vma=False,
    )
```

```python
import functools
import math
from typing import NamedTuple

import jax
import jax.numpy as jnp
import numpy as np
from jax import lax
from jax.experimental import pallas as pl
from jax.experimental.pallas import tpu as pltpu
from jax.sharding import PartitionSpec as P

BF16, F32 = jnp.bfloat16, jnp.float32
LANES = 128


def up(value, step):
    return -(-value // step) * step


class Plan(NamedTuple):
    maps: int
    width: int
    cols: int
    tiles: int
    heads: int
    feat: int
    convs: int

    @property
    def halo(self):
        return self.convs

    @property
    def sides(self):
        return min(2, self.tiles - 1)

    @property
    def edges(self):
        return self.sides * self.halo

    @property
    def edge_rows(self):
        return up(self.maps * self.edges, 8)

    @property
    def map_rows(self):
        return up(self.maps, 16)

    @property
    def tail_rows(self):
        return up((1 + self.tiles) * self.edge_rows + 3 * self.tiles * self.map_rows, 16)

    @property
    def band(self):
        return self.width // self.heads

    @property
    def rows(self):
        return self.band + 2 * self.halo

    @property
    def slots(self):
        return self.cols // self.rows

    @property
    def groups(self):
        return -(-self.maps // self.slots)

    @property
    def side_rows(self):
        return self.groups * self.edges

    @property
    def sets(self):
        return self.maps // 8

    @property
    def rest(self):
        return self.maps % 8

    @property
    def pitch(self):
        return up(self.width + 24, 2) + 1

    @property
    def chips(self):
        return self.heads // 2

    @property
    def lone(self):
        return self.band // 8

    @property
    def shared(self):
        return 2 * self.halo // 8

    @property
    def group_rows(self):
        return 8 * self.maps

    @property
    def lead(self):
        return self.lone * self.group_rows + self.side_rows

    @property
    def half_rows(self):
        return self.lead + self.shared * self.group_rows

    @property
    def block_rows(self):
        return up(self.lead + self.half_rows, 16)

    @property
    def stride(self):
        return self.cols + 2 * self.halo

    @property
    def start(self):
        return up(self.stride, LANES) - LANES

    @property
    def chunk(self):
        return 256

    @property
    def lanes(self):
        return up(self.start + self.rows * self.stride, LANES) + 6 * self.chunk + 3 * LANES


def partner(mine, step, count, back=False):
    if count & (count - 1) == 0:
        return mine ^ step
    return (mine - step if back else mine + step) % count


def far_near(plan):
    steps = list(range(plan.chips - 1, 0, -1))
    return steps[: plan.chips // 2], steps[plan.chips // 2 :]


def step_order(plan):
    far, near = far_near(plan)
    return far + near + [0]


def half(plan, block, core):
    return jnp.where(
        core == 0, block[: plan.half_rows], block[plan.lead : plan.lead + plan.half_rows]
    )


def edge_start(plan, tile, side):
    left, right = plan.cols * tile - plan.halo, plan.cols * (tile + 1)
    if plan.sides == 1:
        return jnp.where(tile > 0, left, right)
    return (left, right)[side]


def edge_select(plan, tile, row, position, index):
    hit = None
    for side in range(plan.sides):
        first = index * plan.edges + side * plan.halo
        inside = (row >= first) & (row < first + plan.halo)
        one = inside & (position == row - first + edge_start(plan, tile, side))
        hit = one if hit is None else hit | one
    return hit


def across(a, b):
    return lax.dot_general(a, b, (((1,), (1,)), ((), ())), preferred_element_type=F32)


def dot(a, b):
    return jnp.dot(a, b, preferred_element_type=F32)


def mirror_pack(plan, maps_ref, out_ref, sums_ref, edge_ref):
    me = lax.axis_index("tile")
    count, cols, width, tiles = plan.maps, plan.cols, plan.width, plan.tiles
    head, edge = plan.map_rows, plan.edge_rows

    def pick(rows, span, base, tile, index):
        row = lax.broadcasted_iota(jnp.int32, (rows, span), 0)
        position = lax.broadcasted_iota(jnp.int32, (rows, span), 1) + base
        return edge_select(plan, tile, row, position, index).astype(F32)

    def total(span, index):
        return (lax.broadcasted_iota(jnp.int32, (head, span), 0) == index).astype(F32)

    for shift in range(1, tiles):
        dest = lax.rem(me + shift, tiles)
        by_col = by_row = None
        for index in range(count):
            block = maps_ref[index]
            out_ref[shift - 1, index * cols : (index + 1) * cols, :] = maps_ref[
                index, pl.ds(pl.multiple_of(dest * cols, cols), cols), :
            ]
            left = [pick(edge, cols, me * cols, dest, index)]
            upper = [pick(edge, width, 0, dest, index)]
            if shift == 1:
                left.append(total(cols, index))
                upper.append(total(width, index))
                upper.append(pick(edge, width, 0, me, index))
            by_c = across(jnp.concatenate(left, axis=0).astype(BF16), block)
            by_r = dot(jnp.concatenate(upper, axis=0).astype(BF16), block)
            by_col = by_c if by_col is None else by_col + by_c
            by_row = by_r if by_row is None else by_row + by_r
        if shift == 1:
            sums_ref[...] = by_col[edge : edge + head]
            own = pl.ds(pl.multiple_of(me * cols, cols), cols)
            sums_ref[:, own] = sums_ref[:, own] + by_row[edge : edge + head]
            edge_ref[...] = by_row[edge + head :]
            sums = sums_ref[...]
            high = sums.astype(BF16).astype(F32)
            middle = (sums - high).astype(BF16).astype(F32)
            low = sums - high - middle
        pieces = [by_row[:edge]]
        for wide in (by_col[:edge], high, middle, low):
            pieces += [wide[:, k * cols : (k + 1) * cols] for k in range(tiles)]
        used = (1 + tiles) * edge + 3 * tiles * head
        if plan.tail_rows > used:
            pieces.append(jnp.zeros((plan.tail_rows - used, cols), F32))
        out_ref[shift - 1, count * cols :, :] = jnp.concatenate(pieces, axis=0).astype(BF16)


def correct_pack(plan, maps_ref, recv_ref, sums_ref, edge_ref, *refs):
    *out_refs, field_ref, turned_ref = refs
    me, chip = lax.axis_index("tile"), lax.axis_index("head") // 2
    count, cols, width, tiles = plan.maps, plan.cols, plan.width, plan.tiles
    head, edge, halo = plan.map_rows, plan.edge_rows, plan.halo
    tails = [recv_ref[k, count * cols :, :].astype(F32) for k in range(tiles - 1)]

    rowsum = []
    for b in range(tiles):
        value = sums_ref[:, b * cols : (b + 1) * cols]
        for tail in tails:
            base = (1 + tiles) * edge
            parts = [
                tail[base + (k * tiles + b) * head : base + (k * tiles + b + 1) * head]
                for k in range(3)
            ]
            value = value + ((parts[0] + parts[1]) + parts[2])
        rowsum.append(value)
    grand = sum(jnp.sum(value, axis=1, keepdims=True) for value in rowsum)
    grand = jnp.where(lax.broadcasted_iota(jnp.int32, (head, 1), 0) < count, grand, 1.0)
    scaled = [value / grand for value in rowsum]
    for b in range(tiles):
        square = jnp.concatenate([rowsum[b], jnp.zeros((LANES - head, cols), F32)], axis=0)
        turned_ref[b * cols : (b + 1) * cols, :] = square.T
    mine = scaled[0]
    for b in range(1, tiles):
        mine = jnp.where(me == b, scaled[b], mine)

    eye = (
        lax.broadcasted_iota(jnp.int32, (cols, cols), 0)
        == lax.broadcasted_iota(jnp.int32, (cols, cols), 1)
    ).astype(F32).astype(BF16)
    margin = 8 + halo
    for index in range(count):
        origin = index * plan.pitch
        field_ref[origin : origin + margin, :] = jnp.zeros((margin, cols), F32)
        field_ref[origin + margin + width : origin + plan.pitch, :] = jnp.zeros(
            (plan.pitch - margin - width, cols), F32
        )
        for b in range(tiles):
            shift = lax.rem(b - me + tiles, tiles)
            other = recv_ref[
                jnp.maximum(shift - 1, 0), index * cols : (index + 1) * cols, :
            ]
            own = maps_ref[index, b * cols : (b + 1) * cols, :]
            mirror = across(eye, jnp.where(shift == 0, own, other))
            column = turned_ref[b * cols : (b + 1) * cols, index : index + 1]
            field_ref[origin + margin + b * cols : origin + margin + (b + 1) * cols, :] = (
                own.astype(F32) + mirror - column * mine[index : index + 1]
            )

    strips = []
    for b in range(tiles):
        strip = edge_ref[...]
        for k, tail in enumerate(tails):
            strip = jnp.where(lax.rem(me + k + 1, tiles) == b, tail[:edge], strip)
        for tail in tails:
            strip = strip + tail[(1 + b) * edge : (2 + b) * edge]
        strips.append(strip)
    strip = jnp.concatenate(strips, axis=1)
    wide = jnp.concatenate(scaled, axis=1)
    before = pl.multiple_of(jnp.maximum(me * cols - 8, 0), 8)
    after = pl.multiple_of(jnp.minimum((me + 1) * cols, width - 8), 8)
    left = turned_ref[pl.ds(before, 8), :][8 - halo :]
    right = turned_ref[pl.ds(after, 8), :][:halo]
    if plan.sides == 1:
        beside = jnp.where(me > 0, left, right)
    else:
        beside = jnp.concatenate([left, right], axis=0)
    lines = [
        strip[k * plan.edges : (k + 1) * plan.edges] - beside[:, k : k + 1] * wide[k : k + 1]
        for k in range(count)
    ]
    rows, slots = plan.rows, plan.slots
    stacks = []
    for slot in range(slots):
        members = []
        for group in range(plan.groups):
            k = group * slots + slot
            members.append(lines[k] if k < count else jnp.zeros((plan.edges, width), F32))
        stacks.append(jnp.concatenate(members, axis=0))
    lane = lax.broadcasted_iota(jnp.int32, (plan.side_rows, cols), 1)
    spare = plan.block_rows - plan.lead - plan.half_rows
    for step, out_ref in zip(step_order(plan), out_refs):
        first = partner(chip, step, plan.chips) * 2 * plan.band

        def section(begin, size):
            found = [
                field_ref[pl.ds(8 * k * plan.pitch + first + 8 + begin + r, 8, stride=plan.pitch), :]
                for r in range(size)
                for k in range(plan.sets)
            ]
            for k in range(8 * plan.sets, count):
                found.append(field_ref[pl.ds(k * plan.pitch + first + 8 + begin, size), :])
            return found

        lone, shared = 8 * plan.lone, 8 * plan.shared
        sides = []
        for core in range(2):
            side = jnp.zeros((plan.side_rows, cols), F32)
            for slot in range(slots):
                amount = lax.rem(slot * rows + halo + width - core * plan.band - first, width)
                moved = pltpu.roll(stacks[slot], amount, 1)[:, :cols]
                side = jnp.where((lane >= slot * rows) & (lane < (slot + 1) * rows), moved, side)
            sides.append(side)
        pieces = section(0, lone) + sides[:1] + section(lone, shared)
        pieces += section(lone + shared, lone) + sides[1:]
        if spare:
            pieces.append(jnp.zeros((spare, cols), F32))
        out_ref[...] = jnp.concatenate(pieces, axis=0).astype(BF16)


def core_pack(plan, *refs):
    *block_refs, out_ref = refs
    other = 1 - lax.axis_index("head") % 2
    for k, block_ref in enumerate(block_refs):
        out_ref[k] = half(plan, block_ref[...].astype(F32), other).astype(BF16)


def kernel_pack(blocks_ref, out_ref):
    layers, convs, height, breadth = blocks_ref.shape[:4]
    for b in range(layers):
        for m in range(convs):
            out_ref[b * convs + m] = jnp.concatenate(
                [
                    jnp.concatenate(
                        [blocks_ref[b, m, dy, dx].astype(F32) for dy in range(height)], axis=1
                    )
                    for dx in range(breadth)
                ],
                axis=0,
            ).astype(BF16)


def lanes(base, size):
    return pl.ds(base if isinstance(base, int) else pl.multiple_of(base, LANES), size)


def shifted(ref, rows, base, offset, size):
    low = offset // LANES * LANES
    rest = offset - low
    if rest == 0:
        return ref[rows, lanes(base + low, size)]
    return pltpu.roll(ref[rows, lanes(base + low, size + LANES)], size + LANES - rest, 1)[:, :size]


def stack(plan, order, *refs):
    chips = plan.chips
    own_refs, swap_refs = refs[:chips], refs[chips : chips + len(order)]
    refs = refs[chips + len(order) :]
    proj_ref, side_ref, kernel_ref, vector_ref, mask_ref, spots_ref, out_ref = refs[:7]
    maps_ref, others_ref, sides_ref, field_ref, stream_ref, hidden_ref, taps_ref, logit_ref = refs[7:]
    count, cols, rows, halo = plan.maps, plan.cols, plan.rows, plan.halo
    heads, feat, chunk, stride = plan.heads, plan.feat, plan.chunk, plan.stride
    head = lax.axis_index("head")
    chip, core = head // 2, head % 2
    lone, shared = 8 * plan.lone, 8 * plan.shared
    wide = 8 * plan.sets

    def rows_of(sections):
        sets, others = [], []
        for begin, size in sections:
            sets += [begin + r * wide for r in range(size)]
            others += [begin + size * wide + r for r in range(0, size, 8)]
        return sets, others, [size for _, size in sections for _ in range(0, size, 8)]

    early = rows_of([(0, lone), (plan.lead, shared)])
    late = rows_of([(0, shared), (shared * count, lone)])

    def spread(block, source):
        def pick(a, b, size):
            if a == b:
                return block[a : a + size]
            return jnp.where(core == 0, block[a : a + size], block[b : b + size])

        for r, (a, b) in enumerate(zip(early[0], late[0])):
            place = pl.multiple_of(source * wide, 8) + r * heads * wide
            maps_ref[pl.ds(pl.multiple_of(place, 8), wide), :] = pick(a, b, wide)
        for k, (a, b, m, n) in enumerate(zip(early[1], late[1], early[2], late[2])):
            for j in range(plan.rest):
                place = (source * plan.rest + j) * rows + 8 * k
                others_ref[pl.ds(pl.multiple_of(place, 8), 8), :] = pick(a + j * m, b + j * n, 8)
        side = pick(lone * count, plan.half_rows - plan.side_rows, plan.side_rows)
        place = pl.multiple_of(source * plan.side_rows, 8)
        sides_ref[pl.ds(place, plan.side_rows), :] = side

    for steps, swap_ref in zip(order, swap_refs):
        for k, step in enumerate(steps):
            source = 2 * partner(chip, step, chips, back=True)
            spread(half(plan, own_refs[step_order(plan).index(step)][...].astype(F32), core), source + core)
            spread(swap_ref[k].astype(F32), source + 1 - core)
    bias = vector_ref[:, 0:1]

    slots, members = plan.slots, heads * plan.groups
    lane = lax.broadcasted_iota(jnp.int32, (members, cols), 1)
    placed = []
    for first in range(0, plan.edges, slots):
        parts = [jnp.zeros((members, cols), F32) for _ in range(slots)]
        for at in range(min(slots, plan.edges - first)):
            value = sides_ref[pl.ds(first + at, members, stride=plan.edges), :]
            keep = (lane >= at * rows) & (lane < (at + 1) * rows)
            for slot in range(slots):
                moved = value
                if at != slot:
                    moved = pltpu.roll(value, ((at - slot) * rows) % cols, 1)
                parts[slot] = jnp.where(keep, moved, parts[slot])
        stacked = jnp.concatenate(parts, axis=0).astype(BF16)
        placed.append((dot(side_ref[...], stacked) + bias).astype(BF16))

    chunks = -(-(rows * stride + plan.start) // chunk)
    for i in range(chunks):
        here = slice(i * chunk, (i + 1) * chunk)
        field_ref[:, here] = sum(
            dot(columns, spots_ref[k, :, here]) for k, columns in enumerate(placed)
        )

    weight = proj_ref[...]
    spot = lax.broadcasted_iota(jnp.int32, (feat, cols), 1)
    per = 2
    for r in range(0, rows, per):
        blocks = []
        for k in range(per):
            block = maps_ref[(r + k) * heads * wide : (r + k + 1) * heads * wide, :]
            if plan.rest:
                others = others_ref[pl.ds(r + k, heads * plan.rest, stride=rows), :]
                block = jnp.concatenate([block, others], axis=0)
            blocks.append(block.astype(BF16))
        pair = dot(weight, jnp.concatenate(blocks, axis=1)) + bias
        for k in range(per):
            begin = plan.start + (r + k) * stride + halo
            low, rest = begin // LANES * LANES, begin % LANES
            value = pair[:, k * cols : (k + 1) * cols]
            if rest == 0:
                field_ref[:, low : low + cols] += value
                continue
            value = pltpu.roll(value, rest, 1)
            field_ref[:, low : low + cols] += jnp.where(spot >= rest, value, 0.0)
            field_ref[:, low + cols : low + 2 * cols] += jnp.where(spot < rest, value, 0.0)

    for i in range(chunks):
        here = slice(i * chunk, (i + 1) * chunk)
        stream_ref[:, here] = jnp.where(mask_ref[:, here] > 0, field_ref[:, here], 0.0).astype(BF16)

    chunk = 2 * chunk
    everything = slice(None)
    for n in range(plan.convs):
        source = hidden_ref if n % 2 else stream_ref
        low = (plan.start + (n + 1) * stride) // LANES * LANES
        steps = -(-(plan.start + (rows - n - 1) * stride - n - 1 - low) // chunk)
        offsets = vector_ref[:, n + 1 : n + 2]

        def multiply(base, size):
            window = jnp.concatenate(
                [shifted(source, everything, base, d * stride, size) for d in (-1, 0, 1)], axis=0
            )
            taps_ref[:, lanes(base, size)] = dot(kernel_ref[n], window)

        def finish(base):
            here = lanes(base, chunk)
            value = taps_ref[feat : 2 * feat, here]
            value = value + shifted(taps_ref, slice(0, feat), base, -1, chunk)
            value = value + shifted(taps_ref, slice(2 * feat, 3 * feat), base, 1, chunk)
            value = value + offsets
            keep = mask_ref[:, here] > 0
            if n % 2 == 0:
                value = jnp.where(value > 0, value, jnp.exp(jnp.minimum(value, 0.0)) - 1.0)
                hidden_ref[:, here] = jnp.where(keep, value, 0.0).astype(BF16)
                return
            value = (stream_ref[:, here].astype(F32) + value).astype(BF16)
            if n < plan.convs - 1:
                stream_ref[:, here] = jnp.where(keep, value.astype(F32), 0.0).astype(BF16)
                return
            readout = vector_ref[:, plan.convs + 1 : plan.convs + 2]
            logit_ref[0:1, here] = jnp.sum(value.astype(F32) * readout, axis=0, keepdims=True)

        multiply(low, chunk + LANES)

        def advance(i, carry):
            base = low + i * chunk
            finish(base)
            multiply(base + chunk + LANES, chunk)
            return carry

        lax.fori_loop(0, steps - 1, advance, 0)
        finish(low + (steps - 1) * chunk)

    for r in range(plan.band):
        begin = plan.start + (r + halo) * stride + halo
        low = begin // LANES * LANES
        out_ref[r : r + 1, :] = shifted(logit_ref, slice(0, 1), low, begin - low, cols)


def call(kernel, name, args, outs, scratch=(), held_out=True):
    held = sum(math.prod(x.shape) * jnp.dtype(x.dtype).itemsize for x in [*args, *outs, *scratch])
    vmem = pl.BlockSpec(memory_space=pltpu.VMEM)
    return pl.pallas_call(
        kernel,
        out_shape=[pltpu.VMEM(x.shape, x.dtype) if held_out else x for x in outs],
        in_specs=[vmem] * len(args),
        out_specs=[vmem] * len(outs),
        scratch_shapes=list(scratch),
        compiler_params=pltpu.CompilerParams(vmem_limit_bytes=held * 5 // 4 + 4 * 1024 * 1024),
        name=name,
    )(*args)


def array(dtype, *shape):
    return jax.ShapeDtypeStruct(shape, dtype)


def on_device(attention, proj_weight, proj_bias, conv_weight, conv_bias, out_weight):
    maps, width, cols = attention.shape
    feat = proj_weight.shape[0]
    blocks, convs = conv_weight.shape[:2]
    tiles, heads = lax.axis_size("tile"), lax.axis_size("head")
    plan = Plan(maps, width, cols, tiles, heads, feat, blocks * convs)
    me, band_index = lax.axis_index("tile"), lax.axis_index("head")

    payload, sums, edge = call(
        functools.partial(mirror_pack, plan),
        "mirror_pack",
        [attention],
        [
            array(BF16, tiles - 1, maps * cols + plan.tail_rows, cols),
            array(F32, plan.map_rows, width),
            array(F32, plan.edge_rows, cols),
        ],
    )
    received = jnp.stack(
        [
            lax.ppermute(payload[s - 1], "tile", [(i, (i + s) % tiles) for i in range(tiles)])
            for s in range(tiles - 1, 0, -1)
        ]
    )

    stride, start = plan.stride, plan.start
    side_weight = proj_weight.reshape(feat, heads, maps)
    side_weight = jnp.pad(side_weight, ((0, 0), (0, 0), (0, plan.groups * plan.slots - maps)))
    side_weight = side_weight.reshape(feat, heads, plan.groups, plan.slots)
    side_weight = side_weight.transpose(0, 3, 1, 2).reshape(feat, -1)
    (kernels,) = call(
        kernel_pack,
        "kernel_pack",
        [conv_weight.transpose(0, 1, 4, 5, 2, 3)],
        [array(BF16, plan.convs, 3 * feat, 3 * feat)],
    )
    vectors = jnp.concatenate(
        [proj_bias[None], conv_bias.reshape(-1, feat), out_weight[None]], axis=0
    ).T
    spot = np.arange(plan.lanes) - start
    row = band_index * plan.band - plan.halo + (spot // stride).astype(np.int32)
    col = me * cols - plan.halo + (spot % stride).astype(np.int32)
    mask = (row >= 0) & (row < width) & (col >= 0) & (col < width)
    mask = mask.astype(F32)[None]

    key = np.arange(cols)
    member, line = key // plan.rows, key % plan.rows
    spots = []
    for first in range(0, plan.edges, plan.slots):
        column = first + member
        fits = (member < plan.slots) & (column < plan.edges)
        places = (0, plan.halo + cols) if plan.sides == 1 else (np.where(column < plan.halo, 0, cols),)
        target = [np.where(fits, start + line * stride + column + p, -1) for p in places]
        hit = [jnp.arange(plan.lanes)[None] == jnp.asarray(p, jnp.int32)[:, None] for p in target]
        spots.append(functools.reduce(jnp.logical_or, hit).astype(BF16))
    spots = jnp.stack(spots)

    by_map = proj_weight.reshape(feat, heads, maps)
    sets = by_map[:, :, : 8 * plan.sets].reshape(feat, -1)
    others = by_map[:, :, 8 * plan.sets :].reshape(feat, -1)
    map_weight = jnp.concatenate([sets, others], axis=1)
    weights = (map_weight, side_weight, kernels, vectors, mask, spots)
    received, weights = lax.optimization_barrier((received, weights))
    chips = plan.chips
    blocks = call(
        functools.partial(correct_pack, plan),
        "correct_pack",
        [attention, received, sums, edge],
        [array(BF16, plan.block_rows, cols)] * chips,
        [pltpu.VMEM((maps * plan.pitch, cols), F32), pltpu.VMEM((width, LANES), F32)],
    )
    arrived = {}
    for step, block in zip(step_order(plan), blocks):
        pairs = [(i, 2 * partner(i // 2, step, chips) + i % 2) for i in range(heads)]
        arrived[step] = lax.ppermute(block, "head", pairs) if step else block
    far, near = far_near(plan)
    order = [far, near + [0]]
    swapped = []
    for steps in order:
        (packed,) = call(
            functools.partial(core_pack, plan),
            "core_pack",
            [arrived[k] for k in steps],
            [array(BF16, len(steps), plan.half_rows, cols)],
        )
        swapped.append(lax.ppermute(packed, "head", [(i, i ^ 1) for i in range(heads)]))

    (logits,) = call(
        functools.partial(stack, plan, order),
        "stack",
        [*arrived.values(), *swapped, *weights],
        [array(F32, plan.band, cols)],
        [
            pltpu.VMEM((heads * 8 * plan.sets * plan.rows, cols), F32),
            pltpu.VMEM((heads * max(plan.rest, 1) * plan.rows, cols), F32),
            pltpu.VMEM((heads * plan.side_rows, cols), F32),
            pltpu.VMEM((feat, plan.lanes), F32),
            pltpu.VMEM((feat, plan.lanes), BF16),
            pltpu.VMEM((feat, plan.lanes), BF16),
            pltpu.VMEM((3 * feat, plan.lanes), F32),
            pltpu.VMEM((8, plan.lanes), F32),
        ],
        held_out=False,
    )
    return logits


def solution(mesh):
    return jax.shard_map(
        on_device,
        mesh=mesh,
        in_specs=(P(("grp", "head"), None, "tile"), P(), P(), P(), P(), P()),
        out_specs=P(("grp", "head"), "tile"),
        check_vma=False,
    )
```

```python
import functools
import math
from typing import NamedTuple

import jax
import jax.numpy as jnp
import numpy as np
from jax import lax
from jax.experimental import pallas as pl
from jax.experimental.pallas import tpu as pltpu
from jax.sharding import PartitionSpec as P

BF16, F32 = jnp.bfloat16, jnp.float32
LANES = 128


def up(value, step):
    return -(-value // step) * step


class Plan(NamedTuple):
    maps: int
    width: int
    cols: int
    tiles: int
    heads: int
    feat: int
    convs: int

    @property
    def halo(self):
        return self.convs

    @property
    def sides(self):
        return min(2, self.tiles - 1)

    @property
    def edges(self):
        return self.sides * self.halo

    @property
    def edge_rows(self):
        return up(self.maps * self.edges, 8)

    @property
    def map_rows(self):
        return up(self.maps, 16)

    @property
    def tail_rows(self):
        return up((1 + self.tiles) * self.edge_rows + 3 * self.tiles * self.map_rows, 16)

    @property
    def band(self):
        return self.width // self.heads

    @property
    def rows(self):
        return self.band + 2 * self.halo

    @property
    def slots(self):
        return self.cols // self.rows

    @property
    def groups(self):
        return -(-self.maps // self.slots)

    @property
    def side_rows(self):
        return self.groups * self.edges

    @property
    def sets(self):
        return self.maps // 8

    @property
    def rest(self):
        return self.maps % 8

    @property
    def pitch(self):
        return up(self.width + 24, 2) + 1

    @property
    def chips(self):
        return self.heads // 2

    @property
    def lone(self):
        return self.band // 8

    @property
    def shared(self):
        return 2 * self.halo // 8

    @property
    def group_rows(self):
        return 8 * self.maps

    @property
    def lead(self):
        return self.lone * self.group_rows + self.side_rows

    @property
    def half_rows(self):
        return self.lead + self.shared * self.group_rows

    @property
    def block_rows(self):
        return up(self.lead + self.half_rows, 16)

    @property
    def stride(self):
        return self.cols + 2 * self.halo

    @property
    def start(self):
        return up(self.stride, LANES) - LANES

    @property
    def chunk(self):
        return 256

    @property
    def lanes(self):
        return up(self.start + self.rows * self.stride, LANES) + 6 * self.chunk + 3 * LANES


def partner(mine, step, count, back=False):
    if count & (count - 1) == 0:
        return mine ^ step
    return (mine - step if back else mine + step) % count


def far_near(plan):
    steps = list(range(plan.chips - 1, 0, -1))
    return steps[: plan.chips // 2], steps[plan.chips // 2 :]


def step_order(plan):
    far, near = far_near(plan)
    return far + near + [0]


def half(plan, block, core):
    return jnp.where(
        core == 0, block[: plan.half_rows], block[plan.lead : plan.lead + plan.half_rows]
    )


def edge_start(plan, tile, side):
    left, right = plan.cols * tile - plan.halo, plan.cols * (tile + 1)
    if plan.sides == 1:
        return jnp.where(tile > 0, left, right)
    return (left, right)[side]


def edge_select(plan, tile, row, position, index):
    hit = None
    for side in range(plan.sides):
        first = index * plan.edges + side * plan.halo
        inside = (row >= first) & (row < first + plan.halo)
        one = inside & (position == row - first + edge_start(plan, tile, side))
        hit = one if hit is None else hit | one
    return hit


def across(a, b):
    return lax.dot_general(a, b, (((1,), (1,)), ((), ())), preferred_element_type=F32)


def dot(a, b):
    return jnp.dot(a, b, preferred_element_type=F32)


def mirror_pack(plan, maps_ref, out_ref, sums_ref, edge_ref):
    me = lax.axis_index("tile")
    count, cols, width, tiles = plan.maps, plan.cols, plan.width, plan.tiles
    head, edge = plan.map_rows, plan.edge_rows

    def pick(rows, span, base, tile, index):
        row = lax.broadcasted_iota(jnp.int32, (rows, span), 0)
        position = lax.broadcasted_iota(jnp.int32, (rows, span), 1) + base
        return edge_select(plan, tile, row, position, index).astype(F32)

    def total(span, index):
        return (lax.broadcasted_iota(jnp.int32, (head, span), 0) == index).astype(F32)

    for shift in range(1, tiles):
        dest = lax.rem(me + shift, tiles)
        by_col = by_row = None
        for index in range(count):
            block = maps_ref[index]
            out_ref[shift - 1, index * cols : (index + 1) * cols, :] = maps_ref[
                index, pl.ds(pl.multiple_of(dest * cols, cols), cols), :
            ]
            left = [pick(edge, cols, me * cols, dest, index)]
            upper = [pick(edge, width, 0, dest, index)]
            if shift == 1:
                left.append(total(cols, index))
                upper.append(total(width, index))
                upper.append(pick(edge, width, 0, me, index))
            by_c = across(jnp.concatenate(left, axis=0).astype(BF16), block)
            by_r = dot(jnp.concatenate(upper, axis=0).astype(BF16), block)
            by_col = by_c if by_col is None else by_col + by_c
            by_row = by_r if by_row is None else by_row + by_r
        if shift == 1:
            sums_ref[...] = by_col[edge : edge + head]
            own = pl.ds(pl.multiple_of(me * cols, cols), cols)
            sums_ref[:, own] = sums_ref[:, own] + by_row[edge : edge + head]
            edge_ref[...] = by_row[edge + head :]
            sums = sums_ref[...]
            high = sums.astype(BF16).astype(F32)
            middle = (sums - high).astype(BF16).astype(F32)
            low = sums - high - middle
        pieces = [by_row[:edge]]
        for wide in (by_col[:edge], high, middle, low):
            pieces += [wide[:, k * cols : (k + 1) * cols] for k in range(tiles)]
        used = (1 + tiles) * edge + 3 * tiles * head
        if plan.tail_rows > used:
            pieces.append(jnp.zeros((plan.tail_rows - used, cols), F32))
        out_ref[shift - 1, count * cols :, :] = jnp.concatenate(pieces, axis=0).astype(BF16)


def correct_pack(plan, maps_ref, recv_ref, sums_ref, edge_ref, *refs):
    *out_refs, field_ref, turned_ref = refs
    me, chip = lax.axis_index("tile"), lax.axis_index("head") // 2
    count, cols, width, tiles = plan.maps, plan.cols, plan.width, plan.tiles
    head, edge, halo = plan.map_rows, plan.edge_rows, plan.halo
    tails = [recv_ref[k, count * cols :, :].astype(F32) for k in range(tiles - 1)]

    rowsum = []
    for b in range(tiles):
        value = sums_ref[:, b * cols : (b + 1) * cols]
        for tail in tails:
            base = (1 + tiles) * edge
            parts = [
                tail[base + (k * tiles + b) * head : base + (k * tiles + b + 1) * head]
                for k in range(3)
            ]
            value = value + ((parts[0] + parts[1]) + parts[2])
        rowsum.append(value)
    grand = sum(jnp.sum(value, axis=1, keepdims=True) for value in rowsum)
    grand = jnp.where(lax.broadcasted_iota(jnp.int32, (head, 1), 0) < count, grand, 1.0)
    scaled = [value / grand for value in rowsum]
    for b in range(tiles):
        square = jnp.concatenate([rowsum[b], jnp.zeros((LANES - head, cols), F32)], axis=0)
        turned_ref[b * cols : (b + 1) * cols, :] = square.T
    mine = scaled[0]
    for b in range(1, tiles):
        mine = jnp.where(me == b, scaled[b], mine)

    eye = (
        lax.broadcasted_iota(jnp.int32, (cols, cols), 0)
        == lax.broadcasted_iota(jnp.int32, (cols, cols), 1)
    ).astype(F32).astype(BF16)
    margin = 8 + halo
    for index in range(count):
        origin = index * plan.pitch
        field_ref[origin : origin + margin, :] = jnp.zeros((margin, cols), F32)
        field_ref[origin + margin + width : origin + plan.pitch, :] = jnp.zeros(
            (plan.pitch - margin - width, cols), F32
        )
        for b in range(tiles):
            shift = lax.rem(b - me + tiles, tiles)
            other = recv_ref[
                jnp.maximum(shift - 1, 0), index * cols : (index + 1) * cols, :
            ]
            own = maps_ref[index, b * cols : (b + 1) * cols, :]
            mirror = across(eye, jnp.where(shift == 0, own, other))
            column = turned_ref[b * cols : (b + 1) * cols, index : index + 1]
            field_ref[origin + margin + b * cols : origin + margin + (b + 1) * cols, :] = (
                own.astype(F32) + mirror - column * mine[index : index + 1]
            )

    strips = []
    for b in range(tiles):
        strip = edge_ref[...]
        for k, tail in enumerate(tails):
            strip = jnp.where(lax.rem(me + k + 1, tiles) == b, tail[:edge], strip)
        for tail in tails:
            strip = strip + tail[(1 + b) * edge : (2 + b) * edge]
        strips.append(strip)
    strip = jnp.concatenate(strips, axis=1)
    wide = jnp.concatenate(scaled, axis=1)
    before = pl.multiple_of(jnp.maximum(me * cols - 8, 0), 8)
    after = pl.multiple_of(jnp.minimum((me + 1) * cols, width - 8), 8)
    left = turned_ref[pl.ds(before, 8), :][8 - halo :]
    right = turned_ref[pl.ds(after, 8), :][:halo]
    if plan.sides == 1:
        beside = jnp.where(me > 0, left, right)
    else:
        beside = jnp.concatenate([left, right], axis=0)
    lines = [
        strip[k * plan.edges : (k + 1) * plan.edges] - beside[:, k : k + 1] * wide[k : k + 1]
        for k in range(count)
    ]
    rows, slots = plan.rows, plan.slots
    stacks = []
    for slot in range(slots):
        members = []
        for group in range(plan.groups):
            k = group * slots + slot
            members.append(lines[k] if k < count else jnp.zeros((plan.edges, width), F32))
        stacks.append(jnp.concatenate(members, axis=0))
    lane = lax.broadcasted_iota(jnp.int32, (plan.side_rows, cols), 1)
    spare = plan.block_rows - plan.lead - plan.half_rows
    for step, out_ref in zip(step_order(plan), out_refs):
        first = partner(chip, step, plan.chips) * 2 * plan.band

        def section(begin, size):
            found = [
                field_ref[pl.ds(8 * k * plan.pitch + first + 8 + begin + r, 8, stride=plan.pitch), :]
                for r in range(size)
                for k in range(plan.sets)
            ]
            for k in range(8 * plan.sets, count):
                found.append(field_ref[pl.ds(k * plan.pitch + first + 8 + begin, size), :])
            return found

        lone, shared = 8 * plan.lone, 8 * plan.shared
        sides = []
        for core in range(2):
            side = jnp.zeros((plan.side_rows, cols), F32)
            for slot in range(slots):
                amount = lax.rem(slot * rows + halo + width - core * plan.band - first, width)
                moved = pltpu.roll(stacks[slot], amount, 1)[:, :cols]
                side = jnp.where((lane >= slot * rows) & (lane < (slot + 1) * rows), moved, side)
            sides.append(side)
        pieces = section(0, lone) + sides[:1] + section(lone, shared)
        pieces += section(lone + shared, lone) + sides[1:]
        if spare:
            pieces.append(jnp.zeros((spare, cols), F32))
        out_ref[...] = jnp.concatenate(pieces, axis=0).astype(BF16)


def core_pack(plan, *refs):
    *block_refs, out_ref = refs
    other = 1 - lax.axis_index("head") % 2
    for k, block_ref in enumerate(block_refs):
        out_ref[k] = half(plan, block_ref[...].astype(F32), other).astype(BF16)


def weight_pack(blocks_ref, proj_ref, set_ref, slot_ref, out_ref, map_ref, side_ref):
    map_ref[...] = dot(proj_ref[...], set_ref[...]).astype(BF16)
    side_ref[...] = dot(proj_ref[...], slot_ref[...]).astype(BF16)
    layers, convs, height, breadth = blocks_ref.shape[:4]
    for b in range(layers):
        for m in range(convs):
            out_ref[b * convs + m] = jnp.concatenate(
                [
                    jnp.concatenate(
                        [blocks_ref[b, m, dy, dx].astype(F32) for dy in range(height)], axis=1
                    )
                    for dx in range(breadth)
                ],
                axis=0,
            ).astype(BF16)


def lanes(base, size):
    return pl.ds(base if isinstance(base, int) else pl.multiple_of(base, LANES), size)


def shifted(ref, rows, base, offset, size):
    low = offset // LANES * LANES
    rest = offset - low
    if rest == 0:
        return ref[rows, lanes(base + low, size)]
    return pltpu.roll(ref[rows, lanes(base + low, size + LANES)], size + LANES - rest, 1)[:, :size]


def stack(plan, order, *refs):
    chips = plan.chips
    own_refs, swap_refs = refs[:chips], refs[chips : chips + len(order)]
    refs = refs[chips + len(order) :]
    proj_ref, side_ref, kernel_ref, vector_ref, mask_ref, spots_ref, out_ref = refs[:7]
    maps_ref, others_ref, sides_ref, stream_ref, hidden_ref, taps_ref, logit_ref = refs[7:]
    count, cols, rows, halo = plan.maps, plan.cols, plan.rows, plan.halo
    heads, feat, chunk, stride = plan.heads, plan.feat, plan.chunk, plan.stride
    head = lax.axis_index("head")
    chip, core = head // 2, head % 2
    lone, shared = 8 * plan.lone, 8 * plan.shared
    wide = 8 * plan.sets

    def rows_of(sections):
        sets, others = [], []
        for begin, size in sections:
            sets += [begin + r * wide for r in range(size)]
            others += [begin + size * wide + r for r in range(0, size, 8)]
        return sets, others, [size for _, size in sections for _ in range(0, size, 8)]

    early = rows_of([(0, lone), (plan.lead, shared)])
    late = rows_of([(0, shared), (shared * count, lone)])

    def spread(block, source):
        def pick(a, b, size):
            if a == b:
                return block[a : a + size]
            return jnp.where(core == 0, block[a : a + size], block[b : b + size])

        for r, (a, b) in enumerate(zip(early[0], late[0])):
            place = pl.multiple_of(source * wide, 8) + r * heads * wide
            maps_ref[pl.ds(pl.multiple_of(place, 8), wide), :] = pick(a, b, wide)
        for k, (a, b, m, n) in enumerate(zip(early[1], late[1], early[2], late[2])):
            for j in range(plan.rest):
                place = (source * plan.rest + j) * rows + 8 * k
                others_ref[pl.ds(pl.multiple_of(place, 8), 8), :] = pick(a + j * m, b + j * n, 8)
        side = pick(lone * count, plan.half_rows - plan.side_rows, plan.side_rows)
        place = pl.multiple_of(source * plan.side_rows, 8)
        sides_ref[pl.ds(place, plan.side_rows), :] = side

    for steps, swap_ref in zip(order, swap_refs):
        for k, step in enumerate(steps):
            source = 2 * partner(chip, step, chips, back=True)
            spread(half(plan, own_refs[step_order(plan).index(step)][...].astype(F32), core), source + core)
            spread(swap_ref[k].astype(F32), source + 1 - core)
    bias = vector_ref[:, 0:1]

    slots, members = plan.slots, heads * plan.groups
    lane = lax.broadcasted_iota(jnp.int32, (members, cols), 1)
    placed = []
    for first in range(0, plan.edges, slots):
        parts = [jnp.zeros((members, cols), F32) for _ in range(slots)]
        for at in range(min(slots, plan.edges - first)):
            value = sides_ref[pl.ds(first + at, members, stride=plan.edges), :]
            keep = (lane >= at * rows) & (lane < (at + 1) * rows)
            for slot in range(slots):
                moved = value
                if at != slot:
                    moved = pltpu.roll(value, ((at - slot) * rows) % cols, 1)
                parts[slot] = jnp.where(keep, moved, parts[slot])
        stacked = jnp.concatenate(parts, axis=0).astype(BF16)
        placed.append((dot(side_ref[...], stacked) + bias).astype(BF16))

    edge = sum(dot(columns, spots_ref[k]) for k, columns in enumerate(placed))

    weight = proj_ref[...]
    spot = lax.broadcasted_iota(jnp.int32, (feat, LANES), 1)
    spans = []

    def compose(tile):
        low, value = tile * LANES, None
        for begin, size, source, lead in spans:
            left, right = max(begin, low), min(begin + size, low + LANES)
            if left >= right:
                continue
            k = (lead + low) // LANES
            piece = source[:, k * LANES : (k + 1) * LANES]
            if value is None:
                value = piece
            else:
                value = jnp.where((spot >= left - low) & (spot < right - low), piece, value)
        here = slice(low, low + LANES)
        stream_ref[:, here] = jnp.where(mask_ref[:, here] > 0, value, 0.0).astype(BF16)

    done = plan.start // LANES
    for r in range(rows + 1):
        begin = plan.start + r * stride - halo
        between = LANES + r * 2 * halo - halo
        spans.append((begin, 2 * halo, edge, between - begin))
        if r < rows:
            block = maps_ref[r * heads * wide : (r + 1) * heads * wide, :]
            if plan.rest:
                others = others_ref[pl.ds(r, heads * plan.rest, stride=rows), :]
                block = jnp.concatenate([block, others], axis=0)
            value = dot(weight, block.astype(BF16)) + bias
            begin = plan.start + r * stride + halo
            turn = begin % LANES
            value = jnp.concatenate([value, jnp.zeros((feat, LANES), F32)], axis=1)
            spans.append((begin, cols, pltpu.roll(value, turn, 1), turn - begin))
        full = (plan.start + (r + 1) * stride - halo) // LANES if r < rows else done + 1
        while done < full:
            compose(done)
            done += 1
        spans = [span for span in spans if span[0] + span[1] > done * LANES]

    everything = slice(None)
    for n in range(plan.convs):
        source = hidden_ref if n % 2 else stream_ref
        low = (plan.start + (n + 1) * stride) // LANES * LANES
        steps = -(-(plan.start + (rows - n - 1) * stride - n - 1 - low) // chunk)
        offsets = vector_ref[:, n + 1 : n + 2]

        def multiply(base, size):
            window = jnp.concatenate(
                [shifted(source, everything, base, d * stride, size) for d in (-1, 0, 1)], axis=0
            )
            taps_ref[:, lanes(base, size)] = dot(kernel_ref[n], window)

        def finish(base):
            here = lanes(base, chunk)
            value = taps_ref[feat : 2 * feat, here]
            value = value + shifted(taps_ref, slice(0, feat), base, -1, chunk)
            value = value + shifted(taps_ref, slice(2 * feat, 3 * feat), base, 1, chunk)
            value = value + offsets
            keep = mask_ref[:, here] > 0
            if n % 2 == 0:
                value = jnp.where(value > 0, value, jnp.exp(jnp.minimum(value, 0.0)) - 1.0)
                hidden_ref[:, here] = jnp.where(keep, value, 0.0).astype(BF16)
                return
            value = (stream_ref[:, here].astype(F32) + value).astype(BF16)
            if n < plan.convs - 1:
                stream_ref[:, here] = jnp.where(keep, value.astype(F32), 0.0).astype(BF16)
                return
            readout = vector_ref[:, plan.convs + 1 : plan.convs + 2]
            logit_ref[0:1, here] = jnp.sum(value.astype(F32) * readout, axis=0, keepdims=True)

        multiply(low, chunk + LANES)

        def advance(i, carry):
            base = low + i * chunk
            finish(base)
            multiply(base + chunk + LANES, chunk)
            return carry

        lax.fori_loop(0, steps - 1, advance, 0)
        finish(low + (steps - 1) * chunk)

    for r in range(plan.band):
        begin = plan.start + (r + halo) * stride + halo
        low = begin // LANES * LANES
        out_ref[r : r + 1, :] = shifted(logit_ref, slice(0, 1), low, begin - low, cols)


def call(kernel, name, args, outs, scratch=(), held_out=True):
    held = sum(math.prod(x.shape) * jnp.dtype(x.dtype).itemsize for x in [*args, *outs, *scratch])
    vmem = pl.BlockSpec(memory_space=pltpu.VMEM)
    return pl.pallas_call(
        kernel,
        out_shape=[pltpu.VMEM(x.shape, x.dtype) if held_out else x for x in outs],
        in_specs=[vmem] * len(args),
        out_specs=[vmem] * len(outs),
        scratch_shapes=list(scratch),
        compiler_params=pltpu.CompilerParams(vmem_limit_bytes=held * 5 // 4 + 4 * 1024 * 1024),
        name=name,
    )(*args)


def array(dtype, *shape):
    return jax.ShapeDtypeStruct(shape, dtype)


def on_device(attention, proj_weight, proj_bias, conv_weight, conv_bias, out_weight):
    maps, width, cols = attention.shape
    feat = proj_weight.shape[0]
    blocks, convs = conv_weight.shape[:2]
    tiles, heads = lax.axis_size("tile"), lax.axis_size("head")
    plan = Plan(maps, width, cols, tiles, heads, feat, blocks * convs)
    me, band_index = lax.axis_index("tile"), lax.axis_index("head")

    payload, sums, edge = call(
        functools.partial(mirror_pack, plan),
        "mirror_pack",
        [attention],
        [
            array(BF16, tiles - 1, maps * cols + plan.tail_rows, cols),
            array(F32, plan.map_rows, width),
            array(F32, plan.edge_rows, cols),
        ],
    )
    received = jnp.stack(
        [
            lax.ppermute(payload[s - 1], "tile", [(i, (i + s) % tiles) for i in range(tiles)])
            for s in range(tiles - 1, 0, -1)
        ]
    )

    stride, start = plan.stride, plan.start
    source, index = np.divmod(np.arange(heads * maps), maps)
    wide = 8 * plan.sets
    by_set = np.where(
        index < wide, source * wide + index, heads * wide + source * plan.rest + index - wide
    )
    group, slot = np.divmod(index, plan.slots)
    by_slot = (slot * heads + source) * plan.groups + group
    picks = [
        jnp.asarray(place[:, None] == np.arange(size)[None], BF16)
        for place, size in (
            (by_set, heads * maps),
            (by_slot, plan.slots * heads * plan.groups),
        )
    ]
    kernels, map_weight, side_weight = call(
        weight_pack,
        "weight_pack",
        [conv_weight.transpose(0, 1, 4, 5, 2, 3), proj_weight, *picks],
        [
            array(BF16, plan.convs, 3 * feat, 3 * feat),
            array(BF16, feat, picks[0].shape[1]),
            array(BF16, feat, picks[1].shape[1]),
        ],
    )
    vectors = jnp.concatenate(
        [proj_bias[None], conv_bias.reshape(-1, feat), out_weight[None]], axis=0
    ).T
    spot = np.arange(plan.lanes) - start
    row = band_index * plan.band - plan.halo + (spot // stride).astype(np.int32)
    col = me * cols - plan.halo + (spot % stride).astype(np.int32)
    mask = (row >= 0) & (row < width) & (col >= 0) & (col < width)
    mask = mask.astype(F32)[None]

    key = np.arange(cols)
    member, line = key // plan.rows, key % plan.rows
    lane = np.arange(up(LANES + (plan.rows + 1) * 2 * plan.halo, LANES))
    spots = []
    for first in range(0, plan.edges, plan.slots):
        column = first + member
        fits = (member < plan.slots) & (column < plan.edges)
        left = LANES + line * 2 * plan.halo + column
        right = left + plan.halo
        if plan.sides == 1:
            places = [left, right]
        else:
            places = [np.where(column < plan.halo, left, right - plan.halo)]
        hit = [np.where(fits, place, -1)[:, None] == lane[None] for place in places]
        spots.append(functools.reduce(np.logical_or, hit))
    spots = jnp.asarray(np.stack(spots), BF16)

    chips = plan.chips
    blocks = call(
        functools.partial(correct_pack, plan),
        "correct_pack",
        [attention, received, sums, edge],
        [array(BF16, plan.block_rows, cols)] * chips,
        [pltpu.VMEM((maps * plan.pitch, cols), F32), pltpu.VMEM((width, LANES), F32)],
    )
    arrived = {}
    for step, block in zip(step_order(plan), blocks):
        pairs = [(i, 2 * partner(i // 2, step, chips) + i % 2) for i in range(heads)]
        arrived[step] = lax.ppermute(block, "head", pairs) if step else block
    far, near = far_near(plan)
    order = [far, near + [0]]
    weights = (map_weight, side_weight, kernels, vectors, mask, spots)
    swapped = []
    for steps in order:
        (packed,) = call(
            functools.partial(core_pack, plan),
            "core_pack",
            [arrived[k] for k in steps],
            [array(BF16, len(steps), plan.half_rows, cols)],
        )
        if steps is far:
            packed, weights = lax.optimization_barrier((packed, weights))
        swapped.append(lax.ppermute(packed, "head", [(i, i ^ 1) for i in range(heads)]))

    (logits,) = call(
        functools.partial(stack, plan, order),
        "stack",
        [*arrived.values(), *swapped, *weights],
        [array(F32, plan.band, cols)],
        [
            pltpu.VMEM((heads * 8 * plan.sets * plan.rows, cols), F32),
            pltpu.VMEM((heads * max(plan.rest, 1) * plan.rows, cols), F32),
            pltpu.VMEM((heads * plan.side_rows, cols), F32),
            pltpu.VMEM((feat, plan.lanes), BF16),
            pltpu.VMEM((feat, plan.lanes), BF16),
            pltpu.VMEM((3 * feat, plan.lanes), F32),
            pltpu.VMEM((8, plan.lanes), F32),
        ],
        held_out=False,
    )
    return logits


def solution(mesh):
    return jax.shard_map(
        on_device,
        mesh=mesh,
        in_specs=(P(("grp", "head"), None, "tile"), P(), P(), P(), P(), P()),
        out_specs=P(("grp", "head"), "tile"),
        check_vma=False,
    )
```

```python
import functools
import math
from typing import NamedTuple

import jax
import jax.numpy as jnp
import numpy as np
from jax import lax
from jax.experimental import pallas as pl
from jax.experimental.pallas import tpu as pltpu
from jax.sharding import PartitionSpec as P

BF16, F32 = jnp.bfloat16, jnp.float32
LANES = 128


def up(value, step):
    return -(-value // step) * step


class Plan(NamedTuple):
    maps: int
    width: int
    cols: int
    tiles: int
    heads: int
    feat: int
    convs: int

    @property
    def halo(self):
        return self.convs

    @property
    def sides(self):
        return min(2, self.tiles - 1)

    @property
    def edges(self):
        return self.sides * self.halo

    @property
    def edge_rows(self):
        return up(self.maps * self.edges, 8)

    @property
    def map_rows(self):
        return up(self.maps, 16)

    @property
    def tail_rows(self):
        return up((1 + self.tiles) * self.edge_rows + 3 * self.tiles * self.map_rows, 16)

    @property
    def band(self):
        return self.width // self.heads

    @property
    def rows(self):
        return self.band + 2 * self.halo

    @property
    def slots(self):
        return self.cols // self.rows

    @property
    def groups(self):
        return -(-self.maps // self.slots)

    @property
    def side_rows(self):
        return self.groups * self.edges

    @property
    def sets(self):
        return self.maps // 8

    @property
    def rest(self):
        return self.maps % 8

    @property
    def pitch(self):
        return up(self.width + 24, 2) + 1

    @property
    def chips(self):
        return self.heads // 2

    @property
    def lone(self):
        return self.band // 8

    @property
    def shared(self):
        return 2 * self.halo // 8

    @property
    def group_rows(self):
        return 8 * self.maps

    @property
    def lead(self):
        return self.lone * self.group_rows + self.side_rows

    @property
    def half_rows(self):
        return self.lead + self.shared * self.group_rows

    @property
    def block_rows(self):
        return up(self.lead + self.half_rows, 16)

    @property
    def stride(self):
        return self.cols + 2 * self.halo

    @property
    def start(self):
        return up(self.stride, LANES) - LANES

    @property
    def batch(self):
        return 8

    @property
    def chunk(self):
        return 1536

    @property
    def lanes(self):
        return up(self.start + self.rows * self.stride, LANES) + 4 * self.halo * LANES


def partner(mine, step, count, back=False):
    if count & (count - 1) == 0:
        return mine ^ step
    return (mine - step if back else mine + step) % count


def far_near(plan):
    steps = list(range(plan.chips - 1, 0, -1))
    return steps[: plan.chips // 2], steps[plan.chips // 2 :]


def step_order(plan):
    far, near = far_near(plan)
    return far + near + [0]


def half(plan, block, core):
    return jnp.where(
        core == 0, block[: plan.half_rows], block[plan.lead : plan.lead + plan.half_rows]
    )


def edge_start(plan, tile, side):
    left, right = plan.cols * tile - plan.halo, plan.cols * (tile + 1)
    if plan.sides == 1:
        return jnp.where(tile > 0, left, right)
    return (left, right)[side]


def edge_select(plan, tile, row, position, index):
    hit = None
    for side in range(plan.sides):
        first = index * plan.edges + side * plan.halo
        inside = (row >= first) & (row < first + plan.halo)
        one = inside & (position == row - first + edge_start(plan, tile, side))
        hit = one if hit is None else hit | one
    return hit


def across(a, b):
    return lax.dot_general(a, b, (((1,), (1,)), ((), ())), preferred_element_type=F32)


def dot(a, b):
    return jnp.dot(a, b, preferred_element_type=F32)


def mirror_pack(plan, maps_ref, out_ref, sums_ref, edge_ref):
    me = lax.axis_index("tile")
    count, cols, width, tiles = plan.maps, plan.cols, plan.width, plan.tiles
    head, edge = plan.map_rows, plan.edge_rows

    def pick(rows, span, base, tile, index):
        row = lax.broadcasted_iota(jnp.int32, (rows, span), 0)
        position = lax.broadcasted_iota(jnp.int32, (rows, span), 1) + base
        return edge_select(plan, tile, row, position, index).astype(F32)

    def total(span, index):
        return (lax.broadcasted_iota(jnp.int32, (head, span), 0) == index).astype(F32)

    for shift in range(1, tiles):
        dest = lax.rem(me + shift, tiles)
        by_col = by_row = None
        for index in range(count):
            block = maps_ref[index]
            out_ref[shift - 1, index * cols : (index + 1) * cols, :] = maps_ref[
                index, pl.ds(pl.multiple_of(dest * cols, cols), cols), :
            ]
            left = [pick(edge, cols, me * cols, dest, index)]
            upper = [pick(edge, width, 0, dest, index)]
            if shift == 1:
                left.append(total(cols, index))
                upper.append(total(width, index))
                upper.append(pick(edge, width, 0, me, index))
            by_c = across(jnp.concatenate(left, axis=0).astype(BF16), block)
            by_r = dot(jnp.concatenate(upper, axis=0).astype(BF16), block)
            by_col = by_c if by_col is None else by_col + by_c
            by_row = by_r if by_row is None else by_row + by_r
        if shift == 1:
            sums_ref[...] = by_col[edge : edge + head]
            own = pl.ds(pl.multiple_of(me * cols, cols), cols)
            sums_ref[:, own] = sums_ref[:, own] + by_row[edge : edge + head]
            edge_ref[...] = by_row[edge + head :]
            sums = sums_ref[...]
            high = sums.astype(BF16).astype(F32)
            middle = (sums - high).astype(BF16).astype(F32)
            low = sums - high - middle
        pieces = [by_row[:edge]]
        for wide in (by_col[:edge], high, middle, low):
            pieces += [wide[:, k * cols : (k + 1) * cols] for k in range(tiles)]
        used = (1 + tiles) * edge + 3 * tiles * head
        if plan.tail_rows > used:
            pieces.append(jnp.zeros((plan.tail_rows - used, cols), F32))
        out_ref[shift - 1, count * cols :, :] = jnp.concatenate(pieces, axis=0).astype(BF16)


def correct_pack(plan, maps_ref, recv_ref, sums_ref, edge_ref, *refs):
    *out_refs, field_ref, turned_ref = refs
    me, chip = lax.axis_index("tile"), lax.axis_index("head") // 2
    count, cols, width, tiles = plan.maps, plan.cols, plan.width, plan.tiles
    head, edge, halo = plan.map_rows, plan.edge_rows, plan.halo
    tails = [recv_ref[k, count * cols :, :].astype(F32) for k in range(tiles - 1)]

    rowsum = []
    for b in range(tiles):
        value = sums_ref[:, b * cols : (b + 1) * cols]
        for tail in tails:
            base = (1 + tiles) * edge
            parts = [
                tail[base + (k * tiles + b) * head : base + (k * tiles + b + 1) * head]
                for k in range(3)
            ]
            value = value + ((parts[0] + parts[1]) + parts[2])
        rowsum.append(value)
    grand = sum(jnp.sum(value, axis=1, keepdims=True) for value in rowsum)
    grand = jnp.where(lax.broadcasted_iota(jnp.int32, (head, 1), 0) < count, grand, 1.0)
    scaled = [value / grand for value in rowsum]
    for b in range(tiles):
        square = jnp.concatenate([rowsum[b], jnp.zeros((LANES - head, cols), F32)], axis=0)
        turned_ref[b * cols : (b + 1) * cols, :] = square.T
    mine = scaled[0]
    for b in range(1, tiles):
        mine = jnp.where(me == b, scaled[b], mine)

    eye = (
        lax.broadcasted_iota(jnp.int32, (cols, cols), 0)
        == lax.broadcasted_iota(jnp.int32, (cols, cols), 1)
    ).astype(F32).astype(BF16)
    margin = 8 + halo
    for index in range(count):
        origin = index * plan.pitch
        field_ref[origin : origin + margin, :] = jnp.zeros((margin, cols), F32)
        field_ref[origin + margin + width : origin + plan.pitch, :] = jnp.zeros(
            (plan.pitch - margin - width, cols), F32
        )
        for b in range(tiles):
            shift = lax.rem(b - me + tiles, tiles)
            other = recv_ref[
                jnp.maximum(shift - 1, 0), index * cols : (index + 1) * cols, :
            ]
            own = maps_ref[index, b * cols : (b + 1) * cols, :]
            mirror = across(eye, jnp.where(shift == 0, own, other))
            column = turned_ref[b * cols : (b + 1) * cols, index : index + 1]
            field_ref[origin + margin + b * cols : origin + margin + (b + 1) * cols, :] = (
                own.astype(F32) + mirror - column * mine[index : index + 1]
            )

    strips = []
    for b in range(tiles):
        strip = edge_ref[...]
        for k, tail in enumerate(tails):
            strip = jnp.where(lax.rem(me + k + 1, tiles) == b, tail[:edge], strip)
        for tail in tails:
            strip = strip + tail[(1 + b) * edge : (2 + b) * edge]
        strips.append(strip)
    strip = jnp.concatenate(strips, axis=1)
    wide = jnp.concatenate(scaled, axis=1)
    before = pl.multiple_of(jnp.maximum(me * cols - 8, 0), 8)
    after = pl.multiple_of(jnp.minimum((me + 1) * cols, width - 8), 8)
    left = turned_ref[pl.ds(before, 8), :][8 - halo :]
    right = turned_ref[pl.ds(after, 8), :][:halo]
    if plan.sides == 1:
        beside = jnp.where(me > 0, left, right)
    else:
        beside = jnp.concatenate([left, right], axis=0)
    lines = [
        strip[k * plan.edges : (k + 1) * plan.edges] - beside[:, k : k + 1] * wide[k : k + 1]
        for k in range(count)
    ]
    rows, slots = plan.rows, plan.slots
    stacks = []
    for slot in range(slots):
        members = []
        for group in range(plan.groups):
            k = group * slots + slot
            members.append(lines[k] if k < count else jnp.zeros((plan.edges, width), F32))
        stacks.append(jnp.concatenate(members, axis=0))
    lane = lax.broadcasted_iota(jnp.int32, (plan.side_rows, cols), 1)
    spare = plan.block_rows - plan.lead - plan.half_rows
    for step, out_ref in zip(step_order(plan), out_refs):
        first = partner(chip, step, plan.chips) * 2 * plan.band

        def section(begin, size):
            found = [
                field_ref[pl.ds(8 * k * plan.pitch + first + 8 + begin + r, 8, stride=plan.pitch), :]
                for r in range(size)
                for k in range(plan.sets)
            ]
            for k in range(8 * plan.sets, count):
                found.append(field_ref[pl.ds(k * plan.pitch + first + 8 + begin, size), :])
            return found

        lone, shared = 8 * plan.lone, 8 * plan.shared
        sides = []
        for core in range(2):
            side = jnp.zeros((plan.side_rows, cols), F32)
            for slot in range(slots):
                amount = lax.rem(slot * rows + halo + width - core * plan.band - first, width)
                moved = pltpu.roll(stacks[slot], amount, 1)[:, :cols]
                side = jnp.where((lane >= slot * rows) & (lane < (slot + 1) * rows), moved, side)
            sides.append(side)
        pieces = section(0, lone) + sides[:1] + section(lone, shared)
        pieces += section(lone + shared, lone) + sides[1:]
        if spare:
            pieces.append(jnp.zeros((spare, cols), F32))
        out_ref[...] = jnp.concatenate(pieces, axis=0).astype(BF16)


def core_pack(plan, *refs):
    *block_refs, out_ref = refs
    other = 1 - lax.axis_index("head") % 2
    for k, block_ref in enumerate(block_refs):
        out_ref[k] = half(plan, block_ref[...].astype(F32), other).astype(BF16)


def weight_pack(blocks_ref, proj_ref, set_ref, slot_ref, out_ref, map_ref, side_ref):
    map_ref[...] = dot(proj_ref[...], set_ref[...]).astype(BF16)
    side_ref[...] = dot(proj_ref[...], slot_ref[...]).astype(BF16)
    layers, convs, height, breadth = blocks_ref.shape[:4]
    for b in range(layers):
        for m in range(convs):
            out_ref[b * convs + m] = jnp.concatenate(
                [
                    jnp.concatenate(
                        [blocks_ref[b, m, dy, dx].astype(F32) for dy in range(height)], axis=1
                    )
                    for dx in range(breadth)
                ],
                axis=0,
            ).astype(BF16)


def lanes(base, size):
    return pl.ds(base if isinstance(base, int) else pl.multiple_of(base, LANES), size)


def shifted(ref, rows, base, offset, size):
    low = offset // LANES * LANES
    rest = offset - low
    if rest == 0:
        return ref[rows, lanes(base + low, size)]
    return pltpu.roll(ref[rows, lanes(base + low, size + LANES)], size + LANES - rest, 1)[:, :size]


def stack(plan, order, *refs):
    chips = plan.chips
    own_refs, swap_refs = refs[:chips], refs[chips : chips + len(order)]
    refs = refs[chips + len(order) :]
    proj_ref, side_ref, kernel_ref, vector_ref, mask_ref, spots_ref, out_ref = refs[:7]
    maps_ref, others_ref, sides_ref, stream_ref, hidden_ref, taps_ref, logit_ref = refs[7:]
    count, cols, rows, halo = plan.maps, plan.cols, plan.rows, plan.halo
    heads, feat, stride = plan.heads, plan.feat, plan.stride
    head = lax.axis_index("head")
    chip, core = head // 2, head % 2
    lone, shared = 8 * plan.lone, 8 * plan.shared
    wide = 8 * plan.sets

    def rows_of(sections):
        sets, others = [], []
        for begin, size in sections:
            sets += [begin + r * wide for r in range(size)]
            others += [begin + size * wide + r for r in range(0, size, 8)]
        return sets, others, [size for _, size in sections for _ in range(0, size, 8)]

    early = rows_of([(0, lone), (plan.lead, shared)])
    late = rows_of([(0, shared), (shared * count, lone)])

    def spread(block, source):
        def pick(a, b, size):
            if a == b:
                return block[a : a + size]
            return jnp.where(core == 0, block[a : a + size], block[b : b + size])

        for r, (a, b) in enumerate(zip(early[0], late[0])):
            place = pl.multiple_of(source * wide, 8) + r * heads * wide
            maps_ref[pl.ds(pl.multiple_of(place, 8), wide), :] = pick(a, b, wide)
        for k, (a, b, m, n) in enumerate(zip(early[1], late[1], early[2], late[2])):
            for j in range(plan.rest):
                place = (source * plan.rest + j) * rows + 8 * k
                others_ref[pl.ds(pl.multiple_of(place, 8), 8), :] = pick(a + j * m, b + j * n, 8)
        side = pick(lone * count, plan.half_rows - plan.side_rows, plan.side_rows)
        place = pl.multiple_of(source * plan.side_rows, 8)
        sides_ref[pl.ds(place, plan.side_rows), :] = side

    for steps, swap_ref in zip(order, swap_refs):
        for k, step in enumerate(steps):
            source = 2 * partner(chip, step, chips, back=True)
            spread(half(plan, own_refs[step_order(plan).index(step)][...].astype(F32), core), source + core)
            spread(swap_ref[k].astype(F32), source + 1 - core)
    bias = vector_ref[:, 0:1]

    slots, members = plan.slots, heads * plan.groups
    lane = lax.broadcasted_iota(jnp.int32, (members, cols), 1)
    placed = []
    for first in range(0, plan.edges, slots):
        parts = [jnp.zeros((members, cols), F32) for _ in range(slots)]
        for at in range(min(slots, plan.edges - first)):
            value = sides_ref[pl.ds(first + at, members, stride=plan.edges), :]
            keep = (lane >= at * rows) & (lane < (at + 1) * rows)
            for slot in range(slots):
                moved = value
                if at != slot:
                    moved = pltpu.roll(value, ((at - slot) * rows) % cols, 1)
                parts[slot] = jnp.where(keep, moved, parts[slot])
        stacked = jnp.concatenate(parts, axis=0).astype(BF16)
        placed.append((dot(side_ref[...], stacked) + bias).astype(BF16))

    edge = sum(dot(columns, spots_ref[k]) for k, columns in enumerate(placed))

    weight = proj_ref[...]
    spot = lax.broadcasted_iota(jnp.int32, (feat, LANES), 1)
    spans = []

    def compose(tile):
        low, value = tile * LANES, None
        for begin, size, source, lead in spans:
            left, right = max(begin, low), min(begin + size, low + LANES)
            if left >= right:
                continue
            k = (lead + low) // LANES
            piece = source[:, k * LANES : (k + 1) * LANES]
            if value is None:
                value = piece
            else:
                value = jnp.where((spot >= left - low) & (spot < right - low), piece, value)
        here = slice(low, low + LANES)
        stream_ref[:, here] = jnp.where(mask_ref[:, here] > 0, value, 0.0).astype(BF16)

    def gather(chosen):
        blocks = []
        for r in chosen:
            block = maps_ref[r * heads * wide : (r + 1) * heads * wide, :]
            if plan.rest:
                others = others_ref[pl.ds(r, heads * plan.rest, stride=rows), :]
                block = jnp.concatenate([block, others], axis=0)
            blocks.append(block.astype(BF16))
        return jnp.concatenate(blocks, axis=1)

    done = plan.start // LANES
    for r in range(rows + 1):
        begin = plan.start + r * stride - halo
        between = LANES + r * 2 * halo - halo
        spans.append((begin, 2 * halo, edge, between - begin))
        if r < rows:
            if r % plan.batch == 0:
                batch = dot(weight, gather(range(r, min(r + plan.batch, rows)))) + bias
            value = batch[:, r % plan.batch * cols : (r % plan.batch + 1) * cols]
            begin = plan.start + r * stride + halo
            turn = begin % LANES
            value = jnp.concatenate([value, jnp.zeros((feat, LANES), F32)], axis=1)
            spans.append((begin, cols, pltpu.roll(value, turn, 1), turn - begin))
        full = (plan.start + (r + 1) * stride - halo) // LANES if r < rows else done + 1
        while done < full:
            compose(done)
            done += 1
        spans = [span for span in spans if span[0] + span[1] > done * LANES]

    everything = slice(None)
    for n in range(plan.convs):
        source = hidden_ref if n % 2 else stream_ref
        low = (plan.start + (n + 1) * stride) // LANES * LANES
        span = plan.start + (rows - n - 1) * stride - n - 1 - low
        steps = -(-span // plan.chunk)
        size = up(-(-span // steps), LANES)
        offsets = vector_ref[:, n + 1 : n + 2]

        def multiply(base, size):
            window = jnp.concatenate(
                [shifted(source, everything, base, d * stride, size) for d in (-1, 0, 1)], axis=0
            )
            taps_ref[:, lanes(base, size)] = dot(kernel_ref[n], window)

        def finish(base):
            here = lanes(base, size)
            value = taps_ref[feat : 2 * feat, here]
            value = value + shifted(taps_ref, slice(0, feat), base, -1, size)
            value = value + shifted(taps_ref, slice(2 * feat, 3 * feat), base, 1, size)
            value = value + offsets
            keep = mask_ref[:, here] > 0
            if n % 2 == 0:
                value = jnp.where(value > 0, value, jnp.exp(jnp.minimum(value, 0.0)) - 1.0)
                hidden_ref[:, here] = jnp.where(keep, value, 0.0).astype(BF16)
                return
            value = (stream_ref[:, here].astype(F32) + value).astype(BF16)
            if n < plan.convs - 1:
                stream_ref[:, here] = jnp.where(keep, value.astype(F32), 0.0).astype(BF16)
                return
            readout = vector_ref[:, plan.convs + 1 : plan.convs + 2]
            logit_ref[0:1, here] = jnp.sum(value.astype(F32) * readout, axis=0, keepdims=True)

        multiply(low, size + LANES)
        for i in range(steps):
            if i + 1 < steps:
                multiply(low + (i + 1) * size + LANES, size)
            finish(low + i * size)

    for r in range(plan.band):
        begin = plan.start + (r + halo) * stride + halo
        low = begin // LANES * LANES
        out_ref[r : r + 1, :] = shifted(logit_ref, slice(0, 1), low, begin - low, cols)


def call(kernel, name, args, outs, scratch=(), held_out=True):
    held = sum(math.prod(x.shape) * jnp.dtype(x.dtype).itemsize for x in [*args, *outs, *scratch])
    vmem = pl.BlockSpec(memory_space=pltpu.VMEM)
    return pl.pallas_call(
        kernel,
        out_shape=[pltpu.VMEM(x.shape, x.dtype) if held_out else x for x in outs],
        in_specs=[vmem] * len(args),
        out_specs=[vmem] * len(outs),
        scratch_shapes=list(scratch),
        compiler_params=pltpu.CompilerParams(vmem_limit_bytes=held * 5 // 4 + 4 * 1024 * 1024),
        name=name,
    )(*args)


def array(dtype, *shape):
    return jax.ShapeDtypeStruct(shape, dtype)


def on_device(attention, proj_weight, proj_bias, conv_weight, conv_bias, out_weight):
    maps, width, cols = attention.shape
    feat = proj_weight.shape[0]
    blocks, convs = conv_weight.shape[:2]
    tiles, heads = lax.axis_size("tile"), lax.axis_size("head")
    plan = Plan(maps, width, cols, tiles, heads, feat, blocks * convs)
    me, band_index = lax.axis_index("tile"), lax.axis_index("head")

    payload, sums, edge = call(
        functools.partial(mirror_pack, plan),
        "mirror_pack",
        [attention],
        [
            array(BF16, tiles - 1, maps * cols + plan.tail_rows, cols),
            array(F32, plan.map_rows, width),
            array(F32, plan.edge_rows, cols),
        ],
    )
    received = jnp.stack(
        [
            lax.ppermute(payload[s - 1], "tile", [(i, (i + s) % tiles) for i in range(tiles)])
            for s in range(tiles - 1, 0, -1)
        ]
    )

    stride, start = plan.stride, plan.start
    source, index = np.divmod(np.arange(heads * maps), maps)
    wide = 8 * plan.sets
    by_set = np.where(
        index < wide, source * wide + index, heads * wide + source * plan.rest + index - wide
    )
    group, slot = np.divmod(index, plan.slots)
    by_slot = (slot * heads + source) * plan.groups + group
    picks = [
        jnp.asarray(place[:, None] == np.arange(size)[None], BF16)
        for place, size in (
            (by_set, heads * maps),
            (by_slot, plan.slots * heads * plan.groups),
        )
    ]
    kernels, map_weight, side_weight = call(
        weight_pack,
        "weight_pack",
        [conv_weight.transpose(0, 1, 4, 5, 2, 3), proj_weight, *picks],
        [
            array(BF16, plan.convs, 3 * feat, 3 * feat),
            array(BF16, feat, picks[0].shape[1]),
            array(BF16, feat, picks[1].shape[1]),
        ],
    )
    vectors = jnp.concatenate(
        [proj_bias[None], conv_bias.reshape(-1, feat), out_weight[None]], axis=0
    ).T
    spot = np.arange(plan.lanes) - start
    row = band_index * plan.band - plan.halo + (spot // stride).astype(np.int32)
    col = me * cols - plan.halo + (spot % stride).astype(np.int32)
    mask = (row >= 0) & (row < width) & (col >= 0) & (col < width)
    mask = mask.astype(F32)[None]

    key = np.arange(cols)
    member, line = key // plan.rows, key % plan.rows
    lane = np.arange(up(LANES + (plan.rows + 1) * 2 * plan.halo, LANES))
    spots = []
    for first in range(0, plan.edges, plan.slots):
        column = first + member
        fits = (member < plan.slots) & (column < plan.edges)
        left = LANES + line * 2 * plan.halo + column
        right = left + plan.halo
        if plan.sides == 1:
            places = [left, right]
        else:
            places = [np.where(column < plan.halo, left, right - plan.halo)]
        hit = [np.where(fits, place, -1)[:, None] == lane[None] for place in places]
        spots.append(functools.reduce(np.logical_or, hit))
    spots = jnp.asarray(np.stack(spots), BF16)

    chips = plan.chips
    blocks = call(
        functools.partial(correct_pack, plan),
        "correct_pack",
        [attention, received, sums, edge],
        [array(BF16, plan.block_rows, cols)] * chips,
        [pltpu.VMEM((maps * plan.pitch, cols), F32), pltpu.VMEM((width, LANES), F32)],
    )
    arrived = {}
    for step, block in zip(step_order(plan), blocks):
        pairs = [(i, 2 * partner(i // 2, step, chips) + i % 2) for i in range(heads)]
        arrived[step] = lax.ppermute(block, "head", pairs) if step else block
    far, near = far_near(plan)
    order = [far, near + [0]]
    weights = (map_weight, side_weight, kernels, vectors, mask, spots)
    swapped = []
    for steps in order:
        (packed,) = call(
            functools.partial(core_pack, plan),
            "core_pack",
            [arrived[k] for k in steps],
            [array(BF16, len(steps), plan.half_rows, cols)],
        )
        if steps is far:
            packed, weights = lax.optimization_barrier((packed, weights))
        swapped.append(lax.ppermute(packed, "head", [(i, i ^ 1) for i in range(heads)]))

    (logits,) = call(
        functools.partial(stack, plan, order),
        "stack",
        [*arrived.values(), *swapped, *weights],
        [array(F32, plan.band, cols)],
        [
            pltpu.VMEM((heads * 8 * plan.sets * plan.rows, cols), F32),
            pltpu.VMEM((heads * max(plan.rest, 1) * plan.rows, cols), F32),
            pltpu.VMEM((heads * plan.side_rows, cols), F32),
            pltpu.VMEM((feat, plan.lanes), BF16),
            pltpu.VMEM((feat, plan.lanes), BF16),
            pltpu.VMEM((3 * feat, plan.lanes), F32),
            pltpu.VMEM((8, plan.lanes), F32),
        ],
        held_out=False,
    )
    return logits


def solution(mesh):
    return jax.shard_map(
        on_device,
        mesh=mesh,
        in_specs=(P(("grp", "head"), None, "tile"), P(), P(), P(), P(), P()),
        out_specs=P(("grp", "head"), "tile"),
        check_vma=False,
    )
```

```python
import functools
import math
from typing import NamedTuple

import jax
import jax.numpy as jnp
import numpy as np
from jax import lax
from jax.experimental import pallas as pl
from jax.experimental.pallas import tpu as pltpu
from jax.sharding import PartitionSpec as P

BF16, F32 = jnp.bfloat16, jnp.float32
LANES = 128


def up(value, step):
    return -(-value // step) * step


class Plan(NamedTuple):
    maps: int
    width: int
    cols: int
    tiles: int
    heads: int
    feat: int
    convs: int

    @property
    def halo(self):
        return self.convs

    @property
    def sides(self):
        return min(2, self.tiles - 1)

    @property
    def edges(self):
        return self.sides * self.halo

    @property
    def edge_rows(self):
        return up(self.maps * self.edges, 8)

    @property
    def map_rows(self):
        return up(self.maps, 16)

    @property
    def tail_rows(self):
        return up((1 + self.tiles) * self.edge_rows + 3 * self.tiles * self.map_rows, 16)

    @property
    def band(self):
        return self.width // self.heads

    @property
    def rows(self):
        return self.band + 2 * self.halo

    @property
    def slots(self):
        return self.cols // self.rows

    @property
    def groups(self):
        return -(-self.maps // self.slots)

    @property
    def side_rows(self):
        return self.groups * self.edges

    @property
    def sets(self):
        return self.maps // 8

    @property
    def rest(self):
        return self.maps % 8

    @property
    def pitch(self):
        return up(self.width + 24, 2) + 1

    @property
    def chips(self):
        return self.heads // 2

    @property
    def lone(self):
        return self.band // 8

    @property
    def shared(self):
        return 2 * self.halo // 8

    @property
    def group_rows(self):
        return 8 * self.maps

    @property
    def lead(self):
        return self.lone * self.group_rows + self.side_rows

    @property
    def half_rows(self):
        return self.lead + self.shared * self.group_rows

    @property
    def block_rows(self):
        return self.lead + self.half_rows

    @property
    def stride(self):
        return self.cols + 2 * self.halo

    @property
    def start(self):
        return up(self.stride, LANES) - LANES

    @property
    def batch(self):
        return 8

    @property
    def chunk(self):
        return 1536

    @property
    def lanes(self):
        return up(self.start + self.rows * self.stride, LANES) + 4 * self.halo * LANES


def partner(mine, step, count, back=False):
    if count & (count - 1) == 0:
        return mine ^ step
    return (mine - step if back else mine + step) % count


def far_near(plan):
    steps = list(range(plan.chips - 1, 0, -1))
    return steps[: plan.chips // 2], steps[plan.chips // 2 :]


def step_order(plan):
    far, near = far_near(plan)
    middle = len(far) // 2
    return far[:middle] + near + far[middle:] + [0]


def half(plan, block, core):
    return jnp.where(
        core == 0, block[: plan.half_rows], block[plan.lead : plan.lead + plan.half_rows]
    )


def edge_start(plan, tile, side):
    left, right = plan.cols * tile - plan.halo, plan.cols * (tile + 1)
    if plan.sides == 1:
        return jnp.where(tile > 0, left, right)
    return (left, right)[side]


def edge_select(plan, tile, row, position, index):
    hit = None
    for side in range(plan.sides):
        first = index * plan.edges + side * plan.halo
        inside = (row >= first) & (row < first + plan.halo)
        one = inside & (position == row - first + edge_start(plan, tile, side))
        hit = one if hit is None else hit | one
    return hit


def across(a, b):
    return lax.dot_general(a, b, (((1,), (1,)), ((), ())), preferred_element_type=F32)


def dot(a, b):
    return jnp.dot(a, b, preferred_element_type=F32)


def mirror_pack(plan, maps_ref, out_ref, sums_ref, edge_ref):
    me = lax.axis_index("tile")
    count, cols, width, tiles = plan.maps, plan.cols, plan.width, plan.tiles
    head, edge = plan.map_rows, plan.edge_rows

    def pick(rows, span, base, tile, index):
        row = lax.broadcasted_iota(jnp.int32, (rows, span), 0)
        position = lax.broadcasted_iota(jnp.int32, (rows, span), 1) + base
        return edge_select(plan, tile, row, position, index).astype(F32)

    def total(span, index):
        return (lax.broadcasted_iota(jnp.int32, (head, span), 0) == index).astype(F32)

    for shift in range(1, tiles):
        dest = lax.rem(me + shift, tiles)
        by_col = by_row = None
        for index in range(count):
            block = maps_ref[index]
            out_ref[shift - 1, index * cols : (index + 1) * cols, :] = maps_ref[
                index, pl.ds(pl.multiple_of(dest * cols, cols), cols), :
            ]
            left = [pick(edge, cols, me * cols, dest, index)]
            upper = [pick(edge, width, 0, dest, index)]
            if shift == 1:
                left.append(total(cols, index))
                upper.append(total(width, index))
                upper.append(pick(edge, width, 0, me, index))
            by_c = across(jnp.concatenate(left, axis=0).astype(BF16), block)
            by_r = dot(jnp.concatenate(upper, axis=0).astype(BF16), block)
            by_col = by_c if by_col is None else by_col + by_c
            by_row = by_r if by_row is None else by_row + by_r
        if shift == 1:
            sums_ref[...] = by_col[edge : edge + head]
            own = pl.ds(pl.multiple_of(me * cols, cols), cols)
            sums_ref[:, own] = sums_ref[:, own] + by_row[edge : edge + head]
            edge_ref[...] = by_row[edge + head :]
            sums = sums_ref[...]
            high = sums.astype(BF16).astype(F32)
            middle = (sums - high).astype(BF16).astype(F32)
            low = sums - high - middle
        pieces = [by_row[:edge]]
        for wide in (by_col[:edge], high, middle, low):
            pieces += [wide[:, k * cols : (k + 1) * cols] for k in range(tiles)]
        used = (1 + tiles) * edge + 3 * tiles * head
        if plan.tail_rows > used:
            pieces.append(jnp.zeros((plan.tail_rows - used, cols), F32))
        out_ref[shift - 1, count * cols :, :] = jnp.concatenate(pieces, axis=0).astype(BF16)


def correct_pack(plan, maps_ref, recv_ref, sums_ref, edge_ref, *refs):
    *out_refs, field_ref, turned_ref = refs
    me, chip = lax.axis_index("tile"), lax.axis_index("head") // 2
    count, cols, width, tiles = plan.maps, plan.cols, plan.width, plan.tiles
    head, edge, halo = plan.map_rows, plan.edge_rows, plan.halo
    tails = [recv_ref[k, count * cols :, :].astype(F32) for k in range(tiles - 1)]

    rowsum = []
    for b in range(tiles):
        value = sums_ref[:, b * cols : (b + 1) * cols]
        for tail in tails:
            base = (1 + tiles) * edge
            parts = [
                tail[base + (k * tiles + b) * head : base + (k * tiles + b + 1) * head]
                for k in range(3)
            ]
            value = value + ((parts[0] + parts[1]) + parts[2])
        rowsum.append(value)
    grand = sum(jnp.sum(value, axis=1, keepdims=True) for value in rowsum)
    grand = jnp.where(lax.broadcasted_iota(jnp.int32, (head, 1), 0) < count, grand, 1.0)
    scaled = [value / grand for value in rowsum]
    for b in range(tiles):
        square = jnp.concatenate([rowsum[b], jnp.zeros((LANES - head, cols), F32)], axis=0)
        turned_ref[b * cols : (b + 1) * cols, :] = square.T
    mine = scaled[0]
    for b in range(1, tiles):
        mine = jnp.where(me == b, scaled[b], mine)

    eye = (
        lax.broadcasted_iota(jnp.int32, (cols, cols), 0)
        == lax.broadcasted_iota(jnp.int32, (cols, cols), 1)
    ).astype(F32).astype(BF16)
    margin = 8 + halo
    mirrors = []
    for b in range(tiles):
        shift = lax.rem(b - me + tiles, tiles)
        other = recv_ref[jnp.maximum(shift - 1, 0), : count * cols, :]
        own = [maps_ref[k, b * cols : (b + 1) * cols, :] for k in range(count)]
        mirrors.append(across(eye, jnp.where(shift == 0, jnp.concatenate(own, axis=0), other)))
    for index in range(count):
        origin = index * plan.pitch
        field_ref[origin : origin + margin, :] = jnp.zeros((margin, cols), F32)
        field_ref[origin + margin + width : origin + plan.pitch, :] = jnp.zeros(
            (plan.pitch - margin - width, cols), F32
        )
        for b in range(tiles):
            own = maps_ref[index, b * cols : (b + 1) * cols, :]
            mirror = mirrors[b][:, index * cols : (index + 1) * cols]
            column = turned_ref[b * cols : (b + 1) * cols, index : index + 1]
            field_ref[origin + margin + b * cols : origin + margin + (b + 1) * cols, :] = (
                own.astype(F32) + mirror - column * mine[index : index + 1]
            )

    strips = []
    for b in range(tiles):
        strip = edge_ref[...]
        for k, tail in enumerate(tails):
            strip = jnp.where(lax.rem(me + k + 1, tiles) == b, tail[:edge], strip)
        for tail in tails:
            strip = strip + tail[(1 + b) * edge : (2 + b) * edge]
        strips.append(strip)
    strip = jnp.concatenate(strips, axis=1)
    wide = jnp.concatenate(scaled, axis=1)
    before = pl.multiple_of(jnp.maximum(me * cols - 8, 0), 8)
    after = pl.multiple_of(jnp.minimum((me + 1) * cols, width - 8), 8)
    left = turned_ref[pl.ds(before, 8), :][8 - halo :]
    right = turned_ref[pl.ds(after, 8), :][:halo]
    if plan.sides == 1:
        beside = jnp.where(me > 0, left, right)
    else:
        beside = jnp.concatenate([left, right], axis=0)
    lines = [
        strip[k * plan.edges : (k + 1) * plan.edges] - beside[:, k : k + 1] * wide[k : k + 1]
        for k in range(count)
    ]
    rows, slots = plan.rows, plan.slots
    stacks = []
    for slot in range(slots):
        members = []
        for group in range(plan.groups):
            k = group * slots + slot
            members.append(lines[k] if k < count else jnp.zeros((plan.edges, width), F32))
        stacks.append(jnp.concatenate(members, axis=0))
    lane = lax.broadcasted_iota(jnp.int32, (plan.side_rows, cols), 1)
    spare = plan.block_rows - plan.lead - plan.half_rows
    for step, out_ref in zip(step_order(plan), out_refs):
        first = partner(chip, step, plan.chips) * 2 * plan.band

        def section(begin, size):
            found = [
                field_ref[pl.ds(8 * k * plan.pitch + first + 8 + begin + r, 8, stride=plan.pitch), :]
                for r in range(size)
                for k in range(plan.sets)
            ]
            for k in range(8 * plan.sets, count):
                found.append(field_ref[pl.ds(k * plan.pitch + first + 8 + begin, size), :])
            return found

        lone, shared = 8 * plan.lone, 8 * plan.shared
        sides = []
        for core in range(2):
            side = jnp.zeros((plan.side_rows, cols), F32)
            for slot in range(slots):
                amount = lax.rem(slot * rows + halo + width - core * plan.band - first, width)
                moved = pltpu.roll(stacks[slot], amount, 1)[:, :cols]
                side = jnp.where((lane >= slot * rows) & (lane < (slot + 1) * rows), moved, side)
            sides.append(side)
        pieces = section(0, lone) + sides[:1] + section(lone, shared)
        pieces += section(lone + shared, lone) + sides[1:]
        if spare:
            pieces.append(jnp.zeros((spare, cols), F32))
        out_ref[...] = jnp.concatenate(pieces, axis=0).astype(BF16)


def core_pack(plan, *refs):
    *block_refs, out_ref = refs
    other = 1 - lax.axis_index("head") % 2
    for k, block_ref in enumerate(block_refs):
        out_ref[k] = half(plan, block_ref[...].astype(F32), other).astype(BF16)


def weight_pack(blocks_ref, proj_ref, set_ref, slot_ref, out_ref, map_ref, side_ref):
    map_ref[...] = dot(proj_ref[...], set_ref[...]).astype(BF16)
    side_ref[...] = dot(proj_ref[...], slot_ref[...]).astype(BF16)
    layers, convs, height, breadth = blocks_ref.shape[:4]
    for b in range(layers):
        for m in range(convs):
            out_ref[b * convs + m] = jnp.concatenate(
                [
                    jnp.concatenate(
                        [blocks_ref[b, m, dy, dx].astype(F32) for dy in range(height)], axis=1
                    )
                    for dx in range(breadth)
                ],
                axis=0,
            ).astype(BF16)


def lanes(base, size):
    return pl.ds(base if isinstance(base, int) else pl.multiple_of(base, LANES), size)


def shifted(ref, rows, base, offset, size):
    low = offset // LANES * LANES
    rest = offset - low
    if rest == 0:
        return ref[rows, lanes(base + low, size)]
    return pltpu.roll(ref[rows, lanes(base + low, size + LANES)], size + LANES - rest, 1)[:, :size]


def stack(plan, order, *refs):
    chips = plan.chips
    own_refs, swap_refs = refs[:chips], refs[chips : chips + len(order)]
    refs = refs[chips + len(order) :]
    proj_ref, side_ref, kernel_ref, vector_ref, mask_ref, spots_ref, out_ref = refs[:7]
    maps_ref, others_ref, sides_ref, stream_ref, hidden_ref, taps_ref, logit_ref = refs[7:]
    count, cols, rows, halo = plan.maps, plan.cols, plan.rows, plan.halo
    heads, feat, stride = plan.heads, plan.feat, plan.stride
    head = lax.axis_index("head")
    chip, core = head // 2, head % 2
    lone, shared = 8 * plan.lone, 8 * plan.shared
    wide = 8 * plan.sets

    def rows_of(sections):
        sets, others = [], []
        for begin, size in sections:
            sets += [begin + r * wide for r in range(size)]
            others += [begin + size * wide + r for r in range(0, size, 8)]
        return sets, others, [size for _, size in sections for _ in range(0, size, 8)]

    early = rows_of([(0, lone), (plan.lead, shared)])
    late = rows_of([(0, shared), (shared * count, lone)])

    def spread(block, source):
        def pick(a, b, size):
            if a == b:
                return block[a : a + size]
            return jnp.where(core == 0, block[a : a + size], block[b : b + size])

        for r, (a, b) in enumerate(zip(early[0], late[0])):
            place = pl.multiple_of(source * wide, 8) + r * heads * wide
            maps_ref[pl.ds(pl.multiple_of(place, 8), wide), :] = pick(a, b, wide)
        for k, (a, b, m, n) in enumerate(zip(early[1], late[1], early[2], late[2])):
            for j in range(plan.rest):
                place = (source * plan.rest + j) * rows + 8 * k
                others_ref[pl.ds(pl.multiple_of(place, 8), 8), :] = pick(a + j * m, b + j * n, 8)
        side = pick(lone * count, plan.half_rows - plan.side_rows, plan.side_rows)
        place = pl.multiple_of(source * plan.side_rows, 8)
        sides_ref[pl.ds(place, plan.side_rows), :] = side

    for steps, swap_ref in zip(order, swap_refs):
        for k, step in enumerate(steps):
            source = 2 * partner(chip, step, chips, back=True)
            spread(half(plan, own_refs[step_order(plan).index(step)][...].astype(F32), core), source + core)
            spread(swap_ref[k].astype(F32), source + 1 - core)
    bias = vector_ref[:, 0:1]

    slots, members = plan.slots, heads * plan.groups
    lane = lax.broadcasted_iota(jnp.int32, (members, cols), 1)
    placed = []
    for first in range(0, plan.edges, slots):
        parts = [jnp.zeros((members, cols), F32) for _ in range(slots)]
        for at in range(min(slots, plan.edges - first)):
            value = sides_ref[pl.ds(first + at, members, stride=plan.edges), :]
            keep = (lane >= at * rows) & (lane < (at + 1) * rows)
            for slot in range(slots):
                moved = value
                if at != slot:
                    moved = pltpu.roll(value, ((at - slot) * rows) % cols, 1)
                parts[slot] = jnp.where(keep, moved, parts[slot])
        stacked = jnp.concatenate(parts, axis=0).astype(BF16)
        placed.append((dot(side_ref[...], stacked) + bias).astype(BF16))

    edge = sum(dot(columns, spots_ref[k]) for k, columns in enumerate(placed))

    weight = proj_ref[...]
    spot = lax.broadcasted_iota(jnp.int32, (feat, LANES), 1)
    spans = []

    def compose(tile):
        low, value = tile * LANES, None
        for begin, size, source, lead in spans:
            left, right = max(begin, low), min(begin + size, low + LANES)
            if left >= right:
                continue
            k = (lead + low) // LANES
            piece = source[:, k * LANES : (k + 1) * LANES]
            if value is None:
                value = piece
            else:
                value = jnp.where((spot >= left - low) & (spot < right - low), piece, value)
        here = slice(low, low + LANES)
        stream_ref[:, here] = jnp.where(mask_ref[:, here] > 0, value, 0.0).astype(BF16)

    def gather(chosen):
        blocks = []
        for r in chosen:
            block = maps_ref[r * heads * wide : (r + 1) * heads * wide, :]
            if plan.rest:
                others = others_ref[pl.ds(r, heads * plan.rest, stride=rows), :]
                block = jnp.concatenate([block, others], axis=0)
            blocks.append(block.astype(BF16))
        return jnp.concatenate(blocks, axis=1)

    done = plan.start // LANES
    for r in range(rows + 1):
        begin = plan.start + r * stride - halo
        between = LANES + r * 2 * halo - halo
        spans.append((begin, 2 * halo, edge, between - begin))
        if r < rows:
            if r % plan.batch == 0:
                batch = dot(weight, gather(range(r, min(r + plan.batch, rows)))) + bias
            value = batch[:, r % plan.batch * cols : (r % plan.batch + 1) * cols]
            begin = plan.start + r * stride + halo
            turn = begin % LANES
            value = jnp.concatenate([value, jnp.zeros((feat, LANES), F32)], axis=1)
            spans.append((begin, cols, pltpu.roll(value, turn, 1), turn - begin))
        full = (plan.start + (r + 1) * stride - halo) // LANES if r < rows else done + 1
        while done < full:
            compose(done)
            done += 1
        spans = [span for span in spans if span[0] + span[1] > done * LANES]

    everything = slice(None)
    for n in range(plan.convs):
        source = hidden_ref if n % 2 else stream_ref
        low = (plan.start + (n + 1) * stride) // LANES * LANES
        span = plan.start + (rows - n - 1) * stride - n - 1 - low
        steps = -(-span // plan.chunk)
        size = up(-(-span // steps), LANES)
        offsets = vector_ref[:, n + 1 : n + 2]

        def multiply(base, size):
            window = jnp.concatenate(
                [shifted(source, everything, base, d * stride, size) for d in (-1, 0, 1)], axis=0
            )
            taps_ref[:, lanes(base, size)] = dot(kernel_ref[n], window)

        def finish(base):
            here = lanes(base, size)
            value = taps_ref[feat : 2 * feat, here]
            value = value + shifted(taps_ref, slice(0, feat), base, -1, size)
            value = value + shifted(taps_ref, slice(2 * feat, 3 * feat), base, 1, size)
            value = value + offsets
            keep = mask_ref[:, here] > 0
            if n % 2 == 0:
                value = jnp.where(value > 0, value, jnp.exp(jnp.minimum(value, 0.0)) - 1.0)
                hidden_ref[:, here] = jnp.where(keep, value, 0.0).astype(BF16)
                return
            value = (stream_ref[:, here].astype(F32) + value).astype(BF16)
            if n < plan.convs - 1:
                stream_ref[:, here] = jnp.where(keep, value.astype(F32), 0.0).astype(BF16)
                return
            readout = vector_ref[:, plan.convs + 1 : plan.convs + 2]
            logit_ref[0:1, here] = jnp.sum(value.astype(F32) * readout, axis=0, keepdims=True)

        multiply(low, size + LANES)
        for i in range(steps):
            if i + 1 < steps:
                multiply(low + (i + 1) * size + LANES, size)
            finish(low + i * size)

    for r in range(plan.band):
        begin = plan.start + (r + halo) * stride + halo
        low = begin // LANES * LANES
        out_ref[r : r + 1, :] = shifted(logit_ref, slice(0, 1), low, begin - low, cols)


def call(kernel, name, args, outs, scratch=(), held_out=True):
    held = sum(math.prod(x.shape) * jnp.dtype(x.dtype).itemsize for x in [*args, *outs, *scratch])
    vmem = pl.BlockSpec(memory_space=pltpu.VMEM)
    return pl.pallas_call(
        kernel,
        out_shape=[pltpu.VMEM(x.shape, x.dtype) if held_out else x for x in outs],
        in_specs=[vmem] * len(args),
        out_specs=[vmem] * len(outs),
        scratch_shapes=list(scratch),
        compiler_params=pltpu.CompilerParams(vmem_limit_bytes=held * 5 // 4 + 4 * 1024 * 1024),
        name=name,
    )(*args)


def array(dtype, *shape):
    return jax.ShapeDtypeStruct(shape, dtype)


def on_device(attention, proj_weight, proj_bias, conv_weight, conv_bias, out_weight):
    maps, width, cols = attention.shape
    feat = proj_weight.shape[0]
    blocks, convs = conv_weight.shape[:2]
    tiles, heads = lax.axis_size("tile"), lax.axis_size("head")
    plan = Plan(maps, width, cols, tiles, heads, feat, blocks * convs)
    me, band_index = lax.axis_index("tile"), lax.axis_index("head")

    payload, sums, edge = call(
        functools.partial(mirror_pack, plan),
        "mirror_pack",
        [attention],
        [
            array(BF16, tiles - 1, maps * cols + plan.tail_rows, cols),
            array(F32, plan.map_rows, width),
            array(F32, plan.edge_rows, cols),
        ],
    )
    received = jnp.stack(
        [
            lax.ppermute(payload[s - 1], "tile", [(i, (i + s) % tiles) for i in range(tiles)])
            for s in range(tiles - 1, 0, -1)
        ]
    )

    stride, start = plan.stride, plan.start
    source, index = np.divmod(np.arange(heads * maps), maps)
    wide = 8 * plan.sets
    by_set = np.where(
        index < wide, source * wide + index, heads * wide + source * plan.rest + index - wide
    )
    group, slot = np.divmod(index, plan.slots)
    by_slot = (slot * heads + source) * plan.groups + group
    picks = [
        jnp.asarray(place[:, None] == np.arange(size)[None], BF16)
        for place, size in (
            (by_set, heads * maps),
            (by_slot, plan.slots * heads * plan.groups),
        )
    ]
    kernels, map_weight, side_weight = call(
        weight_pack,
        "weight_pack",
        [conv_weight.transpose(0, 1, 4, 5, 2, 3), proj_weight, *picks],
        [
            array(BF16, plan.convs, 3 * feat, 3 * feat),
            array(BF16, feat, picks[0].shape[1]),
            array(BF16, feat, picks[1].shape[1]),
        ],
    )
    vectors = jnp.concatenate(
        [proj_bias[None], conv_bias.reshape(-1, feat), out_weight[None]], axis=0
    ).T
    spot = np.arange(plan.lanes) - start
    row = band_index * plan.band - plan.halo + (spot // stride).astype(np.int32)
    col = me * cols - plan.halo + (spot % stride).astype(np.int32)
    mask = (row >= 0) & (row < width) & (col >= 0) & (col < width)
    mask = mask.astype(F32)[None]

    key = np.arange(cols)
    member, line = key // plan.rows, key % plan.rows
    lane = np.arange(up(LANES + (plan.rows + 1) * 2 * plan.halo, LANES))
    spots = []
    for first in range(0, plan.edges, plan.slots):
        column = first + member
        fits = (member < plan.slots) & (column < plan.edges)
        left = LANES + line * 2 * plan.halo + column
        right = left + plan.halo
        if plan.sides == 1:
            places = [left, right]
        else:
            places = [np.where(column < plan.halo, left, right - plan.halo)]
        hit = [np.where(fits, place, -1)[:, None] == lane[None] for place in places]
        spots.append(functools.reduce(np.logical_or, hit))
    spots = jnp.asarray(np.stack(spots), BF16)

    chips = plan.chips
    blocks = call(
        functools.partial(correct_pack, plan),
        "correct_pack",
        [attention, received, sums, edge],
        [array(BF16, plan.block_rows, cols)] * chips,
        [pltpu.VMEM((maps * plan.pitch, cols), F32), pltpu.VMEM((width, LANES), F32)],
    )
    arrived = {}
    for step, block in zip(step_order(plan), blocks):
        pairs = [(i, 2 * partner(i // 2, step, chips) + i % 2) for i in range(heads)]
        arrived[step] = lax.ppermute(block, "head", pairs) if step else block
    steps = step_order(plan)
    early = steps[: chips // 2]
    late = [step for step in steps if step not in early]
    order = [early, late]
    weights = (map_weight, side_weight, kernels, vectors, mask, spots)
    swapped = []
    for steps in order:
        (packed,) = call(
            functools.partial(core_pack, plan),
            "core_pack",
            [arrived[k] for k in steps],
            [array(BF16, len(steps), plan.half_rows, cols)],
        )
        if steps is late:
            packed, weights = lax.optimization_barrier((packed, weights))
        swapped.append(lax.ppermute(packed, "head", [(i, i ^ 1) for i in range(heads)]))

    (logits,) = call(
        functools.partial(stack, plan, order),
        "stack",
        [*arrived.values(), *swapped, *weights],
        [array(F32, plan.band, cols)],
        [
            pltpu.VMEM((heads * 8 * plan.sets * plan.rows, cols), F32),
            pltpu.VMEM((heads * max(plan.rest, 1) * plan.rows, cols), F32),
            pltpu.VMEM((heads * plan.side_rows, cols), F32),
            pltpu.VMEM((feat, plan.lanes), BF16),
            pltpu.VMEM((feat, plan.lanes), BF16),
            pltpu.VMEM((3 * feat, plan.lanes), F32),
            pltpu.VMEM((8, plan.lanes), F32),
        ],
        held_out=False,
    )
    return logits


def solution(mesh):
    return jax.shard_map(
        on_device,
        mesh=mesh,
        in_specs=(P(("grp", "head"), None, "tile"), P(), P(), P(), P(), P()),
        out_specs=P(("grp", "head"), "tile"),
        check_vma=False,
    )
```

```python
import functools
import math
from typing import NamedTuple

import jax
import jax.numpy as jnp
import numpy as np
from jax import lax
from jax.experimental import pallas as pl
from jax.experimental.pallas import tpu as pltpu
from jax.sharding import PartitionSpec as P

BF16, F32 = jnp.bfloat16, jnp.float32
LANES = 128


def up(value, step):
    return -(-value // step) * step


class Plan(NamedTuple):
    maps: int
    width: int
    cols: int
    tiles: int
    heads: int
    feat: int
    convs: int

    @property
    def halo(self):
        return self.convs

    @property
    def sides(self):
        return min(2, self.tiles - 1)

    @property
    def edges(self):
        return self.sides * self.halo

    @property
    def edge_rows(self):
        return up(self.maps * self.edges, 8)

    @property
    def map_rows(self):
        return up(self.maps, 16)

    @property
    def tail_rows(self):
        return up((1 + self.tiles) * self.edge_rows + 3 * self.tiles * self.map_rows, 16)

    @property
    def band(self):
        return self.width // self.heads

    @property
    def rows(self):
        return self.band + 2 * self.halo

    @property
    def slots(self):
        return self.cols // self.rows

    @property
    def groups(self):
        return -(-self.maps // self.slots)

    @property
    def side_rows(self):
        return self.groups * self.edges

    @property
    def sets(self):
        return self.maps // 8

    @property
    def rest(self):
        return self.maps % 8

    @property
    def pitch(self):
        return up(self.width + 24, 2) + 1

    @property
    def chips(self):
        return self.heads // 2

    @property
    def lone(self):
        return self.band // 8

    @property
    def shared(self):
        return 2 * self.halo // 8

    @property
    def group_rows(self):
        return 8 * self.maps

    @property
    def lead(self):
        return self.lone * self.group_rows + self.side_rows

    @property
    def half_rows(self):
        return self.lead + self.shared * self.group_rows

    @property
    def block_rows(self):
        return self.lead + self.half_rows

    @property
    def stride(self):
        return self.cols + 2 * self.halo

    @property
    def start(self):
        return up(self.stride, LANES) - LANES

    @property
    def batch(self):
        return 32

    @property
    def chunk(self):
        return 3072

    @property
    def lanes(self):
        return up(self.start + self.rows * self.stride, LANES) + 4 * self.halo * LANES


def partner(mine, step, count, back=False):
    if count & (count - 1) == 0:
        return mine ^ step
    return (mine - step if back else mine + step) % count


def far_near(plan):
    steps = list(range(plan.chips - 1, 0, -1))
    return steps[: plan.chips // 2], steps[plan.chips // 2 :]


def step_order(plan):
    far, near = far_near(plan)
    middle = len(far) // 2
    return far[:middle] + near + far[middle:] + [0]


def half(plan, block, core):
    return jnp.where(
        core == 0, block[: plan.half_rows], block[plan.lead : plan.lead + plan.half_rows]
    )


def edge_start(plan, tile, side):
    left, right = plan.cols * tile - plan.halo, plan.cols * (tile + 1)
    if plan.sides == 1:
        return jnp.where(tile > 0, left, right)
    return (left, right)[side]


def edge_select(plan, tile, row, position, index):
    hit = None
    for side in range(plan.sides):
        first = index * plan.edges + side * plan.halo
        inside = (row >= first) & (row < first + plan.halo)
        one = inside & (position == row - first + edge_start(plan, tile, side))
        hit = one if hit is None else hit | one
    return hit


def across(a, b):
    return lax.dot_general(a, b, (((1,), (1,)), ((), ())), preferred_element_type=F32)


def dot(a, b):
    return jnp.dot(a, b, preferred_element_type=F32)


def mirror_pack(plan, maps_ref, out_ref, sums_ref, edge_ref):
    me = lax.axis_index("tile")
    count, cols, width, tiles = plan.maps, plan.cols, plan.width, plan.tiles
    head, edge = plan.map_rows, plan.edge_rows

    def pick(rows, span, base, tile, index):
        row = lax.broadcasted_iota(jnp.int32, (rows, span), 0)
        position = lax.broadcasted_iota(jnp.int32, (rows, span), 1) + base
        return edge_select(plan, tile, row, position, index).astype(F32)

    def total(span, index):
        return (lax.broadcasted_iota(jnp.int32, (head, span), 0) == index).astype(F32)

    for shift in range(1, tiles):
        dest = lax.rem(me + shift, tiles)
        by_col = by_row = None
        for index in range(count):
            block = maps_ref[index]
            out_ref[shift - 1, index * cols : (index + 1) * cols, :] = maps_ref[
                index, pl.ds(pl.multiple_of(dest * cols, cols), cols), :
            ]
            left = [pick(edge, cols, me * cols, dest, index)]
            upper = [pick(edge, width, 0, dest, index)]
            if shift == 1:
                left.append(total(cols, index))
                upper.append(total(width, index))
                upper.append(pick(edge, width, 0, me, index))
            by_c = across(jnp.concatenate(left, axis=0).astype(BF16), block)
            by_r = dot(jnp.concatenate(upper, axis=0).astype(BF16), block)
            by_col = by_c if by_col is None else by_col + by_c
            by_row = by_r if by_row is None else by_row + by_r
        if shift == 1:
            sums_ref[...] = by_col[edge : edge + head]
            own = pl.ds(pl.multiple_of(me * cols, cols), cols)
            sums_ref[:, own] = sums_ref[:, own] + by_row[edge : edge + head]
            edge_ref[...] = by_row[edge + head :]
            sums = sums_ref[...]
            high = sums.astype(BF16).astype(F32)
            middle = (sums - high).astype(BF16).astype(F32)
            low = sums - high - middle
        pieces = [by_row[:edge]]
        for wide in (by_col[:edge], high, middle, low):
            pieces += [wide[:, k * cols : (k + 1) * cols] for k in range(tiles)]
        used = (1 + tiles) * edge + 3 * tiles * head
        if plan.tail_rows > used:
            pieces.append(jnp.zeros((plan.tail_rows - used, cols), F32))
        out_ref[shift - 1, count * cols :, :] = jnp.concatenate(pieces, axis=0).astype(BF16)


def correct_pack(plan, maps_ref, recv_ref, sums_ref, edge_ref, *refs):
    *out_refs, field_ref, turned_ref = refs
    me, chip = lax.axis_index("tile"), lax.axis_index("head") // 2
    count, cols, width, tiles = plan.maps, plan.cols, plan.width, plan.tiles
    head, edge, halo = plan.map_rows, plan.edge_rows, plan.halo
    tails = [recv_ref[k, count * cols :, :].astype(F32) for k in range(tiles - 1)]

    rowsum = []
    for b in range(tiles):
        value = sums_ref[:, b * cols : (b + 1) * cols]
        for tail in tails:
            base = (1 + tiles) * edge
            parts = [
                tail[base + (k * tiles + b) * head : base + (k * tiles + b + 1) * head]
                for k in range(3)
            ]
            value = value + ((parts[0] + parts[1]) + parts[2])
        rowsum.append(value)
    grand = sum(jnp.sum(value, axis=1, keepdims=True) for value in rowsum)
    grand = jnp.where(lax.broadcasted_iota(jnp.int32, (head, 1), 0) < count, grand, 1.0)
    scaled = [value / grand for value in rowsum]
    for b in range(tiles):
        square = jnp.concatenate([rowsum[b], jnp.zeros((LANES - head, cols), F32)], axis=0)
        turned_ref[b * cols : (b + 1) * cols, :] = square.T
    mine = scaled[0]
    for b in range(1, tiles):
        mine = jnp.where(me == b, scaled[b], mine)

    eye = (
        lax.broadcasted_iota(jnp.int32, (cols, cols), 0)
        == lax.broadcasted_iota(jnp.int32, (cols, cols), 1)
    ).astype(F32).astype(BF16)
    margin = 8 + halo
    mirrors = []
    for b in range(tiles):
        shift = lax.rem(b - me + tiles, tiles)
        other = recv_ref[jnp.maximum(shift - 1, 0), : count * cols, :]
        own = [maps_ref[k, b * cols : (b + 1) * cols, :] for k in range(count)]
        mirrors.append(across(eye, jnp.where(shift == 0, jnp.concatenate(own, axis=0), other)))
    for index in range(count):
        origin = index * plan.pitch
        field_ref[origin : origin + margin, :] = jnp.zeros((margin, cols), F32)
        field_ref[origin + margin + width : origin + plan.pitch, :] = jnp.zeros(
            (plan.pitch - margin - width, cols), F32
        )
        for b in range(tiles):
            own = maps_ref[index, b * cols : (b + 1) * cols, :]
            mirror = mirrors[b][:, index * cols : (index + 1) * cols]
            column = turned_ref[b * cols : (b + 1) * cols, index : index + 1]
            field_ref[origin + margin + b * cols : origin + margin + (b + 1) * cols, :] = (
                own.astype(F32) + mirror - column * mine[index : index + 1]
            )

    strips = []
    for b in range(tiles):
        strip = edge_ref[...]
        for k, tail in enumerate(tails):
            strip = jnp.where(lax.rem(me + k + 1, tiles) == b, tail[:edge], strip)
        for tail in tails:
            strip = strip + tail[(1 + b) * edge : (2 + b) * edge]
        strips.append(strip)
    strip = jnp.concatenate(strips, axis=1)
    wide = jnp.concatenate(scaled, axis=1)
    before = pl.multiple_of(jnp.maximum(me * cols - 8, 0), 8)
    after = pl.multiple_of(jnp.minimum((me + 1) * cols, width - 8), 8)
    left = turned_ref[pl.ds(before, 8), :][8 - halo :]
    right = turned_ref[pl.ds(after, 8), :][:halo]
    if plan.sides == 1:
        beside = jnp.where(me > 0, left, right)
    else:
        beside = jnp.concatenate([left, right], axis=0)
    lines = [
        strip[k * plan.edges : (k + 1) * plan.edges] - beside[:, k : k + 1] * wide[k : k + 1]
        for k in range(count)
    ]
    rows, slots = plan.rows, plan.slots
    stacks = []
    for slot in range(slots):
        members = []
        for group in range(plan.groups):
            k = group * slots + slot
            members.append(lines[k] if k < count else jnp.zeros((plan.edges, width), F32))
        stacks.append(jnp.concatenate(members, axis=0))
    lane = lax.broadcasted_iota(jnp.int32, (plan.side_rows, cols), 1)
    spare = plan.block_rows - plan.lead - plan.half_rows
    for step, out_ref in zip(step_order(plan), out_refs):
        first = partner(chip, step, plan.chips) * 2 * plan.band

        def section(begin, size):
            found = [
                field_ref[pl.ds(8 * k * plan.pitch + first + 8 + begin + r, 8, stride=plan.pitch), :]
                for r in range(size)
                for k in range(plan.sets)
            ]
            for k in range(8 * plan.sets, count):
                found.append(field_ref[pl.ds(k * plan.pitch + first + 8 + begin, size), :])
            return found

        lone, shared = 8 * plan.lone, 8 * plan.shared
        sides = []
        for core in range(2):
            side = jnp.zeros((plan.side_rows, cols), F32)
            for slot in range(slots):
                amount = lax.rem(slot * rows + halo + width - core * plan.band - first, width)
                moved = pltpu.roll(stacks[slot], amount, 1)[:, :cols]
                side = jnp.where((lane >= slot * rows) & (lane < (slot + 1) * rows), moved, side)
            sides.append(side)
        pieces = section(0, lone) + sides[:1] + section(lone, shared)
        pieces += section(lone + shared, lone) + sides[1:]
        if spare:
            pieces.append(jnp.zeros((spare, cols), F32))
        out_ref[...] = jnp.concatenate(pieces, axis=0).astype(BF16)


def core_pack(plan, *refs):
    *block_refs, out_ref = refs
    other = 1 - lax.axis_index("head") % 2
    for k, block_ref in enumerate(block_refs):
        out_ref[k] = half(plan, block_ref[...].astype(F32), other).astype(BF16)


def weight_pack(blocks_ref, proj_ref, set_ref, slot_ref, out_ref, map_ref, side_ref):
    map_ref[...] = dot(proj_ref[...], set_ref[...]).astype(BF16)
    side_ref[...] = dot(proj_ref[...], slot_ref[...]).astype(BF16)
    layers, convs, height, breadth = blocks_ref.shape[:4]
    for b in range(layers):
        for m in range(convs):
            out_ref[b * convs + m] = jnp.concatenate(
                [
                    jnp.concatenate(
                        [blocks_ref[b, m, dy, dx].astype(F32) for dy in range(height)], axis=1
                    )
                    for dx in range(breadth)
                ],
                axis=0,
            ).astype(BF16)


def lanes(base, size):
    return pl.ds(base if isinstance(base, int) else pl.multiple_of(base, LANES), size)


def shifted(ref, rows, base, offset, size):
    low = offset // LANES * LANES
    rest = offset - low
    if rest == 0:
        return ref[rows, lanes(base + low, size)]
    return pltpu.roll(ref[rows, lanes(base + low, size + LANES)], size + LANES - rest, 1)[:, :size]


def stack(plan, order, *refs):
    chips = plan.chips
    own_refs, swap_refs = refs[:chips], refs[chips : chips + len(order)]
    refs = refs[chips + len(order) :]
    proj_ref, side_ref, kernel_ref, vector_ref, mask_ref, spots_ref, out_ref = refs[:7]
    maps_ref, others_ref, sides_ref, stream_ref, hidden_ref, taps_ref, logit_ref = refs[7:]
    count, cols, rows, halo = plan.maps, plan.cols, plan.rows, plan.halo
    heads, feat, stride = plan.heads, plan.feat, plan.stride
    head = lax.axis_index("head")
    chip, core = head // 2, head % 2
    lone, shared = 8 * plan.lone, 8 * plan.shared
    wide = 8 * plan.sets

    def rows_of(sections):
        sets, others = [], []
        for begin, size in sections:
            sets += [begin + r * wide for r in range(size)]
            others += [begin + size * wide + r for r in range(0, size, 8)]
        return sets, others, [size for _, size in sections for _ in range(0, size, 8)]

    early = rows_of([(0, lone), (plan.lead, shared)])
    late = rows_of([(0, shared), (shared * count, lone)])

    def spread(block, source):
        def pick(a, b, size):
            if a == b:
                return block[a : a + size]
            return jnp.where(core == 0, block[a : a + size], block[b : b + size])

        for r, (a, b) in enumerate(zip(early[0], late[0])):
            place = pl.multiple_of(source * wide, 8) + r * heads * wide
            maps_ref[pl.ds(pl.multiple_of(place, 8), wide), :] = pick(a, b, wide)
        for k, (a, b, m, n) in enumerate(zip(early[1], late[1], early[2], late[2])):
            for j in range(plan.rest):
                place = (source * plan.rest + j) * rows + 8 * k
                others_ref[pl.ds(pl.multiple_of(place, 8), 8), :] = pick(a + j * m, b + j * n, 8)
        side = pick(lone * count, plan.half_rows - plan.side_rows, plan.side_rows)
        place = pl.multiple_of(source * plan.side_rows, 8)
        sides_ref[pl.ds(place, plan.side_rows), :] = side

    for steps, swap_ref in zip(order, swap_refs):
        for k, step in enumerate(steps):
            source = 2 * partner(chip, step, chips, back=True)
            spread(half(plan, own_refs[step_order(plan).index(step)][...].astype(F32), core), source + core)
            spread(swap_ref[k].astype(F32), source + 1 - core)
    bias = vector_ref[:, 0:1]

    slots, members = plan.slots, heads * plan.groups
    lane = lax.broadcasted_iota(jnp.int32, (members, cols), 1)
    placed = []
    for first in range(0, plan.edges, slots):
        parts = [jnp.zeros((members, cols), F32) for _ in range(slots)]
        for at in range(min(slots, plan.edges - first)):
            value = sides_ref[pl.ds(first + at, members, stride=plan.edges), :]
            keep = (lane >= at * rows) & (lane < (at + 1) * rows)
            for slot in range(slots):
                moved = value
                if at != slot:
                    moved = pltpu.roll(value, ((at - slot) * rows) % cols, 1)
                parts[slot] = jnp.where(keep, moved, parts[slot])
        stacked = jnp.concatenate(parts, axis=0).astype(BF16)
        placed.append((dot(side_ref[...], stacked) + bias).astype(BF16))

    edge = sum(dot(columns, spots_ref[k]) for k, columns in enumerate(placed))

    weight = proj_ref[...]
    spot = lax.broadcasted_iota(jnp.int32, (feat, LANES), 1)
    spans = []

    def compose(tile):
        low, value = tile * LANES, None
        for begin, size, source, lead in spans:
            left, right = max(begin, low), min(begin + size, low + LANES)
            if left >= right:
                continue
            k = (lead + low) // LANES
            piece = source[:, k * LANES : (k + 1) * LANES]
            if value is None:
                value = piece
            else:
                value = jnp.where((spot >= left - low) & (spot < right - low), piece, value)
        here = slice(low, low + LANES)
        stream_ref[:, here] = jnp.where(mask_ref[:, here] > 0, value, 0.0).astype(BF16)

    def gather(chosen):
        blocks = []
        for r in chosen:
            block = maps_ref[r * heads * wide : (r + 1) * heads * wide, :]
            if plan.rest:
                others = others_ref[pl.ds(r, heads * plan.rest, stride=rows), :]
                block = jnp.concatenate([block, others], axis=0)
            blocks.append(block.astype(BF16))
        return jnp.concatenate(blocks, axis=1)

    done = plan.start // LANES
    for r in range(rows + 1):
        begin = plan.start + r * stride - halo
        between = LANES + r * 2 * halo - halo
        spans.append((begin, 2 * halo, edge, between - begin))
        if r < rows:
            if r % plan.batch == 0:
                batch = dot(weight, gather(range(r, min(r + plan.batch, rows)))) + bias
            value = batch[:, r % plan.batch * cols : (r % plan.batch + 1) * cols]
            begin = plan.start + r * stride + halo
            turn = begin % LANES
            value = jnp.concatenate([value, jnp.zeros((feat, LANES), F32)], axis=1)
            spans.append((begin, cols, pltpu.roll(value, turn, 1), turn - begin))
        full = (plan.start + (r + 1) * stride - halo) // LANES if r < rows else done + 1
        while done < full:
            compose(done)
            done += 1
        spans = [span for span in spans if span[0] + span[1] > done * LANES]

    everything = slice(None)
    for n in range(plan.convs):
        source = hidden_ref if n % 2 else stream_ref
        low = (plan.start + (n + 1) * stride) // LANES * LANES
        span = plan.start + (rows - n - 1) * stride - n - 1 - low
        steps = -(-span // plan.chunk)
        size = up(-(-span // steps), LANES)
        offsets = vector_ref[:, n + 1 : n + 2]

        def multiply(base, size):
            window = jnp.concatenate(
                [shifted(source, everything, base, d * stride, size) for d in (-1, 0, 1)], axis=0
            )
            taps_ref[:, lanes(base, size)] = dot(kernel_ref[n], window)

        def finish(base):
            here = lanes(base, size)
            value = taps_ref[feat : 2 * feat, here]
            value = value + shifted(taps_ref, slice(0, feat), base, -1, size)
            value = value + shifted(taps_ref, slice(2 * feat, 3 * feat), base, 1, size)
            value = value + offsets
            keep = mask_ref[:, here] > 0
            if n % 2 == 0:
                value = jnp.where(value > 0, value, jnp.exp(jnp.minimum(value, 0.0)) - 1.0)
                hidden_ref[:, here] = jnp.where(keep, value, 0.0).astype(BF16)
                return
            value = (stream_ref[:, here].astype(F32) + value).astype(BF16)
            if n < plan.convs - 1:
                stream_ref[:, here] = jnp.where(keep, value.astype(F32), 0.0).astype(BF16)
                return
            readout = vector_ref[:, plan.convs + 1 : plan.convs + 2]
            logit_ref[0:1, here] = jnp.sum(value.astype(F32) * readout, axis=0, keepdims=True)

        multiply(low, size + LANES)
        for i in range(steps):
            if i + 1 < steps:
                multiply(low + (i + 1) * size + LANES, size)
            finish(low + i * size)

    for r in range(plan.band):
        begin = plan.start + (r + halo) * stride + halo
        low = begin // LANES * LANES
        out_ref[r : r + 1, :] = shifted(logit_ref, slice(0, 1), low, begin - low, cols)


def call(kernel, name, args, outs, scratch=(), held_out=True):
    held = sum(math.prod(x.shape) * jnp.dtype(x.dtype).itemsize for x in [*args, *outs, *scratch])
    vmem = pl.BlockSpec(memory_space=pltpu.VMEM)
    return pl.pallas_call(
        kernel,
        out_shape=[pltpu.VMEM(x.shape, x.dtype) if held_out else x for x in outs],
        in_specs=[vmem] * len(args),
        out_specs=[vmem] * len(outs),
        scratch_shapes=list(scratch),
        compiler_params=pltpu.CompilerParams(vmem_limit_bytes=held * 5 // 4 + 4 * 1024 * 1024),
        name=name,
    )(*args)


def array(dtype, *shape):
    return jax.ShapeDtypeStruct(shape, dtype)


def on_device(attention, proj_weight, proj_bias, conv_weight, conv_bias, out_weight):
    maps, width, cols = attention.shape
    feat = proj_weight.shape[0]
    blocks, convs = conv_weight.shape[:2]
    tiles, heads = lax.axis_size("tile"), lax.axis_size("head")
    plan = Plan(maps, width, cols, tiles, heads, feat, blocks * convs)
    me, band_index = lax.axis_index("tile"), lax.axis_index("head")

    payload, sums, edge = call(
        functools.partial(mirror_pack, plan),
        "mirror_pack",
        [attention],
        [
            array(BF16, tiles - 1, maps * cols + plan.tail_rows, cols),
            array(F32, plan.map_rows, width),
            array(F32, plan.edge_rows, cols),
        ],
    )
    received = jnp.stack(
        [
            lax.ppermute(payload[s - 1], "tile", [(i, (i + s) % tiles) for i in range(tiles)])
            for s in range(tiles - 1, 0, -1)
        ]
    )

    stride, start = plan.stride, plan.start
    source, index = np.divmod(np.arange(heads * maps), maps)
    wide = 8 * plan.sets
    by_set = np.where(
        index < wide, source * wide + index, heads * wide + source * plan.rest + index - wide
    )
    group, slot = np.divmod(index, plan.slots)
    by_slot = (slot * heads + source) * plan.groups + group
    picks = [
        jnp.asarray(place[:, None] == np.arange(size)[None], BF16)
        for place, size in (
            (by_set, heads * maps),
            (by_slot, plan.slots * heads * plan.groups),
        )
    ]
    kernels, map_weight, side_weight = call(
        weight_pack,
        "weight_pack",
        [conv_weight.transpose(0, 1, 4, 5, 2, 3), proj_weight, *picks],
        [
            array(BF16, plan.convs, 3 * feat, 3 * feat),
            array(BF16, feat, picks[0].shape[1]),
            array(BF16, feat, picks[1].shape[1]),
        ],
    )
    vectors = jnp.concatenate(
        [proj_bias[None], conv_bias.reshape(-1, feat), out_weight[None]], axis=0
    ).T
    spot = np.arange(plan.lanes) - start
    row = band_index * plan.band - plan.halo + (spot // stride).astype(np.int32)
    col = me * cols - plan.halo + (spot % stride).astype(np.int32)
    mask = (row >= 0) & (row < width) & (col >= 0) & (col < width)
    mask = mask.astype(F32)[None]

    key = np.arange(cols)
    member, line = key // plan.rows, key % plan.rows
    lane = np.arange(up(LANES + (plan.rows + 1) * 2 * plan.halo, LANES))
    spots = []
    for first in range(0, plan.edges, plan.slots):
        column = first + member
        fits = (member < plan.slots) & (column < plan.edges)
        left = LANES + line * 2 * plan.halo + column
        right = left + plan.halo
        if plan.sides == 1:
            places = [left, right]
        else:
            places = [np.where(column < plan.halo, left, right - plan.halo)]
        hit = [np.where(fits, place, -1)[:, None] == lane[None] for place in places]
        spots.append(functools.reduce(np.logical_or, hit))
    spots = jnp.asarray(np.stack(spots), BF16)

    chips = plan.chips
    blocks = call(
        functools.partial(correct_pack, plan),
        "correct_pack",
        [attention, received, sums, edge],
        [array(BF16, plan.block_rows, cols)] * chips,
        [pltpu.VMEM((maps * plan.pitch, cols), F32), pltpu.VMEM((width, LANES), F32)],
    )
    arrived = {}
    for step, block in zip(step_order(plan), blocks):
        pairs = [(i, 2 * partner(i // 2, step, chips) + i % 2) for i in range(heads)]
        arrived[step] = lax.ppermute(block, "head", pairs) if step else block
    steps = step_order(plan)
    early = steps[: chips // 2]
    late = [step for step in steps if step not in early]
    order = [early, late]
    weights = (map_weight, side_weight, kernels, vectors, mask, spots)
    swapped = []
    for steps in order:
        (packed,) = call(
            functools.partial(core_pack, plan),
            "core_pack",
            [arrived[k] for k in steps],
            [array(BF16, len(steps), plan.half_rows, cols)],
        )
        if steps is late:
            packed, weights = lax.optimization_barrier((packed, weights))
        swapped.append(lax.ppermute(packed, "head", [(i, i ^ 1) for i in range(heads)]))

    (logits,) = call(
        functools.partial(stack, plan, order),
        "stack",
        [*arrived.values(), *swapped, *weights],
        [array(F32, plan.band, cols)],
        [
            pltpu.VMEM((heads * 8 * plan.sets * plan.rows, cols), F32),
            pltpu.VMEM((heads * max(plan.rest, 1) * plan.rows, cols), F32),
            pltpu.VMEM((heads * plan.side_rows, cols), F32),
            pltpu.VMEM((feat, plan.lanes), BF16),
            pltpu.VMEM((feat, plan.lanes), BF16),
            pltpu.VMEM((3 * feat, plan.lanes), F32),
            pltpu.VMEM((8, plan.lanes), F32),
        ],
        held_out=False,
    )
    return logits


def solution(mesh):
    return jax.shard_map(
        on_device,
        mesh=mesh,
        in_specs=(P(("grp", "head"), None, "tile"), P(), P(), P(), P(), P()),
        out_specs=P(("grp", "head"), "tile"),
        check_vma=False,
    )
```

```python
import functools
import math
from typing import NamedTuple

import jax
import jax.numpy as jnp
import numpy as np
from jax import lax
from jax.experimental import pallas as pl
from jax.experimental.pallas import tpu as pltpu
from jax.sharding import PartitionSpec as P

BF16, F32 = jnp.bfloat16, jnp.float32
LANES = 128


def up(value, step):
    return -(-value // step) * step


class Plan(NamedTuple):
    maps: int
    width: int
    cols: int
    tiles: int
    heads: int
    feat: int
    convs: int

    @property
    def halo(self):
        return self.convs

    @property
    def sides(self):
        return min(2, self.tiles - 1)

    @property
    def edges(self):
        return self.sides * self.halo

    @property
    def edge_rows(self):
        return up(self.maps * self.edges, 8)

    @property
    def map_rows(self):
        return up(self.maps, 16)

    @property
    def tail_rows(self):
        return up((1 + self.tiles) * self.edge_rows + 3 * self.tiles * self.map_rows, 16)

    @property
    def band(self):
        return self.width // self.heads

    @property
    def rows(self):
        return self.band + 2 * self.halo

    @property
    def slots(self):
        return self.cols // self.rows

    @property
    def groups(self):
        return -(-self.maps // self.slots)

    @property
    def side_rows(self):
        return self.groups * self.edges

    @property
    def sets(self):
        return self.maps // 8

    @property
    def rest(self):
        return self.maps % 8

    @property
    def pitch(self):
        return up(self.width + 24, 2) + 1

    @property
    def chips(self):
        return self.heads // 2

    @property
    def lone(self):
        return self.band // 8

    @property
    def shared(self):
        return 2 * self.halo // 8

    @property
    def group_rows(self):
        return 8 * self.maps

    @property
    def lead(self):
        return self.lone * self.group_rows + self.side_rows

    @property
    def half_rows(self):
        return self.lead + self.shared * self.group_rows

    @property
    def block_rows(self):
        return self.lead + self.half_rows

    @property
    def stride(self):
        return self.cols + 2 * self.halo

    @property
    def start(self):
        return up(self.stride, LANES) - LANES

    @property
    def batch(self):
        return 8

    @property
    def chunk(self):
        return 1536

    @property
    def lanes(self):
        return up(self.start + self.rows * self.stride, LANES) + 4 * self.halo * LANES


def partner(mine, step, count, back=False):
    if count & (count - 1) == 0:
        return mine ^ step
    return (mine - step if back else mine + step) % count


def far_near(plan):
    steps = list(range(plan.chips - 1, 0, -1))
    return steps[: plan.chips // 2], steps[plan.chips // 2 :]


def step_order(plan):
    far, near = far_near(plan)
    middle = len(far) // 2
    return far[:middle] + near + far[middle:] + [0]


def half(plan, block, core):
    return jnp.where(
        core == 0, block[: plan.half_rows], block[plan.lead : plan.lead + plan.half_rows]
    )


def edge_start(plan, tile, side):
    left, right = plan.cols * tile - plan.halo, plan.cols * (tile + 1)
    if plan.sides == 1:
        return jnp.where(tile > 0, left, right)
    return (left, right)[side]


def edge_select(plan, tile, row, position, index):
    hit = None
    for side in range(plan.sides):
        first = index * plan.edges + side * plan.halo
        inside = (row >= first) & (row < first + plan.halo)
        one = inside & (position == row - first + edge_start(plan, tile, side))
        hit = one if hit is None else hit | one
    return hit


def across(a, b):
    return lax.dot_general(a, b, (((1,), (1,)), ((), ())), preferred_element_type=F32)


def dot(a, b):
    return jnp.dot(a, b, preferred_element_type=F32)


def mirror_pack(plan, maps_ref, out_ref, sums_ref, edge_ref):
    me = lax.axis_index("tile")
    count, cols, width, tiles = plan.maps, plan.cols, plan.width, plan.tiles
    head, edge = plan.map_rows, plan.edge_rows

    def pick(rows, span, base, tile, index):
        row = lax.broadcasted_iota(jnp.int32, (rows, span), 0)
        position = lax.broadcasted_iota(jnp.int32, (rows, span), 1) + base
        return edge_select(plan, tile, row, position, index).astype(F32)

    def total(span, index):
        return (lax.broadcasted_iota(jnp.int32, (head, span), 0) == index).astype(F32)

    for shift in range(1, tiles):
        dest = lax.rem(me + shift, tiles)
        by_col = by_row = None
        for index in range(count):
            block = maps_ref[index]
            left = [pick(edge, cols, me * cols, dest, index)]
            upper = [pick(edge, width, 0, dest, index)]
            if shift == 1:
                left.append(total(cols, index))
                upper.append(total(width, index))
                upper.append(pick(edge, width, 0, me, index))
            by_c = across(jnp.concatenate(left, axis=0).astype(BF16), block)
            by_r = dot(jnp.concatenate(upper, axis=0).astype(BF16), block)
            by_col = by_c if by_col is None else by_col + by_c
            by_row = by_r if by_row is None else by_row + by_r
        if shift == 1:
            sums_ref[...] = by_col[edge : edge + head]
            own = pl.ds(pl.multiple_of(me * cols, cols), cols)
            sums_ref[:, own] = sums_ref[:, own] + by_row[edge : edge + head]
            edge_ref[...] = by_row[edge + head :]
            sums = sums_ref[...]
            high = sums.astype(BF16).astype(F32)
            middle = (sums - high).astype(BF16).astype(F32)
            low = sums - high - middle
        pieces = [by_row[:edge]]
        for wide in (by_col[:edge], high, middle, low):
            pieces += [wide[:, k * cols : (k + 1) * cols] for k in range(tiles)]
        used = (1 + tiles) * edge + 3 * tiles * head
        if plan.tail_rows > used:
            pieces.append(jnp.zeros((plan.tail_rows - used, cols), F32))
        out_ref[shift - 1] = jnp.concatenate(pieces, axis=0).astype(BF16)


def correct_pack(plan, maps_ref, recv_ref, tail_ref, sums_ref, edge_ref, *refs):
    *out_refs, field_ref, turned_ref = refs
    me, chip = lax.axis_index("tile"), lax.axis_index("head") // 2
    count, cols, width, tiles = plan.maps, plan.cols, plan.width, plan.tiles
    head, edge, halo = plan.map_rows, plan.edge_rows, plan.halo
    tails = [tail_ref[k].astype(F32) for k in range(tiles - 1)]

    rowsum = []
    for b in range(tiles):
        value = sums_ref[:, b * cols : (b + 1) * cols]
        for tail in tails:
            base = (1 + tiles) * edge
            parts = [
                tail[base + (k * tiles + b) * head : base + (k * tiles + b + 1) * head]
                for k in range(3)
            ]
            value = value + ((parts[0] + parts[1]) + parts[2])
        rowsum.append(value)
    grand = sum(jnp.sum(value, axis=1, keepdims=True) for value in rowsum)
    grand = jnp.where(lax.broadcasted_iota(jnp.int32, (head, 1), 0) < count, grand, 1.0)
    scaled = [value / grand for value in rowsum]
    for b in range(tiles):
        square = jnp.concatenate([rowsum[b], jnp.zeros((LANES - head, cols), F32)], axis=0)
        turned_ref[b * cols : (b + 1) * cols, :] = square.T
    mine = scaled[0]
    for b in range(1, tiles):
        mine = jnp.where(me == b, scaled[b], mine)

    eye = (
        lax.broadcasted_iota(jnp.int32, (cols, cols), 0)
        == lax.broadcasted_iota(jnp.int32, (cols, cols), 1)
    ).astype(F32).astype(BF16)
    margin = 8 + halo
    mirrors = []
    for b in range(tiles):
        shift = lax.rem(b - me + tiles, tiles)
        other = recv_ref[jnp.maximum(shift - 1, 0)]
        own = [maps_ref[k, b * cols : (b + 1) * cols, :] for k in range(count)]
        mirrors.append(across(eye, jnp.where(shift == 0, jnp.concatenate(own, axis=0), other)))
    for index in range(count):
        origin = index * plan.pitch
        field_ref[origin : origin + margin, :] = jnp.zeros((margin, cols), F32)
        field_ref[origin + margin + width : origin + plan.pitch, :] = jnp.zeros(
            (plan.pitch - margin - width, cols), F32
        )
        for b in range(tiles):
            own = maps_ref[index, b * cols : (b + 1) * cols, :]
            mirror = mirrors[b][:, index * cols : (index + 1) * cols]
            column = turned_ref[b * cols : (b + 1) * cols, index : index + 1]
            field_ref[origin + margin + b * cols : origin + margin + (b + 1) * cols, :] = (
                own.astype(F32) + mirror - column * mine[index : index + 1]
            )

    strips = []
    for b in range(tiles):
        strip = edge_ref[...]
        for k, tail in enumerate(tails):
            strip = jnp.where(lax.rem(me + k + 1, tiles) == b, tail[:edge], strip)
        for tail in tails:
            strip = strip + tail[(1 + b) * edge : (2 + b) * edge]
        strips.append(strip)
    strip = jnp.concatenate(strips, axis=1)
    wide = jnp.concatenate(scaled, axis=1)
    before = pl.multiple_of(jnp.maximum(me * cols - 8, 0), 8)
    after = pl.multiple_of(jnp.minimum((me + 1) * cols, width - 8), 8)
    left = turned_ref[pl.ds(before, 8), :][8 - halo :]
    right = turned_ref[pl.ds(after, 8), :][:halo]
    if plan.sides == 1:
        beside = jnp.where(me > 0, left, right)
    else:
        beside = jnp.concatenate([left, right], axis=0)
    lines = [
        strip[k * plan.edges : (k + 1) * plan.edges] - beside[:, k : k + 1] * wide[k : k + 1]
        for k in range(count)
    ]
    rows, slots = plan.rows, plan.slots
    stacks = []
    for slot in range(slots):
        members = []
        for group in range(plan.groups):
            k = group * slots + slot
            members.append(lines[k] if k < count else jnp.zeros((plan.edges, width), F32))
        stacks.append(jnp.concatenate(members, axis=0))
    lane = lax.broadcasted_iota(jnp.int32, (plan.side_rows, cols), 1)
    spare = plan.block_rows - plan.lead - plan.half_rows
    for step, out_ref in zip(step_order(plan), out_refs):
        first = partner(chip, step, plan.chips) * 2 * plan.band

        def section(begin, size):
            found = [
                field_ref[pl.ds(8 * k * plan.pitch + first + 8 + begin + r, 8, stride=plan.pitch), :]
                for r in range(size)
                for k in range(plan.sets)
            ]
            for k in range(8 * plan.sets, count):
                found.append(field_ref[pl.ds(k * plan.pitch + first + 8 + begin, size), :])
            return found

        lone, shared = 8 * plan.lone, 8 * plan.shared
        sides = []
        for core in range(2):
            side = jnp.zeros((plan.side_rows, cols), F32)
            for slot in range(slots):
                amount = lax.rem(slot * rows + halo + width - core * plan.band - first, width)
                moved = pltpu.roll(stacks[slot], amount, 1)[:, :cols]
                side = jnp.where((lane >= slot * rows) & (lane < (slot + 1) * rows), moved, side)
            sides.append(side)
        pieces = section(0, lone) + sides[:1] + section(lone, shared)
        pieces += section(lone + shared, lone) + sides[1:]
        if spare:
            pieces.append(jnp.zeros((spare, cols), F32))
        out_ref[...] = jnp.concatenate(pieces, axis=0).astype(BF16)


def core_pack(plan, *refs):
    *block_refs, out_ref = refs
    other = 1 - lax.axis_index("head") % 2
    for k, block_ref in enumerate(block_refs):
        out_ref[k] = half(plan, block_ref[...].astype(F32), other).astype(BF16)


def weight_pack(blocks_ref, proj_ref, set_ref, slot_ref, out_ref, map_ref, side_ref):
    map_ref[...] = dot(proj_ref[...], set_ref[...]).astype(BF16)
    side_ref[...] = dot(proj_ref[...], slot_ref[...]).astype(BF16)
    layers, convs, height, breadth = blocks_ref.shape[:4]
    for b in range(layers):
        for m in range(convs):
            out_ref[b * convs + m] = jnp.concatenate(
                [
                    jnp.concatenate(
                        [blocks_ref[b, m, dy, dx].astype(F32) for dy in range(height)], axis=1
                    )
                    for dx in range(breadth)
                ],
                axis=0,
            ).astype(BF16)


def lanes(base, size):
    return pl.ds(base if isinstance(base, int) else pl.multiple_of(base, LANES), size)


def shifted(ref, rows, base, offset, size):
    low = offset // LANES * LANES
    rest = offset - low
    if rest == 0:
        return ref[rows, lanes(base + low, size)]
    return pltpu.roll(ref[rows, lanes(base + low, size + LANES)], size + LANES - rest, 1)[:, :size]


def stack(plan, order, *refs):
    chips = plan.chips
    own_refs, swap_refs = refs[:chips], refs[chips : chips + len(order)]
    refs = refs[chips + len(order) :]
    proj_ref, side_ref, kernel_ref, vector_ref, mask_ref, spots_ref, out_ref = refs[:7]
    maps_ref, others_ref, sides_ref, stream_ref, hidden_ref, taps_ref, logit_ref = refs[7:]
    count, cols, rows, halo = plan.maps, plan.cols, plan.rows, plan.halo
    heads, feat, stride = plan.heads, plan.feat, plan.stride
    head = lax.axis_index("head")
    chip, core = head // 2, head % 2
    lone, shared = 8 * plan.lone, 8 * plan.shared
    wide = 8 * plan.sets

    def rows_of(sections):
        sets, others = [], []
        for begin, size in sections:
            sets += [begin + r * wide for r in range(size)]
            others += [begin + size * wide + r for r in range(0, size, 8)]
        return sets, others, [size for _, size in sections for _ in range(0, size, 8)]

    early = rows_of([(0, lone), (plan.lead, shared)])
    late = rows_of([(0, shared), (shared * count, lone)])

    def spread(block, source):
        def pick(a, b, size):
            if a == b:
                return block[a : a + size]
            return jnp.where(core == 0, block[a : a + size], block[b : b + size])

        for r, (a, b) in enumerate(zip(early[0], late[0])):
            place = pl.multiple_of(source * wide, 8) + r * heads * wide
            maps_ref[pl.ds(pl.multiple_of(place, 8), wide), :] = pick(a, b, wide)
        for k, (a, b, m, n) in enumerate(zip(early[1], late[1], early[2], late[2])):
            for j in range(plan.rest):
                place = (source * plan.rest + j) * rows + 8 * k
                others_ref[pl.ds(pl.multiple_of(place, 8), 8), :] = pick(a + j * m, b + j * n, 8)
        side = pick(lone * count, plan.half_rows - plan.side_rows, plan.side_rows)
        place = pl.multiple_of(source * plan.side_rows, 8)
        sides_ref[pl.ds(place, plan.side_rows), :] = side

    for steps, swap_ref in zip(order, swap_refs):
        for k, step in enumerate(steps):
            source = 2 * partner(chip, step, chips, back=True)
            spread(half(plan, own_refs[step_order(plan).index(step)][...].astype(F32), core), source + core)
            spread(swap_ref[k].astype(F32), source + 1 - core)
    bias = vector_ref[:, 0:1]

    slots, members = plan.slots, heads * plan.groups
    lane = lax.broadcasted_iota(jnp.int32, (members, cols), 1)
    placed = []
    for first in range(0, plan.edges, slots):
        parts = [jnp.zeros((members, cols), F32) for _ in range(slots)]
        for at in range(min(slots, plan.edges - first)):
            value = sides_ref[pl.ds(first + at, members, stride=plan.edges), :]
            keep = (lane >= at * rows) & (lane < (at + 1) * rows)
            for slot in range(slots):
                moved = value
                if at != slot:
                    moved = pltpu.roll(value, ((at - slot) * rows) % cols, 1)
                parts[slot] = jnp.where(keep, moved, parts[slot])
        stacked = jnp.concatenate(parts, axis=0).astype(BF16)
        placed.append((dot(side_ref[...], stacked) + bias).astype(BF16))

    edge = sum(dot(columns, spots_ref[k]) for k, columns in enumerate(placed))

    weight = proj_ref[...]
    spot = lax.broadcasted_iota(jnp.int32, (feat, LANES), 1)
    spans = []

    def compose(tile):
        low, value = tile * LANES, None
        for begin, size, source, lead in spans:
            left, right = max(begin, low), min(begin + size, low + LANES)
            if left >= right:
                continue
            k = (lead + low) // LANES
            piece = source[:, k * LANES : (k + 1) * LANES]
            if value is None:
                value = piece
            else:
                value = jnp.where((spot >= left - low) & (spot < right - low), piece, value)
        here = slice(low, low + LANES)
        stream_ref[:, here] = jnp.where(mask_ref[:, here] > 0, value, 0.0).astype(BF16)

    def gather(chosen):
        blocks = []
        for r in chosen:
            block = maps_ref[r * heads * wide : (r + 1) * heads * wide, :]
            if plan.rest:
                others = others_ref[pl.ds(r, heads * plan.rest, stride=rows), :]
                block = jnp.concatenate([block, others], axis=0)
            blocks.append(block.astype(BF16))
        return jnp.concatenate(blocks, axis=1)

    done = plan.start // LANES
    for r in range(rows + 1):
        begin = plan.start + r * stride - halo
        between = LANES + r * 2 * halo - halo
        spans.append((begin, 2 * halo, edge, between - begin))
        if r < rows:
            if r % plan.batch == 0:
                batch = dot(weight, gather(range(r, min(r + plan.batch, rows)))) + bias
            value = batch[:, r % plan.batch * cols : (r % plan.batch + 1) * cols]
            begin = plan.start + r * stride + halo
            turn = begin % LANES
            value = jnp.concatenate([value, jnp.zeros((feat, LANES), F32)], axis=1)
            spans.append((begin, cols, pltpu.roll(value, turn, 1), turn - begin))
        full = (plan.start + (r + 1) * stride - halo) // LANES if r < rows else done + 1
        while done < full:
            compose(done)
            done += 1
        spans = [span for span in spans if span[0] + span[1] > done * LANES]

    everything = slice(None)
    for n in range(plan.convs):
        source = hidden_ref if n % 2 else stream_ref
        low = (plan.start + (n + 1) * stride) // LANES * LANES
        span = plan.start + (rows - n - 1) * stride - n - 1 - low
        steps = -(-span // plan.chunk)
        size = up(-(-span // steps), LANES)
        offsets = vector_ref[:, n + 1 : n + 2]

        def multiply(base, size):
            window = jnp.concatenate(
                [shifted(source, everything, base, d * stride, size) for d in (-1, 0, 1)], axis=0
            )
            taps_ref[:, lanes(base, size)] = dot(kernel_ref[n], window)

        def finish(base):
            here = lanes(base, size)
            value = taps_ref[feat : 2 * feat, here]
            value = value + shifted(taps_ref, slice(0, feat), base, -1, size)
            value = value + shifted(taps_ref, slice(2 * feat, 3 * feat), base, 1, size)
            value = value + offsets
            keep = mask_ref[:, here] > 0
            if n % 2 == 0:
                value = jnp.where(value > 0, value, jnp.exp(jnp.minimum(value, 0.0)) - 1.0)
                hidden_ref[:, here] = jnp.where(keep, value, 0.0).astype(BF16)
                return
            value = (stream_ref[:, here].astype(F32) + value).astype(BF16)
            if n < plan.convs - 1:
                stream_ref[:, here] = jnp.where(keep, value.astype(F32), 0.0).astype(BF16)
                return
            readout = vector_ref[:, plan.convs + 1 : plan.convs + 2]
            logit_ref[0:1, here] = jnp.sum(value.astype(F32) * readout, axis=0, keepdims=True)

        multiply(low, size + LANES)
        for i in range(steps):
            if i + 1 < steps:
                multiply(low + (i + 1) * size + LANES, size)
            finish(low + i * size)

    for r in range(plan.band):
        begin = plan.start + (r + halo) * stride + halo
        low = begin // LANES * LANES
        out_ref[r : r + 1, :] = shifted(logit_ref, slice(0, 1), low, begin - low, cols)


def call(kernel, name, args, outs, scratch=(), held_out=True):
    held = sum(math.prod(x.shape) * jnp.dtype(x.dtype).itemsize for x in [*args, *outs, *scratch])
    vmem = pl.BlockSpec(memory_space=pltpu.VMEM)
    return pl.pallas_call(
        kernel,
        out_shape=[pltpu.VMEM(x.shape, x.dtype) if held_out else x for x in outs],
        in_specs=[vmem] * len(args),
        out_specs=[vmem] * len(outs),
        scratch_shapes=list(scratch),
        compiler_params=pltpu.CompilerParams(vmem_limit_bytes=held * 5 // 4 + 4 * 1024 * 1024),
        name=name,
    )(*args)


def array(dtype, *shape):
    return jax.ShapeDtypeStruct(shape, dtype)


def on_device(attention, proj_weight, proj_bias, conv_weight, conv_bias, out_weight):
    maps, width, cols = attention.shape
    feat = proj_weight.shape[0]
    blocks, convs = conv_weight.shape[:2]
    tiles, heads = lax.axis_size("tile"), lax.axis_size("head")
    plan = Plan(maps, width, cols, tiles, heads, feat, blocks * convs)
    me, band_index = lax.axis_index("tile"), lax.axis_index("head")

    tail, sums, edge = call(
        functools.partial(mirror_pack, plan),
        "mirror_pack",
        [attention],
        [
            array(BF16, tiles - 1, plan.tail_rows, cols),
            array(F32, plan.map_rows, width),
            array(F32, plan.edge_rows, cols),
        ],
    )

    def mirror(block):
        return jnp.stack(
            [
                lax.ppermute(block(s), "tile", [(i, (i + s) % tiles) for i in range(tiles)])
                for s in range(tiles - 1, 0, -1)
            ]
        )

    def facing(s):
        block = lax.dynamic_slice_in_dim(attention, (me + s) % tiles * cols, cols, 1)
        return block.reshape(maps * cols, cols)

    received, tails = mirror(facing), mirror(lambda s: tail[s - 1])

    stride, start = plan.stride, plan.start
    source, index = np.divmod(np.arange(heads * maps), maps)
    wide = 8 * plan.sets
    by_set = np.where(
        index < wide, source * wide + index, heads * wide + source * plan.rest + index - wide
    )
    group, slot = np.divmod(index, plan.slots)
    by_slot = (slot * heads + source) * plan.groups + group
    picks = [
        jnp.asarray(place[:, None] == np.arange(size)[None], BF16)
        for place, size in (
            (by_set, heads * maps),
            (by_slot, plan.slots * heads * plan.groups),
        )
    ]
    kernels, map_weight, side_weight = call(
        weight_pack,
        "weight_pack",
        [conv_weight.transpose(0, 1, 4, 5, 2, 3), proj_weight, *picks],
        [
            array(BF16, plan.convs, 3 * feat, 3 * feat),
            array(BF16, feat, picks[0].shape[1]),
            array(BF16, feat, picks[1].shape[1]),
        ],
    )
    vectors = jnp.concatenate(
        [proj_bias[None], conv_bias.reshape(-1, feat), out_weight[None]], axis=0
    ).T
    spot = np.arange(plan.lanes) - start
    row = band_index * plan.band - plan.halo + (spot // stride).astype(np.int32)
    col = me * cols - plan.halo + (spot % stride).astype(np.int32)
    mask = (row >= 0) & (row < width) & (col >= 0) & (col < width)
    mask = mask.astype(F32)[None]

    key = np.arange(cols)
    member, line = key // plan.rows, key % plan.rows
    lane = np.arange(up(LANES + (plan.rows + 1) * 2 * plan.halo, LANES))
    spots = []
    for first in range(0, plan.edges, plan.slots):
        column = first + member
        fits = (member < plan.slots) & (column < plan.edges)
        left = LANES + line * 2 * plan.halo + column
        right = left + plan.halo
        if plan.sides == 1:
            places = [left, right]
        else:
            places = [np.where(column < plan.halo, left, right - plan.halo)]
        hit = [np.where(fits, place, -1)[:, None] == lane[None] for place in places]
        spots.append(functools.reduce(np.logical_or, hit))
    spots = jnp.asarray(np.stack(spots), BF16)

    chips = plan.chips
    blocks = call(
        functools.partial(correct_pack, plan),
        "correct_pack",
        [attention, received, tails, sums, edge],
        [array(BF16, plan.block_rows, cols)] * chips,
        [pltpu.VMEM((maps * plan.pitch, cols), F32), pltpu.VMEM((width, LANES), F32)],
    )
    arrived = {}
    for step, block in zip(step_order(plan), blocks):
        pairs = [(i, 2 * partner(i // 2, step, chips) + i % 2) for i in range(heads)]
        arrived[step] = lax.ppermute(block, "head", pairs) if step else block
    steps = step_order(plan)
    early = steps[: chips // 2]
    late = [step for step in steps if step not in early]
    order = [early, late]
    weights = (map_weight, side_weight, kernels, vectors, mask, spots)
    swapped = []
    for steps in order:
        (packed,) = call(
            functools.partial(core_pack, plan),
            "core_pack",
            [arrived[k] for k in steps],
            [array(BF16, len(steps), plan.half_rows, cols)],
        )
        if steps is late:
            packed, weights = lax.optimization_barrier((packed, weights))
        swapped.append(lax.ppermute(packed, "head", [(i, i ^ 1) for i in range(heads)]))

    (logits,) = call(
        functools.partial(stack, plan, order),
        "stack",
        [*arrived.values(), *swapped, *weights],
        [array(F32, plan.band, cols)],
        [
            pltpu.VMEM((heads * 8 * plan.sets * plan.rows, cols), F32),
            pltpu.VMEM((heads * max(plan.rest, 1) * plan.rows, cols), F32),
            pltpu.VMEM((heads * plan.side_rows, cols), F32),
            pltpu.VMEM((feat, plan.lanes), BF16),
            pltpu.VMEM((feat, plan.lanes), BF16),
            pltpu.VMEM((3 * feat, plan.lanes), F32),
            pltpu.VMEM((8, plan.lanes), F32),
        ],
        held_out=False,
    )
    return logits


def solution(mesh):
    return jax.shard_map(
        on_device,
        mesh=mesh,
        in_specs=(P(("grp", "head"), None, "tile"), P(), P(), P(), P(), P()),
        out_specs=P(("grp", "head"), "tile"),
        check_vma=False,
    )
```

```python
import functools
import math
from typing import NamedTuple

import jax
import jax.numpy as jnp
import numpy as np
from jax import lax
from jax.experimental import pallas as pl
from jax.experimental.pallas import tpu as pltpu
from jax.sharding import PartitionSpec as P

BF16, F32 = jnp.bfloat16, jnp.float32
LANES = 128


def up(value, step):
    return -(-value // step) * step


class Plan(NamedTuple):
    maps: int
    width: int
    cols: int
    tiles: int
    heads: int
    feat: int
    convs: int

    @property
    def halo(self):
        return self.convs

    @property
    def sides(self):
        return min(2, self.tiles - 1)

    @property
    def edges(self):
        return self.sides * self.halo

    @property
    def edge_rows(self):
        return up(self.maps * self.edges, 8)

    @property
    def map_rows(self):
        return up(self.maps, 16)

    @property
    def tail_rows(self):
        return up((1 + self.tiles) * self.edge_rows + 3 * self.tiles * self.map_rows, 16)

    @property
    def band(self):
        return self.width // self.heads

    @property
    def rows(self):
        return self.band + 2 * self.halo

    @property
    def slots(self):
        return self.cols // self.rows

    @property
    def groups(self):
        return -(-self.maps // self.slots)

    @property
    def side_rows(self):
        return self.groups * self.edges

    @property
    def sets(self):
        return self.maps // 8

    @property
    def rest(self):
        return self.maps % 8

    @property
    def pitch(self):
        return up(self.width + 24, 2) + 1

    @property
    def chips(self):
        return self.heads // 2

    @property
    def lone(self):
        return self.band // 8

    @property
    def shared(self):
        return 2 * self.halo // 8

    @property
    def group_rows(self):
        return 8 * self.maps

    @property
    def lead(self):
        return self.lone * self.group_rows + self.side_rows

    @property
    def half_rows(self):
        return self.lead + self.shared * self.group_rows

    @property
    def block_rows(self):
        return self.lead + self.half_rows

    @property
    def stride(self):
        return self.cols + 2 * self.halo

    @property
    def start(self):
        return up(self.stride, LANES) - LANES

    @property
    def batch(self):
        return 8

    @property
    def chunk(self):
        return 1024

    @property
    def lanes(self):
        return up(self.start + self.rows * self.stride, LANES) + 4 * self.halo * LANES


def partner(mine, step, count, back=False):
    if count & (count - 1) == 0:
        return mine ^ step
    return (mine - step if back else mine + step) % count


def far_near(plan):
    steps = list(range(plan.chips - 1, 0, -1))
    return steps[: plan.chips // 2], steps[plan.chips // 2 :]


def step_order(plan):
    far, near = far_near(plan)
    middle = len(far) // 2
    return far[:middle] + near + far[middle:] + [0]


def half(plan, block, core):
    return jnp.where(
        core == 0, block[: plan.half_rows], block[plan.lead : plan.lead + plan.half_rows]
    )


def edge_start(plan, tile, side):
    left, right = plan.cols * tile - plan.halo, plan.cols * (tile + 1)
    if plan.sides == 1:
        return jnp.where(tile > 0, left, right)
    return (left, right)[side]


def edge_select(plan, tile, row, position, index):
    hit = None
    for side in range(plan.sides):
        first = index * plan.edges + side * plan.halo
        inside = (row >= first) & (row < first + plan.halo)
        one = inside & (position == row - first + edge_start(plan, tile, side))
        hit = one if hit is None else hit | one
    return hit


def across(a, b):
    return lax.dot_general(a, b, (((1,), (1,)), ((), ())), preferred_element_type=F32)


def dot(a, b):
    return jnp.dot(a, b, preferred_element_type=F32)


def mirror_pack(plan, maps_ref, out_ref, sums_ref, edge_ref):
    me = lax.axis_index("tile")
    count, cols, width, tiles = plan.maps, plan.cols, plan.width, plan.tiles
    head, edge = plan.map_rows, plan.edge_rows

    def pick(rows, span, base, tile, index):
        row = lax.broadcasted_iota(jnp.int32, (rows, span), 0)
        position = lax.broadcasted_iota(jnp.int32, (rows, span), 1) + base
        return edge_select(plan, tile, row, position, index).astype(F32)

    def total(span, index):
        return (lax.broadcasted_iota(jnp.int32, (head, span), 0) == index).astype(F32)

    for shift in range(1, tiles):
        dest = lax.rem(me + shift, tiles)
        by_col = by_row = None
        for index in range(count):
            block = maps_ref[index]
            left = [pick(edge, cols, me * cols, dest, index)]
            upper = [pick(edge, width, 0, dest, index)]
            if shift == 1:
                left.append(total(cols, index))
                upper.append(total(width, index))
                upper.append(pick(edge, width, 0, me, index))
            by_c = across(jnp.concatenate(left, axis=0).astype(BF16), block)
            by_r = dot(jnp.concatenate(upper, axis=0).astype(BF16), block)
            by_col = by_c if by_col is None else by_col + by_c
            by_row = by_r if by_row is None else by_row + by_r
        if shift == 1:
            sums_ref[...] = by_col[edge : edge + head]
            own = pl.ds(pl.multiple_of(me * cols, cols), cols)
            sums_ref[:, own] = sums_ref[:, own] + by_row[edge : edge + head]
            edge_ref[...] = by_row[edge + head :]
            sums = sums_ref[...]
            high = sums.astype(BF16).astype(F32)
            middle = (sums - high).astype(BF16).astype(F32)
            low = sums - high - middle
        pieces = [by_row[:edge]]
        for wide in (by_col[:edge], high, middle, low):
            pieces += [wide[:, k * cols : (k + 1) * cols] for k in range(tiles)]
        used = (1 + tiles) * edge + 3 * tiles * head
        if plan.tail_rows > used:
            pieces.append(jnp.zeros((plan.tail_rows - used, cols), F32))
        out_ref[shift - 1] = jnp.concatenate(pieces, axis=0).astype(BF16)


def correct_pack(plan, maps_ref, first_ref, second_ref, tail_ref, sums_ref, edge_ref, *refs):
    *out_refs, field_ref, turned_ref = refs
    me, chip = lax.axis_index("tile"), lax.axis_index("head") // 2
    count, cols, width, tiles = plan.maps, plan.cols, plan.width, plan.tiles
    head, edge, halo = plan.map_rows, plan.edge_rows, plan.halo
    tails = [tail_ref[k].astype(F32) for k in range(tiles - 1)]

    rowsum = []
    for b in range(tiles):
        value = sums_ref[:, b * cols : (b + 1) * cols]
        for tail in tails:
            base = (1 + tiles) * edge
            parts = [
                tail[base + (k * tiles + b) * head : base + (k * tiles + b + 1) * head]
                for k in range(3)
            ]
            value = value + ((parts[0] + parts[1]) + parts[2])
        rowsum.append(value)
    grand = sum(jnp.sum(value, axis=1, keepdims=True) for value in rowsum)
    grand = jnp.where(lax.broadcasted_iota(jnp.int32, (head, 1), 0) < count, grand, 1.0)
    scaled = [value / grand for value in rowsum]
    for b in range(tiles):
        square = jnp.concatenate([rowsum[b], jnp.zeros((LANES - head, cols), F32)], axis=0)
        turned_ref[b * cols : (b + 1) * cols, :] = square.T
    mine = scaled[0]
    for b in range(1, tiles):
        mine = jnp.where(me == b, scaled[b], mine)

    eye = (
        lax.broadcasted_iota(jnp.int32, (cols, cols), 0)
        == lax.broadcasted_iota(jnp.int32, (cols, cols), 1)
    ).astype(F32).astype(BF16)
    margin = 8 + halo
    mirrors = []
    for b in range(tiles):
        shift = lax.rem(b - me + tiles, tiles)
        sender = jnp.maximum(shift - 1, 0)
        other = jnp.concatenate([first_ref[sender], second_ref[sender]], axis=0)
        own = [maps_ref[k, b * cols : (b + 1) * cols, :] for k in range(count)]
        mirrors.append(across(eye, jnp.where(shift == 0, jnp.concatenate(own, axis=0), other)))
    for index in range(count):
        origin = index * plan.pitch
        field_ref[origin : origin + margin, :] = jnp.zeros((margin, cols), F32)
        field_ref[origin + margin + width : origin + plan.pitch, :] = jnp.zeros(
            (plan.pitch - margin - width, cols), F32
        )
        for b in range(tiles):
            own = maps_ref[index, b * cols : (b + 1) * cols, :]
            mirror = mirrors[b][:, index * cols : (index + 1) * cols]
            column = turned_ref[b * cols : (b + 1) * cols, index : index + 1]
            field_ref[origin + margin + b * cols : origin + margin + (b + 1) * cols, :] = (
                own.astype(F32) + mirror - column * mine[index : index + 1]
            )

    strips = []
    for b in range(tiles):
        strip = edge_ref[...]
        for k, tail in enumerate(tails):
            strip = jnp.where(lax.rem(me + k + 1, tiles) == b, tail[:edge], strip)
        for tail in tails:
            strip = strip + tail[(1 + b) * edge : (2 + b) * edge]
        strips.append(strip)
    strip = jnp.concatenate(strips, axis=1)
    wide = jnp.concatenate(scaled, axis=1)
    before = pl.multiple_of(jnp.maximum(me * cols - 8, 0), 8)
    after = pl.multiple_of(jnp.minimum((me + 1) * cols, width - 8), 8)
    left = turned_ref[pl.ds(before, 8), :][8 - halo :]
    right = turned_ref[pl.ds(after, 8), :][:halo]
    if plan.sides == 1:
        beside = jnp.where(me > 0, left, right)
    else:
        beside = jnp.concatenate([left, right], axis=0)
    lines = [
        strip[k * plan.edges : (k + 1) * plan.edges] - beside[:, k : k + 1] * wide[k : k + 1]
        for k in range(count)
    ]
    rows, slots = plan.rows, plan.slots
    stacks = []
    for slot in range(slots):
        members = []
        for group in range(plan.groups):
            k = group * slots + slot
            members.append(lines[k] if k < count else jnp.zeros((plan.edges, width), F32))
        stacks.append(jnp.concatenate(members, axis=0))
    lane = lax.broadcasted_iota(jnp.int32, (plan.side_rows, cols), 1)
    spare = plan.block_rows - plan.lead - plan.half_rows
    for step, out_ref in zip(step_order(plan), out_refs):
        first = partner(chip, step, plan.chips) * 2 * plan.band

        def section(begin, size):
            found = [
                field_ref[pl.ds(8 * k * plan.pitch + first + 8 + begin + r, 8, stride=plan.pitch), :]
                for r in range(size)
                for k in range(plan.sets)
            ]
            for k in range(8 * plan.sets, count):
                found.append(field_ref[pl.ds(k * plan.pitch + first + 8 + begin, size), :])
            return found

        lone, shared = 8 * plan.lone, 8 * plan.shared
        sides = []
        for core in range(2):
            side = jnp.zeros((plan.side_rows, cols), F32)
            for slot in range(slots):
                amount = lax.rem(slot * rows + halo + width - core * plan.band - first, width)
                moved = pltpu.roll(stacks[slot], amount, 1)[:, :cols]
                side = jnp.where((lane >= slot * rows) & (lane < (slot + 1) * rows), moved, side)
            sides.append(side)
        pieces = section(0, lone) + sides[:1] + section(lone, shared)
        pieces += section(lone + shared, lone) + sides[1:]
        if spare:
            pieces.append(jnp.zeros((spare, cols), F32))
        out_ref[...] = jnp.concatenate(pieces, axis=0).astype(BF16)


def core_pack(plan, *refs):
    *block_refs, out_ref = refs
    other = 1 - lax.axis_index("head") % 2
    for k, block_ref in enumerate(block_refs):
        out_ref[k] = half(plan, block_ref[...].astype(F32), other).astype(BF16)


def weight_pack(blocks_ref, proj_ref, set_ref, slot_ref, out_ref, map_ref, side_ref):
    map_ref[...] = dot(proj_ref[...], set_ref[...]).astype(BF16)
    side_ref[...] = dot(proj_ref[...], slot_ref[...]).astype(BF16)
    layers, convs, height, breadth = blocks_ref.shape[:4]
    for b in range(layers):
        for m in range(convs):
            out_ref[b * convs + m] = jnp.concatenate(
                [
                    jnp.concatenate(
                        [blocks_ref[b, m, dy, dx].astype(F32) for dy in range(height)], axis=1
                    )
                    for dx in range(breadth)
                ],
                axis=0,
            ).astype(BF16)


def lanes(base, size):
    return pl.ds(base if isinstance(base, int) else pl.multiple_of(base, LANES), size)


def shifted(ref, rows, base, offset, size):
    low = offset // LANES * LANES
    rest = offset - low
    if rest == 0:
        return ref[rows, lanes(base + low, size)]
    return pltpu.roll(ref[rows, lanes(base + low, size + LANES)], size + LANES - rest, 1)[:, :size]


def stack(plan, order, *refs):
    chips = plan.chips
    own_refs, swap_refs = refs[:chips], refs[chips : chips + len(order)]
    refs = refs[chips + len(order) :]
    proj_ref, side_ref, kernel_ref, vector_ref, mask_ref, spots_ref, out_ref = refs[:7]
    maps_ref, others_ref, sides_ref, stream_ref, hidden_ref, taps_ref, logit_ref = refs[7:]
    count, cols, rows, halo = plan.maps, plan.cols, plan.rows, plan.halo
    heads, feat, stride = plan.heads, plan.feat, plan.stride
    head = lax.axis_index("head")
    chip, core = head // 2, head % 2
    lone, shared = 8 * plan.lone, 8 * plan.shared
    wide = 8 * plan.sets

    def rows_of(sections):
        sets, others = [], []
        for begin, size in sections:
            sets += [begin + r * wide for r in range(size)]
            others += [begin + size * wide + r for r in range(0, size, 8)]
        return sets, others, [size for _, size in sections for _ in range(0, size, 8)]

    early = rows_of([(0, lone), (plan.lead, shared)])
    late = rows_of([(0, shared), (shared * count, lone)])

    def spread(block, source):
        def pick(a, b, size):
            if a == b:
                return block[a : a + size]
            return jnp.where(core == 0, block[a : a + size], block[b : b + size])

        for r, (a, b) in enumerate(zip(early[0], late[0])):
            place = pl.multiple_of(source * wide, 8) + r * heads * wide
            maps_ref[pl.ds(pl.multiple_of(place, 8), wide), :] = pick(a, b, wide)
        for k, (a, b, m, n) in enumerate(zip(early[1], late[1], early[2], late[2])):
            for j in range(plan.rest):
                place = (source * plan.rest + j) * rows + 8 * k
                others_ref[pl.ds(pl.multiple_of(place, 8), 8), :] = pick(a + j * m, b + j * n, 8)
        side = pick(lone * count, plan.half_rows - plan.side_rows, plan.side_rows)
        place = pl.multiple_of(source * plan.side_rows, 8)
        sides_ref[pl.ds(place, plan.side_rows), :] = side

    for steps, swap_ref in zip(order, swap_refs):
        for k, step in enumerate(steps):
            source = 2 * partner(chip, step, chips, back=True)
            spread(half(plan, own_refs[step_order(plan).index(step)][...].astype(F32), core), source + core)
            spread(swap_ref[k].astype(F32), source + 1 - core)
    bias = vector_ref[:, 0:1]

    slots, members = plan.slots, heads * plan.groups
    lane = lax.broadcasted_iota(jnp.int32, (members, cols), 1)
    placed = []
    for first in range(0, plan.edges, slots):
        parts = [jnp.zeros((members, cols), F32) for _ in range(slots)]
        for at in range(min(slots, plan.edges - first)):
            value = sides_ref[pl.ds(first + at, members, stride=plan.edges), :]
            keep = (lane >= at * rows) & (lane < (at + 1) * rows)
            for slot in range(slots):
                moved = value
                if at != slot:
                    moved = pltpu.roll(value, ((at - slot) * rows) % cols, 1)
                parts[slot] = jnp.where(keep, moved, parts[slot])
        stacked = jnp.concatenate(parts, axis=0).astype(BF16)
        placed.append((dot(side_ref[...], stacked) + bias).astype(BF16))

    edge = sum(dot(columns, spots_ref[k]) for k, columns in enumerate(placed))

    weight = proj_ref[...]
    spot = lax.broadcasted_iota(jnp.int32, (feat, LANES), 1)
    spans = []

    def compose(tile):
        low, value = tile * LANES, None
        for begin, size, source, lead in spans:
            left, right = max(begin, low), min(begin + size, low + LANES)
            if left >= right:
                continue
            k = (lead + low) // LANES
            piece = source[:, k * LANES : (k + 1) * LANES]
            if value is None:
                value = piece
            else:
                value = jnp.where((spot >= left - low) & (spot < right - low), piece, value)
        here = slice(low, low + LANES)
        stream_ref[:, here] = jnp.where(mask_ref[:, here] > 0, value, 0.0).astype(BF16)

    def gather(chosen):
        blocks = []
        for r in chosen:
            block = maps_ref[r * heads * wide : (r + 1) * heads * wide, :]
            if plan.rest:
                others = others_ref[pl.ds(r, heads * plan.rest, stride=rows), :]
                block = jnp.concatenate([block, others], axis=0)
            blocks.append(block.astype(BF16))
        return jnp.concatenate(blocks, axis=1)

    done = plan.start // LANES
    for r in range(rows + 1):
        begin = plan.start + r * stride - halo
        between = LANES + r * 2 * halo - halo
        spans.append((begin, 2 * halo, edge, between - begin))
        if r < rows:
            if r % plan.batch == 0:
                batch = dot(weight, gather(range(r, min(r + plan.batch, rows)))) + bias
            value = batch[:, r % plan.batch * cols : (r % plan.batch + 1) * cols]
            begin = plan.start + r * stride + halo
            turn = begin % LANES
            value = jnp.concatenate([value, jnp.zeros((feat, LANES), F32)], axis=1)
            spans.append((begin, cols, pltpu.roll(value, turn, 1), turn - begin))
        full = (plan.start + (r + 1) * stride - halo) // LANES if r < rows else done + 1
        while done < full:
            compose(done)
            done += 1
        spans = [span for span in spans if span[0] + span[1] > done * LANES]

    everything = slice(None)
    for n in range(plan.convs):
        source = hidden_ref if n % 2 else stream_ref
        low = (plan.start + (n + 1) * stride) // LANES * LANES
        span = plan.start + (rows - n - 1) * stride - n - 1 - low
        steps = -(-span // plan.chunk)
        size = up(-(-span // steps), LANES)
        offsets = vector_ref[:, n + 1 : n + 2]

        def multiply(base, size):
            window = jnp.concatenate(
                [shifted(source, everything, base, d * stride, size) for d in (-1, 0, 1)], axis=0
            )
            taps_ref[:, lanes(base, size)] = dot(kernel_ref[n], window)

        def finish(base):
            here = lanes(base, size)
            value = taps_ref[feat : 2 * feat, here]
            value = value + shifted(taps_ref, slice(0, feat), base, -1, size)
            value = value + shifted(taps_ref, slice(2 * feat, 3 * feat), base, 1, size)
            value = value + offsets
            keep = mask_ref[:, here] > 0
            if n % 2 == 0:
                value = jnp.where(value > 0, value, jnp.exp(jnp.minimum(value, 0.0)) - 1.0)
                hidden_ref[:, here] = jnp.where(keep, value, 0.0).astype(BF16)
                return
            value = (stream_ref[:, here].astype(F32) + value).astype(BF16)
            if n < plan.convs - 1:
                stream_ref[:, here] = jnp.where(keep, value.astype(F32), 0.0).astype(BF16)
                return
            readout = vector_ref[:, plan.convs + 1 : plan.convs + 2]
            logit_ref[0:1, here] = jnp.sum(value.astype(F32) * readout, axis=0, keepdims=True)

        multiply(low, size + LANES)
        for i in range(steps):
            if i + 1 < steps:
                multiply(low + (i + 1) * size + LANES, size)
            finish(low + i * size)

    for r in range(plan.band):
        begin = plan.start + (r + halo) * stride + halo
        low = begin // LANES * LANES
        out_ref[r : r + 1, :] = shifted(logit_ref, slice(0, 1), low, begin - low, cols)


def call(kernel, name, args, outs, scratch=(), held_out=True):
    held = sum(math.prod(x.shape) * jnp.dtype(x.dtype).itemsize for x in [*args, *outs, *scratch])
    vmem = pl.BlockSpec(memory_space=pltpu.VMEM)
    return pl.pallas_call(
        kernel,
        out_shape=[pltpu.VMEM(x.shape, x.dtype) if held_out else x for x in outs],
        in_specs=[vmem] * len(args),
        out_specs=[vmem] * len(outs),
        scratch_shapes=list(scratch),
        compiler_params=pltpu.CompilerParams(vmem_limit_bytes=held * 5 // 4 + 4 * 1024 * 1024),
        name=name,
    )(*args)


def array(dtype, *shape):
    return jax.ShapeDtypeStruct(shape, dtype)


def on_device(attention, proj_weight, proj_bias, conv_weight, conv_bias, out_weight):
    maps, width, cols = attention.shape
    feat = proj_weight.shape[0]
    blocks, convs = conv_weight.shape[:2]
    tiles, heads = lax.axis_size("tile"), lax.axis_size("head")
    plan = Plan(maps, width, cols, tiles, heads, feat, blocks * convs)
    me, band_index = lax.axis_index("tile"), lax.axis_index("head")

    tail, sums, edge = call(
        functools.partial(mirror_pack, plan),
        "mirror_pack",
        [attention],
        [
            array(BF16, tiles - 1, plan.tail_rows, cols),
            array(F32, plan.map_rows, width),
            array(F32, plan.edge_rows, cols),
        ],
    )

    def mirror(block):
        return jnp.stack(
            [
                lax.ppermute(block(s), "tile", [(i, (i + s) % tiles) for i in range(tiles)])
                for s in range(tiles - 1, 0, -1)
            ]
        )

    def facing(first, count):
        def block(s):
            start = (first, (me + s) % tiles * cols, 0)
            found = lax.dynamic_slice(attention, start, (count, cols, cols))
            return found.reshape(count * cols, cols)

        return block

    received = [mirror(facing(0, maps // 2)), mirror(facing(maps // 2, maps - maps // 2))]
    tails = mirror(lambda s: tail[s - 1])

    stride, start = plan.stride, plan.start
    source, index = np.divmod(np.arange(heads * maps), maps)
    wide = 8 * plan.sets
    by_set = np.where(
        index < wide, source * wide + index, heads * wide + source * plan.rest + index - wide
    )
    group, slot = np.divmod(index, plan.slots)
    by_slot = (slot * heads + source) * plan.groups + group
    picks = [
        jnp.asarray(place[:, None] == np.arange(size)[None], BF16)
        for place, size in (
            (by_set, heads * maps),
            (by_slot, plan.slots * heads * plan.groups),
        )
    ]
    kernels, map_weight, side_weight = call(
        weight_pack,
        "weight_pack",
        [conv_weight.transpose(0, 1, 4, 5, 2, 3), proj_weight, *picks],
        [
            array(BF16, plan.convs, 3 * feat, 3 * feat),
            array(BF16, feat, picks[0].shape[1]),
            array(BF16, feat, picks[1].shape[1]),
        ],
    )
    vectors = jnp.concatenate(
        [proj_bias[None], conv_bias.reshape(-1, feat), out_weight[None]], axis=0
    ).T
    spot = np.arange(plan.lanes) - start
    row = band_index * plan.band - plan.halo + (spot // stride).astype(np.int32)
    col = me * cols - plan.halo + (spot % stride).astype(np.int32)
    mask = (row >= 0) & (row < width) & (col >= 0) & (col < width)
    mask = mask.astype(F32)[None]

    key = np.arange(cols)
    member, line = key // plan.rows, key % plan.rows
    lane = np.arange(up(LANES + (plan.rows + 1) * 2 * plan.halo, LANES))
    spots = []
    for first in range(0, plan.edges, plan.slots):
        column = first + member
        fits = (member < plan.slots) & (column < plan.edges)
        left = LANES + line * 2 * plan.halo + column
        right = left + plan.halo
        if plan.sides == 1:
            places = [left, right]
        else:
            places = [np.where(column < plan.halo, left, right - plan.halo)]
        hit = [np.where(fits, place, -1)[:, None] == lane[None] for place in places]
        spots.append(functools.reduce(np.logical_or, hit))
    spots = jnp.asarray(np.stack(spots), BF16)

    chips = plan.chips
    blocks = call(
        functools.partial(correct_pack, plan),
        "correct_pack",
        [attention, *received, tails, sums, edge],
        [array(BF16, plan.block_rows, cols)] * chips,
        [pltpu.VMEM((maps * plan.pitch, cols), F32), pltpu.VMEM((width, LANES), F32)],
    )
    arrived = {}
    for step, block in zip(step_order(plan), blocks):
        pairs = [(i, 2 * partner(i // 2, step, chips) + i % 2) for i in range(heads)]
        arrived[step] = lax.ppermute(block, "head", pairs) if step else block
    steps = step_order(plan)
    early = steps[: chips // 2]
    late = [step for step in steps if step not in early]
    order = [early, late]
    weights = (map_weight, side_weight, kernels, vectors, mask, spots)
    swapped = []
    for steps in order:
        (packed,) = call(
            functools.partial(core_pack, plan),
            "core_pack",
            [arrived[k] for k in steps],
            [array(BF16, len(steps), plan.half_rows, cols)],
        )
        if steps is late:
            packed, weights = lax.optimization_barrier((packed, weights))
        swapped.append(lax.ppermute(packed, "head", [(i, i ^ 1) for i in range(heads)]))

    (logits,) = call(
        functools.partial(stack, plan, order),
        "stack",
        [*arrived.values(), *swapped, *weights],
        [array(F32, plan.band, cols)],
        [
            pltpu.VMEM((heads * 8 * plan.sets * plan.rows, cols), F32),
            pltpu.VMEM((heads * max(plan.rest, 1) * plan.rows, cols), F32),
            pltpu.VMEM((heads * plan.side_rows, cols), F32),
            pltpu.VMEM((feat, plan.lanes), BF16),
            pltpu.VMEM((feat, plan.lanes), BF16),
            pltpu.VMEM((3 * feat, plan.lanes), F32),
            pltpu.VMEM((8, plan.lanes), F32),
        ],
        held_out=False,
    )
    return logits


def solution(mesh):
    return jax.shard_map(
        on_device,
        mesh=mesh,
        in_specs=(P(("grp", "head"), None, "tile"), P(), P(), P(), P(), P()),
        out_specs=P(("grp", "head"), "tile"),
        check_vma=False,
    )
```

```python
import functools
import math
from typing import NamedTuple

import jax
import jax.numpy as jnp
import numpy as np
from jax import lax
from jax.experimental import pallas as pl
from jax.experimental.pallas import tpu as pltpu
from jax.sharding import PartitionSpec as P

BF16, F32 = jnp.bfloat16, jnp.float32
LANES = 128


def up(value, step):
    return -(-value // step) * step


class Plan(NamedTuple):
    maps: int
    width: int
    cols: int
    tiles: int
    heads: int
    feat: int
    convs: int

    @property
    def halo(self):
        return self.convs

    @property
    def sides(self):
        return min(2, self.tiles - 1)

    @property
    def edges(self):
        return self.sides * self.halo

    @property
    def edge_rows(self):
        return up(self.maps * self.edges, 8)

    @property
    def map_rows(self):
        return up(self.maps, 16)

    @property
    def tail_rows(self):
        return up((1 + self.tiles) * self.edge_rows + 3 * self.tiles * self.map_rows, 16)

    @property
    def band(self):
        return self.width // self.heads

    @property
    def rows(self):
        return self.band + 2 * self.halo

    @property
    def slots(self):
        return self.cols // self.rows

    @property
    def groups(self):
        return -(-self.maps // self.slots)

    @property
    def side_rows(self):
        return self.groups * self.edges

    @property
    def sets(self):
        return self.maps // 8

    @property
    def rest(self):
        return self.maps % 8

    @property
    def pitch(self):
        return up(self.width + 24, 2) + 1

    @property
    def chips(self):
        return self.heads // 2

    @property
    def lone(self):
        return self.band // 8

    @property
    def shared(self):
        return 2 * self.halo // 8

    @property
    def group_rows(self):
        return 8 * self.maps

    @property
    def lead(self):
        return self.lone * self.group_rows + self.side_rows

    @property
    def half_rows(self):
        return self.lead + self.shared * self.group_rows

    @property
    def block_rows(self):
        return self.lead + self.half_rows

    @property
    def stride(self):
        return self.cols + 2 * self.halo

    @property
    def start(self):
        return up(self.stride, LANES) - LANES

    @property
    def batch(self):
        return 8

    @property
    def chunk(self):
        return 1536

    @property
    def lanes(self):
        return up(self.start + self.rows * self.stride, LANES) + 4 * self.halo * LANES


def partner(mine, step, count, back=False):
    if count & (count - 1) == 0:
        return mine ^ step
    return (mine - step if back else mine + step) % count


def far_near(plan):
    steps = list(range(plan.chips - 1, 0, -1))
    return steps[: plan.chips // 2], steps[plan.chips // 2 :]


def step_order(plan):
    far, near = far_near(plan)
    middle = len(far) // 2
    return far[:middle] + near + far[middle:] + [0]


def half(plan, block, core):
    return jnp.where(
        core == 0, block[: plan.half_rows], block[plan.lead : plan.lead + plan.half_rows]
    )


def edge_start(plan, tile, side):
    left, right = plan.cols * tile - plan.halo, plan.cols * (tile + 1)
    if plan.sides == 1:
        return jnp.where(tile > 0, left, right)
    return (left, right)[side]


def edge_select(plan, tile, row, position, index):
    hit = None
    for side in range(plan.sides):
        first = index * plan.edges + side * plan.halo
        inside = (row >= first) & (row < first + plan.halo)
        one = inside & (position == row - first + edge_start(plan, tile, side))
        hit = one if hit is None else hit | one
    return hit


def across(a, b):
    return lax.dot_general(a, b, (((1,), (1,)), ((), ())), preferred_element_type=F32)


def dot(a, b):
    return jnp.dot(a, b, preferred_element_type=F32)


def mirror_pack(plan, maps_ref, out_ref, sums_ref, edge_ref):
    me = lax.axis_index("tile")
    count, cols, width, tiles = plan.maps, plan.cols, plan.width, plan.tiles
    head, edge = plan.map_rows, plan.edge_rows

    def pick(rows, span, base, tile, index):
        row = lax.broadcasted_iota(jnp.int32, (rows, span), 0)
        position = lax.broadcasted_iota(jnp.int32, (rows, span), 1) + base
        return edge_select(plan, tile, row, position, index).astype(F32)

    def total(span, index):
        return (lax.broadcasted_iota(jnp.int32, (head, span), 0) == index).astype(F32)

    for shift in range(1, tiles):
        dest = lax.rem(me + shift, tiles)
        by_col = by_row = None
        for index in range(count):
            block = maps_ref[index]
            left = [pick(edge, cols, me * cols, dest, index)]
            upper = [pick(edge, width, 0, dest, index)]
            if shift == 1:
                left.append(total(cols, index))
                upper.append(total(width, index))
                upper.append(pick(edge, width, 0, me, index))
            by_c = across(jnp.concatenate(left, axis=0).astype(BF16), block)
            by_r = dot(jnp.concatenate(upper, axis=0).astype(BF16), block)
            by_col = by_c if by_col is None else by_col + by_c
            by_row = by_r if by_row is None else by_row + by_r
        if shift == 1:
            sums_ref[...] = by_col[edge : edge + head]
            own = pl.ds(pl.multiple_of(me * cols, cols), cols)
            sums_ref[:, own] = sums_ref[:, own] + by_row[edge : edge + head]
            edge_ref[...] = by_row[edge + head :]
            sums = sums_ref[...]
            high = sums.astype(BF16).astype(F32)
            middle = (sums - high).astype(BF16).astype(F32)
            low = sums - high - middle
        pieces = [by_row[:edge]]
        for wide in (by_col[:edge], high, middle, low):
            pieces += [wide[:, k * cols : (k + 1) * cols] for k in range(tiles)]
        used = (1 + tiles) * edge + 3 * tiles * head
        if plan.tail_rows > used:
            pieces.append(jnp.zeros((plan.tail_rows - used, cols), F32))
        out_ref[shift - 1] = jnp.concatenate(pieces, axis=0).astype(BF16)


def correct_pack(plan, maps_ref, recv_ref, tail_ref, sums_ref, edge_ref, *refs):
    *out_refs, field_ref, stack_ref, turned_ref = refs
    me = lax.axis_index("tile")
    count, cols, width, tiles = plan.maps, plan.cols, plan.width, plan.tiles
    head, edge, halo = plan.map_rows, plan.edge_rows, plan.halo
    tails = [tail_ref[k].astype(F32) for k in range(tiles - 1)]

    rowsum = []
    for b in range(tiles):
        value = sums_ref[:, b * cols : (b + 1) * cols]
        for tail in tails:
            base = (1 + tiles) * edge
            parts = [
                tail[base + (k * tiles + b) * head : base + (k * tiles + b + 1) * head]
                for k in range(3)
            ]
            value = value + ((parts[0] + parts[1]) + parts[2])
        rowsum.append(value)
    grand = sum(jnp.sum(value, axis=1, keepdims=True) for value in rowsum)
    grand = jnp.where(lax.broadcasted_iota(jnp.int32, (head, 1), 0) < count, grand, 1.0)
    scaled = [value / grand for value in rowsum]
    for b in range(tiles):
        square = jnp.concatenate([rowsum[b], jnp.zeros((LANES - head, cols), F32)], axis=0)
        turned_ref[b * cols : (b + 1) * cols, :] = square.T
    mine = scaled[0]
    for b in range(1, tiles):
        mine = jnp.where(me == b, scaled[b], mine)

    eye = (
        lax.broadcasted_iota(jnp.int32, (cols, cols), 0)
        == lax.broadcasted_iota(jnp.int32, (cols, cols), 1)
    ).astype(F32).astype(BF16)
    margin = 8 + halo
    faces = []
    for b in range(tiles):
        shift = lax.rem(b - me + tiles, tiles)
        other = recv_ref[jnp.maximum(shift - 1, 0)]
        own = [maps_ref[k, b * cols : (b + 1) * cols, :] for k in range(count)]
        faces.append(jnp.where(shift == 0, jnp.concatenate(own, axis=0), other))
    mirrors = across(eye, jnp.concatenate(faces, axis=0))
    for index in range(count):
        origin = index * plan.pitch
        field_ref[origin : origin + margin, :] = jnp.zeros((margin, cols), F32)
        field_ref[origin + margin + width : origin + plan.pitch, :] = jnp.zeros(
            (plan.pitch - margin - width, cols), F32
        )
        for b in range(tiles):
            own = maps_ref[index, b * cols : (b + 1) * cols, :]
            place = (b * count + index) * cols
            mirror = mirrors[:, place : place + cols]
            column = turned_ref[b * cols : (b + 1) * cols, index : index + 1]
            field_ref[origin + margin + b * cols : origin + margin + (b + 1) * cols, :] = (
                own.astype(F32) + mirror - column * mine[index : index + 1]
            )

    strips = []
    for b in range(tiles):
        strip = edge_ref[...]
        for k, tail in enumerate(tails):
            strip = jnp.where(lax.rem(me + k + 1, tiles) == b, tail[:edge], strip)
        for tail in tails:
            strip = strip + tail[(1 + b) * edge : (2 + b) * edge]
        strips.append(strip)
    strip = jnp.concatenate(strips, axis=1)
    wide = jnp.concatenate(scaled, axis=1)
    before = pl.multiple_of(jnp.maximum(me * cols - 8, 0), 8)
    after = pl.multiple_of(jnp.minimum((me + 1) * cols, width - 8), 8)
    left = turned_ref[pl.ds(before, 8), :][8 - halo :]
    right = turned_ref[pl.ds(after, 8), :][:halo]
    if plan.sides == 1:
        beside = jnp.where(me > 0, left, right)
    else:
        beside = jnp.concatenate([left, right], axis=0)
    lines = [
        strip[k * plan.edges : (k + 1) * plan.edges] - beside[:, k : k + 1] * wide[k : k + 1]
        for k in range(count)
    ]
    for slot in range(plan.slots):
        members = []
        for group in range(plan.groups):
            k = group * plan.slots + slot
            members.append(lines[k] if k < count else jnp.zeros((plan.edges, width), F32))
        stack_ref[slot] = jnp.concatenate(members, axis=0)
    pack(plan, step_order(plan)[: len(out_refs)], out_refs, field_ref, stack_ref)


def pack_rest(plan, field_ref, stack_ref, *out_refs):
    pack(plan, step_order(plan)[-len(out_refs) :], out_refs, field_ref, stack_ref)


def pack(plan, steps, out_refs, field_ref, stack_ref):
    chip = lax.axis_index("head") // 2
    count, cols, width, halo = plan.maps, plan.cols, plan.width, plan.halo
    rows, slots = plan.rows, plan.slots
    lane = lax.broadcasted_iota(jnp.int32, (plan.side_rows, cols), 1)
    spare = plan.block_rows - plan.lead - plan.half_rows
    for step, out_ref in zip(steps, out_refs):
        first = partner(chip, step, plan.chips) * 2 * plan.band

        def section(begin, size):
            found = [
                field_ref[pl.ds(8 * k * plan.pitch + first + 8 + begin + r, 8, stride=plan.pitch), :]
                for r in range(size)
                for k in range(plan.sets)
            ]
            for k in range(8 * plan.sets, count):
                found.append(field_ref[pl.ds(k * plan.pitch + first + 8 + begin, size), :])
            return found

        lone, shared = 8 * plan.lone, 8 * plan.shared
        sides = []
        for core in range(2):
            side = jnp.zeros((plan.side_rows, cols), F32)
            for slot in range(slots):
                amount = lax.rem(slot * rows + halo + width - core * plan.band - first, width)
                moved = pltpu.roll(stack_ref[slot], amount, 1)[:, :cols]
                side = jnp.where((lane >= slot * rows) & (lane < (slot + 1) * rows), moved, side)
            sides.append(side)
        pieces = section(0, lone) + sides[:1] + section(lone, shared)
        pieces += section(lone + shared, lone) + sides[1:]
        if spare:
            pieces.append(jnp.zeros((spare, cols), F32))
        out_ref[...] = jnp.concatenate(pieces, axis=0).astype(BF16)


def core_pack(plan, *refs):
    *block_refs, out_ref = refs
    other = 1 - lax.axis_index("head") % 2
    for k, block_ref in enumerate(block_refs):
        out_ref[k] = half(plan, block_ref[...].astype(F32), other).astype(BF16)


def weight_pack(blocks_ref, proj_ref, set_ref, slot_ref, out_ref, map_ref, side_ref):
    map_ref[...] = dot(proj_ref[...], set_ref[...]).astype(BF16)
    side_ref[...] = dot(proj_ref[...], slot_ref[...]).astype(BF16)
    layers, convs, height, breadth = blocks_ref.shape[:4]
    for b in range(layers):
        for m in range(convs):
            out_ref[b * convs + m] = jnp.concatenate(
                [
                    jnp.concatenate(
                        [blocks_ref[b, m, dy, dx].astype(F32) for dy in range(height)], axis=1
                    )
                    for dx in range(breadth)
                ],
                axis=0,
            ).astype(BF16)


def lanes(base, size):
    return pl.ds(base if isinstance(base, int) else pl.multiple_of(base, LANES), size)


def shifted(ref, rows, base, offset, size):
    low = offset // LANES * LANES
    rest = offset - low
    if rest == 0:
        return ref[rows, lanes(base + low, size)]
    return pltpu.roll(ref[rows, lanes(base + low, size + LANES)], size + LANES - rest, 1)[:, :size]


def stack(plan, order, *refs):
    chips = plan.chips
    own_refs, swap_refs = refs[:chips], refs[chips : chips + len(order)]
    refs = refs[chips + len(order) :]
    proj_ref, side_ref, kernel_ref, vector_ref, mask_ref, spots_ref, out_ref = refs[:7]
    maps_ref, others_ref, sides_ref, stream_ref, hidden_ref, taps_ref, logit_ref = refs[7:]
    count, cols, rows, halo = plan.maps, plan.cols, plan.rows, plan.halo
    heads, feat, stride = plan.heads, plan.feat, plan.stride
    head = lax.axis_index("head")
    chip, core = head // 2, head % 2
    lone, shared = 8 * plan.lone, 8 * plan.shared
    wide = 8 * plan.sets

    def rows_of(sections):
        sets, others = [], []
        for begin, size in sections:
            sets += [begin + r * wide for r in range(size)]
            others += [begin + size * wide + r for r in range(0, size, 8)]
        return sets, others, [size for _, size in sections for _ in range(0, size, 8)]

    early = rows_of([(0, lone), (plan.lead, shared)])
    late = rows_of([(0, shared), (shared * count, lone)])

    def spread(block, source):
        def pick(a, b, size):
            if a == b:
                return block[a : a + size]
            return jnp.where(core == 0, block[a : a + size], block[b : b + size])

        for r, (a, b) in enumerate(zip(early[0], late[0])):
            place = pl.multiple_of(source * wide, 8) + r * heads * wide
            maps_ref[pl.ds(pl.multiple_of(place, 8), wide), :] = pick(a, b, wide)
        for k, (a, b, m, n) in enumerate(zip(early[1], late[1], early[2], late[2])):
            for j in range(plan.rest):
                place = (source * plan.rest + j) * rows + 8 * k
                others_ref[pl.ds(pl.multiple_of(place, 8), 8), :] = pick(a + j * m, b + j * n, 8)
        side = pick(lone * count, plan.half_rows - plan.side_rows, plan.side_rows)
        place = pl.multiple_of(source * plan.side_rows, 8)
        sides_ref[pl.ds(place, plan.side_rows), :] = side

    for steps, swap_ref in zip(order, swap_refs):
        for k, step in enumerate(steps):
            source = 2 * partner(chip, step, chips, back=True)
            spread(half(plan, own_refs[step_order(plan).index(step)][...].astype(F32), core), source + core)
            spread(swap_ref[k].astype(F32), source + 1 - core)
    bias = vector_ref[:, 0:1]

    slots, members = plan.slots, heads * plan.groups
    lane = lax.broadcasted_iota(jnp.int32, (members, cols), 1)
    placed = []
    for first in range(0, plan.edges, slots):
        parts = [jnp.zeros((members, cols), F32) for _ in range(slots)]
        for at in range(min(slots, plan.edges - first)):
            value = sides_ref[pl.ds(first + at, members, stride=plan.edges), :]
            keep = (lane >= at * rows) & (lane < (at + 1) * rows)
            for slot in range(slots):
                moved = value
                if at != slot:
                    moved = pltpu.roll(value, ((at - slot) * rows) % cols, 1)
                parts[slot] = jnp.where(keep, moved, parts[slot])
        stacked = jnp.concatenate(parts, axis=0).astype(BF16)
        placed.append((dot(side_ref[...], stacked) + bias).astype(BF16))

    edge = sum(dot(columns, spots_ref[k]) for k, columns in enumerate(placed))

    weight = proj_ref[...]
    spot = lax.broadcasted_iota(jnp.int32, (feat, LANES), 1)
    spans = []

    def compose(tile):
        low, value = tile * LANES, None
        for begin, size, source, lead in spans:
            left, right = max(begin, low), min(begin + size, low + LANES)
            if left >= right:
                continue
            k = (lead + low) // LANES
            piece = source[:, k * LANES : (k + 1) * LANES]
            if value is None:
                value = piece
            else:
                value = jnp.where((spot >= left - low) & (spot < right - low), piece, value)
        here = slice(low, low + LANES)
        stream_ref[:, here] = jnp.where(mask_ref[:, here] > 0, value, 0.0).astype(BF16)

    def gather(chosen):
        blocks = []
        for r in chosen:
            block = maps_ref[r * heads * wide : (r + 1) * heads * wide, :]
            if plan.rest:
                others = others_ref[pl.ds(r, heads * plan.rest, stride=rows), :]
                block = jnp.concatenate([block, others], axis=0)
            blocks.append(block.astype(BF16))
        return jnp.concatenate(blocks, axis=1)

    done = plan.start // LANES
    for r in range(rows + 1):
        begin = plan.start + r * stride - halo
        between = LANES + r * 2 * halo - halo
        spans.append((begin, 2 * halo, edge, between - begin))
        if r < rows:
            if r % plan.batch == 0:
                batch = dot(weight, gather(range(r, min(r + plan.batch, rows)))) + bias
            value = batch[:, r % plan.batch * cols : (r % plan.batch + 1) * cols]
            begin = plan.start + r * stride + halo
            turn = begin % LANES
            value = jnp.concatenate([value, jnp.zeros((feat, LANES), F32)], axis=1)
            spans.append((begin, cols, pltpu.roll(value, turn, 1), turn - begin))
        full = (plan.start + (r + 1) * stride - halo) // LANES if r < rows else done + 1
        while done < full:
            compose(done)
            done += 1
        spans = [span for span in spans if span[0] + span[1] > done * LANES]

    everything = slice(None)
    for n in range(plan.convs):
        source = hidden_ref if n % 2 else stream_ref
        low = (plan.start + (n + 1) * stride) // LANES * LANES
        span = plan.start + (rows - n - 1) * stride - n - 1 - low
        steps = -(-span // plan.chunk)
        size = up(-(-span // steps), LANES)
        offsets = vector_ref[:, n + 1 : n + 2]

        def multiply(base, size):
            window = jnp.concatenate(
                [shifted(source, everything, base, d * stride, size) for d in (-1, 0, 1)], axis=0
            )
            taps_ref[:, lanes(base, size)] = dot(kernel_ref[n], window)

        def finish(base):
            here = lanes(base, size)
            value = taps_ref[feat : 2 * feat, here]
            value = value + shifted(taps_ref, slice(0, feat), base, -1, size)
            value = value + shifted(taps_ref, slice(2 * feat, 3 * feat), base, 1, size)
            value = value + offsets
            keep = mask_ref[:, here] > 0
            if n % 2 == 0:
                value = jnp.where(value > 0, value, jnp.exp(jnp.minimum(value, 0.0)) - 1.0)
                hidden_ref[:, here] = jnp.where(keep, value, 0.0).astype(BF16)
                return
            value = (stream_ref[:, here].astype(F32) + value).astype(BF16)
            if n < plan.convs - 1:
                stream_ref[:, here] = jnp.where(keep, value.astype(F32), 0.0).astype(BF16)
                return
            readout = vector_ref[:, plan.convs + 1 : plan.convs + 2]
            logit_ref[0:1, here] = jnp.sum(value.astype(F32) * readout, axis=0, keepdims=True)

        multiply(low, size + LANES)
        for i in range(steps):
            if i + 1 < steps:
                multiply(low + (i + 1) * size + LANES, size)
            finish(low + i * size)

    for r in range(plan.band):
        begin = plan.start + (r + halo) * stride + halo
        low = begin // LANES * LANES
        out_ref[r : r + 1, :] = shifted(logit_ref, slice(0, 1), low, begin - low, cols)


def call(kernel, name, args, outs, scratch=(), held_out=True):
    held = sum(math.prod(x.shape) * jnp.dtype(x.dtype).itemsize for x in [*args, *outs, *scratch])
    vmem = pl.BlockSpec(memory_space=pltpu.VMEM)
    return pl.pallas_call(
        kernel,
        out_shape=[pltpu.VMEM(x.shape, x.dtype) if held_out else x for x in outs],
        in_specs=[vmem] * len(args),
        out_specs=[vmem] * len(outs),
        scratch_shapes=list(scratch),
        compiler_params=pltpu.CompilerParams(vmem_limit_bytes=held * 5 // 4 + 4 * 1024 * 1024),
        name=name,
    )(*args)


def array(dtype, *shape):
    return jax.ShapeDtypeStruct(shape, dtype)


def on_device(attention, proj_weight, proj_bias, conv_weight, conv_bias, out_weight):
    maps, width, cols = attention.shape
    feat = proj_weight.shape[0]
    blocks, convs = conv_weight.shape[:2]
    tiles, heads = lax.axis_size("tile"), lax.axis_size("head")
    plan = Plan(maps, width, cols, tiles, heads, feat, blocks * convs)
    me, band_index = lax.axis_index("tile"), lax.axis_index("head")

    tail, sums, edge = call(
        functools.partial(mirror_pack, plan),
        "mirror_pack",
        [attention],
        [
            array(BF16, tiles - 1, plan.tail_rows, cols),
            array(F32, plan.map_rows, width),
            array(F32, plan.edge_rows, cols),
        ],
    )

    def mirror(block):
        return jnp.stack(
            [
                lax.ppermute(block(s), "tile", [(i, (i + s) % tiles) for i in range(tiles)])
                for s in range(tiles - 1, 0, -1)
            ]
        )

    def facing(s):
        block = lax.dynamic_slice_in_dim(attention, (me + s) % tiles * cols, cols, 1)
        return block.reshape(maps * cols, cols)

    received, tails = mirror(facing), mirror(lambda s: tail[s - 1])

    stride, start = plan.stride, plan.start
    source, index = np.divmod(np.arange(heads * maps), maps)
    wide = 8 * plan.sets
    by_set = np.where(
        index < wide, source * wide + index, heads * wide + source * plan.rest + index - wide
    )
    group, slot = np.divmod(index, plan.slots)
    by_slot = (slot * heads + source) * plan.groups + group
    picks = [
        jnp.asarray(place[:, None] == np.arange(size)[None], BF16)
        for place, size in (
            (by_set, heads * maps),
            (by_slot, plan.slots * heads * plan.groups),
        )
    ]
    kernels, map_weight, side_weight = call(
        weight_pack,
        "weight_pack",
        [conv_weight.transpose(0, 1, 4, 5, 2, 3), proj_weight, *picks],
        [
            array(BF16, plan.convs, 3 * feat, 3 * feat),
            array(BF16, feat, picks[0].shape[1]),
            array(BF16, feat, picks[1].shape[1]),
        ],
    )
    vectors = jnp.concatenate(
        [proj_bias[None], conv_bias.reshape(-1, feat), out_weight[None]], axis=0
    ).T
    spot = np.arange(plan.lanes) - start
    row = band_index * plan.band - plan.halo + (spot // stride).astype(np.int32)
    col = me * cols - plan.halo + (spot % stride).astype(np.int32)
    mask = (row >= 0) & (row < width) & (col >= 0) & (col < width)
    mask = mask.astype(F32)[None]

    key = np.arange(cols)
    member, line = key // plan.rows, key % plan.rows
    lane = np.arange(up(LANES + (plan.rows + 1) * 2 * plan.halo, LANES))
    spots = []
    for first in range(0, plan.edges, plan.slots):
        column = first + member
        fits = (member < plan.slots) & (column < plan.edges)
        left = LANES + line * 2 * plan.halo + column
        right = left + plan.halo
        if plan.sides == 1:
            places = [left, right]
        else:
            places = [np.where(column < plan.halo, left, right - plan.halo)]
        hit = [np.where(fits, place, -1)[:, None] == lane[None] for place in places]
        spots.append(functools.reduce(np.logical_or, hit))
    spots = jnp.asarray(np.stack(spots), BF16)

    chips = plan.chips
    ahead = chips // 4
    *blocks, field, stacks = call(
        functools.partial(correct_pack, plan),
        "correct_pack",
        [attention, received, tails, sums, edge],
        [array(BF16, plan.block_rows, cols)] * ahead
        + [array(F32, maps * plan.pitch, cols), array(F32, plan.slots, plan.side_rows, width)],
        [pltpu.VMEM((width, LANES), F32)],
    )
    blocks += call(
        functools.partial(pack_rest, plan),
        "pack_rest",
        [field, stacks],
        [array(BF16, plan.block_rows, cols)] * (chips - ahead),
    )
    arrived = {}
    for step, block in zip(step_order(plan), blocks):
        pairs = [(i, 2 * partner(i // 2, step, chips) + i % 2) for i in range(heads)]
        arrived[step] = lax.ppermute(block, "head", pairs) if step else block
    steps = step_order(plan)
    early = steps[: chips // 2]
    late = [step for step in steps if step not in early]
    order = [early, late]
    weights = (map_weight, side_weight, kernels, vectors, mask, spots)
    swapped = []
    for steps in order:
        (packed,) = call(
            functools.partial(core_pack, plan),
            "core_pack",
            [arrived[k] for k in steps],
            [array(BF16, len(steps), plan.half_rows, cols)],
        )
        if steps is late:
            packed, weights = lax.optimization_barrier((packed, weights))
        swapped.append(lax.ppermute(packed, "head", [(i, i ^ 1) for i in range(heads)]))

    (logits,) = call(
        functools.partial(stack, plan, order),
        "stack",
        [*arrived.values(), *swapped, *weights],
        [array(F32, plan.band, cols)],
        [
            pltpu.VMEM((heads * 8 * plan.sets * plan.rows, cols), F32),
            pltpu.VMEM(((heads * plan.rest + 1) * plan.rows, cols), F32),
            pltpu.VMEM(((heads + 1) * plan.side_rows, cols), F32),
            pltpu.VMEM((feat, plan.lanes), BF16),
            pltpu.VMEM((feat, plan.lanes), BF16),
            pltpu.VMEM((3 * feat, plan.lanes), F32),
            pltpu.VMEM((8, plan.lanes), F32),
        ],
        held_out=False,
    )
    return logits


def solution(mesh):
    return jax.shard_map(
        on_device,
        mesh=mesh,
        in_specs=(P(("grp", "head"), None, "tile"), P(), P(), P(), P(), P()),
        out_specs=P(("grp", "head"), "tile"),
        check_vma=False,
    )
```

```python
import functools
import math
from typing import NamedTuple

import jax
import jax.numpy as jnp
import numpy as np
from jax import lax
from jax.experimental import pallas as pl
from jax.experimental.pallas import tpu as pltpu
from jax.sharding import PartitionSpec as P

BF16, F32 = jnp.bfloat16, jnp.float32
LANES = 128


def up(value, step):
    return -(-value // step) * step


class Plan(NamedTuple):
    maps: int
    width: int
    cols: int
    tiles: int
    heads: int
    feat: int
    convs: int

    @property
    def halo(self):
        return self.convs

    @property
    def sides(self):
        return min(2, self.tiles - 1)

    @property
    def edges(self):
        return self.sides * self.halo

    @property
    def edge_rows(self):
        return up(self.maps * self.edges, 8)

    @property
    def map_rows(self):
        return up(self.maps, 16)

    @property
    def tail_rows(self):
        return up((1 + self.tiles) * self.edge_rows + 3 * self.tiles * self.map_rows, 16)

    @property
    def band(self):
        return self.width // self.heads

    @property
    def rows(self):
        return self.band + 2 * self.halo

    @property
    def slots(self):
        return self.cols // self.rows

    @property
    def groups(self):
        return -(-self.maps // self.slots)

    @property
    def side_rows(self):
        return self.groups * self.edges

    @property
    def sets(self):
        return self.maps // 8

    @property
    def rest(self):
        return self.maps % 8

    @property
    def pitch(self):
        return up(self.width + 24, 2) + 1

    @property
    def chips(self):
        return self.heads // 2

    @property
    def lone(self):
        return self.band // 8

    @property
    def shared(self):
        return 2 * self.halo // 8

    @property
    def group_rows(self):
        return 8 * self.maps

    @property
    def lead(self):
        return self.lone * self.group_rows + self.side_rows

    @property
    def half_rows(self):
        return self.lead + self.shared * self.group_rows

    @property
    def block_rows(self):
        return self.lead + self.half_rows

    @property
    def stride(self):
        return self.cols + 2 * self.halo

    @property
    def start(self):
        return up(self.stride, LANES) - LANES

    @property
    def batch(self):
        return 8

    @property
    def chunk(self):
        return 1536

    @property
    def lanes(self):
        return up(self.start + self.rows * self.stride, LANES) + 4 * self.halo * LANES


def partner(mine, step, count, back=False):
    if count & (count - 1) == 0:
        return mine ^ step
    return (mine - step if back else mine + step) % count


def far_near(plan):
    steps = list(range(plan.chips - 1, 0, -1))
    return steps[: plan.chips // 2], steps[plan.chips // 2 :]


def step_order(plan):
    far, near = far_near(plan)
    middle = len(far) // 2
    return far[:middle] + near + far[middle:] + [0]


def half(plan, block, core):
    return jnp.where(
        core == 0, block[: plan.half_rows], block[plan.lead : plan.lead + plan.half_rows]
    )


def edge_start(plan, tile, side):
    left, right = plan.cols * tile - plan.halo, plan.cols * (tile + 1)
    if plan.sides == 1:
        return jnp.where(tile > 0, left, right)
    return (left, right)[side]


def edge_select(plan, tile, row, position, index):
    hit = None
    for side in range(plan.sides):
        first = index * plan.edges + side * plan.halo
        inside = (row >= first) & (row < first + plan.halo)
        one = inside & (position == row - first + edge_start(plan, tile, side))
        hit = one if hit is None else hit | one
    return hit


def across(a, b):
    return lax.dot_general(a, b, (((1,), (1,)), ((), ())), preferred_element_type=F32)


def dot(a, b):
    return jnp.dot(a, b, preferred_element_type=F32)


def mirror_pack(plan, maps_ref, out_ref, sums_ref, edge_ref):
    me = lax.axis_index("tile")
    count, cols, width, tiles = plan.maps, plan.cols, plan.width, plan.tiles
    head, edge = plan.map_rows, plan.edge_rows

    def pick(rows, span, base, tile, index):
        row = lax.broadcasted_iota(jnp.int32, (rows, span), 0)
        position = lax.broadcasted_iota(jnp.int32, (rows, span), 1) + base
        return edge_select(plan, tile, row, position, index).astype(F32)

    def total(span, index):
        return (lax.broadcasted_iota(jnp.int32, (head, span), 0) == index).astype(F32)

    for shift in range(1, tiles):
        dest = lax.rem(me + shift, tiles)
        by_col = by_row = None
        for index in range(count):
            block = maps_ref[index]
            left = [pick(edge, cols, me * cols, dest, index)]
            upper = [pick(edge, width, 0, dest, index)]
            if shift == 1:
                left.append(total(cols, index))
                upper.append(total(width, index))
                upper.append(pick(edge, width, 0, me, index))
            by_c = across(jnp.concatenate(left, axis=0).astype(BF16), block)
            by_r = dot(jnp.concatenate(upper, axis=0).astype(BF16), block)
            by_col = by_c if by_col is None else by_col + by_c
            by_row = by_r if by_row is None else by_row + by_r
        if shift == 1:
            sums_ref[...] = by_col[edge : edge + head]
            own = pl.ds(pl.multiple_of(me * cols, cols), cols)
            sums_ref[:, own] = sums_ref[:, own] + by_row[edge : edge + head]
            edge_ref[...] = by_row[edge + head :]
            sums = sums_ref[...]
            high = sums.astype(BF16).astype(F32)
            middle = (sums - high).astype(BF16).astype(F32)
            low = sums - high - middle
        pieces = [by_row[:edge]]
        for wide in (by_col[:edge], high, middle, low):
            pieces += [wide[:, k * cols : (k + 1) * cols] for k in range(tiles)]
        used = (1 + tiles) * edge + 3 * tiles * head
        if plan.tail_rows > used:
            pieces.append(jnp.zeros((plan.tail_rows - used, cols), F32))
        out_ref[shift - 1] = jnp.concatenate(pieces, axis=0).astype(BF16)


def correct_pack(plan, maps_ref, recv_ref, tail_ref, sums_ref, edge_ref, *refs):
    *out_refs, field_ref, stack_ref, turned_ref = refs
    me = lax.axis_index("tile")
    count, cols, width, tiles = plan.maps, plan.cols, plan.width, plan.tiles
    head, edge, halo = plan.map_rows, plan.edge_rows, plan.halo
    tails = [tail_ref[k].astype(F32) for k in range(tiles - 1)]

    rowsum = []
    for b in range(tiles):
        value = sums_ref[:, b * cols : (b + 1) * cols]
        for tail in tails:
            base = (1 + tiles) * edge
            parts = [
                tail[base + (k * tiles + b) * head : base + (k * tiles + b + 1) * head]
                for k in range(3)
            ]
            value = value + ((parts[0] + parts[1]) + parts[2])
        rowsum.append(value)
    grand = sum(jnp.sum(value, axis=1, keepdims=True) for value in rowsum)
    grand = jnp.where(lax.broadcasted_iota(jnp.int32, (head, 1), 0) < count, grand, 1.0)
    scaled = [value / grand for value in rowsum]
    for b in range(tiles):
        square = jnp.concatenate([rowsum[b], jnp.zeros((LANES - head, cols), F32)], axis=0)
        turned_ref[b * cols : (b + 1) * cols, :] = square.T
    mine = scaled[0]
    for b in range(1, tiles):
        mine = jnp.where(me == b, scaled[b], mine)

    eye = (
        lax.broadcasted_iota(jnp.int32, (cols, cols), 0)
        == lax.broadcasted_iota(jnp.int32, (cols, cols), 1)
    ).astype(F32).astype(BF16)
    margin = 8 + halo
    faces = []
    for b in range(tiles):
        shift = lax.rem(b - me + tiles, tiles)
        other = recv_ref[jnp.maximum(shift - 1, 0)]
        own = [maps_ref[k, b * cols : (b + 1) * cols, :] for k in range(count)]
        faces.append(jnp.where(shift == 0, jnp.concatenate(own, axis=0), other))
    mirrors = across(eye, jnp.concatenate(faces, axis=0))
    for index in range(count):
        origin = index * plan.pitch
        field_ref[origin : origin + margin, :] = jnp.zeros((margin, cols), F32)
        field_ref[origin + margin + width : origin + plan.pitch, :] = jnp.zeros(
            (plan.pitch - margin - width, cols), F32
        )
        for b in range(tiles):
            own = maps_ref[index, b * cols : (b + 1) * cols, :]
            place = (b * count + index) * cols
            mirror = mirrors[:, place : place + cols]
            column = turned_ref[b * cols : (b + 1) * cols, index : index + 1]
            field_ref[origin + margin + b * cols : origin + margin + (b + 1) * cols, :] = (
                own.astype(F32) + mirror - column * mine[index : index + 1]
            )

    strips = []
    for b in range(tiles):
        strip = edge_ref[...]
        for k, tail in enumerate(tails):
            strip = jnp.where(lax.rem(me + k + 1, tiles) == b, tail[:edge], strip)
        for tail in tails:
            strip = strip + tail[(1 + b) * edge : (2 + b) * edge]
        strips.append(strip)
    strip = jnp.concatenate(strips, axis=1)
    wide = jnp.concatenate(scaled, axis=1)
    before = pl.multiple_of(jnp.maximum(me * cols - 8, 0), 8)
    after = pl.multiple_of(jnp.minimum((me + 1) * cols, width - 8), 8)
    left = turned_ref[pl.ds(before, 8), :][8 - halo :]
    right = turned_ref[pl.ds(after, 8), :][:halo]
    if plan.sides == 1:
        beside = jnp.where(me > 0, left, right)
    else:
        beside = jnp.concatenate([left, right], axis=0)
    lines = [
        strip[k * plan.edges : (k + 1) * plan.edges] - beside[:, k : k + 1] * wide[k : k + 1]
        for k in range(count)
    ]
    for slot in range(plan.slots):
        members = []
        for group in range(plan.groups):
            k = group * plan.slots + slot
            members.append(lines[k] if k < count else jnp.zeros((plan.edges, width), F32))
        stack_ref[slot] = jnp.concatenate(members, axis=0)
    pack(plan, step_order(plan)[: len(out_refs)], out_refs, field_ref, stack_ref)


def pack_rest(plan, field_ref, stack_ref, *out_refs):
    pack(plan, step_order(plan)[-len(out_refs) :], out_refs, field_ref, stack_ref)


def pack(plan, steps, out_refs, field_ref, stack_ref):
    chip = lax.axis_index("head") // 2
    count, cols, width, halo = plan.maps, plan.cols, plan.width, plan.halo
    rows, slots = plan.rows, plan.slots
    lane = lax.broadcasted_iota(jnp.int32, (plan.side_rows, cols), 1)
    spare = plan.block_rows - plan.lead - plan.half_rows
    for step, out_ref in zip(steps, out_refs):
        first = partner(chip, step, plan.chips) * 2 * plan.band

        def section(begin, size):
            found = [
                field_ref[pl.ds(8 * k * plan.pitch + first + 8 + begin + r, 8, stride=plan.pitch), :]
                for r in range(size)
                for k in range(plan.sets)
            ]
            for k in range(8 * plan.sets, count):
                found.append(field_ref[pl.ds(k * plan.pitch + first + 8 + begin, size), :])
            return found

        lone, shared = 8 * plan.lone, 8 * plan.shared
        sides = []
        for core in range(2):
            side = jnp.zeros((plan.side_rows, cols), F32)
            for slot in range(slots):
                amount = lax.rem(slot * rows + halo + width - core * plan.band - first, width)
                moved = pltpu.roll(stack_ref[slot], amount, 1)[:, :cols]
                side = jnp.where((lane >= slot * rows) & (lane < (slot + 1) * rows), moved, side)
            sides.append(side)
        pieces = section(0, lone) + sides[:1] + section(lone, shared)
        pieces += section(lone + shared, lone) + sides[1:]
        if spare:
            pieces.append(jnp.zeros((spare, cols), F32))
        out_ref[...] = jnp.concatenate(pieces, axis=0).astype(BF16)


def core_pack(plan, *refs):
    *block_refs, out_ref = refs
    other = 1 - lax.axis_index("head") % 2
    for k, block_ref in enumerate(block_refs):
        out_ref[k] = half(plan, block_ref[...].astype(F32), other).astype(BF16)


def weight_pack(blocks_ref, proj_ref, set_ref, slot_ref, out_ref, map_ref, side_ref):
    map_ref[...] = dot(proj_ref[...], set_ref[...]).astype(BF16)
    side_ref[...] = dot(proj_ref[...], slot_ref[...]).astype(BF16)
    layers, convs, height, breadth = blocks_ref.shape[:4]
    for b in range(layers):
        for m in range(convs):
            out_ref[b * convs + m] = jnp.concatenate(
                [
                    jnp.concatenate(
                        [blocks_ref[b, m, dy, dx].astype(F32) for dy in range(height)], axis=1
                    )
                    for dx in range(breadth)
                ],
                axis=0,
            ).astype(BF16)


def lanes(base, size):
    return pl.ds(base if isinstance(base, int) else pl.multiple_of(base, LANES), size)


def shifted(ref, rows, base, offset, size):
    low = offset // LANES * LANES
    rest = offset - low
    if rest == 0:
        return ref[rows, lanes(base + low, size)]
    return pltpu.roll(ref[rows, lanes(base + low, size + LANES)], size + LANES - rest, 1)[:, :size]


def stack(plan, order, *refs):
    chips = plan.chips
    own_refs, swap_refs = refs[:chips], refs[chips : chips + len(order)]
    refs = refs[chips + len(order) :]
    proj_ref, side_ref, kernel_ref, vector_ref, mask_ref, spots_ref, out_ref = refs[:7]
    maps_ref, others_ref, sides_ref, stream_ref, hidden_ref, taps_ref, logit_ref = refs[7:]
    count, cols, rows, halo = plan.maps, plan.cols, plan.rows, plan.halo
    heads, feat, stride = plan.heads, plan.feat, plan.stride
    head = lax.axis_index("head")
    chip, core = head // 2, head % 2
    lone, shared = 8 * plan.lone, 8 * plan.shared
    wide = 8 * plan.sets

    def rows_of(sections):
        sets, others = [], []
        for begin, size in sections:
            sets += [begin + r * wide for r in range(size)]
            others += [begin + size * wide + r for r in range(0, size, 8)]
        return sets, others, [size for _, size in sections for _ in range(0, size, 8)]

    early = rows_of([(0, lone), (plan.lead, shared)])
    late = rows_of([(0, shared), (shared * count, lone)])

    def spread(block, source):
        def pick(a, b, size):
            if a == b:
                return block[a : a + size]
            return jnp.where(core == 0, block[a : a + size], block[b : b + size])

        for r, (a, b) in enumerate(zip(early[0], late[0])):
            place = pl.multiple_of(source * wide, 8) + r * heads * wide
            maps_ref[pl.ds(pl.multiple_of(place, 8), wide), :] = pick(a, b, wide)
        for k, (a, b, m, n) in enumerate(zip(early[1], late[1], early[2], late[2])):
            for j in range(plan.rest):
                place = (source * plan.rest + j) * rows + 8 * k
                others_ref[pl.ds(pl.multiple_of(place, 8), 8), :] = pick(a + j * m, b + j * n, 8)
        side = pick(lone * count, plan.half_rows - plan.side_rows, plan.side_rows)
        place = pl.multiple_of(source * plan.side_rows, 8)
        sides_ref[pl.ds(place, plan.side_rows), :] = side

    for steps, swap_ref in zip(order, swap_refs):
        for k, step in enumerate(steps):
            source = 2 * partner(chip, step, chips, back=True)
            spread(half(plan, own_refs[step_order(plan).index(step)][...].astype(F32), core), source + core)
            spread(swap_ref[k].astype(F32), source + 1 - core)
    bias = vector_ref[:, 0:1]

    slots, members = plan.slots, heads * plan.groups
    lane = lax.broadcasted_iota(jnp.int32, (members, cols), 1)
    placed = []
    for first in range(0, plan.edges, slots):
        parts = [jnp.zeros((members, cols), F32) for _ in range(slots)]
        for at in range(min(slots, plan.edges - first)):
            value = sides_ref[pl.ds(first + at, members, stride=plan.edges), :]
            keep = (lane >= at * rows) & (lane < (at + 1) * rows)
            for slot in range(slots):
                moved = value
                if at != slot:
                    moved = pltpu.roll(value, ((at - slot) * rows) % cols, 1)
                parts[slot] = jnp.where(keep, moved, parts[slot])
        stacked = jnp.concatenate(parts, axis=0).astype(BF16)
        placed.append((dot(side_ref[...], stacked) + bias).astype(BF16))

    edge = sum(dot(columns, spots_ref[k]) for k, columns in enumerate(placed))

    weight = proj_ref[...]
    spot = lax.broadcasted_iota(jnp.int32, (feat, LANES), 1)
    spans = []

    def compose(tile):
        low, value = tile * LANES, None
        for begin, size, source, lead in spans:
            left, right = max(begin, low), min(begin + size, low + LANES)
            if left >= right:
                continue
            k = (lead + low) // LANES
            piece = source[:, k * LANES : (k + 1) * LANES]
            if value is None:
                value = piece
            else:
                value = jnp.where((spot >= left - low) & (spot < right - low), piece, value)
        here = slice(low, low + LANES)
        stream_ref[:, here] = jnp.where(mask_ref[:, here] > 0, value, 0.0).astype(BF16)

    def gather(chosen):
        blocks = []
        for r in chosen:
            block = maps_ref[r * heads * wide : (r + 1) * heads * wide, :]
            if plan.rest:
                others = others_ref[pl.ds(r, heads * plan.rest, stride=rows), :]
                block = jnp.concatenate([block, others], axis=0)
            blocks.append(block.astype(BF16))
        return jnp.concatenate(blocks, axis=1)

    done = plan.start // LANES
    for r in range(rows + 1):
        begin = plan.start + r * stride - halo
        between = LANES + r * 2 * halo - halo
        spans.append((begin, 2 * halo, edge, between - begin))
        if r < rows:
            if r % plan.batch == 0:
                batch = dot(weight, gather(range(r, min(r + plan.batch, rows)))) + bias
            value = batch[:, r % plan.batch * cols : (r % plan.batch + 1) * cols]
            begin = plan.start + r * stride + halo
            turn = begin % LANES
            value = jnp.concatenate([value, jnp.zeros((feat, LANES), F32)], axis=1)
            spans.append((begin, cols, pltpu.roll(value, turn, 1), turn - begin))
        full = (plan.start + (r + 1) * stride - halo) // LANES if r < rows else done + 1
        while done < full:
            compose(done)
            done += 1
        spans = [span for span in spans if span[0] + span[1] > done * LANES]

    everything, convs = slice(None), range(plan.convs)
    slack = 2 * LANES + stride // LANES * LANES
    lows = [(plan.start + (n + 1) * stride) // LANES * LANES for n in convs]
    ends = [up(plan.start + (rows - n - 1) * stride - n - 1, LANES) for n in convs]
    steps = -(-(ends[0] - lows[0]) // plan.chunk)
    size = up(-(-(ends[0] - lows[0]) // steps), LANES)
    lead = lows[0] + size + up(slack * (plan.convs - 1) // 2, LANES)
    cuts = [[lows[n], *(lead + j * size - n * slack for j in range(steps - 1)), ends[n]] for n in convs]

    def multiply(n, j):
        source = hidden_ref if n % 2 else stream_ref
        base = cuts[n][j] + (LANES if j else 0)
        size = cuts[n][j + 1] + LANES - base
        window = jnp.concatenate(
            [shifted(source, everything, base, d * stride, size) for d in (-1, 0, 1)], axis=0
        )
        taps_ref[:, lanes(base, size)] = dot(kernel_ref[n], window)

    def finish(n, j):
        base, size = cuts[n][j], cuts[n][j + 1] - cuts[n][j]
        here = lanes(base, size)
        value = taps_ref[feat : 2 * feat, here]
        value = value + shifted(taps_ref, slice(0, feat), base, -1, size)
        value = value + shifted(taps_ref, slice(2 * feat, 3 * feat), base, 1, size)
        value = value + vector_ref[:, n + 1 : n + 2]
        keep = mask_ref[:, here] > 0
        if n % 2 == 0:
            value = jnp.where(value > 0, value, jnp.exp(jnp.minimum(value, 0.0)) - 1.0)
            hidden_ref[:, here] = jnp.where(keep, value, 0.0).astype(BF16)
            return
        value = (stream_ref[:, here].astype(F32) + value).astype(BF16)
        if n < plan.convs - 1:
            stream_ref[:, here] = jnp.where(keep, value.astype(F32), 0.0).astype(BF16)
            return
        readout = vector_ref[:, plan.convs + 1 : plan.convs + 2]
        logit_ref[0:1, here] = jnp.sum(value.astype(F32) * readout, axis=0, keepdims=True)

    for turn in range(plan.convs + steps - 1):
        together = [(n, turn - n) for n in convs if 0 <= turn - n < steps]
        for n, j in together:
            multiply(n, j)
        for n, j in together:
            finish(n, j)

    for r in range(plan.band):
        begin = plan.start + (r + halo) * stride + halo
        low = begin // LANES * LANES
        out_ref[r : r + 1, :] = shifted(logit_ref, slice(0, 1), low, begin - low, cols)


def call(kernel, name, args, outs, scratch=(), held_out=True):
    held = sum(math.prod(x.shape) * jnp.dtype(x.dtype).itemsize for x in [*args, *outs, *scratch])
    vmem = pl.BlockSpec(memory_space=pltpu.VMEM)
    return pl.pallas_call(
        kernel,
        out_shape=[pltpu.VMEM(x.shape, x.dtype) if held_out else x for x in outs],
        in_specs=[vmem] * len(args),
        out_specs=[vmem] * len(outs),
        scratch_shapes=list(scratch),
        compiler_params=pltpu.CompilerParams(vmem_limit_bytes=held * 5 // 4 + 4 * 1024 * 1024),
        name=name,
    )(*args)


def array(dtype, *shape):
    return jax.ShapeDtypeStruct(shape, dtype)


def on_device(attention, proj_weight, proj_bias, conv_weight, conv_bias, out_weight):
    maps, width, cols = attention.shape
    feat = proj_weight.shape[0]
    blocks, convs = conv_weight.shape[:2]
    tiles, heads = lax.axis_size("tile"), lax.axis_size("head")
    plan = Plan(maps, width, cols, tiles, heads, feat, blocks * convs)
    me, band_index = lax.axis_index("tile"), lax.axis_index("head")

    tail, sums, edge = call(
        functools.partial(mirror_pack, plan),
        "mirror_pack",
        [attention],
        [
            array(BF16, tiles - 1, plan.tail_rows, cols),
            array(F32, plan.map_rows, width),
            array(F32, plan.edge_rows, cols),
        ],
    )

    def mirror(block):
        return jnp.stack(
            [
                lax.ppermute(block(s), "tile", [(i, (i + s) % tiles) for i in range(tiles)])
                for s in range(tiles - 1, 0, -1)
            ]
        )

    def facing(s):
        block = lax.dynamic_slice_in_dim(attention, (me + s) % tiles * cols, cols, 1)
        return block.reshape(maps * cols, cols)

    received, tails = mirror(facing), mirror(lambda s: tail[s - 1])

    stride, start = plan.stride, plan.start
    source, index = np.divmod(np.arange(heads * maps), maps)
    wide = 8 * plan.sets
    by_set = np.where(
        index < wide, source * wide + index, heads * wide + source * plan.rest + index - wide
    )
    group, slot = np.divmod(index, plan.slots)
    by_slot = (slot * heads + source) * plan.groups + group
    picks = [
        jnp.asarray(place[:, None] == np.arange(size)[None], BF16)
        for place, size in (
            (by_set, heads * maps),
            (by_slot, plan.slots * heads * plan.groups),
        )
    ]
    kernels, map_weight, side_weight = call(
        weight_pack,
        "weight_pack",
        [conv_weight.transpose(0, 1, 4, 5, 2, 3), proj_weight, *picks],
        [
            array(BF16, plan.convs, 3 * feat, 3 * feat),
            array(BF16, feat, picks[0].shape[1]),
            array(BF16, feat, picks[1].shape[1]),
        ],
    )
    vectors = jnp.concatenate(
        [proj_bias[None], conv_bias.reshape(-1, feat), out_weight[None]], axis=0
    ).T
    spot = np.arange(plan.lanes) - start
    row = band_index * plan.band - plan.halo + (spot // stride).astype(np.int32)
    col = me * cols - plan.halo + (spot % stride).astype(np.int32)
    mask = (row >= 0) & (row < width) & (col >= 0) & (col < width)
    mask = mask.astype(F32)[None]

    key = np.arange(cols)
    member, line = key // plan.rows, key % plan.rows
    lane = np.arange(up(LANES + (plan.rows + 1) * 2 * plan.halo, LANES))
    spots = []
    for first in range(0, plan.edges, plan.slots):
        column = first + member
        fits = (member < plan.slots) & (column < plan.edges)
        left = LANES + line * 2 * plan.halo + column
        right = left + plan.halo
        if plan.sides == 1:
            places = [left, right]
        else:
            places = [np.where(column < plan.halo, left, right - plan.halo)]
        hit = [np.where(fits, place, -1)[:, None] == lane[None] for place in places]
        spots.append(functools.reduce(np.logical_or, hit))
    spots = jnp.asarray(np.stack(spots), BF16)

    chips = plan.chips
    ahead = chips // 4
    *blocks, field, stacks = call(
        functools.partial(correct_pack, plan),
        "correct_pack",
        [attention, received, tails, sums, edge],
        [array(BF16, plan.block_rows, cols)] * ahead
        + [array(F32, maps * plan.pitch, cols), array(F32, plan.slots, plan.side_rows, width)],
        [pltpu.VMEM((width, LANES), F32)],
    )
    blocks += call(
        functools.partial(pack_rest, plan),
        "pack_rest",
        [field, stacks],
        [array(BF16, plan.block_rows, cols)] * (chips - ahead),
    )
    arrived = {}
    for step, block in zip(step_order(plan), blocks):
        pairs = [(i, 2 * partner(i // 2, step, chips) + i % 2) for i in range(heads)]
        arrived[step] = lax.ppermute(block, "head", pairs) if step else block
    steps = step_order(plan)
    early = steps[: chips // 2]
    late = [step for step in steps if step not in early]
    order = [early, late]
    weights = (map_weight, side_weight, kernels, vectors, mask, spots)
    swapped = []
    for steps in order:
        (packed,) = call(
            functools.partial(core_pack, plan),
            "core_pack",
            [arrived[k] for k in steps],
            [array(BF16, len(steps), plan.half_rows, cols)],
        )
        if steps is late:
            packed, weights = lax.optimization_barrier((packed, weights))
        swapped.append(lax.ppermute(packed, "head", [(i, i ^ 1) for i in range(heads)]))

    (logits,) = call(
        functools.partial(stack, plan, order),
        "stack",
        [*arrived.values(), *swapped, *weights],
        [array(F32, plan.band, cols)],
        [
            pltpu.VMEM((heads * 8 * plan.sets * plan.rows, cols), F32),
            pltpu.VMEM(((heads * plan.rest + 1) * plan.rows, cols), F32),
            pltpu.VMEM(((heads + 1) * plan.side_rows, cols), F32),
            pltpu.VMEM((feat, plan.lanes), BF16),
            pltpu.VMEM((feat, plan.lanes), BF16),
            pltpu.VMEM((3 * feat, plan.lanes), F32),
            pltpu.VMEM((8, plan.lanes), F32),
        ],
        held_out=False,
    )
    return logits


def solution(mesh):
    return jax.shard_map(
        on_device,
        mesh=mesh,
        in_specs=(P(("grp", "head"), None, "tile"), P(), P(), P(), P(), P()),
        out_specs=P(("grp", "head"), "tile"),
        check_vma=False,
    )
```

```python
import functools
import math
from typing import NamedTuple

import jax
import jax.numpy as jnp
import numpy as np
from jax import lax
from jax.experimental import pallas as pl
from jax.experimental.pallas import tpu as pltpu
from jax.sharding import PartitionSpec as P

BF16, F32 = jnp.bfloat16, jnp.float32
LANES = 128


def up(value, step):
    return -(-value // step) * step


class Plan(NamedTuple):
    maps: int
    width: int
    cols: int
    tiles: int
    heads: int
    feat: int
    convs: int

    @property
    def halo(self):
        return self.convs

    @property
    def sides(self):
        return min(2, self.tiles - 1)

    @property
    def edges(self):
        return self.sides * self.halo

    @property
    def edge_rows(self):
        return up(self.maps * self.edges, 8)

    @property
    def map_rows(self):
        return up(self.maps, 16)

    @property
    def tail_rows(self):
        return up((1 + self.tiles) * self.edge_rows + self.sum_rows, 16)

    @property
    def sum_rows(self):
        return 3 * self.tiles * 8 * self.sets + up(3 * self.tiles * self.rest, 8)

    @property
    def band(self):
        return self.width // self.heads

    @property
    def rows(self):
        return self.band + 2 * self.halo

    @property
    def slots(self):
        return self.cols // self.rows

    @property
    def groups(self):
        return -(-self.maps // self.slots)

    @property
    def side_rows(self):
        return self.groups * self.edges

    @property
    def sets(self):
        return self.maps // 8

    @property
    def rest(self):
        return self.maps % 8

    @property
    def pitch(self):
        return up(self.width + 24, 2) + 1

    @property
    def chips(self):
        return self.heads // 2

    @property
    def lone(self):
        return self.band // 8

    @property
    def shared(self):
        return 2 * self.halo // 8

    @property
    def group_rows(self):
        return 8 * self.maps

    @property
    def lead(self):
        return self.lone * self.group_rows + self.side_rows

    @property
    def half_rows(self):
        return self.lead + self.shared * self.group_rows

    @property
    def block_rows(self):
        return self.lead + self.half_rows

    @property
    def stride(self):
        return self.cols + 2 * self.halo

    @property
    def start(self):
        return up(self.stride, LANES) - LANES

    @property
    def batch(self):
        return 8

    @property
    def chunk(self):
        return 1536

    @property
    def lanes(self):
        return up(self.start + self.rows * self.stride, LANES) + 4 * self.halo * LANES


def partner(mine, step, count, back=False):
    if count & (count - 1) == 0:
        return mine ^ step
    return (mine - step if back else mine + step) % count


def far_near(plan):
    steps = list(range(plan.chips - 1, 0, -1))
    return steps[: plan.chips // 2], steps[plan.chips // 2 :]


def step_order(plan):
    far, near = far_near(plan)
    middle = len(far) // 2
    return far[:middle] + near + far[middle:] + [0]


def half(plan, block, core):
    return jnp.where(
        core == 0, block[: plan.half_rows], block[plan.lead : plan.lead + plan.half_rows]
    )


def edge_start(plan, tile, side):
    left, right = plan.cols * tile - plan.halo, plan.cols * (tile + 1)
    if plan.sides == 1:
        return jnp.where(tile > 0, left, right)
    return (left, right)[side]


def edge_select(plan, tile, row, position, index):
    hit = None
    for side in range(plan.sides):
        first = index * plan.edges + side * plan.halo
        inside = (row >= first) & (row < first + plan.halo)
        one = inside & (position == row - first + edge_start(plan, tile, side))
        hit = one if hit is None else hit | one
    return hit


def across(a, b):
    return lax.dot_general(a, b, (((1,), (1,)), ((), ())), preferred_element_type=F32)


def dot(a, b):
    return jnp.dot(a, b, preferred_element_type=F32)


def mirror_pack(plan, maps_ref, out_ref, sums_ref, edge_ref):
    me = lax.axis_index("tile")
    count, cols, width, tiles = plan.maps, plan.cols, plan.width, plan.tiles
    head, edge = plan.map_rows, plan.edge_rows

    def pick(rows, span, base, tile, index):
        row = lax.broadcasted_iota(jnp.int32, (rows, span), 0)
        position = lax.broadcasted_iota(jnp.int32, (rows, span), 1) + base
        return edge_select(plan, tile, row, position, index).astype(F32)

    def total(span, index):
        return (lax.broadcasted_iota(jnp.int32, (head, span), 0) == index).astype(F32)

    for shift in range(1, tiles):
        dest = lax.rem(me + shift, tiles)
        by_col = by_row = None
        for index in range(count):
            block = maps_ref[index]
            left = [pick(edge, cols, me * cols, dest, index)]
            upper = [pick(edge, width, 0, dest, index)]
            if shift == 1:
                left.append(total(cols, index))
                upper.append(total(width, index))
                upper.append(pick(edge, width, 0, me, index))
            by_c = across(jnp.concatenate(left, axis=0).astype(BF16), block)
            by_r = dot(jnp.concatenate(upper, axis=0).astype(BF16), block)
            by_col = by_c if by_col is None else by_col + by_c
            by_row = by_r if by_row is None else by_row + by_r
        if shift == 1:
            sums_ref[...] = by_col[edge : edge + head]
            own = pl.ds(pl.multiple_of(me * cols, cols), cols)
            sums_ref[:, own] = sums_ref[:, own] + by_row[edge : edge + head]
            edge_ref[...] = by_row[edge + head :]
            sums = sums_ref[...]
            high = sums.astype(BF16).astype(F32)
            middle = (sums - high).astype(BF16).astype(F32)
            low = sums - high - middle
        pieces = [by_row[:edge]]
        pieces += [by_col[:edge, k * cols : (k + 1) * cols] for k in range(tiles)]
        parts = [
            part[:, k * cols : (k + 1) * cols] for part in (high, middle, low) for k in range(tiles)
        ]
        sets, rest = 8 * plan.sets, plan.rest
        pieces += [part[:sets] for part in parts if sets]
        if rest:
            spare = up(len(parts) * rest, 8)
            row = lax.broadcasted_iota(jnp.int32, (spare, cols), 0)
            others = jnp.zeros((spare, cols), F32)
            for k, part in enumerate(parts):
                for j in range(rest):
                    others = jnp.where(row == k * rest + j, part[sets + j : sets + j + 1], others)
            pieces.append(others)
        used = (1 + tiles) * edge + plan.sum_rows
        if plan.tail_rows > used:
            pieces.append(jnp.zeros((plan.tail_rows - used, cols), F32))
        out_ref[shift - 1] = jnp.concatenate(pieces, axis=0).astype(BF16)


def correct_pack(plan, maps_ref, recv_ref, tail_ref, sums_ref, edge_ref, *refs):
    *out_refs, field_ref, stack_ref, turned_ref = refs
    me = lax.axis_index("tile")
    count, cols, width, tiles = plan.maps, plan.cols, plan.width, plan.tiles
    head, edge, halo = plan.map_rows, plan.edge_rows, plan.halo
    tails = [tail_ref[k].astype(F32) for k in range(tiles - 1)]

    sets, rest = 8 * plan.sets, plan.rest
    line = lax.broadcasted_iota(jnp.int32, (head - sets, cols), 0)

    def sums_of(tail, k):
        base = (1 + tiles) * edge
        begin = base + 3 * tiles * sets + k * rest
        others = jnp.zeros((head - sets, cols), F32)
        for j in range(rest):
            others = jnp.where(line == j, tail[begin + j : begin + j + 1], others)
        return jnp.concatenate([tail[base + k * sets : base + (k + 1) * sets], others], axis=0)

    rowsum = []
    for b in range(tiles):
        value = sums_ref[:, b * cols : (b + 1) * cols]
        for tail in tails:
            parts = [sums_of(tail, k * tiles + b) for k in range(3)]
            value = value + ((parts[0] + parts[1]) + parts[2])
        rowsum.append(value)
    grand = sum(jnp.sum(value, axis=1, keepdims=True) for value in rowsum)
    grand = jnp.where(lax.broadcasted_iota(jnp.int32, (head, 1), 0) < count, grand, 1.0)
    scaled = [value / grand for value in rowsum]
    for b in range(tiles):
        square = jnp.concatenate([rowsum[b], jnp.zeros((LANES - head, cols), F32)], axis=0)
        turned_ref[b * cols : (b + 1) * cols, :] = square.T
    mine = scaled[0]
    for b in range(1, tiles):
        mine = jnp.where(me == b, scaled[b], mine)

    eye = (
        lax.broadcasted_iota(jnp.int32, (cols, cols), 0)
        == lax.broadcasted_iota(jnp.int32, (cols, cols), 1)
    ).astype(F32).astype(BF16)
    margin = 8 + halo
    faces = []
    for b in range(tiles):
        shift = lax.rem(b - me + tiles, tiles)
        other = recv_ref[jnp.maximum(shift - 1, 0)]
        own = [maps_ref[k, b * cols : (b + 1) * cols, :] for k in range(count)]
        faces.append(jnp.where(shift == 0, jnp.concatenate(own, axis=0), other))
    mirrors = across(eye, jnp.concatenate(faces, axis=0))
    for index in range(count):
        origin = index * plan.pitch
        field_ref[origin : origin + margin, :] = jnp.zeros((margin, cols), F32)
        field_ref[origin + margin + width : origin + plan.pitch, :] = jnp.zeros(
            (plan.pitch - margin - width, cols), F32
        )
        for b in range(tiles):
            own = maps_ref[index, b * cols : (b + 1) * cols, :]
            place = (b * count + index) * cols
            mirror = mirrors[:, place : place + cols]
            column = turned_ref[b * cols : (b + 1) * cols, index : index + 1]
            field_ref[origin + margin + b * cols : origin + margin + (b + 1) * cols, :] = (
                own.astype(F32) + mirror - column * mine[index : index + 1]
            )

    strips = []
    for b in range(tiles):
        strip = edge_ref[...]
        for k, tail in enumerate(tails):
            strip = jnp.where(lax.rem(me + k + 1, tiles) == b, tail[:edge], strip)
        for tail in tails:
            strip = strip + tail[(1 + b) * edge : (2 + b) * edge]
        strips.append(strip)
    strip = jnp.concatenate(strips, axis=1)
    wide = jnp.concatenate(scaled, axis=1)
    before = pl.multiple_of(jnp.maximum(me * cols - 8, 0), 8)
    after = pl.multiple_of(jnp.minimum((me + 1) * cols, width - 8), 8)
    left = turned_ref[pl.ds(before, 8), :][8 - halo :]
    right = turned_ref[pl.ds(after, 8), :][:halo]
    if plan.sides == 1:
        beside = jnp.where(me > 0, left, right)
    else:
        beside = jnp.concatenate([left, right], axis=0)
    lines = [
        strip[k * plan.edges : (k + 1) * plan.edges] - beside[:, k : k + 1] * wide[k : k + 1]
        for k in range(count)
    ]
    for slot in range(plan.slots):
        members = []
        for group in range(plan.groups):
            k = group * plan.slots + slot
            members.append(lines[k] if k < count else jnp.zeros((plan.edges, width), F32))
        stack_ref[slot] = jnp.concatenate(members, axis=0)
    pack(plan, step_order(plan)[: len(out_refs)], out_refs, field_ref, stack_ref)


def pack_rest(plan, field_ref, stack_ref, *out_refs):
    pack(plan, step_order(plan)[-len(out_refs) :], out_refs, field_ref, stack_ref)


def pack(plan, steps, out_refs, field_ref, stack_ref):
    chip = lax.axis_index("head") // 2
    count, cols, width, halo = plan.maps, plan.cols, plan.width, plan.halo
    rows, slots = plan.rows, plan.slots
    lane = lax.broadcasted_iota(jnp.int32, (plan.side_rows, cols), 1)
    spare = plan.block_rows - plan.lead - plan.half_rows
    for step, out_ref in zip(steps, out_refs):
        first = partner(chip, step, plan.chips) * 2 * plan.band

        def section(begin, size):
            found = [
                field_ref[pl.ds(8 * k * plan.pitch + first + 8 + begin + r, 8, stride=plan.pitch), :]
                for r in range(size)
                for k in range(plan.sets)
            ]
            for k in range(8 * plan.sets, count):
                found.append(field_ref[pl.ds(k * plan.pitch + first + 8 + begin, size), :])
            return found

        lone, shared = 8 * plan.lone, 8 * plan.shared
        sides = []
        for core in range(2):
            side = jnp.zeros((plan.side_rows, cols), F32)
            for slot in range(slots):
                amount = lax.rem(slot * rows + halo + width - core * plan.band - first, width)
                moved = pltpu.roll(stack_ref[slot], amount, 1)[:, :cols]
                side = jnp.where((lane >= slot * rows) & (lane < (slot + 1) * rows), moved, side)
            sides.append(side)
        pieces = section(0, lone) + sides[:1] + section(lone, shared)
        pieces += section(lone + shared, lone) + sides[1:]
        if spare:
            pieces.append(jnp.zeros((spare, cols), F32))
        out_ref[...] = jnp.concatenate(pieces, axis=0).astype(BF16)


def core_pack(plan, *refs):
    *block_refs, out_ref = refs
    other = 1 - lax.axis_index("head") % 2
    for k, block_ref in enumerate(block_refs):
        out_ref[k] = half(plan, block_ref[...].astype(F32), other).astype(BF16)


def weight_pack(blocks_ref, proj_ref, set_ref, slot_ref, out_ref, map_ref, side_ref):
    map_ref[...] = dot(proj_ref[...], set_ref[...]).astype(BF16)
    side_ref[...] = dot(proj_ref[...], slot_ref[...]).astype(BF16)
    layers, convs, height, breadth = blocks_ref.shape[:4]
    for b in range(layers):
        for m in range(convs):
            out_ref[b * convs + m] = jnp.concatenate(
                [
                    jnp.concatenate(
                        [blocks_ref[b, m, dy, dx].astype(F32) for dy in range(height)], axis=1
                    )
                    for dx in range(breadth)
                ],
                axis=0,
            ).astype(BF16)


def lanes(base, size):
    return pl.ds(base if isinstance(base, int) else pl.multiple_of(base, LANES), size)


def shifted(ref, rows, base, offset, size):
    low = offset // LANES * LANES
    rest = offset - low
    if rest == 0:
        return ref[rows, lanes(base + low, size)]
    return pltpu.roll(ref[rows, lanes(base + low, size + LANES)], size + LANES - rest, 1)[:, :size]


def stack(plan, order, *refs):
    chips = plan.chips
    own_refs, swap_refs = refs[:chips], refs[chips : chips + len(order)]
    refs = refs[chips + len(order) :]
    proj_ref, side_ref, kernel_ref, vector_ref, mask_ref, spots_ref, out_ref = refs[:7]
    maps_ref, others_ref, sides_ref, stream_ref, hidden_ref, taps_ref, logit_ref = refs[7:]
    count, cols, rows, halo = plan.maps, plan.cols, plan.rows, plan.halo
    heads, feat, stride = plan.heads, plan.feat, plan.stride
    head = lax.axis_index("head")
    chip, core = head // 2, head % 2
    lone, shared = 8 * plan.lone, 8 * plan.shared
    wide = 8 * plan.sets

    def rows_of(sections):
        sets, others = [], []
        for begin, size in sections:
            sets += [begin + r * wide for r in range(size)]
            others += [begin + size * wide + r for r in range(0, size, 8)]
        return sets, others, [size for _, size in sections for _ in range(0, size, 8)]

    early = rows_of([(0, lone), (plan.lead, shared)])
    late = rows_of([(0, shared), (shared * count, lone)])

    def spread(block, source):
        def pick(a, b, size):
            if a == b:
                return block[a : a + size]
            return jnp.where(core == 0, block[a : a + size], block[b : b + size])

        for r, (a, b) in enumerate(zip(early[0], late[0])):
            place = pl.multiple_of(source * wide, 8) + r * heads * wide
            maps_ref[pl.ds(pl.multiple_of(place, 8), wide), :] = pick(a, b, wide)
        for k, (a, b, m, n) in enumerate(zip(early[1], late[1], early[2], late[2])):
            for j in range(plan.rest):
                place = (source * plan.rest + j) * rows + 8 * k
                others_ref[pl.ds(pl.multiple_of(place, 8), 8), :] = pick(a + j * m, b + j * n, 8)
        side = pick(lone * count, plan.half_rows - plan.side_rows, plan.side_rows)
        place = pl.multiple_of(source * plan.side_rows, 8)
        sides_ref[pl.ds(place, plan.side_rows), :] = side

    for steps, swap_ref in zip(order, swap_refs):
        for k, step in enumerate(steps):
            source = 2 * partner(chip, step, chips, back=True)
            spread(half(plan, own_refs[step_order(plan).index(step)][...].astype(F32), core), source + core)
            spread(swap_ref[k].astype(F32), source + 1 - core)
    bias = vector_ref[:, 0:1]

    slots, members = plan.slots, heads * plan.groups
    lane = lax.broadcasted_iota(jnp.int32, (members, cols), 1)
    placed = []
    for first in range(0, plan.edges, slots):
        parts = [jnp.zeros((members, cols), F32) for _ in range(slots)]
        for at in range(min(slots, plan.edges - first)):
            value = sides_ref[pl.ds(first + at, members, stride=plan.edges), :]
            keep = (lane >= at * rows) & (lane < (at + 1) * rows)
            for slot in range(slots):
                moved = value
                if at != slot:
                    moved = pltpu.roll(value, ((at - slot) * rows) % cols, 1)
                parts[slot] = jnp.where(keep, moved, parts[slot])
        stacked = jnp.concatenate(parts, axis=0).astype(BF16)
        placed.append((dot(side_ref[...], stacked) + bias).astype(BF16))

    edge = sum(dot(columns, spots_ref[k]) for k, columns in enumerate(placed))

    weight = proj_ref[...]
    spot = lax.broadcasted_iota(jnp.int32, (feat, LANES), 1)
    spans = []

    def compose(tile):
        low, value = tile * LANES, None
        for begin, size, source, lead in spans:
            left, right = max(begin, low), min(begin + size, low + LANES)
            if left >= right:
                continue
            k = (lead + low) // LANES
            piece = source[:, k * LANES : (k + 1) * LANES]
            if value is None:
                value = piece
            else:
                value = jnp.where((spot >= left - low) & (spot < right - low), piece, value)
        here = slice(low, low + LANES)
        stream_ref[:, here] = jnp.where(mask_ref[:, here] > 0, value, 0.0).astype(BF16)

    def gather(chosen):
        blocks = []
        for r in chosen:
            block = maps_ref[r * heads * wide : (r + 1) * heads * wide, :]
            if plan.rest:
                others = others_ref[pl.ds(r, heads * plan.rest, stride=rows), :]
                block = jnp.concatenate([block, others], axis=0)
            blocks.append(block.astype(BF16))
        return jnp.concatenate(blocks, axis=1)

    done = plan.start // LANES
    for r in range(rows + 1):
        begin = plan.start + r * stride - halo
        between = LANES + r * 2 * halo - halo
        spans.append((begin, 2 * halo, edge, between - begin))
        if r < rows:
            if r % plan.batch == 0:
                batch = dot(weight, gather(range(r, min(r + plan.batch, rows)))) + bias
            value = batch[:, r % plan.batch * cols : (r % plan.batch + 1) * cols]
            begin = plan.start + r * stride + halo
            turn = begin % LANES
            value = jnp.concatenate([value, jnp.zeros((feat, LANES), F32)], axis=1)
            spans.append((begin, cols, pltpu.roll(value, turn, 1), turn - begin))
        full = (plan.start + (r + 1) * stride - halo) // LANES if r < rows else done + 1
        while done < full:
            compose(done)
            done += 1
        spans = [span for span in spans if span[0] + span[1] > done * LANES]

    everything = slice(None)
    for n in range(plan.convs):
        source = hidden_ref if n % 2 else stream_ref
        low = (plan.start + (n + 1) * stride) // LANES * LANES
        span = plan.start + (rows - n - 1) * stride - n - 1 - low
        steps = -(-span // plan.chunk)
        size = up(-(-span // steps), LANES)
        offsets = vector_ref[:, n + 1 : n + 2]

        def multiply(base, size):
            window = jnp.concatenate(
                [shifted(source, everything, base, d * stride, size) for d in (-1, 0, 1)], axis=0
            )
            taps_ref[:, lanes(base, size)] = dot(kernel_ref[n], window)

        def finish(base):
            here = lanes(base, size)
            value = taps_ref[feat : 2 * feat, here]
            value = value + shifted(taps_ref, slice(0, feat), base, -1, size)
            value = value + shifted(taps_ref, slice(2 * feat, 3 * feat), base, 1, size)
            value = value + offsets
            keep = mask_ref[:, here] > 0
            if n % 2 == 0:
                value = jnp.where(value > 0, value, jnp.exp(jnp.minimum(value, 0.0)) - 1.0)
                hidden_ref[:, here] = jnp.where(keep, value, 0.0).astype(BF16)
                return
            value = (stream_ref[:, here].astype(F32) + value).astype(BF16)
            if n < plan.convs - 1:
                stream_ref[:, here] = jnp.where(keep, value.astype(F32), 0.0).astype(BF16)
                return
            readout = vector_ref[:, plan.convs + 1 : plan.convs + 2]
            logit_ref[0:1, here] = jnp.sum(value.astype(F32) * readout, axis=0, keepdims=True)

        multiply(low, size + LANES)
        for i in range(steps):
            if i + 1 < steps:
                multiply(low + (i + 1) * size + LANES, size)
            finish(low + i * size)

    for r in range(plan.band):
        begin = plan.start + (r + halo) * stride + halo
        low = begin // LANES * LANES
        out_ref[r : r + 1, :] = shifted(logit_ref, slice(0, 1), low, begin - low, cols)


def call(kernel, name, args, outs, scratch=(), held_out=True):
    held = sum(math.prod(x.shape) * jnp.dtype(x.dtype).itemsize for x in [*args, *outs, *scratch])
    vmem = pl.BlockSpec(memory_space=pltpu.VMEM)
    return pl.pallas_call(
        kernel,
        out_shape=[pltpu.VMEM(x.shape, x.dtype) if held_out else x for x in outs],
        in_specs=[vmem] * len(args),
        out_specs=[vmem] * len(outs),
        scratch_shapes=list(scratch),
        compiler_params=pltpu.CompilerParams(vmem_limit_bytes=held * 5 // 4 + 4 * 1024 * 1024),
        name=name,
    )(*args)


def array(dtype, *shape):
    return jax.ShapeDtypeStruct(shape, dtype)


def on_device(attention, proj_weight, proj_bias, conv_weight, conv_bias, out_weight):
    maps, width, cols = attention.shape
    feat = proj_weight.shape[0]
    blocks, convs = conv_weight.shape[:2]
    tiles, heads = lax.axis_size("tile"), lax.axis_size("head")
    plan = Plan(maps, width, cols, tiles, heads, feat, blocks * convs)
    me, band_index = lax.axis_index("tile"), lax.axis_index("head")

    tail, sums, edge = call(
        functools.partial(mirror_pack, plan),
        "mirror_pack",
        [attention],
        [
            array(BF16, tiles - 1, plan.tail_rows, cols),
            array(F32, plan.map_rows, width),
            array(F32, plan.edge_rows, cols),
        ],
    )

    def mirror(block):
        return jnp.stack(
            [
                lax.ppermute(block(s), "tile", [(i, (i + s) % tiles) for i in range(tiles)])
                for s in range(tiles - 1, 0, -1)
            ]
        )

    def facing(s):
        block = lax.dynamic_slice_in_dim(attention, (me + s) % tiles * cols, cols, 1)
        return block.reshape(maps * cols, cols)

    received, tails = mirror(facing), mirror(lambda s: tail[s - 1])

    stride, start = plan.stride, plan.start
    source, index = np.divmod(np.arange(heads * maps), maps)
    wide = 8 * plan.sets
    by_set = np.where(
        index < wide, source * wide + index, heads * wide + source * plan.rest + index - wide
    )
    group, slot = np.divmod(index, plan.slots)
    by_slot = (slot * heads + source) * plan.groups + group
    picks = [
        jnp.asarray(place[:, None] == np.arange(size)[None], BF16)
        for place, size in (
            (by_set, heads * maps),
            (by_slot, plan.slots * heads * plan.groups),
        )
    ]
    kernels, map_weight, side_weight = call(
        weight_pack,
        "weight_pack",
        [conv_weight.transpose(0, 1, 4, 5, 2, 3), proj_weight, *picks],
        [
            array(BF16, plan.convs, 3 * feat, 3 * feat),
            array(BF16, feat, picks[0].shape[1]),
            array(BF16, feat, picks[1].shape[1]),
        ],
    )
    vectors = jnp.concatenate(
        [proj_bias[None], conv_bias.reshape(-1, feat), out_weight[None]], axis=0
    ).T
    spot = np.arange(plan.lanes) - start
    row = band_index * plan.band - plan.halo + (spot // stride).astype(np.int32)
    col = me * cols - plan.halo + (spot % stride).astype(np.int32)
    mask = (row >= 0) & (row < width) & (col >= 0) & (col < width)
    mask = mask.astype(F32)[None]

    key = np.arange(cols)
    member, line = key // plan.rows, key % plan.rows
    lane = np.arange(up(LANES + (plan.rows + 1) * 2 * plan.halo, LANES))
    spots = []
    for first in range(0, plan.edges, plan.slots):
        column = first + member
        fits = (member < plan.slots) & (column < plan.edges)
        left = LANES + line * 2 * plan.halo + column
        right = left + plan.halo
        if plan.sides == 1:
            places = [left, right]
        else:
            places = [np.where(column < plan.halo, left, right - plan.halo)]
        hit = [np.where(fits, place, -1)[:, None] == lane[None] for place in places]
        spots.append(functools.reduce(np.logical_or, hit))
    spots = jnp.asarray(np.stack(spots), BF16)

    chips = plan.chips
    ahead = chips // 4
    *blocks, field, stacks = call(
        functools.partial(correct_pack, plan),
        "correct_pack",
        [attention, received, tails, sums, edge],
        [array(BF16, plan.block_rows, cols)] * ahead
        + [array(F32, maps * plan.pitch, cols), array(F32, plan.slots, plan.side_rows, width)],
        [pltpu.VMEM((width, LANES), F32)],
    )
    blocks += call(
        functools.partial(pack_rest, plan),
        "pack_rest",
        [field, stacks],
        [array(BF16, plan.block_rows, cols)] * (chips - ahead),
    )
    arrived = {}
    for step, block in zip(step_order(plan), blocks):
        pairs = [(i, 2 * partner(i // 2, step, chips) + i % 2) for i in range(heads)]
        arrived[step] = lax.ppermute(block, "head", pairs) if step else block
    steps = step_order(plan)
    early = steps[: chips // 2]
    late = [step for step in steps if step not in early]
    order = [early, late]
    weights = (map_weight, side_weight, kernels, vectors, mask, spots)
    swapped = []
    for steps in order:
        (packed,) = call(
            functools.partial(core_pack, plan),
            "core_pack",
            [arrived[k] for k in steps],
            [array(BF16, len(steps), plan.half_rows, cols)],
        )
        if steps is late:
            packed, weights = lax.optimization_barrier((packed, weights))
        swapped.append(lax.ppermute(packed, "head", [(i, i ^ 1) for i in range(heads)]))

    (logits,) = call(
        functools.partial(stack, plan, order),
        "stack",
        [*arrived.values(), *swapped, *weights],
        [array(F32, plan.band, cols)],
        [
            pltpu.VMEM((heads * 8 * plan.sets * plan.rows, cols), F32),
            pltpu.VMEM(((heads * plan.rest + 1) * plan.rows, cols), F32),
            pltpu.VMEM(((heads + 1) * plan.side_rows, cols), F32),
            pltpu.VMEM((feat, plan.lanes), BF16),
            pltpu.VMEM((feat, plan.lanes), BF16),
            pltpu.VMEM((3 * feat, plan.lanes), F32),
            pltpu.VMEM((8, plan.lanes), F32),
        ],
        held_out=False,
    )
    return logits


def solution(mesh):
    return jax.shard_map(
        on_device,
        mesh=mesh,
        in_specs=(P(("grp", "head"), None, "tile"), P(), P(), P(), P(), P()),
        out_specs=P(("grp", "head"), "tile"),
        check_vma=False,
    )
```

```python
import functools
import math
from typing import NamedTuple

import jax
import jax.numpy as jnp
import numpy as np
from jax import lax
from jax.experimental import pallas as pl
from jax.experimental.pallas import tpu as pltpu
from jax.sharding import PartitionSpec as P

BF16, F32 = jnp.bfloat16, jnp.float32
LANES = 128


def up(value, step):
    return -(-value // step) * step


class Plan(NamedTuple):
    maps: int
    width: int
    cols: int
    tiles: int
    heads: int
    feat: int
    convs: int

    @property
    def halo(self):
        return self.convs

    @property
    def sides(self):
        return min(2, self.tiles - 1)

    @property
    def edges(self):
        return self.sides * self.halo

    @property
    def edge_rows(self):
        return up(self.maps * self.edges, 8)

    @property
    def map_rows(self):
        return up(self.maps, 16)

    @property
    def tail_rows(self):
        return up((1 + self.tiles) * self.edge_rows + self.sum_rows, 16)

    @property
    def sum_rows(self):
        return 3 * self.tiles * 8 * self.sets + up(3 * self.tiles * self.rest, 8)

    @property
    def band(self):
        return self.width // self.heads

    @property
    def rows(self):
        return self.band + 2 * self.halo

    @property
    def slots(self):
        return self.cols // self.rows

    @property
    def groups(self):
        return -(-self.maps // self.slots)

    @property
    def side_rows(self):
        return self.groups * self.edges

    @property
    def sets(self):
        return self.maps // 8

    @property
    def rest(self):
        return self.maps % 8

    @property
    def pitch(self):
        return up(self.width + 24, 2) + 1

    @property
    def chips(self):
        return self.heads // 2

    @property
    def lone(self):
        return self.band // 8

    @property
    def shared(self):
        return 2 * self.halo // 8

    @property
    def group_rows(self):
        return 8 * self.maps

    @property
    def lead(self):
        return self.lone * self.group_rows + self.side_rows

    @property
    def half_rows(self):
        return self.lead + self.shared * self.group_rows

    @property
    def block_rows(self):
        return self.lead + self.half_rows

    @property
    def stride(self):
        return self.cols + 2 * self.halo

    @property
    def start(self):
        return up(self.stride, LANES) - LANES

    @property
    def batch(self):
        return 12

    @property
    def chunk(self):
        return 1536

    @property
    def lanes(self):
        return up(self.start + self.rows * self.stride, LANES) + 4 * self.halo * LANES


def partner(mine, step, count, back=False):
    if count & (count - 1) == 0:
        return mine ^ step
    return (mine - step if back else mine + step) % count


def far_near(plan):
    steps = list(range(plan.chips - 1, 0, -1))
    return steps[: plan.chips // 2], steps[plan.chips // 2 :]


def step_order(plan):
    far, near = far_near(plan)
    middle = len(far) // 2
    return far[:middle] + near + far[middle:] + [0]


def half(plan, block, core):
    return jnp.where(
        core == 0, block[: plan.half_rows], block[plan.lead : plan.lead + plan.half_rows]
    )


def edge_start(plan, tile, side):
    left, right = plan.cols * tile - plan.halo, plan.cols * (tile + 1)
    if plan.sides == 1:
        return jnp.where(tile > 0, left, right)
    return (left, right)[side]


def edge_select(plan, tile, row, position, index):
    hit = None
    for side in range(plan.sides):
        first = index * plan.edges + side * plan.halo
        inside = (row >= first) & (row < first + plan.halo)
        one = inside & (position == row - first + edge_start(plan, tile, side))
        hit = one if hit is None else hit | one
    return hit


def across(a, b):
    return lax.dot_general(a, b, (((1,), (1,)), ((), ())), preferred_element_type=F32)


def dot(a, b):
    return jnp.dot(a, b, preferred_element_type=F32)


def mirror_pack(plan, maps_ref, out_ref, sums_ref, edge_ref):
    me = lax.axis_index("tile")
    count, cols, width, tiles = plan.maps, plan.cols, plan.width, plan.tiles
    head, edge = plan.map_rows, plan.edge_rows

    def pick(rows, span, base, tile, index):
        row = lax.broadcasted_iota(jnp.int32, (rows, span), 0)
        position = lax.broadcasted_iota(jnp.int32, (rows, span), 1) + base
        return edge_select(plan, tile, row, position, index).astype(F32)

    def total(span, index):
        return (lax.broadcasted_iota(jnp.int32, (head, span), 0) == index).astype(F32)

    for shift in range(1, tiles):
        dest = lax.rem(me + shift, tiles)
        by_col = by_row = None
        for index in range(count):
            block = maps_ref[index]
            left = [pick(edge, cols, me * cols, dest, index)]
            upper = [pick(edge, width, 0, dest, index)]
            if shift == 1:
                left.append(total(cols, index))
                upper.append(total(width, index))
                upper.append(pick(edge, width, 0, me, index))
            by_c = across(jnp.concatenate(left, axis=0).astype(BF16), block)
            by_r = dot(jnp.concatenate(upper, axis=0).astype(BF16), block)
            by_col = by_c if by_col is None else by_col + by_c
            by_row = by_r if by_row is None else by_row + by_r
        if shift == 1:
            sums_ref[...] = by_col[edge : edge + head]
            own = pl.ds(pl.multiple_of(me * cols, cols), cols)
            sums_ref[:, own] = sums_ref[:, own] + by_row[edge : edge + head]
            edge_ref[...] = by_row[edge + head :]
            sums = sums_ref[...]
            high = sums.astype(BF16).astype(F32)
            middle = (sums - high).astype(BF16).astype(F32)
            low = sums - high - middle
        pieces = [by_row[:edge]]
        pieces += [by_col[:edge, k * cols : (k + 1) * cols] for k in range(tiles)]
        parts = [
            part[:, k * cols : (k + 1) * cols] for part in (high, middle, low) for k in range(tiles)
        ]
        sets, rest = 8 * plan.sets, plan.rest
        pieces += [part[:sets] for part in parts if sets]
        if rest:
            spare = up(len(parts) * rest, 8)
            row = lax.broadcasted_iota(jnp.int32, (spare, cols), 0)
            others = jnp.zeros((spare, cols), F32)
            for k, part in enumerate(parts):
                for j in range(rest):
                    others = jnp.where(row == k * rest + j, part[sets + j : sets + j + 1], others)
            pieces.append(others)
        used = (1 + tiles) * edge + plan.sum_rows
        if plan.tail_rows > used:
            pieces.append(jnp.zeros((plan.tail_rows - used, cols), F32))
        out_ref[shift - 1] = jnp.concatenate(pieces, axis=0).astype(BF16)


def correct_pack(plan, maps_ref, recv_ref, tail_ref, sums_ref, edge_ref, *refs):
    *out_refs, field_ref, stack_ref, turned_ref = refs
    me = lax.axis_index("tile")
    count, cols, width, tiles = plan.maps, plan.cols, plan.width, plan.tiles
    head, edge, halo = plan.map_rows, plan.edge_rows, plan.halo
    tails = [tail_ref[k].astype(F32) for k in range(tiles - 1)]

    sets, rest = 8 * plan.sets, plan.rest
    line = lax.broadcasted_iota(jnp.int32, (head - sets, cols), 0)

    def sums_of(tail, k):
        base = (1 + tiles) * edge
        begin = base + 3 * tiles * sets + k * rest
        others = jnp.zeros((head - sets, cols), F32)
        for j in range(rest):
            others = jnp.where(line == j, tail[begin + j : begin + j + 1], others)
        return jnp.concatenate([tail[base + k * sets : base + (k + 1) * sets], others], axis=0)

    rowsum = []
    for b in range(tiles):
        value = sums_ref[:, b * cols : (b + 1) * cols]
        for tail in tails:
            parts = [sums_of(tail, k * tiles + b) for k in range(3)]
            value = value + ((parts[0] + parts[1]) + parts[2])
        rowsum.append(value)
    grand = sum(jnp.sum(value, axis=1, keepdims=True) for value in rowsum)
    grand = jnp.where(lax.broadcasted_iota(jnp.int32, (head, 1), 0) < count, grand, 1.0)
    scaled = [value / grand for value in rowsum]
    for b in range(tiles):
        square = jnp.concatenate([rowsum[b], jnp.zeros((LANES - head, cols), F32)], axis=0)
        turned_ref[b * cols : (b + 1) * cols, :] = square.T
    mine = scaled[0]
    for b in range(1, tiles):
        mine = jnp.where(me == b, scaled[b], mine)

    eye = (
        lax.broadcasted_iota(jnp.int32, (cols, cols), 0)
        == lax.broadcasted_iota(jnp.int32, (cols, cols), 1)
    ).astype(F32).astype(BF16)
    margin = 8 + halo
    faces = []
    for b in range(tiles):
        shift = lax.rem(b - me + tiles, tiles)
        other = recv_ref[jnp.maximum(shift - 1, 0)]
        own = [maps_ref[k, b * cols : (b + 1) * cols, :] for k in range(count)]
        faces.append(jnp.where(shift == 0, jnp.concatenate(own, axis=0), other))
    mirrors = across(eye, jnp.concatenate(faces, axis=0))
    for index in range(count):
        origin = index * plan.pitch
        field_ref[origin : origin + margin, :] = jnp.zeros((margin, cols), F32)
        field_ref[origin + margin + width : origin + plan.pitch, :] = jnp.zeros(
            (plan.pitch - margin - width, cols), F32
        )
        for b in range(tiles):
            own = maps_ref[index, b * cols : (b + 1) * cols, :]
            place = (b * count + index) * cols
            mirror = mirrors[:, place : place + cols]
            column = turned_ref[b * cols : (b + 1) * cols, index : index + 1]
            field_ref[origin + margin + b * cols : origin + margin + (b + 1) * cols, :] = (
                own.astype(F32) + mirror - column * mine[index : index + 1]
            )

    strips = []
    for b in range(tiles):
        strip = edge_ref[...]
        for k, tail in enumerate(tails):
            strip = jnp.where(lax.rem(me + k + 1, tiles) == b, tail[:edge], strip)
        for tail in tails:
            strip = strip + tail[(1 + b) * edge : (2 + b) * edge]
        strips.append(strip)
    strip = jnp.concatenate(strips, axis=1)
    wide = jnp.concatenate(scaled, axis=1)
    before = pl.multiple_of(jnp.maximum(me * cols - 8, 0), 8)
    after = pl.multiple_of(jnp.minimum((me + 1) * cols, width - 8), 8)
    left = turned_ref[pl.ds(before, 8), :][8 - halo :]
    right = turned_ref[pl.ds(after, 8), :][:halo]
    if plan.sides == 1:
        beside = jnp.where(me > 0, left, right)
    else:
        beside = jnp.concatenate([left, right], axis=0)
    lines = [
        strip[k * plan.edges : (k + 1) * plan.edges] - beside[:, k : k + 1] * wide[k : k + 1]
        for k in range(count)
    ]
    for slot in range(plan.slots):
        members = []
        for group in range(plan.groups):
            k = group * plan.slots + slot
            members.append(lines[k] if k < count else jnp.zeros((plan.edges, width), F32))
        stack_ref[slot] = jnp.concatenate(members, axis=0)
    pack(plan, step_order(plan)[: len(out_refs)], out_refs, field_ref, stack_ref)


def pack_rest(plan, field_ref, stack_ref, *out_refs):
    pack(plan, step_order(plan)[-len(out_refs) :], out_refs, field_ref, stack_ref)


def pack(plan, steps, out_refs, field_ref, stack_ref):
    chip = lax.axis_index("head") // 2
    count, cols, width, halo = plan.maps, plan.cols, plan.width, plan.halo
    rows, slots = plan.rows, plan.slots
    lane = lax.broadcasted_iota(jnp.int32, (plan.side_rows, cols), 1)
    spare = plan.block_rows - plan.lead - plan.half_rows
    for step, out_ref in zip(steps, out_refs):
        first = partner(chip, step, plan.chips) * 2 * plan.band

        def section(begin, size):
            found = [
                field_ref[pl.ds(8 * k * plan.pitch + first + 8 + begin + r, 8, stride=plan.pitch), :]
                for r in range(size)
                for k in range(plan.sets)
            ]
            for k in range(8 * plan.sets, count):
                found.append(field_ref[pl.ds(k * plan.pitch + first + 8 + begin, size), :])
            return found

        lone, shared = 8 * plan.lone, 8 * plan.shared
        sides = []
        for core in range(2):
            side = jnp.zeros((plan.side_rows, cols), F32)
            for slot in range(slots):
                amount = lax.rem(slot * rows + halo + width - core * plan.band - first, width)
                moved = pltpu.roll(stack_ref[slot], amount, 1)[:, :cols]
                side = jnp.where((lane >= slot * rows) & (lane < (slot + 1) * rows), moved, side)
            sides.append(side)
        pieces = section(0, lone) + sides[:1] + section(lone, shared)
        pieces += section(lone + shared, lone) + sides[1:]
        if spare:
            pieces.append(jnp.zeros((spare, cols), F32))
        out_ref[...] = jnp.concatenate(pieces, axis=0).astype(BF16)


def core_pack(plan, *refs):
    *block_refs, out_ref = refs
    other = 1 - lax.axis_index("head") % 2
    for k, block_ref in enumerate(block_refs):
        out_ref[k] = half(plan, block_ref[...].astype(F32), other).astype(BF16)


def weight_pack(blocks_ref, proj_ref, set_ref, slot_ref, out_ref, map_ref, side_ref):
    map_ref[...] = dot(proj_ref[...], set_ref[...]).astype(BF16)
    side_ref[...] = dot(proj_ref[...], slot_ref[...]).astype(BF16)
    layers, convs, height, breadth = blocks_ref.shape[:4]
    for b in range(layers):
        for m in range(convs):
            out_ref[b * convs + m] = jnp.concatenate(
                [
                    jnp.concatenate(
                        [blocks_ref[b, m, dy, dx].astype(F32) for dy in range(height)], axis=1
                    )
                    for dx in range(breadth)
                ],
                axis=0,
            ).astype(BF16)


def lanes(base, size):
    return pl.ds(base if isinstance(base, int) else pl.multiple_of(base, LANES), size)


def shifted(ref, rows, base, offset, size):
    low = offset // LANES * LANES
    rest = offset - low
    if rest == 0:
        return ref[rows, lanes(base + low, size)]
    return pltpu.roll(ref[rows, lanes(base + low, size + LANES)], size + LANES - rest, 1)[:, :size]


def stack(plan, order, *refs):
    chips = plan.chips
    own_refs, swap_refs = refs[:chips], refs[chips : chips + len(order)]
    refs = refs[chips + len(order) :]
    proj_ref, side_ref, kernel_ref, vector_ref, mask_ref, spots_ref, out_ref = refs[:7]
    maps_ref, others_ref, sides_ref, stream_ref, hidden_ref, taps_ref, logit_ref = refs[7:]
    count, cols, rows, halo = plan.maps, plan.cols, plan.rows, plan.halo
    heads, feat, stride = plan.heads, plan.feat, plan.stride
    head = lax.axis_index("head")
    chip, core = head // 2, head % 2
    lone, shared = 8 * plan.lone, 8 * plan.shared
    wide = 8 * plan.sets

    def rows_of(sections):
        sets, others = [], []
        for begin, size in sections:
            sets += [begin + r * wide for r in range(size)]
            others += [begin + size * wide + r for r in range(0, size, 8)]
        return sets, others, [size for _, size in sections for _ in range(0, size, 8)]

    early = rows_of([(0, lone), (plan.lead, shared)])
    late = rows_of([(0, shared), (shared * count, lone)])

    def spread(block, source):
        def pick(a, b, size):
            if a == b:
                return block[a : a + size]
            return jnp.where(core == 0, block[a : a + size], block[b : b + size])

        for r, (a, b) in enumerate(zip(early[0], late[0])):
            place = pl.multiple_of(source * wide, 8) + r * heads * wide
            maps_ref[pl.ds(pl.multiple_of(place, 8), wide), :] = pick(a, b, wide)
        for k, (a, b, m, n) in enumerate(zip(early[1], late[1], early[2], late[2])):
            for j in range(plan.rest):
                place = (source * plan.rest + j) * rows + 8 * k
                others_ref[pl.ds(pl.multiple_of(place, 8), 8), :] = pick(a + j * m, b + j * n, 8)
        side = pick(lone * count, plan.half_rows - plan.side_rows, plan.side_rows)
        place = pl.multiple_of(source * plan.side_rows, 8)
        sides_ref[pl.ds(place, plan.side_rows), :] = side

    for steps, swap_ref in zip(order, swap_refs):
        for k, step in enumerate(steps):
            source = 2 * partner(chip, step, chips, back=True)
            spread(half(plan, own_refs[step_order(plan).index(step)][...].astype(F32), core), source + core)
            spread(swap_ref[k].astype(F32), source + 1 - core)
    bias = vector_ref[:, 0:1]

    slots, members = plan.slots, heads * plan.groups
    lane = lax.broadcasted_iota(jnp.int32, (members, cols), 1)
    placed = []
    for first in range(0, plan.edges, slots):
        parts = [jnp.zeros((members, cols), F32) for _ in range(slots)]
        for at in range(min(slots, plan.edges - first)):
            value = sides_ref[pl.ds(first + at, members, stride=plan.edges), :]
            keep = (lane >= at * rows) & (lane < (at + 1) * rows)
            for slot in range(slots):
                moved = value
                if at != slot:
                    moved = pltpu.roll(value, ((at - slot) * rows) % cols, 1)
                parts[slot] = jnp.where(keep, moved, parts[slot])
        stacked = jnp.concatenate(parts, axis=0).astype(BF16)
        placed.append((dot(side_ref[...], stacked) + bias).astype(BF16))

    edge = sum(dot(columns, spots_ref[k]) for k, columns in enumerate(placed))

    weight = proj_ref[...]
    spot = lax.broadcasted_iota(jnp.int32, (feat, LANES), 1)
    spans = []

    def compose(tile):
        low, value = tile * LANES, None
        for begin, size, source, lead in spans:
            left, right = max(begin, low), min(begin + size, low + LANES)
            if left >= right:
                continue
            k = (lead + low) // LANES
            piece = source[:, k * LANES : (k + 1) * LANES]
            if value is None:
                value = piece
            else:
                value = jnp.where((spot >= left - low) & (spot < right - low), piece, value)
        here = slice(low, low + LANES)
        stream_ref[:, here] = jnp.where(mask_ref[:, here] > 0, value, 0.0).astype(BF16)

    def gather(chosen):
        blocks = []
        for r in chosen:
            block = maps_ref[r * heads * wide : (r + 1) * heads * wide, :]
            if plan.rest:
                others = others_ref[pl.ds(r, heads * plan.rest, stride=rows), :]
                block = jnp.concatenate([block, others], axis=0)
            blocks.append(block.astype(BF16))
        return jnp.concatenate(blocks, axis=1)

    done = plan.start // LANES
    for r in range(rows + 1):
        begin = plan.start + r * stride - halo
        between = LANES + r * 2 * halo - halo
        spans.append((begin, 2 * halo, edge, between - begin))
        if r < rows:
            if r % plan.batch == 0:
                batch = dot(weight, gather(range(r, min(r + plan.batch, rows)))) + bias
            value = batch[:, r % plan.batch * cols : (r % plan.batch + 1) * cols]
            begin = plan.start + r * stride + halo
            turn = begin % LANES
            value = jnp.concatenate([value, jnp.zeros((feat, LANES), F32)], axis=1)
            spans.append((begin, cols, pltpu.roll(value, turn, 1), turn - begin))
        full = (plan.start + (r + 1) * stride - halo) // LANES if r < rows else done + 1
        while done < full:
            compose(done)
            done += 1
        spans = [span for span in spans if span[0] + span[1] > done * LANES]

    everything = slice(None)
    for n in range(plan.convs):
        source = hidden_ref if n % 2 else stream_ref
        low = (plan.start + (n + 1) * stride) // LANES * LANES
        span = plan.start + (rows - n - 1) * stride - n - 1 - low
        steps = -(-span // plan.chunk)
        size = up(-(-span // steps), LANES)
        offsets = vector_ref[:, n + 1 : n + 2]

        def multiply(base, size):
            window = jnp.concatenate(
                [shifted(source, everything, base, d * stride, size) for d in (-1, 0, 1)], axis=0
            )
            taps_ref[:, lanes(base, size)] = dot(kernel_ref[n], window)

        def finish(base):
            here = lanes(base, size)
            value = taps_ref[feat : 2 * feat, here]
            value = value + shifted(taps_ref, slice(0, feat), base, -1, size)
            value = value + shifted(taps_ref, slice(2 * feat, 3 * feat), base, 1, size)
            value = value + offsets
            keep = mask_ref[:, here] > 0
            if n % 2 == 0:
                value = jnp.where(value > 0, value, jnp.exp(jnp.minimum(value, 0.0)) - 1.0)
                hidden_ref[:, here] = jnp.where(keep, value, 0.0).astype(BF16)
                return
            value = (stream_ref[:, here].astype(F32) + value).astype(BF16)
            if n < plan.convs - 1:
                stream_ref[:, here] = jnp.where(keep, value.astype(F32), 0.0).astype(BF16)
                return
            readout = vector_ref[:, plan.convs + 1 : plan.convs + 2]
            logit_ref[0:1, here] = jnp.sum(value.astype(F32) * readout, axis=0, keepdims=True)

        multiply(low, size + LANES)
        for i in range(steps):
            if i + 1 < steps:
                multiply(low + (i + 1) * size + LANES, size)
            finish(low + i * size)

    for r in range(plan.band):
        begin = plan.start + (r + halo) * stride + halo
        low = begin // LANES * LANES
        out_ref[r : r + 1, :] = shifted(logit_ref, slice(0, 1), low, begin - low, cols)


def call(kernel, name, args, outs, scratch=(), held_out=True):
    held = sum(math.prod(x.shape) * jnp.dtype(x.dtype).itemsize for x in [*args, *outs, *scratch])
    vmem = pl.BlockSpec(memory_space=pltpu.VMEM)
    return pl.pallas_call(
        kernel,
        out_shape=[pltpu.VMEM(x.shape, x.dtype) if held_out else x for x in outs],
        in_specs=[vmem] * len(args),
        out_specs=[vmem] * len(outs),
        scratch_shapes=list(scratch),
        compiler_params=pltpu.CompilerParams(vmem_limit_bytes=held * 5 // 4 + 4 * 1024 * 1024),
        name=name,
    )(*args)


def array(dtype, *shape):
    return jax.ShapeDtypeStruct(shape, dtype)


def on_device(attention, proj_weight, proj_bias, conv_weight, conv_bias, out_weight):
    maps, width, cols = attention.shape
    feat = proj_weight.shape[0]
    blocks, convs = conv_weight.shape[:2]
    tiles, heads = lax.axis_size("tile"), lax.axis_size("head")
    plan = Plan(maps, width, cols, tiles, heads, feat, blocks * convs)
    me, band_index = lax.axis_index("tile"), lax.axis_index("head")

    tail, sums, edge = call(
        functools.partial(mirror_pack, plan),
        "mirror_pack",
        [attention],
        [
            array(BF16, tiles - 1, plan.tail_rows, cols),
            array(F32, plan.map_rows, width),
            array(F32, plan.edge_rows, cols),
        ],
    )

    def mirror(block):
        return jnp.stack(
            [
                lax.ppermute(block(s), "tile", [(i, (i + s) % tiles) for i in range(tiles)])
                for s in range(tiles - 1, 0, -1)
            ]
        )

    def facing(s):
        block = lax.dynamic_slice_in_dim(attention, (me + s) % tiles * cols, cols, 1)
        return block.reshape(maps * cols, cols)

    received, tails = mirror(facing), mirror(lambda s: tail[s - 1])

    stride, start = plan.stride, plan.start
    source, index = np.divmod(np.arange(heads * maps), maps)
    wide = 8 * plan.sets
    by_set = np.where(
        index < wide, source * wide + index, heads * wide + source * plan.rest + index - wide
    )
    group, slot = np.divmod(index, plan.slots)
    by_slot = (slot * heads + source) * plan.groups + group
    picks = [
        jnp.asarray(place[:, None] == np.arange(size)[None], BF16)
        for place, size in (
            (by_set, heads * maps),
            (by_slot, plan.slots * heads * plan.groups),
        )
    ]
    kernels, map_weight, side_weight = call(
        weight_pack,
        "weight_pack",
        [conv_weight.transpose(0, 1, 4, 5, 2, 3), proj_weight, *picks],
        [
            array(BF16, plan.convs, 3 * feat, 3 * feat),
            array(BF16, feat, picks[0].shape[1]),
            array(BF16, feat, picks[1].shape[1]),
        ],
    )
    vectors = jnp.concatenate(
        [proj_bias[None], conv_bias.reshape(-1, feat), out_weight[None]], axis=0
    ).T
    spot = np.arange(plan.lanes) - start
    row = band_index * plan.band - plan.halo + (spot // stride).astype(np.int32)
    col = me * cols - plan.halo + (spot % stride).astype(np.int32)
    mask = (row >= 0) & (row < width) & (col >= 0) & (col < width)
    mask = mask.astype(F32)[None]

    key = np.arange(cols)
    member, line = key // plan.rows, key % plan.rows
    lane = np.arange(up(LANES + (plan.rows + 1) * 2 * plan.halo, LANES))
    spots = []
    for first in range(0, plan.edges, plan.slots):
        column = first + member
        fits = (member < plan.slots) & (column < plan.edges)
        left = LANES + line * 2 * plan.halo + column
        right = left + plan.halo
        if plan.sides == 1:
            places = [left, right]
        else:
            places = [np.where(column < plan.halo, left, right - plan.halo)]
        hit = [np.where(fits, place, -1)[:, None] == lane[None] for place in places]
        spots.append(functools.reduce(np.logical_or, hit))
    spots = jnp.asarray(np.stack(spots), BF16)

    chips = plan.chips
    ahead = chips // 4
    *blocks, field, stacks = call(
        functools.partial(correct_pack, plan),
        "correct_pack",
        [attention, received, tails, sums, edge],
        [array(BF16, plan.block_rows, cols)] * ahead
        + [array(F32, maps * plan.pitch, cols), array(F32, plan.slots, plan.side_rows, width)],
        [pltpu.VMEM((width, LANES), F32)],
    )
    blocks += call(
        functools.partial(pack_rest, plan),
        "pack_rest",
        [field, stacks],
        [array(BF16, plan.block_rows, cols)] * (chips - ahead),
    )
    arrived = {}
    for step, block in zip(step_order(plan), blocks):
        pairs = [(i, 2 * partner(i // 2, step, chips) + i % 2) for i in range(heads)]
        arrived[step] = lax.ppermute(block, "head", pairs) if step else block
    steps = step_order(plan)
    early = steps[: chips // 2]
    late = [step for step in steps if step not in early]
    order = [early, late]
    weights = (map_weight, side_weight, kernels, vectors, mask, spots)
    swapped = []
    for steps in order:
        (packed,) = call(
            functools.partial(core_pack, plan),
            "core_pack",
            [arrived[k] for k in steps],
            [array(BF16, len(steps), plan.half_rows, cols)],
        )
        if steps is late:
            packed, weights = lax.optimization_barrier((packed, weights))
        swapped.append(lax.ppermute(packed, "head", [(i, i ^ 1) for i in range(heads)]))

    (logits,) = call(
        functools.partial(stack, plan, order),
        "stack",
        [*arrived.values(), *swapped, *weights],
        [array(F32, plan.band, cols)],
        [
            pltpu.VMEM((heads * 8 * plan.sets * plan.rows, cols), F32),
            pltpu.VMEM(((heads * plan.rest + 1) * plan.rows, cols), F32),
            pltpu.VMEM(((heads + 1) * plan.side_rows, cols), F32),
            pltpu.VMEM((feat, plan.lanes), BF16),
            pltpu.VMEM((feat, plan.lanes), BF16),
            pltpu.VMEM((3 * feat, plan.lanes), F32),
            pltpu.VMEM((8, plan.lanes), F32),
        ],
        held_out=False,
    )
    return logits


def solution(mesh):
    return jax.shard_map(
        on_device,
        mesh=mesh,
        in_specs=(P(("grp", "head"), None, "tile"), P(), P(), P(), P(), P()),
        out_specs=P(("grp", "head"), "tile"),
        check_vma=False,
    )
```

```python
import functools
import math
from typing import NamedTuple

import jax
import jax.numpy as jnp
import numpy as np
from jax import lax
from jax.experimental import pallas as pl
from jax.experimental.pallas import tpu as pltpu
from jax.sharding import PartitionSpec as P

BF16, F32 = jnp.bfloat16, jnp.float32
LANES = 128


def up(value, step):
    return -(-value // step) * step


class Plan(NamedTuple):
    maps: int
    width: int
    cols: int
    tiles: int
    heads: int
    feat: int
    convs: int

    @property
    def halo(self):
        return self.convs

    @property
    def sides(self):
        return min(2, self.tiles - 1)

    @property
    def edges(self):
        return self.sides * self.halo

    @property
    def edge_rows(self):
        return up(self.maps * self.edges, 8)

    @property
    def map_rows(self):
        return up(self.maps, 16)

    @property
    def tail_rows(self):
        return up((1 + self.tiles) * self.edge_rows + self.sum_rows, 16)

    @property
    def sum_rows(self):
        return 3 * self.tiles * 8 * self.sets + up(3 * self.tiles * self.rest, 8)

    @property
    def band(self):
        return self.width // self.heads

    @property
    def rows(self):
        return self.band + 2 * self.halo

    @property
    def slots(self):
        return self.cols // self.rows

    @property
    def groups(self):
        return -(-self.maps // self.slots)

    @property
    def side_rows(self):
        return self.groups * self.edges

    @property
    def sets(self):
        return self.maps // 8

    @property
    def rest(self):
        return self.maps % 8

    @property
    def pitch(self):
        return up(self.width + 24, 2) + 1

    @property
    def chips(self):
        return self.heads // 2

    @property
    def lone(self):
        return self.band // 8

    @property
    def shared(self):
        return 2 * self.halo // 8

    @property
    def group_rows(self):
        return 8 * self.maps

    @property
    def lead(self):
        return self.lone * self.group_rows + self.side_rows

    @property
    def half_rows(self):
        return self.lead + self.shared * self.group_rows

    @property
    def block_rows(self):
        return self.lead + self.half_rows

    @property
    def stride(self):
        return self.cols + 2 * self.halo

    @property
    def start(self):
        return up(self.stride, LANES) - LANES

    @property
    def batch(self):
        return 12

    @property
    def chunk(self):
        return 1536

    @property
    def lanes(self):
        return up(self.start + self.rows * self.stride, LANES) + 4 * self.halo * LANES


def partner(mine, step, count, back=False):
    if count & (count - 1) == 0:
        return mine ^ step
    return (mine - step if back else mine + step) % count


def far_near(plan):
    steps = list(range(plan.chips - 1, 0, -1))
    return steps[: plan.chips // 2], steps[plan.chips // 2 :]


def step_order(plan):
    far, near = far_near(plan)
    middle = len(far) // 2
    return far[:middle] + near + far[middle:] + [0]


def half(plan, block, core):
    return jnp.where(
        core == 0, block[: plan.half_rows], block[plan.lead : plan.lead + plan.half_rows]
    )


def edge_start(plan, tile, side):
    left, right = plan.cols * tile - plan.halo, plan.cols * (tile + 1)
    if plan.sides == 1:
        return jnp.where(tile > 0, left, right)
    return (left, right)[side]


def edge_select(plan, tile, row, position, index):
    hit = None
    for side in range(plan.sides):
        first = index * plan.edges + side * plan.halo
        inside = (row >= first) & (row < first + plan.halo)
        one = inside & (position == row - first + edge_start(plan, tile, side))
        hit = one if hit is None else hit | one
    return hit


def across(a, b):
    return lax.dot_general(a, b, (((1,), (1,)), ((), ())), preferred_element_type=F32)


def dot(a, b):
    return jnp.dot(a, b, preferred_element_type=F32)


def mirror_pack(plan, maps_ref, out_ref, sums_ref, edge_ref):
    me = lax.axis_index("tile")
    count, cols, width, tiles = plan.maps, plan.cols, plan.width, plan.tiles
    head, edge = plan.map_rows, plan.edge_rows

    def pick(rows, span, base, tile, index):
        row = lax.broadcasted_iota(jnp.int32, (rows, span), 0)
        position = lax.broadcasted_iota(jnp.int32, (rows, span), 1) + base
        return edge_select(plan, tile, row, position, index).astype(F32)

    def total(span, index):
        return (lax.broadcasted_iota(jnp.int32, (head, span), 0) == index).astype(F32)

    for shift in range(1, tiles):
        dest = lax.rem(me + shift, tiles)
        by_col = by_row = None
        for index in range(count):
            block = maps_ref[index]
            left = [pick(edge, cols, me * cols, dest, index)]
            upper = [pick(edge, width, 0, dest, index)]
            if shift == 1:
                left.append(total(cols, index))
                upper.append(total(width, index))
                upper.append(pick(edge, width, 0, me, index))
            by_c = across(jnp.concatenate(left, axis=0).astype(BF16), block)
            by_r = dot(jnp.concatenate(upper, axis=0).astype(BF16), block)
            by_col = by_c if by_col is None else by_col + by_c
            by_row = by_r if by_row is None else by_row + by_r
        if shift == 1:
            sums_ref[...] = by_col[edge : edge + head]
            own = pl.ds(pl.multiple_of(me * cols, cols), cols)
            sums_ref[:, own] = sums_ref[:, own] + by_row[edge : edge + head]
            edge_ref[...] = by_row[edge + head :]
            sums = sums_ref[...]
            high = sums.astype(BF16).astype(F32)
            middle = (sums - high).astype(BF16).astype(F32)
            low = sums - high - middle
        pieces = [by_row[:edge]]
        pieces += [by_col[:edge, k * cols : (k + 1) * cols] for k in range(tiles)]
        parts = [
            part[:, k * cols : (k + 1) * cols] for part in (high, middle, low) for k in range(tiles)
        ]
        sets, rest = 8 * plan.sets, plan.rest
        pieces += [part[:sets] for part in parts if sets]
        if rest:
            spare = up(len(parts) * rest, 8)
            row = lax.broadcasted_iota(jnp.int32, (spare, cols), 0)
            others = jnp.zeros((spare, cols), F32)
            for k, part in enumerate(parts):
                for j in range(rest):
                    others = jnp.where(row == k * rest + j, part[sets + j : sets + j + 1], others)
            pieces.append(others)
        used = (1 + tiles) * edge + plan.sum_rows
        if plan.tail_rows > used:
            pieces.append(jnp.zeros((plan.tail_rows - used, cols), F32))
        out_ref[shift - 1] = jnp.concatenate(pieces, axis=0).astype(BF16)


def correct_pack(plan, maps_ref, recv_ref, tail_ref, sums_ref, edge_ref, *refs):
    *out_refs, field_ref, stack_ref, turned_ref = refs
    me = lax.axis_index("tile")
    count, cols, width, tiles = plan.maps, plan.cols, plan.width, plan.tiles
    head, edge, halo = plan.map_rows, plan.edge_rows, plan.halo
    tails = [tail_ref[k].astype(F32) for k in range(tiles - 1)]

    sets, rest = 8 * plan.sets, plan.rest
    line = lax.broadcasted_iota(jnp.int32, (head - sets, cols), 0)

    def sums_of(tail, k):
        base = (1 + tiles) * edge
        begin = base + 3 * tiles * sets + k * rest
        others = jnp.zeros((head - sets, cols), F32)
        for j in range(rest):
            others = jnp.where(line == j, tail[begin + j : begin + j + 1], others)
        return jnp.concatenate([tail[base + k * sets : base + (k + 1) * sets], others], axis=0)

    rowsum = []
    for b in range(tiles):
        value = sums_ref[:, b * cols : (b + 1) * cols]
        for tail in tails:
            parts = [sums_of(tail, k * tiles + b) for k in range(3)]
            value = value + ((parts[0] + parts[1]) + parts[2])
        rowsum.append(value)
    grand = sum(jnp.sum(value, axis=1, keepdims=True) for value in rowsum)
    grand = jnp.where(lax.broadcasted_iota(jnp.int32, (head, 1), 0) < count, grand, 1.0)
    scaled = [value / grand for value in rowsum]
    for b in range(tiles):
        square = jnp.concatenate([rowsum[b], jnp.zeros((LANES - head, cols), F32)], axis=0)
        turned_ref[b * cols : (b + 1) * cols, :] = square.T
    mine = scaled[0]
    for b in range(1, tiles):
        mine = jnp.where(me == b, scaled[b], mine)

    eye = (
        lax.broadcasted_iota(jnp.int32, (cols, cols), 0)
        == lax.broadcasted_iota(jnp.int32, (cols, cols), 1)
    ).astype(F32).astype(BF16)
    margin = 8 + halo
    faces = []
    for b in range(tiles):
        shift = lax.rem(b - me + tiles, tiles)
        other = recv_ref[jnp.maximum(shift - 1, 0)]
        own = [maps_ref[k, b * cols : (b + 1) * cols, :] for k in range(count)]
        faces.append(jnp.where(shift == 0, jnp.concatenate(own, axis=0), other))
    mirrors = across(eye, jnp.concatenate(faces, axis=0))
    for index in range(count):
        origin = index * plan.pitch
        field_ref[origin : origin + margin, :] = jnp.zeros((margin, cols), F32)
        field_ref[origin + margin + width : origin + plan.pitch, :] = jnp.zeros(
            (plan.pitch - margin - width, cols), F32
        )
        for b in range(tiles):
            own = maps_ref[index, b * cols : (b + 1) * cols, :]
            place = (b * count + index) * cols
            mirror = mirrors[:, place : place + cols]
            column = turned_ref[b * cols : (b + 1) * cols, index : index + 1]
            field_ref[origin + margin + b * cols : origin + margin + (b + 1) * cols, :] = (
                own.astype(F32) + mirror - column * mine[index : index + 1]
            )

    strips = []
    for b in range(tiles):
        strip = edge_ref[...]
        for k, tail in enumerate(tails):
            strip = jnp.where(lax.rem(me + k + 1, tiles) == b, tail[:edge], strip)
        for tail in tails:
            strip = strip + tail[(1 + b) * edge : (2 + b) * edge]
        strips.append(strip)
    strip = jnp.concatenate(strips, axis=1)
    wide = jnp.concatenate(scaled, axis=1)
    before = pl.multiple_of(jnp.maximum(me * cols - 8, 0), 8)
    after = pl.multiple_of(jnp.minimum((me + 1) * cols, width - 8), 8)
    left = turned_ref[pl.ds(before, 8), :][8 - halo :]
    right = turned_ref[pl.ds(after, 8), :][:halo]
    if plan.sides == 1:
        beside = jnp.where(me > 0, left, right)
    else:
        beside = jnp.concatenate([left, right], axis=0)
    lines = [
        strip[k * plan.edges : (k + 1) * plan.edges] - beside[:, k : k + 1] * wide[k : k + 1]
        for k in range(count)
    ]
    for slot in range(plan.slots):
        members = []
        for group in range(plan.groups):
            k = group * plan.slots + slot
            members.append(lines[k] if k < count else jnp.zeros((plan.edges, width), F32))
        stack_ref[slot] = jnp.concatenate(members, axis=0)
    pack(plan, step_order(plan)[: len(out_refs)], out_refs, field_ref, stack_ref)


def pack_rest(plan, field_ref, stack_ref, *out_refs):
    pack(plan, step_order(plan)[-len(out_refs) :], out_refs, field_ref, stack_ref)


def pack(plan, steps, out_refs, field_ref, stack_ref):
    chip = lax.axis_index("head") // 2
    count, cols, width, halo = plan.maps, plan.cols, plan.width, plan.halo
    rows, slots = plan.rows, plan.slots
    lane = lax.broadcasted_iota(jnp.int32, (plan.side_rows, cols), 1)
    spare = plan.block_rows - plan.lead - plan.half_rows
    for step, out_ref in zip(steps, out_refs):
        first = partner(chip, step, plan.chips) * 2 * plan.band

        def section(begin, size):
            found = [
                field_ref[pl.ds(8 * k * plan.pitch + first + 8 + begin + r, 8, stride=plan.pitch), :]
                for r in range(size)
                for k in range(plan.sets)
            ]
            for k in range(8 * plan.sets, count):
                found.append(field_ref[pl.ds(k * plan.pitch + first + 8 + begin, size), :])
            return found

        lone, shared = 8 * plan.lone, 8 * plan.shared
        sides = []
        for core in range(2):
            side = jnp.zeros((plan.side_rows, cols), F32)
            for slot in range(slots):
                amount = lax.rem(slot * rows + halo + width - core * plan.band - first, width)
                moved = pltpu.roll(stack_ref[slot], amount, 1)[:, :cols]
                side = jnp.where((lane >= slot * rows) & (lane < (slot + 1) * rows), moved, side)
            sides.append(side)
        pieces = section(0, lone) + sides[:1] + section(lone, shared)
        pieces += section(lone + shared, lone) + sides[1:]
        if spare:
            pieces.append(jnp.zeros((spare, cols), F32))
        out_ref[...] = jnp.concatenate(pieces, axis=0).astype(BF16)


def core_pack(plan, *refs):
    *block_refs, out_ref = refs
    other = 1 - lax.axis_index("head") % 2
    for k, block_ref in enumerate(block_refs):
        out_ref[k] = half(plan, block_ref[...].astype(F32), other).astype(BF16)


def weight_pack(blocks_ref, proj_ref, set_ref, slot_ref, out_ref, map_ref, side_ref):
    map_ref[...] = dot(proj_ref[...], set_ref[...]).astype(BF16)
    side_ref[...] = dot(proj_ref[...], slot_ref[...]).astype(BF16)
    layers, convs, height, breadth = blocks_ref.shape[:4]
    for b in range(layers):
        for m in range(convs):
            out_ref[b * convs + m] = jnp.concatenate(
                [
                    jnp.concatenate(
                        [blocks_ref[b, m, dy, dx].astype(F32) for dy in range(height)], axis=1
                    )
                    for dx in range(breadth)
                ],
                axis=0,
            ).astype(BF16)


def lanes(base, size):
    return pl.ds(base if isinstance(base, int) else pl.multiple_of(base, LANES), size)


def shifted(ref, rows, base, offset, size):
    low = offset // LANES * LANES
    rest = offset - low
    if rest == 0:
        return ref[rows, lanes(base + low, size)]
    return pltpu.roll(ref[rows, lanes(base + low, size + LANES)], size + LANES - rest, 1)[:, :size]


def stack(plan, order, *refs):
    chips = plan.chips
    own_refs, swap_refs = refs[:chips], refs[chips : chips + len(order)]
    refs = refs[chips + len(order) :]
    proj_ref, side_ref, kernel_ref, vector_ref, mask_ref, spots_ref, out_ref = refs[:7]
    maps_ref, others_ref, sides_ref, stream_ref, hidden_ref, taps_ref, logit_ref = refs[7:]
    count, cols, rows, halo = plan.maps, plan.cols, plan.rows, plan.halo
    heads, feat, stride = plan.heads, plan.feat, plan.stride
    head = lax.axis_index("head")
    chip, core = head // 2, head % 2
    lone, shared = 8 * plan.lone, 8 * plan.shared
    wide = 8 * plan.sets

    def rows_of(sections):
        sets, others = [], []
        for begin, size in sections:
            sets += [begin + r * wide for r in range(size)]
            others += [begin + size * wide + r for r in range(0, size, 8)]
        return sets, others, [size for _, size in sections for _ in range(0, size, 8)]

    early = rows_of([(0, lone), (plan.lead, shared)])
    late = rows_of([(0, shared), (shared * count, lone)])

    def spread(block, source):
        def pick(a, b, size):
            if a == b:
                return block[a : a + size]
            return jnp.where(core == 0, block[a : a + size], block[b : b + size])

        for r, (a, b) in enumerate(zip(early[0], late[0])):
            place = pl.multiple_of(source * wide, 8) + r * heads * wide
            maps_ref[pl.ds(pl.multiple_of(place, 8), wide), :] = pick(a, b, wide)
        for k, (a, b, m, n) in enumerate(zip(early[1], late[1], early[2], late[2])):
            for j in range(plan.rest):
                place = (source * plan.rest + j) * rows + 8 * k
                others_ref[pl.ds(pl.multiple_of(place, 8), 8), :] = pick(a + j * m, b + j * n, 8)
        side = pick(lone * count, plan.half_rows - plan.side_rows, plan.side_rows)
        place = pl.multiple_of(source * plan.side_rows, 8)
        sides_ref[pl.ds(place, plan.side_rows), :] = side

    for steps, swap_ref in zip(order, swap_refs):
        for k, step in enumerate(steps):
            source = 2 * partner(chip, step, chips, back=True)
            spread(half(plan, own_refs[step_order(plan).index(step)][...].astype(F32), core), source + core)
            spread(swap_ref[k].astype(F32), source + 1 - core)
    bias = vector_ref[:, 0:1]

    slots, members = plan.slots, heads * plan.groups
    lane = lax.broadcasted_iota(jnp.int32, (members, cols), 1)
    placed = []
    for first in range(0, plan.edges, slots):
        parts = [jnp.zeros((members, cols), F32) for _ in range(slots)]
        for at in range(min(slots, plan.edges - first)):
            value = sides_ref[pl.ds(first + at, members, stride=plan.edges), :]
            keep = (lane >= at * rows) & (lane < (at + 1) * rows)
            for slot in range(slots):
                moved = value
                if at != slot:
                    moved = pltpu.roll(value, ((at - slot) * rows) % cols, 1)
                parts[slot] = jnp.where(keep, moved, parts[slot])
        stacked = jnp.concatenate(parts, axis=0).astype(BF16)
        placed.append((dot(side_ref[...], stacked) + bias).astype(BF16))

    edge = sum(dot(columns, spots_ref[k]) for k, columns in enumerate(placed))

    weight = proj_ref[...]
    spot = lax.broadcasted_iota(jnp.int32, (feat, LANES), 1)
    spans = []

    def compose(tile):
        low, value = tile * LANES, None
        for begin, size, source, lead in spans:
            left, right = max(begin, low), min(begin + size, low + LANES)
            if left >= right:
                continue
            k = (lead + low) // LANES
            piece = source[:, k * LANES : (k + 1) * LANES]
            if value is None:
                value = piece
            else:
                value = jnp.where((spot >= left - low) & (spot < right - low), piece, value)
        here = slice(low, low + LANES)
        stream_ref[:, here] = jnp.where(mask_ref[:, here] > 0, value, 0.0).astype(BF16)

    def gather(chosen):
        blocks = []
        for r in chosen:
            block = maps_ref[r * heads * wide : (r + 1) * heads * wide, :]
            if plan.rest:
                others = others_ref[pl.ds(r, heads * plan.rest, stride=rows), :]
                block = jnp.concatenate([block, others], axis=0)
            blocks.append(block.astype(BF16))
        return jnp.concatenate(blocks, axis=1)

    done = plan.start // LANES
    for r in range(rows + 1):
        begin = plan.start + r * stride - halo
        between = LANES + r * 2 * halo - halo
        spans.append((begin, 2 * halo, edge, between - begin))
        if r < rows:
            if r % plan.batch == 0:
                batch = dot(weight, gather(range(r, min(r + plan.batch, rows)))) + bias
            value = batch[:, r % plan.batch * cols : (r % plan.batch + 1) * cols]
            begin = plan.start + r * stride + halo
            turn = begin % LANES
            value = jnp.concatenate([value, jnp.zeros((feat, LANES), F32)], axis=1)
            spans.append((begin, cols, pltpu.roll(value, turn, 1), turn - begin))
        full = (plan.start + (r + 1) * stride - halo) // LANES if r < rows else done + 1
        while done < full:
            compose(done)
            done += 1
        spans = [span for span in spans if span[0] + span[1] > done * LANES]

    everything = slice(None)
    for n in range(plan.convs):
        source = hidden_ref if n % 2 else stream_ref
        low = (plan.start + (n + 1) * stride) // LANES * LANES
        span = plan.start + (rows - n - 1) * stride - n - 1 - low
        steps = -(-span // plan.chunk)
        size = up(-(-span // steps), LANES)
        offsets = vector_ref[:, n + 1 : n + 2]

        def multiply(base, size):
            window = jnp.concatenate(
                [shifted(source, everything, base, d * stride, size) for d in (-1, 0, 1)], axis=0
            )
            taps_ref[:, lanes(base, size)] = dot(kernel_ref[n], window)

        def finish(base):
            here = lanes(base, size)
            value = taps_ref[feat : 2 * feat, here]
            value = value + shifted(taps_ref, slice(0, feat), base, -1, size)
            value = value + shifted(taps_ref, slice(2 * feat, 3 * feat), base, 1, size)
            value = value + offsets
            keep = mask_ref[:, here] > 0
            if n % 2 == 0:
                value = jnp.where(value > 0, value, jnp.exp(jnp.minimum(value, 0.0)) - 1.0)
                hidden_ref[:, here] = jnp.where(keep, value, 0.0).astype(BF16)
                return
            value = (stream_ref[:, here].astype(F32) + value).astype(BF16)
            if n < plan.convs - 1:
                stream_ref[:, here] = jnp.where(keep, value.astype(F32), 0.0).astype(BF16)
                return
            readout = vector_ref[:, plan.convs + 1 : plan.convs + 2]
            logit_ref[0:1, here] = jnp.sum(value.astype(F32) * readout, axis=0, keepdims=True)

        multiply(low, size + LANES)
        for i in range(steps):
            finish(low + i * size)
            if i + 1 < steps:
                multiply(low + (i + 1) * size + LANES, size)

    for r in range(plan.band):
        begin = plan.start + (r + halo) * stride + halo
        low = begin // LANES * LANES
        out_ref[r : r + 1, :] = shifted(logit_ref, slice(0, 1), low, begin - low, cols)


def call(kernel, name, args, outs, scratch=(), held_out=True):
    held = sum(math.prod(x.shape) * jnp.dtype(x.dtype).itemsize for x in [*args, *outs, *scratch])
    vmem = pl.BlockSpec(memory_space=pltpu.VMEM)
    return pl.pallas_call(
        kernel,
        out_shape=[pltpu.VMEM(x.shape, x.dtype) if held_out else x for x in outs],
        in_specs=[vmem] * len(args),
        out_specs=[vmem] * len(outs),
        scratch_shapes=list(scratch),
        compiler_params=pltpu.CompilerParams(vmem_limit_bytes=held * 5 // 4 + 4 * 1024 * 1024),
        name=name,
    )(*args)


def array(dtype, *shape):
    return jax.ShapeDtypeStruct(shape, dtype)


def on_device(attention, proj_weight, proj_bias, conv_weight, conv_bias, out_weight):
    maps, width, cols = attention.shape
    feat = proj_weight.shape[0]
    blocks, convs = conv_weight.shape[:2]
    tiles, heads = lax.axis_size("tile"), lax.axis_size("head")
    plan = Plan(maps, width, cols, tiles, heads, feat, blocks * convs)
    me, band_index = lax.axis_index("tile"), lax.axis_index("head")

    tail, sums, edge = call(
        functools.partial(mirror_pack, plan),
        "mirror_pack",
        [attention],
        [
            array(BF16, tiles - 1, plan.tail_rows, cols),
            array(F32, plan.map_rows, width),
            array(F32, plan.edge_rows, cols),
        ],
    )

    def mirror(block):
        return jnp.stack(
            [
                lax.ppermute(block(s), "tile", [(i, (i + s) % tiles) for i in range(tiles)])
                for s in range(tiles - 1, 0, -1)
            ]
        )

    def facing(s):
        block = lax.dynamic_slice_in_dim(attention, (me + s) % tiles * cols, cols, 1)
        return block.reshape(maps * cols, cols)

    received, tails = mirror(facing), mirror(lambda s: tail[s - 1])

    stride, start = plan.stride, plan.start
    source, index = np.divmod(np.arange(heads * maps), maps)
    wide = 8 * plan.sets
    by_set = np.where(
        index < wide, source * wide + index, heads * wide + source * plan.rest + index - wide
    )
    group, slot = np.divmod(index, plan.slots)
    by_slot = (slot * heads + source) * plan.groups + group
    picks = [
        jnp.asarray(place[:, None] == np.arange(size)[None], BF16)
        for place, size in (
            (by_set, heads * maps),
            (by_slot, plan.slots * heads * plan.groups),
        )
    ]
    kernels, map_weight, side_weight = call(
        weight_pack,
        "weight_pack",
        [conv_weight.transpose(0, 1, 4, 5, 2, 3), proj_weight, *picks],
        [
            array(BF16, plan.convs, 3 * feat, 3 * feat),
            array(BF16, feat, picks[0].shape[1]),
            array(BF16, feat, picks[1].shape[1]),
        ],
    )
    vectors = jnp.concatenate(
        [proj_bias[None], conv_bias.reshape(-1, feat), out_weight[None]], axis=0
    ).T
    spot = np.arange(plan.lanes) - start
    row = band_index * plan.band - plan.halo + (spot // stride).astype(np.int32)
    col = me * cols - plan.halo + (spot % stride).astype(np.int32)
    mask = (row >= 0) & (row < width) & (col >= 0) & (col < width)
    mask = mask.astype(F32)[None]

    key = np.arange(cols)
    member, line = key // plan.rows, key % plan.rows
    lane = np.arange(up(LANES + (plan.rows + 1) * 2 * plan.halo, LANES))
    spots = []
    for first in range(0, plan.edges, plan.slots):
        column = first + member
        fits = (member < plan.slots) & (column < plan.edges)
        left = LANES + line * 2 * plan.halo + column
        right = left + plan.halo
        if plan.sides == 1:
            places = [left, right]
        else:
            places = [np.where(column < plan.halo, left, right - plan.halo)]
        hit = [np.where(fits, place, -1)[:, None] == lane[None] for place in places]
        spots.append(functools.reduce(np.logical_or, hit))
    spots = jnp.asarray(np.stack(spots), BF16)

    chips = plan.chips
    ahead = chips // 4
    *blocks, field, stacks = call(
        functools.partial(correct_pack, plan),
        "correct_pack",
        [attention, received, tails, sums, edge],
        [array(BF16, plan.block_rows, cols)] * ahead
        + [array(F32, maps * plan.pitch, cols), array(F32, plan.slots, plan.side_rows, width)],
        [pltpu.VMEM((width, LANES), F32)],
    )
    blocks += call(
        functools.partial(pack_rest, plan),
        "pack_rest",
        [field, stacks],
        [array(BF16, plan.block_rows, cols)] * (chips - ahead),
    )
    arrived = {}
    for step, block in zip(step_order(plan), blocks):
        pairs = [(i, 2 * partner(i // 2, step, chips) + i % 2) for i in range(heads)]
        arrived[step] = lax.ppermute(block, "head", pairs) if step else block
    steps = step_order(plan)
    early = steps[: chips // 2]
    late = [step for step in steps if step not in early]
    order = [early, late]
    weights = (map_weight, side_weight, kernels, vectors, mask, spots)
    swapped = []
    for steps in order:
        (packed,) = call(
            functools.partial(core_pack, plan),
            "core_pack",
            [arrived[k] for k in steps],
            [array(BF16, len(steps), plan.half_rows, cols)],
        )
        if steps is late:
            packed, weights = lax.optimization_barrier((packed, weights))
        swapped.append(lax.ppermute(packed, "head", [(i, i ^ 1) for i in range(heads)]))

    (logits,) = call(
        functools.partial(stack, plan, order),
        "stack",
        [*arrived.values(), *swapped, *weights],
        [array(F32, plan.band, cols)],
        [
            pltpu.VMEM((heads * 8 * plan.sets * plan.rows, cols), F32),
            pltpu.VMEM(((heads * plan.rest + 1) * plan.rows, cols), F32),
            pltpu.VMEM(((heads + 1) * plan.side_rows, cols), F32),
            pltpu.VMEM((feat, plan.lanes), BF16),
            pltpu.VMEM((feat, plan.lanes), BF16),
            pltpu.VMEM((3 * feat, plan.lanes), F32),
            pltpu.VMEM((8, plan.lanes), F32),
        ],
        held_out=False,
    )
    return logits


def solution(mesh):
    return jax.shard_map(
        on_device,
        mesh=mesh,
        in_specs=(P(("grp", "head"), None, "tile"), P(), P(), P(), P(), P()),
        out_specs=P(("grp", "head"), "tile"),
        check_vma=False,
    )
```
